32 devices in a mesh: dp: 8 (over z, y), fsdp: 4 (over x, core).
Axes of the slice: x: 2, y: 2, z: 4, core: 2. Of those that a mesh axis runs over, the one named last changes fastest.
Arguments:
- tokens: bfloat16 [8, 2064, 1024], P('dp', 'fsdp'), may hold values from -6 to 6
- cotangent: bfloat16 [8, 2064, 1024], P('dp', 'fsdp'), may hold values from -6 to 6
- frame_counts: int32 [8, 2], P('dp'), may hold values from 0 to 8, as said below
- presence: int32 [8, 8, 2], P('dp'), may hold values 0 or 1
- attend_gain: bfloat16 [1024], P('dp'), may hold values from 0.5 to 1.5
- attend_shift: bfloat16 [1024], P('dp'), may hold values from -1.75 to 1.75
- triple_weight: bfloat16 [1024, 3072], P('fsdp', 'dp'), may hold values from -0.1875 to 0.1875
- triple_bias: bfloat16 [3072], P('dp'), may hold values from -3 to 3
- output_weight: bfloat16 [1024, 1024], P('fsdp', 'dp'), may hold values from -0.75 to 0.75
- output_bias: bfloat16 [1024], P('dp'), may hold values from -1.75 to 1.75
- second_gain: bfloat16 [1024], P('dp'), may hold values from 0.5 to 1.5
- second_shift: bfloat16 [1024], P('dp'), may hold values from -1.75 to 1.75
- expand_weight: bfloat16 [1024, 4096], P('fsdp', 'dp'), may hold values from -0.1875 to 0.1875
- expand_bias: bfloat16 [4096], P('dp'), may hold values from -3 to 3
- reduce_weight: bfloat16 [4096, 1024], P('fsdp', 'dp'), may hold values from -0.09375 to 0.09375
- reduce_bias: bfloat16 [1024], P('dp'), may hold values from -1.75 to 1.75
Outputs:
- block_output: bfloat16 [8, 2064, 1024], P('dp', 'fsdp')
- tokens_grad: float32 [8, 2064, 1024], P('dp', 'fsdp')
- attend_gain_grad: float32 [1024], P('dp')
- attend_shift_grad: float32 [1024], P('dp')
- triple_weight_grad: float32 [1024, 3072], P('fsdp', 'dp')
- triple_bias_grad: float32 [3072], P('dp')
- output_weight_grad: float32 [1024, 1024], P('fsdp', 'dp')
- output_bias_grad: float32 [1024], P('dp')
- second_gain_grad: float32 [1024], P('dp')
- second_shift_grad: float32 [1024], P('dp')
- expand_weight_grad: float32 [1024, 4096], P('fsdp', 'dp')
- expand_bias_grad: float32 [4096], P('dp')
- reduce_weight_grad: float32 [4096, 1024], P('fsdp', 'dp')
- reduce_bias_grad: float32 [1024], P('dp')
The draws below stay inside these ranges and needn't reach their ends.
Inputs may be any that keep to these rules, and one draw needn't show every extreme that they name: `frame_counts`: column 0 is the first clip of a sequence, 4 to 8 frames, exactly 8 in sequence 0; column 1 is a second clip of 0 frames or of 4 or more, at most 8 minus column 0; frames after both clips are padding.
All inputs are finite; a program needn't handle non-finite values. No bound on the sum of `presence` on one device may be relied on, other than what follows from the above.
Results may differ from the reference program's by a relative error of at most 0.017.
Values may be sent and summed in bfloat16 or wider, within the bound.
No kernel may reach another device: no remote copies, remote signals or barrier semaphores. Data moves between devices by JAX's collectives and lax.ppermute only.
A program may use at most 256 MiB of HBM per device.

```python
import jax
import jax.numpy as jnp
from jax import lax

D = 1024
HEADS = 16
HEAD = 64
FF = 4096
GRID = 16
FRAMES = 8
LEN = 2064
SEQUENCES = 8


def draw_frame_counts(key, part):
    key = jax.random.fold_in(key, 7)
    first_key, second_key = jax.random.split(key)
    first = jax.random.randint(first_key, (SEQUENCES,), 4, FRAMES + 1)
    first = jnp.where(jnp.arange(SEQUENCES) == 0, FRAMES, first)
    room = FRAMES - first
    picked = jax.random.randint(second_key, (SEQUENCES,), 0, 1 << 20) % jnp.maximum(room - 2, 1)
    second = jnp.where((room >= 4) & (picked > 0), picked + 3, 0)
    return jnp.stack([first, second], 1).astype(jnp.int32)


def plant(drawn, rng, least, largest):
    shape = drawn.shape
    index_at = [jax.random.randint(jax.random.fold_in(rng, axis), (), 0, shape[axis]) for axis in range(len(shape))]
    drawn = drawn.at[tuple(index_at)].set(least)
    longest = shape.index(max(shape))
    index_at[longest] = (index_at[longest] + 1) % shape[longest]
    return drawn.at[tuple(index_at)].set(largest)


def raised(values, stream_key, source, target, shards_of, factor):
    def block_of(dim):
        return (jnp.arange(values.shape[dim]) // (values.shape[dim] // shards_of)).reshape((-1,) + (1,) * (values.ndim - 1 - dim))

    near = jax.random.permutation(stream_key, shards_of)[block_of(target)]
    far = (block_of(target) + shards_of // 2) % shards_of
    return jnp.where((block_of(source) == near) | (block_of(source) == far), factor * values, values)


def block_scale(key, dims, cuts, least, top_value):
    def one(dim, blocks):
        steps = jax.random.uniform(jax.random.fold_in(jax.random.fold_in(key, 6), dim), (blocks,), jnp.float32, least / len(cuts), top_value / len(cuts))
        return jnp.repeat(jnp.exp(steps), dims[dim] // blocks).reshape((-1,) + (1,) * (len(dims) - dim - 1))

    level = one(*cuts[0])
    for cut in cuts[1:]:
        level = level * one(*cut)
    return level


def scatter_about(stream_key, extent, scale, limit, shards=(), held_as=jnp.bfloat16):
    values = jax.random.normal(stream_key, extent, jnp.float32) * scale
    if len(shards) > 0:
        values = block_scale(stream_key, extent, shards, -0.22, 0.18) * values
    return jnp.clip(values, min=-limit, max=limit).astype(held_as)


def noise_with(own_key, dims, width, bound, shards, heavy, kind=jnp.bfloat16):
    entries = width * jax.random.normal(own_key, dims, jnp.float32)
    if shards:
        entries = entries * block_scale(own_key, dims, shards, -0.22, 0.18)
    return jnp.clip(raised(entries, jax.random.fold_in(own_key, 3), *heavy), -bound, bound).astype(kind)


def setup_inputs(seed: int = 0) -> dict:
    streams_of = jax.random.split(jax.random.key(seed), 17)
    return {
        "tokens": scatter_about(streams_of[0], (SEQUENCES, LEN, D), 1.0, 6.0, ((0, 8), (1, 4))),
        "cotangent": noise_with(streams_of[1], (SEQUENCES, LEN, D), 1.0, 6.0, ((0, 8), (1, 4)), (0, 2, 8, 2.0)),
        "frame_counts": draw_frame_counts(jax.random.fold_in(streams_of[16], 71), 0),
        "presence": plant((jax.random.randint(streams_of[3], (SEQUENCES, FRAMES, 2), 0, 4) < 3).astype(jnp.int32), jax.random.fold_in(streams_of[3], 1), 0, 1),
        "attend_gain": jnp.clip(1.0 + 0.1 * jax.random.normal(streams_of[4], (D,), jnp.float32), 0.5, 1.5).astype(jnp.bfloat16),
        "attend_shift": scatter_about(streams_of[5], (D,), 0.3, 1.75, ((0, 8),)),
        "triple_weight": scatter_about(streams_of[6], (D, 3 * D), D ** -0.5, 0.1875, ((0, 4), (1, 8))),
        "triple_bias": scatter_about(streams_of[7], (3 * D,), 0.5, 3.0, ((0, 8),)),
        "output_weight": scatter_about(streams_of[8], (D, D), (D // 16) ** -0.5, 0.75, ((0, 4), (1, 8))),
        "output_bias": scatter_about(streams_of[9], (D,), 0.3, 1.75, ((0, 8),)),
        "second_gain": jnp.clip(1.0 + 0.1 * jax.random.normal(streams_of[10], (D,), jnp.float32), 0.5, 1.5).astype(jnp.bfloat16),
        "second_shift": scatter_about(streams_of[11], (D,), 0.3, 1.75, ((0, 8),)),
        "expand_weight": scatter_about(streams_of[12], (D, FF), D ** -0.5, 0.1875, ((0, 4), (1, 8))),
        "expand_bias": scatter_about(streams_of[13], (FF,), 0.5, 3.0, ((0, 8),)),
        "reduce_weight": scatter_about(streams_of[14], (FF, D), FF ** -0.5, 0.09375, ((0, 4), (1, 8))),
        "reduce_bias": scatter_about(streams_of[15], (D,), 0.3, 1.75, ((0, 8),)),
    }


EPSILON = 1e-06
NEGATIVE = -1000000000.0

@jax.custom_vjp
def low(v):
    return lax.optimization_barrier(v.astype(jnp.bfloat16)).astype(jnp.float32)

@jax.custom_vjp
def low_back(v):
    return v

def low_keep(v):
    return (low(v), None)

def low_pass(kept, grad):
    return (grad,)

def back_keep(v):
    return (v, None)

def back_low(kept, grad):
    return (low(grad),)
low.defvjp(low_keep, low_pass)
low_back.defvjp(back_keep, back_low)

def norm_affine(values, gain, shift):
    center = values - lax.optimization_barrier(jnp.mean(values, -1, keepdims=True))
    spread = lax.optimization_barrier(jnp.mean(center * center, -1, keepdims=True))
    return center * lax.rsqrt(spread + EPSILON) * gain + shift

def rotary(values, cosine, sine):
    pairs = cosine.shape[-1]
    span = 6 * pairs
    leading = values.shape[:-1]
    turned_part = values[..., :span].reshape(leading + (3, 2, pairs))
    first = turned_part[..., 0, :]
    second = turned_part[..., 1, :]
    cos_b = cosine[..., None, :, :]
    sin_b = sine[..., None, :, :]
    new_first = first * cos_b - second * sin_b
    new_second = second * cos_b + first * sin_b
    turned = jnp.stack([new_first, new_second], -2).reshape(leading + (span,))
    return jnp.concatenate([turned, values[..., span:]], -1)

def row_tables(counts, present, row_frame, grid, pairs):
    frames = present.shape[0]
    frame_ids = jnp.arange(frames, dtype=jnp.int32)
    first = counts[0]
    second = counts[1]
    clip_frame = jnp.where(frame_ids < first, 0, jnp.where(frame_ids < first + second, 1, 2)).astype(jnp.int32)
    start = jnp.where(frame_ids < first, 0, first).astype(jnp.int32)
    time_frame = (frame_ids - start).astype(jnp.float32)
    within = jnp.arange(row_frame, dtype=jnp.int32)
    patch = jnp.maximum(within - 2, 0)
    grid_row = jnp.where(within >= 2, patch // grid, 0).astype(jnp.float32)
    grid_col = jnp.where(within >= 2, patch % grid, 0).astype(jnp.float32)
    inclip = clip_frame < 2
    action_on = present[:, 0] == 1
    state_on = present[:, 1] == 1
    live = inclip[:, None] & ((within[None, :] >= 2) | (within[None, :] == 0) & action_on[:, None] | (within[None, :] == 1) & state_on[:, None])
    shape = (frames, row_frame)
    clip = jnp.broadcast_to(clip_frame[:, None], shape).reshape(-1)
    times = jnp.broadcast_to(time_frame[:, None], shape).reshape(-1)
    rows_pos = jnp.broadcast_to(grid_row[None, :], shape).reshape(-1)
    cols_pos = jnp.broadcast_to(grid_col[None, :], shape).reshape(-1)
    position = jnp.stack([times, rows_pos, cols_pos], -1)
    freq = 10000.0 ** (-jnp.arange(pairs, dtype=jnp.float32) / pairs)
    angle = position[:, :, None] * freq
    return (clip, times, live.reshape(-1).astype(jnp.float32), jnp.cos(angle), jnp.sin(angle))

def product(left, right):
    return jnp.dot(left, right, precision=lax.Precision.HIGHEST, preferred_element_type=jnp.float32)

def attend_head(allowed, item):
    query, key_rows, value_rows = item
    scores = low_back(product(query, key_rows.T) * 0.125)
    scores = jnp.where(allowed, scores, NEGATIVE)
    top = lax.optimization_barrier(jnp.max(scores, -1, keepdims=True))
    weights = jnp.exp(scores - top)
    probs = low(weights / lax.optimization_barrier(jnp.sum(weights, -1, keepdims=True)))
    return product(probs, value_rows)

def block(params, values, tables):
    attend_gain, attend_shift, triple_weight, triple_bias, output_weight, output_bias, second_gain, second_shift, expand_weight, expand_bias, reduce_weight, reduce_bias = params
    clip, times, live, cosine, sine = tables
    allowed = (clip[:, None] == clip[None, :]) & (times[None, :] <= times[:, None]) & (live[None, :] > 0.5)
    mask_col = live[:, None]
    length = values.shape[0]
    entered = values * mask_col
    normed = low(norm_affine(entered, attend_gain, attend_shift))
    triple = low_back(product(normed, triple_weight) + triple_bias)
    query = low(rotary(triple[:, :D].reshape(length, HEADS, HEAD), cosine, sine))
    keys = low(rotary(triple[:, D:2 * D].reshape(length, HEADS, HEAD), cosine, sine))
    value_rows = low(triple[:, 2 * D:].reshape(length, HEADS, HEAD))

    def head_fn(item):
        return attend_head(allowed, item)
    attended = lax.map(jax.checkpoint(head_fn), (query.transpose(1, 0, 2), keys.transpose(1, 0, 2), value_rows.transpose(1, 0, 2)))
    mixed = low(low_back(attended.transpose(1, 0, 2).reshape(length, D)))
    branch = low_back(product(mixed, output_weight) + output_bias)
    middle = entered + branch
    second = low(norm_affine(middle, second_gain, second_shift))
    hidden = low_back(product(second, expand_weight) + expand_bias)
    active = low(jax.nn.gelu(hidden, approximate=False))
    final = low_back(product(active, reduce_weight) + reduce_bias)
    return (middle + final) * mask_col

def reference(tokens, cotangent, frame_counts, presence, attend_gain, attend_shift, triple_weight, triple_bias, output_weight, output_bias, second_gain, second_shift, expand_weight, expand_bias, reduce_weight, reduce_bias):
    params = tuple((item.astype(jnp.float32) for item in (attend_gain, attend_shift, triple_weight, triple_bias, output_weight, output_bias, second_gain, second_shift, expand_weight, expand_bias, reduce_weight, reduce_bias)))
    row_frame = GRID * GRID + 2
    pairs = HEAD // 3 // 2

    def one_sequence(totals, item):
        values, cot_rows, counts, present = item
        tables = row_tables(counts, present, row_frame, GRID, pairs)

        def forward(weights, inputs):
            return block(weights, inputs, tables)
        result, pull = jax.vjp(forward, params, values.astype(jnp.float32))
        weight_grads, input_grad = pull(cot_rows.astype(jnp.float32))
        totals = jax.tree.map(lambda left, right: left + right, totals, weight_grads)
        return (totals, (result.astype(jnp.bfloat16), input_grad))
    zeros = jax.tree.map(jnp.zeros_like, params)
    totals, (block_output, tokens_grad) = lax.scan(one_sequence, zeros, (tokens, cotangent, frame_counts, presence))
    return (block_output, tokens_grad, totals[0], totals[1], totals[2], totals[3], totals[4], totals[5], totals[6], totals[7], totals[8], totals[9], totals[10], totals[11])
```

```python
import functools
import math

import jax
import jax.numpy as jnp
import numpy as np
from jax import lax
from jax.experimental import pallas as pl
from jax.experimental.pallas import tpu as pltpu
from jax.sharding import PartitionSpec as P

D = 1024
HEADS = 16
HEAD = 64
FF = 4096
GRID = 16
PATCHES = GRID * GRID
ROW_FRAME = PATCHES + 2
PAIRS = HEAD // 3 // 2
EXTRA = 16

EPSILON = 1e-06
SCALE2 = 0.125 * math.log2(math.e)
MASKED = -8e9
FAR = 1 << 20
VMEM = 60 * 1024 * 1024
BF = jnp.bfloat16
F32 = jnp.float32


def nn(left, right):
    return lax.dot_general(left, right, (((1,), (0,)), ((), ())), preferred_element_type=F32)


def nt(left, right):
    return lax.dot_general(left, right, (((1,), (1,)), ((), ())), preferred_element_type=F32)


def tn(left, right):
    return lax.dot_general(left, right, (((0,), (0,)), ((), ())), preferred_element_type=F32)


def qkv_kernel(normed, weight, bias, turn, cosine, sine, q_out, k_out, v_out, turned, turned_bias):
    width = q_out.shape[-1]
    half = width // 2

    @pl.when(pl.program_id(0) == 0)
    def _():
        for part in range(2):
            span = slice(part * width, (part + 1) * width)
            turned[:, span] = nn(weight[:, span], turn[...]).astype(BF)
            turned_bias[:, span] = nn(bias[:, span], turn[...])

    rows = normed[0]
    cos = cosine[0]
    sin = sine[0]
    for part, out in ((0, q_out), (1, k_out)):
        span = slice(part * width, (part + 1) * width)
        value = nn(rows, turned[:, span]) + turned_bias[:1, span]
        first = value[:, :half]
        second = value[:, half:]
        out[0, :, :half] = (first * cos - second * sin).astype(BF)
        out[0, :, half:] = (second * cos + first * sin).astype(BF)
    span = slice(2 * width, 3 * width)
    v_out[0] = (nn(rows, weight[:, span]) + bias[:1, span].astype(F32)).astype(BF)


def qkv_call(normed, weight, bias, turn, cosine, sine):
    sources, rows, _ = normed.shape
    width = weight.shape[1] // 3
    half = width // 2
    block = pl.BlockSpec((1, rows, width), lambda s: (s, 0, 0))
    table = pl.BlockSpec((1, rows, half), lambda s: (s, 0, 0))

    def whole(shape):
        return pl.BlockSpec(shape, lambda s: (0,) * len(shape))

    shape = jax.ShapeDtypeStruct((sources, rows, width), BF)
    return pl.pallas_call(
        qkv_kernel,
        grid=(sources,),
        in_specs=[
            pl.BlockSpec((1, rows, D), lambda s: (s, 0, 0)),
            whole(weight.shape),
            whole(bias.shape),
            whole(turn.shape),
            table,
            table,
        ],
        out_specs=[block] * 3,
        out_shape=[shape] * 3,
        scratch_shapes=[pltpu.VMEM((D, 2 * width), BF), pltpu.VMEM((bias.shape[0], 2 * width), F32)],
        compiler_params=pltpu.CompilerParams(vmem_limit_bytes=VMEM),
        cost_estimate=pl.CostEstimate(
            flops=2 * sources * rows * D * 3 * width, bytes_accessed=4 * sources * rows * D, transcendentals=0
        ),
        name="qkv_rotary",
    )(normed, weight, bias, turn, cosine, sine)


def turned_lanes(width, head):
    lane = lax.broadcasted_iota(jnp.int32, (1, width), 1)
    return (lane % (width // 2)) // (HEAD // 2) == head


def plain_lanes(width, head):
    lane = lax.broadcasted_iota(jnp.int32, (1, width), 1)
    return lane // HEAD == head


def pick(mask, array):
    return jnp.where(mask, array, jnp.zeros((), array.dtype))


def head_rows(array, head):
    half = array.shape[0] // 2
    step = HEAD // 2
    return jnp.concatenate(
        [array[head * step : (head + 1) * step], array[half + head * step : half + (head + 1) * step]], 0
    )


def value_total(v, frames_local, sources):
    total = jnp.zeros((1, v.shape[-1]), F32)
    real = lax.broadcasted_iota(jnp.int32, (EXTRA, 1), 0) < 2 * frames_local
    for s in range(sources):
        for l in range(frames_local):
            total = total + jnp.sum(v[s, l * PATCHES : (l + 1) * PATCHES].astype(F32), 0, keepdims=True)
        total = total + jnp.sum(pick(real, v[s, frames_local * PATCHES :].astype(F32)), 0, keepdims=True)
    return total


def attend_kernel(
    frames_local, start, key_frame, query_start, query_frame, query_pad, q, k, v, mixed, exact, logs, logs_extra, v_t, acc, state
):
    sources, _, width = q.shape
    heads = width // HEAD
    frames = sources * frames_local
    patch_rows = frames_local * PATCHES
    length = frames * ROW_FRAME
    extra = sources * EXTRA

    def frame_ref(ref, g):
        return ref[g // frames_local, pl.ds(pl.multiple_of((g % frames_local) * PATCHES, PATCHES), PATCHES), :]

    for g in range(frames):
        s, l = g // frames_local, g % frames_local
        v_t[g] = v[s, l * PATCHES : (l + 1) * PATCHES].T
    k_extra = jnp.concatenate([k[s, patch_rows:] for s in range(sources)], 0)
    v_extra = jnp.concatenate([v[s, patch_rows:] for s in range(sources)], 0)
    v_extra_t = v_extra.T
    uniform = jnp.asarray(1.0 / length, BF).astype(F32) * value_total(v, frames_local, sources)
    key_at = key_frame[:, :1]

    def begin(head, query, allowed, slot):
        scores = jnp.where(allowed, nt(k_extra, query), MASKED)
        top = jnp.max(scores, 0, keepdims=True)
        weights = jnp.exp2((scores - top) * SCALE2)
        total = jnp.sum(weights, 0, keepdims=True)
        lanes = query.shape[0]
        acc[head * HEAD : (head + 1) * HEAD, :lanes] = nn(v_extra_t[head * HEAD : (head + 1) * HEAD], weights.astype(BF))
        state[slot, head : head + 1, :lanes] = top
        state[slot + 1, head : head + 1, :lanes] = total

    def step(head, query, keys, values_t, allowed, slot):
        lanes = query.shape[0]
        scores = nt(keys, query)
        if allowed is not None:
            scores = jnp.where(allowed, scores, MASKED)
        before = state[slot, head : head + 1, :lanes]
        top = jnp.maximum(before, jnp.max(scores, 0, keepdims=True))
        fade = jnp.exp2((before - top) * SCALE2)
        weights = jnp.exp2((scores - top) * SCALE2)
        span = slice(head * HEAD, (head + 1) * HEAD)
        state[slot, head : head + 1, :lanes] = top
        state[slot + 1, head : head + 1, :lanes] = state[slot + 1, head : head + 1, :lanes] * fade + jnp.sum(
            weights, 0, keepdims=True
        )
        acc[span, :lanes] = acc[span, :lanes] * fade + nn(values_t[span], weights.astype(BF))

    def finish(lanes):
        parts = []
        for head in range(heads):
            span = slice(head * HEAD, (head + 1) * HEAD)
            parts.append(acc[span, :lanes] / state[1, head : head + 1, :lanes])
        return jnp.concatenate(parts, 0).T

    def one_frame(g, _):
        query = frame_ref(q, g)
        queries = [pick(turned_lanes(width, head), query) for head in range(heads)]
        first = start[g]
        allowed = (key_at >= first) & (key_at <= g)
        for head in range(heads):
            begin(head, queries[head], allowed, 0)

        def one_key(f, _):
            keys = frame_ref(k, f)
            values_t = v_t[f]
            for head in range(heads):
                step(head, queries[head], keys, values_t, None, 0)
            return 0

        lax.fori_loop(first, g + 1, one_key, 0)
        result = jnp.where(first > frames, jnp.broadcast_to(uniform, (PATCHES, width)), finish(PATCHES))
        rows = pl.ds(pl.multiple_of((g % frames_local) * PATCHES, PATCHES), PATCHES)
        exact[g // frames_local, rows, :] = result
        mixed[g // frames_local, rows, :] = result.astype(BF)
        logs[g] = state[0] + jnp.log2(state[1]) * (1.0 / SCALE2)
        return 0

    state[...] = jnp.ones_like(state)
    lax.fori_loop(0, frames, one_frame, 0)

    q_extra = jnp.concatenate([q[s, patch_rows:] for s in range(sources)], 0)
    queries = [pick(turned_lanes(width, head), q_extra) for head in range(heads)]
    first = query_start[:1]
    last = query_frame[:1]
    allowed = (key_at >= first) & (key_at <= last)
    for head in range(heads):
        begin(head, queries[head], allowed, 0)

    def one_key(f, _):
        keys = frame_ref(k, f)
        values_t = v_t[f]
        visible = (first <= f) & (last >= f)
        for head in range(heads):
            step(head, queries[head], keys, values_t, visible, 0)
        return 0

    lax.fori_loop(0, frames, one_key, 0)
    result = finish(extra)
    result = jnp.where(query_pad[:, :1] > 0, jnp.broadcast_to(uniform, result.shape), result)
    for s in range(sources):
        exact[s, patch_rows:, :] = result[s * EXTRA : (s + 1) * EXTRA]
        mixed[s, patch_rows:, :] = result[s * EXTRA : (s + 1) * EXTRA].astype(BF)
    logs_extra[...] = (state[0] + jnp.log2(state[1]) * (1.0 / SCALE2))[:, :extra]


def attend_call(start, key_frame, query_start, query_frame, query_pad, q, k, v):
    sources, rows, width = q.shape
    frames_local = rows // PATCHES
    frames = sources * frames_local
    extra = sources * EXTRA
    lanes = max(PATCHES, extra)
    heads = width // HEAD
    vmem = pl.BlockSpec(memory_space=pltpu.VMEM)
    return pl.pallas_call(
        functools.partial(attend_kernel, frames_local),
        in_specs=[pl.BlockSpec(memory_space=pltpu.SMEM)] + [vmem] * 7,
        out_specs=[vmem] * 4,
        out_shape=[
            jax.ShapeDtypeStruct(q.shape, BF),
            jax.ShapeDtypeStruct(q.shape, F32),
            jax.ShapeDtypeStruct((frames, 8, lanes), F32),
            jax.ShapeDtypeStruct((8, extra), F32),
        ],
        scratch_shapes=[
            pltpu.VMEM((frames, width, PATCHES), BF),
            pltpu.VMEM((width, lanes), F32),
            pltpu.VMEM((2, 8, lanes), F32),
        ],
        compiler_params=pltpu.CompilerParams(vmem_limit_bytes=VMEM),
        cost_estimate=pl.CostEstimate(
            flops=8 * heads * 256 * frames * frames * PATCHES * PATCHES // 2,
            bytes_accessed=10 * sources * rows * width,
            transcendentals=heads * frames * frames * PATCHES * PATCHES // 2,
        ),
        name="attend",
    )(start, key_frame, query_start, query_frame, query_pad, q, k, v)


def attend_back_kernel(
    frames_local,
    start,
    key_frame,
    query_start,
    query_frame,
    query_pad,
    q,
    k,
    v,
    grad,
    exact,
    logs,
    logs_extra,
    cosine,
    sine,
    out,
    k_t,
    dq_t,
    dk,
    dv,
    dq_extra,
    dk_extra,
    dv_extra,
    centers,
):
    sources, _, width = q.shape
    half = width // 2
    heads = width // HEAD
    frames = sources * frames_local
    patch_rows = frames_local * PATCHES
    length = frames * ROW_FRAME
    step_rows = HEAD // 2

    def frame_ref(ref, g):
        return ref[g // frames_local, pl.ds(pl.multiple_of((g % frames_local) * PATCHES, PATCHES), PATCHES), :]

    which = lax.broadcasted_iota(jnp.int32, (8, width), 0)
    lane = lax.broadcasted_iota(jnp.int32, (8, width), 1)
    groups = (lane // HEAD == which).astype(BF)

    def center_of(grads, exacts):
        product = grads.astype(F32) * exacts
        high = product.astype(BF)
        low = (product - high.astype(F32)).astype(BF)
        return nt(groups, high) + nt(groups, low)

    def gather_extra(ref):
        return jnp.concatenate([ref[s, patch_rows:] for s in range(sources)], 0)

    for g in range(frames):
        s, l = g // frames_local, g % frames_local
        k_t[g] = k[s, l * PATCHES : (l + 1) * PATCHES].T
    q_extra = gather_extra(q)
    k_extra = gather_extra(k)
    v_extra = gather_extra(v)
    g_extra = gather_extra(grad)
    k_extra_t = k_extra.T
    dq_t[...] = jnp.zeros_like(dq_t)
    dk[...] = jnp.zeros_like(dk)
    dv[...] = jnp.zeros_like(dv)
    dq_extra[...] = jnp.zeros_like(dq_extra)
    dk_extra[...] = jnp.zeros_like(dk_extra)
    dv_extra[...] = jnp.zeros_like(dv_extra)
    key_at = key_frame[:, :1]

    def tile(head, query, grads, keys, values, keys_t, log, center, allowed):
        scores = nt(keys, query)
        probs = jnp.exp2((scores - log) * SCALE2)
        if allowed is not None:
            probs = jnp.where(allowed, probs, 0.0)
        inner = nt(values, grads)
        change = (probs * (inner - center)).astype(BF)
        dv_part = nn(probs.astype(BF), grads)
        dk_part = nn(change, query)
        dq_part = nn(head_rows(keys_t, head), change)
        return dv_part, dk_part, dq_part

    def add_dq(ref, head, part):
        first = slice(head * step_rows, (head + 1) * step_rows)
        second = slice(half + head * step_rows, half + (head + 1) * step_rows)
        ref[first] += part[:step_rows]
        ref[second] += part[step_rows:]

    def one_frame(g, pad_grad):
        query = frame_ref(q, g)
        grads = frame_ref(grad, g)
        queries = [pick(turned_lanes(width, head), query) for head in range(heads)]
        grad_heads = [pick(plain_lanes(width, head), grads) for head in range(heads)]
        first = start[g]
        centers[...] = center_of(grads, frame_ref(exact, g))
        allowed = (key_at >= first) & (key_at <= g)
        for head in range(heads):
            dv_part, dk_part, dq_part = tile(
                head,
                queries[head],
                grad_heads[head],
                k_extra,
                v_extra,
                k_extra_t,
                logs[g, head : head + 1, :PATCHES],
                centers[head : head + 1],
                allowed,
            )
            dv_extra[...] += dv_part
            dk_extra[...] += dk_part
            add_dq(dq_t.at[g], head, dq_part)

        def one_key(f, _):
            keys = frame_ref(k, f)
            values = frame_ref(v, f)
            keys_t = k_t[f]
            dv_sum = dv[f]
            dk_sum = dk[f]
            for head in range(heads):
                dv_part, dk_part, dq_part = tile(
                    head,
                    queries[head],
                    grad_heads[head],
                    keys,
                    values,
                    keys_t,
                    logs[g, head : head + 1, :PATCHES],
                    centers[head : head + 1],
                    None,
                )
                dv_sum = dv_sum + dv_part
                dk_sum = dk_sum + dk_part
                add_dq(dq_t.at[g], head, dq_part)
            dv[f] = dv_sum
            dk[f] = dk_sum
            return 0

        lax.fori_loop(first, g + 1, one_key, 0)
        return pad_grad + jnp.where(first > frames, jnp.sum(grads.astype(F32), 0, keepdims=True), 0.0)

    pad_grad = lax.fori_loop(0, frames, one_frame, jnp.zeros((1, width), F32))
    pad_grad = pad_grad + jnp.sum(jnp.where(query_pad[:, :1] > 0, g_extra.astype(F32), 0.0), 0, keepdims=True)
    pad_grad = pad_grad * jnp.asarray(1.0 / length, BF).astype(F32)

    queries = [pick(turned_lanes(width, head), q_extra) for head in range(heads)]
    grad_heads = [pick(plain_lanes(width, head), g_extra) for head in range(heads)]
    first = query_start[:1]
    last = query_frame[:1]
    center = center_of(g_extra, gather_extra(exact))
    allowed = (key_at >= first) & (key_at <= last)
    for head in range(heads):
        dv_part, dk_part, dq_part = tile(
            head,
            queries[head],
            grad_heads[head],
            k_extra,
            v_extra,
            k_extra_t,
            logs_extra[head : head + 1],
            center[head : head + 1],
            allowed,
        )
        dv_extra[...] += dv_part
        dk_extra[...] += dk_part
        add_dq(dq_extra, head, dq_part)

    def extra_key(f, _):
        keys = frame_ref(k, f)
        values = frame_ref(v, f)
        keys_t = k_t[f]
        visible = (first <= f) & (last >= f)
        for head in range(heads):
            dv_part, dk_part, dq_part = tile(
                head,
                queries[head],
                grad_heads[head],
                keys,
                values,
                keys_t,
                logs_extra[head : head + 1],
                center[head : head + 1],
                visible,
            )
            dv[f] += dv_part
            dk[f] += dk_part
            add_dq(dq_extra, head, dq_part)
        return 0

    lax.fori_loop(0, frames, extra_key, 0)

    def emit(s, rows, dq_rows, dk_rows, dv_rows):
        cos = cosine[s, rows]
        sin = sine[s, rows]
        for part, array in ((0, dq_rows), (1, dk_rows)):
            a = array[:, :half] * 0.125
            b = array[:, half:] * 0.125
            at = part * width
            out[s, rows, at : at + half] = (a * cos + b * sin).astype(BF)
            out[s, rows, at + half : at + width] = (b * cos - a * sin).astype(BF)
        out[s, rows, 2 * width :] = (dv_rows + pad_grad).astype(BF)

    def emit_frame(g, _):
        rows = pl.ds(pl.multiple_of((g % frames_local) * PATCHES, PATCHES), PATCHES)
        emit(g // frames_local, rows, dq_t[g].T, dk[g], dv[g])
        return 0

    lax.fori_loop(0, frames, emit_frame, 0)
    dq_rows = dq_extra[...].T
    real = lax.broadcasted_iota(jnp.int32, (EXTRA, 1), 0) < 2 * frames_local
    for s in range(sources):
        at = slice(s * EXTRA, (s + 1) * EXTRA)
        rows = slice(patch_rows, patch_rows + EXTRA)
        emit(s, rows, dq_rows[at], dk_extra[at], dv_extra[at])
        out[s, rows, :] = pick(real, out[s, rows, :])


def attend_back_call(start, key_frame, query_start, query_frame, query_pad, q, k, v, grad, exact, logs, logs_extra, cosine, sine):
    sources, rows, width = q.shape
    frames_local = rows // PATCHES
    frames = sources * frames_local
    extra = sources * EXTRA
    heads = width // HEAD
    vmem = pl.BlockSpec(memory_space=pltpu.VMEM)
    return pl.pallas_call(
        functools.partial(attend_back_kernel, frames_local),
        in_specs=[pl.BlockSpec(memory_space=pltpu.SMEM)] + [vmem] * 13,
        out_specs=vmem,
        out_shape=jax.ShapeDtypeStruct((sources, rows, 3 * width), BF),
        scratch_shapes=[
            pltpu.VMEM((frames, width, PATCHES), BF),
            pltpu.VMEM((frames, width, PATCHES), F32),
            pltpu.VMEM((frames, PATCHES, width), F32),
            pltpu.VMEM((frames, PATCHES, width), F32),
            pltpu.VMEM((width, extra), F32),
            pltpu.VMEM((extra, width), F32),
            pltpu.VMEM((extra, width), F32),
            pltpu.VMEM((8, PATCHES), F32),
        ],
        compiler_params=pltpu.CompilerParams(vmem_limit_bytes=VMEM),
        cost_estimate=pl.CostEstimate(
            flops=20 * heads * 256 * frames * frames * PATCHES * PATCHES // 2,
            bytes_accessed=20 * sources * rows * width,
            transcendentals=heads * frames * frames * PATCHES * PATCHES // 2,
        ),
        name="attend_back",
    )(start, key_frame, query_start, query_frame, query_pad, q, k, v, grad, exact, logs, logs_extra, cosine, sine)


def feed_kernel(
    chunk, second, outer, outer_t, expand, expand_bias, reduce, final, second_grad, d_expand, d_reduce, d_bias, second_t, active, slope
):
    rows = second.shape[0]
    wide = expand.shape[-1]

    @pl.when(pl.program_id(0) == 0)
    def _():
        for r in range(0, rows, chunk):
            second_t[:, r : r + chunk] = second[r : r + chunk].T
        final[...] = jnp.zeros_like(final)
        second_grad[...] = jnp.zeros_like(second_grad)

    weight_in = expand[0]
    weight_out = reduce[0]
    add = expand_bias[0, :1].astype(F32)

    d_bias[...] = jnp.zeros_like(d_bias)
    for r in range(0, rows, chunk):
        at = slice(r, r + chunk)
        hidden = nn(second[at], weight_in) + add
        cdf = 0.5 + 0.5 * lax.erf(hidden * math.sqrt(0.5))
        density = jnp.exp(hidden * hidden * -0.5) * (1.0 / math.sqrt(2.0 * math.pi))
        act = (hidden * cdf).astype(BF)
        grad = (nt(outer[at], weight_out) * (cdf + hidden * density)).astype(BF)
        active[at] = act
        slope[at] = grad
        d_bias[0] += jnp.sum(grad.astype(F32), 0, keepdims=True)
        final[at] += nn(act, weight_out)
        second_grad[at] += nt(grad, weight_in)
    d_expand[0] = nn(second_t[...], slope[...]).astype(BF)
    d_reduce[:, 0] = nn(outer_t[...], active[...]).astype(BF).reshape(d_reduce.shape[0], d_reduce.shape[2], wide)


def feed_call(second, outer, outer_t, expand, expand_bias, reduce, n_dp):
    rows = second.shape[0]
    tiles, _, wide = expand.shape
    chunk = rows // 2
    assert chunk % 16 == 0

    def whole(shape):
        return pl.BlockSpec(shape, lambda t: (0,) * len(shape))

    return pl.pallas_call(
        functools.partial(feed_kernel, chunk),
        grid=(tiles,),
        in_specs=[
            whole((rows, D)),
            whole((rows, D)),
            whole((D, rows)),
            pl.BlockSpec((1, D, wide), lambda t: (t, 0, 0)),
            pl.BlockSpec((1, 1, wide), lambda t: (t, 0, 0)),
            pl.BlockSpec((1, wide, D), lambda t: (t, 0, 0)),
        ],
        out_specs=[
            whole((rows, D)),
            whole((rows, D)),
            pl.BlockSpec((1, D, wide), lambda t: (t, 0, 0)),
            pl.BlockSpec((n_dp, 1, D // n_dp, wide), lambda t: (0, t, 0, 0)),
            pl.BlockSpec((1, 1, wide), lambda t: (t, 0, 0)),
        ],
        out_shape=[
            jax.ShapeDtypeStruct((rows, D), F32),
            jax.ShapeDtypeStruct((rows, D), F32),
            jax.ShapeDtypeStruct((tiles, D, wide), BF),
            jax.ShapeDtypeStruct((n_dp, tiles, D // n_dp, wide), BF),
            jax.ShapeDtypeStruct((tiles, 1, wide), F32),
        ],
        scratch_shapes=[
            pltpu.VMEM((D, rows), BF),
            pltpu.VMEM((rows, wide), BF),
            pltpu.VMEM((rows, wide), BF),
        ],
        compiler_params=pltpu.CompilerParams(vmem_limit_bytes=VMEM),
        cost_estimate=pl.CostEstimate(
            flops=10 * rows * D * wide * tiles,
            bytes_accessed=8 * D * wide * tiles + 14 * rows * D,
            transcendentals=2 * rows * wide * tiles,
        ),
        name="feed_forward",
    )(second, outer, outer_t, expand, expand_bias, reduce)


def norm_parts(values):
    center = values - jnp.mean(values, -1, keepdims=True)
    scale = lax.rsqrt(jnp.mean(center * center, -1, keepdims=True) + EPSILON)
    return center * scale, scale


def norm_back(grad, unit, scale, gain):
    scaled = grad * gain
    mean_one = jnp.mean(scaled, -1, keepdims=True)
    mean_two = jnp.mean(scaled * unit, -1, keepdims=True)
    return scale * (scaled - mean_one - unit * mean_two)


def to_block(array, frames_local):
    split = array.reshape(frames_local, ROW_FRAME, D)
    return jnp.concatenate(
        [
            split[:, 2:].reshape(frames_local * PATCHES, D),
            split[:, :2].reshape(frames_local * 2, D),
            jnp.zeros((EXTRA - 2 * frames_local, D), array.dtype),
        ],
        0,
    )


def from_block(array, frames_local):
    patches = array[: frames_local * PATCHES].reshape(frames_local, PATCHES, D)
    extra = array[frames_local * PATCHES : frames_local * ROW_FRAME].reshape(frames_local, 2, D)
    return jnp.concatenate([extra, patches], 1).reshape(1, frames_local * ROW_FRAME, D)


def rows_of(per_frame, per_extra, sources, frames_local, fill):
    patches = jnp.broadcast_to(per_frame.reshape(sources, frames_local, 1), (sources, frames_local, PATCHES))
    pad = jnp.full((sources, EXTRA - 2 * frames_local), fill, per_frame.dtype)
    return jnp.concatenate(
        [patches.reshape(sources, -1), per_extra.reshape(sources, 2 * frames_local), pad], 1
    )


def tables(counts, present, sources, frames_local, heads):
    frames = sources * frames_local
    at = jnp.arange(frames, dtype=jnp.int32)
    first, second = counts[0], counts[1]
    inside = at < first + second
    start = jnp.where(at < first, 0, first).astype(jnp.int32)
    time = (at - start).astype(F32)
    begin = jnp.where(inside, start, FAR)
    live_extra = inside[:, None] & (present == 1)
    time_rows = rows_of(time, jnp.repeat(time, 2), sources, frames_local, 0.0)
    live_rows = rows_of(inside.astype(F32), live_extra.astype(F32), sources, frames_local, 0.0)

    patch = np.arange(PATCHES)
    grid_row = np.zeros(frames_local * PATCHES + EXTRA, np.float32)
    grid_col = np.zeros(frames_local * PATCHES + EXTRA, np.float32)
    for l in range(frames_local):
        grid_row[l * PATCHES : (l + 1) * PATCHES] = patch // GRID
        grid_col[l * PATCHES : (l + 1) * PATCHES] = patch % GRID
    lanes = np.zeros((3, HEAD // 2), np.float32)
    freq = 10000.0 ** (-np.arange(PAIRS, dtype=np.float32) / PAIRS)
    for a in range(3):
        lanes[a, a * PAIRS : (a + 1) * PAIRS] = freq
    lanes = np.tile(lanes, (1, heads))
    angle = time_rows[:, :, None] * lanes[0] + (grid_row[:, None] * lanes[1] + grid_col[:, None] * lanes[2])[None]

    def extra_of(per_frame, fill):
        both = jnp.repeat(per_frame, 2).reshape(sources, 2 * frames_local)
        pad = jnp.full((sources, EXTRA - 2 * frames_local), fill, both.dtype)
        return jnp.concatenate([both, pad], 1).reshape(-1)

    extra = sources * EXTRA
    key_frame = jnp.where(live_extra, at[:, None], -1).reshape(sources, 2 * frames_local)
    key_frame = jnp.concatenate(
        [key_frame, jnp.full((sources, EXTRA - 2 * frames_local), -1, jnp.int32)], 1
    ).reshape(-1)
    query_start = extra_of(begin, FAR)
    query_frame = extra_of(at, -1)

    def column(vector):
        return jnp.broadcast_to(vector[:, None], (extra, 128))

    def row(vector):
        return jnp.broadcast_to(vector[None], (8, extra))

    return (
        live_rows,
        jnp.cos(angle),
        jnp.sin(angle),
        (begin, column(key_frame), row(query_start), row(query_frame), column((query_start == FAR).astype(jnp.int32))),
    )


def turn_matrix(width):
    turn = np.zeros((width, width), np.float32)
    step = HEAD // 2
    for h in range(width // HEAD):
        for d in range(HEAD):
            if d < 6 * PAIRS:
                a, rest = divmod(d, 2 * PAIRS)
                side, k = divmod(rest, PAIRS)
                to = side * (width // 2) + h * step + a * PAIRS + k
            else:
                side, k = divmod(d - 6 * PAIRS, step - 3 * PAIRS)
                to = side * (width // 2) + h * step + 3 * PAIRS + k
            turn[h * HEAD + d, to] = 1.0
    return turn


def shards(sizes, *args):
    (
        tokens,
        cotangent,
        frame_counts,
        presence,
        attend_gain,
        attend_shift,
        triple_weight,
        triple_bias,
        output_weight,
        output_bias,
        second_gain,
        second_shift,
        expand_weight,
        expand_bias,
        reduce_weight,
        reduce_bias,
    ) = args
    n_dp, n_x = sizes
    n_f = n_x * 2
    heads = HEADS // n_f
    width = heads * HEAD
    local_rows = tokens.shape[1]
    frames_local = local_rows // ROW_FRAME
    rows = frames_local * PATCHES + EXTRA
    core = lax.axis_index("core")
    shard = lax.axis_index("x") * 2 + core
    dp_at = lax.axis_index("dp")
    d_part = D // n_dp
    ff_part = FF // n_dp
    ff_half = ff_part // 2

    def swap(array):
        return lax.ppermute(array, "core", [(0, 1), (1, 0)])

    def both_cores(array, axis=0):
        other = swap(array)
        low = jnp.where(core == 0, array, other)
        high = jnp.where(core == 0, other, array)
        return jnp.concatenate([low, high], axis)

    def mine(pair, which):
        return jnp.where(which == 0, pair[0], pair[1])

    vectors = [attend_gain, attend_shift, output_bias, second_gain, second_shift, reduce_bias, triple_bias, expand_bias]
    flat = jnp.concatenate(vectors)
    qkv_part = 3 * D // n_dp
    flat = jnp.pad(flat, (0, 16 * qkv_part - flat.shape[0])).reshape(16, qkv_part)
    packed = jnp.concatenate([triple_weight, flat], 0)
    packed = lax.all_gather(packed, "dp", axis=0)
    small = packed[:, D // n_f :].reshape(n_dp, -1)
    full = []
    at = 0
    for vector in vectors:
        full.append(small[:, at : at + vector.shape[0]].reshape(-1))
        at += vector.shape[0]
    gain_one, shift_one, output_add, gain_two, shift_two, reduce_add = (v.astype(F32)[None] for v in full[:6])
    triple_add, expand_add = full[6], full[7]
    triple_rows = packed[:, : D // n_f].transpose(1, 0, 2).reshape(D // n_f, 3, n_f, width)
    triple_own = lax.all_to_all(triple_rows.transpose(2, 0, 1, 3), ("x", "core"), 0, 0, tiled=True)
    triple_own = triple_own.reshape(D, 3 * width)
    bias_own = lax.dynamic_index_in_dim(triple_add.reshape(3, n_f, width), shard, 1, False).reshape(1, 3 * width)

    expand_keep = mine([expand_weight[:, :ff_half], expand_weight[:, ff_half:]], core)
    expand_give = mine([expand_weight[:, ff_half:], expand_weight[:, :ff_half]], core)
    expand_other = swap(expand_give)
    expand_chip = jnp.concatenate(
        [jnp.where(core == 0, expand_keep, expand_other), jnp.where(core == 0, expand_other, expand_keep)], 0
    )
    blocks = n_dp // n_f
    reduce_split = reduce_weight.reshape(blocks, 2, ff_half, d_part)
    reduce_keep = mine([reduce_split[:, 0], reduce_split[:, 1]], core)
    reduce_other = swap(mine([reduce_split[:, 1], reduce_split[:, 0]], core))
    reduce_chip = jnp.stack(
        [jnp.where(core == 0, reduce_keep, reduce_other), jnp.where(core == 0, reduce_other, reduce_keep)], 0
    )
    expand_all = lax.all_gather(expand_chip, ("dp", "x"), axis=0)
    expand_all = expand_all.reshape(n_dp, D, ff_half)
    reduce_all = lax.all_gather(reduce_chip, ("dp", "x"), axis=0)
    reduce_all = reduce_all.reshape(n_dp, n_dp, ff_half, d_part).transpose(1, 2, 0, 3).reshape(n_dp, ff_half, D)
    output_all = lax.all_gather(output_weight, ("dp", "x"), axis=0)
    output_all = output_all.reshape(n_dp, n_x * width, d_part).transpose(1, 0, 2).reshape(n_x * width, D)
    expand_add_own = lax.dynamic_index_in_dim(expand_add.reshape(n_dp, 2, 1, ff_half), core, 1, False)

    live_all, cosine, sine, guides = tables(frame_counts[0], presence[0], n_f, frames_local, heads)
    live = lax.dynamic_index_in_dim(live_all, shard, 0, False)[:, None]
    entered = to_block(tokens[0], frames_local).astype(F32) * live
    outer = to_block(cotangent[0], frames_local).astype(F32) * live
    outer_low = outer.astype(BF)
    outer_chip = both_cores(outer_low)
    outer_chip_t = outer_chip.T
    unit_one, scale_one = norm_parts(entered)
    normed = (unit_one * gain_one + shift_one).astype(BF)
    normed_all = lax.all_gather(normed, ("x", "core"), axis=0)

    turn = turn_matrix(width)
    q, k, v = qkv_call(normed_all, triple_own, bias_own, jnp.asarray(turn, BF), cosine, sine)
    mixed, exact, logs, logs_extra = attend_call(*guides, q, k, v)

    def over_x(array):
        return lax.all_to_all(array, "x", 0, 0, tiled=True)

    mixed_chip = over_x(mixed.reshape(n_x, 2 * rows, width)).transpose(1, 0, 2).reshape(2 * rows, n_x * width)
    branch_part = nn(mixed_chip, output_all).reshape(2, rows, D)
    branch = mine(branch_part, core) + swap(mine(branch_part[::-1], core).astype(BF)).astype(F32)
    middle = entered + branch + output_add
    unit_two, scale_two = norm_parts(middle)
    second = (unit_two * gain_two + shift_two).astype(BF)
    second_chip = both_cores(second)
    final, second_grad, d_expand, d_reduce, d_expand_bias = feed_call(
        second_chip, outer_chip, outer_chip_t, expand_all, expand_add_own, reduce_all, n_dp
    )
    second_grad = second_grad.reshape(2, rows, D)
    second_grad = mine(second_grad, core) + swap(mine(second_grad[::-1], core).astype(BF)).astype(F32)
    final = final.reshape(2, rows, D)
    final = mine(final, core) + swap(mine(final[::-1], core).astype(BF)).astype(F32)
    block_output = ((middle + final + reduce_add) * live).astype(BF)

    middle_grad = outer + norm_back(second_grad, unit_two, scale_two, gain_two)
    second_gain_grad = jnp.sum(second_grad * unit_two, 0)
    second_shift_grad = jnp.sum(second_grad, 0)
    branch_low = middle_grad.astype(BF)
    branch_chip = both_cores(branch_low)
    mixed_grad = nt(branch_chip, output_all).astype(BF)
    mixed_grad = over_x(mixed_grad.reshape(2 * rows, n_x, width).transpose(1, 0, 2)).reshape(n_f, rows, width)
    d_output = tn(mixed_chip, branch_chip).astype(BF)
    triple_grad = attend_back_call(*guides, q, k, v, mixed_grad, exact, logs, logs_extra, cosine, sine)
    flat_grad = triple_grad.reshape(n_f * rows, 3 * width)
    turned = jnp.asarray(turn, BF)
    natural = jnp.concatenate(
        [
            nt(flat_grad[:, :width], turned).astype(BF),
            nt(flat_grad[:, width : 2 * width], turned).astype(BF),
            flat_grad[:, 2 * width :],
        ],
        1,
    )
    d_triple = tn(normed_all.reshape(n_f * rows, D), natural).astype(BF)
    d_triple_bias = jnp.sum(natural.astype(F32), 0)
    normed_grad = nt(natural, triple_own).astype(BF)
    normed_grad = lax.psum_scatter(normed_grad, ("x", "core"), scatter_dimension=0, tiled=True).astype(F32)
    attend_gain_grad = jnp.sum(normed_grad * unit_one, 0)
    attend_shift_grad = jnp.sum(normed_grad, 0)
    tokens_grad = (middle_grad + norm_back(normed_grad, unit_one, scale_one, gain_one)) * live

    d_triple = lax.all_to_all(d_triple.reshape(n_f, D // n_f, 3, width), ("x", "core"), 0, 0, tiled=True)
    d_triple = d_triple.transpose(1, 2, 0, 3).reshape(D // n_f, 3 * D)
    triple_weight_grad = lax.psum_scatter(d_triple, "dp", scatter_dimension=1, tiled=True).astype(F32)
    d_output = d_output.reshape(n_x, width, n_dp, d_part).transpose(2, 0, 1, 3).reshape(n_dp * n_x * width, d_part)
    output_weight_grad = lax.psum_scatter(d_output, ("dp", "x"), scatter_dimension=0, tiled=True).astype(F32)
    d_expand = d_expand.reshape(n_dp * n_x * (D // n_x), ff_half)
    d_expand = lax.psum_scatter(d_expand, ("dp", "x"), scatter_dimension=0, tiled=True)
    d_expand = d_expand.reshape(2, D // n_f, ff_half)
    expand_keep = mine(d_expand, core)
    expand_other = swap(mine(d_expand[::-1], core))
    expand_weight_grad = jnp.concatenate(
        [jnp.where(core == 0, expand_keep, expand_other), jnp.where(core == 0, expand_other, expand_keep)], 1
    ).astype(F32)
    d_reduce = d_reduce.reshape(n_dp * n_x * 2 * blocks * d_part, ff_half)
    d_reduce = lax.psum_scatter(d_reduce, ("dp", "x"), scatter_dimension=0, tiled=True)
    d_reduce = d_reduce.reshape(2, blocks, d_part, ff_half)
    reduce_keep = mine(d_reduce, core)
    reduce_other = swap(mine(d_reduce[::-1], core))
    reduce_weight_grad = jnp.stack(
        [jnp.where(core == 0, reduce_keep, reduce_other), jnp.where(core == 0, reduce_other, reduce_keep)], 1
    )
    reduce_weight_grad = reduce_weight_grad.transpose(0, 1, 3, 2).reshape(blocks * 2 * ff_half, d_part).astype(F32)

    zero_qkv = jnp.zeros((3, n_f, width), F32)
    triple_bias_part = lax.dynamic_update_slice(zero_qkv, d_triple_bias.reshape(3, 1, width), (0, shard, 0))
    zero_ff = jnp.zeros((n_dp, 2, ff_half), F32)
    expand_bias_part = lax.dynamic_update_slice(zero_ff, d_expand_bias.reshape(n_dp, 1, ff_half), (0, core, 0))
    sums = [
        attend_gain_grad,
        attend_shift_grad,
        jnp.sum(branch_low.astype(F32), 0),
        second_gain_grad,
        second_shift_grad,
        jnp.sum(outer_low.astype(F32), 0),
        triple_bias_part.reshape(-1),
        expand_bias_part.reshape(-1),
    ]
    sums = jnp.concatenate([s.reshape(n_dp, -1) for s in sums], 1)
    device = dp_at * n_f + shard
    total = n_dp * n_f
    bit = 1
    while bit < total:
        sums = sums + lax.ppermute(sums, ("dp", "x", "core"), [(i, i ^ bit) for i in range(total)])
        bit *= 2
    own = lax.dynamic_index_in_dim(sums, dp_at, 0, False)
    parts = []
    at = 0
    for size in [d_part] * 6 + [qkv_part, ff_part]:
        parts.append(own[at : at + size])
        at += size
    return (
        from_block(block_output, frames_local),
        from_block(tokens_grad, frames_local),
        parts[0],
        parts[1],
        triple_weight_grad,
        parts[6],
        output_weight_grad,
        parts[2],
        parts[3],
        parts[4],
        expand_weight_grad,
        parts[7],
        reduce_weight_grad,
        parts[5],
    )


def solution(mesh):
    n_dp, n_f = mesh.shape["dp"], mesh.shape["fsdp"]
    n_x = n_f // 2
    inner = jax.sharding.Mesh(mesh.devices.reshape(n_dp, n_x, 2), ("dp", "x", "core"))
    fsdp = ("x", "core")
    rows = P("dp", fsdp, None)
    weight = P(fsdp, "dp")
    vector = P("dp")
    return jax.shard_map(
        functools.partial(shards, (n_dp, n_x)),
        mesh=inner,
        in_specs=(
            rows,
            rows,
            P("dp", None),
            P("dp", None, None),
            vector,
            vector,
            weight,
            vector,
            weight,
            vector,
            vector,
            vector,
            weight,
            vector,
            weight,
            vector,
        ),
        out_specs=(
            rows,
            rows,
            vector,
            vector,
            weight,
            vector,
            weight,
            vector,
            vector,
            vector,
            weight,
            vector,
            weight,
            vector,
        ),
        check_vma=False,
    )
```

```python
import functools
import math

import jax
import jax.numpy as jnp
import numpy as np
from jax import lax
from jax.experimental import pallas as pl
from jax.experimental.pallas import tpu as pltpu
from jax.sharding import PartitionSpec as P

D = 1024
HEADS = 16
HEAD = 64
FF = 4096
GRID = 16
PATCHES = GRID * GRID
ROW_FRAME = PATCHES + 2
PAIRS = HEAD // 3 // 2
EXTRA = 16

EPSILON = 1e-06
SCALE2 = 0.125 * math.log2(math.e)
MASKED = -8e9
FAR = 1 << 20
VMEM = 60 * 1024 * 1024
BF = jnp.bfloat16
F32 = jnp.float32


def nn(left, right):
    return lax.dot_general(left, right, (((1,), (0,)), ((), ())), preferred_element_type=F32)


def nt(left, right):
    return lax.dot_general(left, right, (((1,), (1,)), ((), ())), preferred_element_type=F32)


def tn(left, right):
    return lax.dot_general(left, right, (((0,), (0,)), ((), ())), preferred_element_type=F32)


def qkv_kernel(normed, weight, bias, turn, cosine, sine, q_out, k_out, v_out, turned, turned_bias):
    width = q_out.shape[-1]
    half = width // 2

    @pl.when(pl.program_id(0) == 0)
    def _():
        for part in range(2):
            span = slice(part * width, (part + 1) * width)
            turned[:, span] = nn(weight[:, span], turn[...]).astype(BF)
            turned_bias[:, span] = nn(bias[:, span], turn[...])

    rows = normed[0]
    cos = cosine[0]
    sin = sine[0]
    for part, out in ((0, q_out), (1, k_out)):
        span = slice(part * width, (part + 1) * width)
        value = nn(rows, turned[:, span]) + turned_bias[:1, span]
        first = value[:, :half]
        second = value[:, half:]
        out[0, :, :half] = (first * cos - second * sin).astype(BF)
        out[0, :, half:] = (second * cos + first * sin).astype(BF)
    span = slice(2 * width, 3 * width)
    v_out[0] = (nn(rows, weight[:, span]) + bias[:1, span].astype(F32)).astype(BF)


def qkv_call(normed, weight, bias, turn, cosine, sine):
    sources, rows, _ = normed.shape
    width = weight.shape[1] // 3
    half = width // 2
    block = pl.BlockSpec((1, rows, width), lambda s: (s, 0, 0))
    table = pl.BlockSpec((1, rows, half), lambda s: (s, 0, 0))

    def whole(shape):
        return pl.BlockSpec(shape, lambda s: (0,) * len(shape))

    shape = jax.ShapeDtypeStruct((sources, rows, width), BF)
    return pl.pallas_call(
        qkv_kernel,
        grid=(sources,),
        in_specs=[
            pl.BlockSpec((1, rows, D), lambda s: (s, 0, 0)),
            whole(weight.shape),
            whole(bias.shape),
            whole(turn.shape),
            table,
            table,
        ],
        out_specs=[block] * 3,
        out_shape=[shape] * 3,
        scratch_shapes=[pltpu.VMEM((D, 2 * width), BF), pltpu.VMEM((bias.shape[0], 2 * width), F32)],
        compiler_params=pltpu.CompilerParams(vmem_limit_bytes=VMEM),
        cost_estimate=pl.CostEstimate(
            flops=2 * sources * rows * D * 3 * width, bytes_accessed=4 * sources * rows * D, transcendentals=0
        ),
        name="qkv_rotary",
    )(normed, weight, bias, turn, cosine, sine)


def turned_lanes(width, head):
    lane = lax.broadcasted_iota(jnp.int32, (1, width), 1)
    return (lane % (width // 2)) // (HEAD // 2) == head


def plain_lanes(width, head):
    lane = lax.broadcasted_iota(jnp.int32, (1, width), 1)
    return lane // HEAD == head


def pick(mask, array):
    return jnp.where(mask, array, jnp.zeros((), array.dtype))


def stack_heads(array, lanes):
    width = array.shape[-1]
    return jnp.concatenate([pick(lanes(width, head), array) for head in range(width // HEAD)], 0)


def unstack_heads(array, lanes):
    width = array.shape[-1]
    heads = width // HEAD
    step = array.shape[0] // heads
    total = pick(lanes(width, 0), array[:step])
    for head in range(1, heads):
        total = total + pick(lanes(width, head), array[head * step : (head + 1) * step])
    return total


def head_rows(array, head):
    half = array.shape[0] // 2
    step = HEAD // 2
    return jnp.concatenate(
        [array[head * step : (head + 1) * step], array[half + head * step : half + (head + 1) * step]], 0
    )


def value_total(v, frames_local, sources):
    total = jnp.zeros((1, v.shape[-1]), F32)
    real = lax.broadcasted_iota(jnp.int32, (EXTRA, 1), 0) < 2 * frames_local
    for s in range(sources):
        for l in range(frames_local):
            total = total + jnp.sum(v[s, l * PATCHES : (l + 1) * PATCHES].astype(F32), 0, keepdims=True)
        total = total + jnp.sum(pick(real, v[s, frames_local * PATCHES :].astype(F32)), 0, keepdims=True)
    return total


def attend_kernel(
    frames_local,
    start,
    key_frame,
    query_start,
    query_frame,
    query_pad,
    q,
    k,
    v,
    mixed,
    exact,
    logs,
    logs_extra,
    v_t,
    queries,
    acc,
    acc_extra,
    state,
    state_extra,
):
    sources, _, width = q.shape
    heads = width // HEAD
    frames = sources * frames_local
    patch_rows = frames_local * PATCHES
    length = frames * ROW_FRAME

    def frame_ref(ref, g):
        return ref[g // frames_local, pl.ds(pl.multiple_of((g % frames_local) * PATCHES, PATCHES), PATCHES), :]

    for g in range(frames):
        s, l = g // frames_local, g % frames_local
        v_t[g] = v[s, l * PATCHES : (l + 1) * PATCHES].T
    k_extra = jnp.concatenate([k[s, patch_rows:] for s in range(sources)], 0)
    v_extra_t = jnp.concatenate([v[s, patch_rows:] for s in range(sources)], 0).T
    uniform = jnp.asarray(1.0 / length, BF).astype(F32) * value_total(v, frames_local, sources)
    key_at = key_frame[:, :1]

    def weigh(scores, top):
        return jnp.exp2((scores - top) * SCALE2)

    def mix(values_t, weights, head):
        return nn(values_t[head * HEAD : (head + 1) * HEAD], weights[:, head * PATCHES : (head + 1) * PATCHES])

    def one_frame(g, _):
        first = start[g]
        queries[...] = stack_heads(frame_ref(q, g), turned_lanes)
        allowed = (key_at >= first) & (key_at <= g)
        scores_extra = jnp.where(allowed, nt(k_extra, queries[...]), MASKED)
        scores = nt(frame_ref(k, g), queries[...])
        top = jnp.maximum(jnp.max(scores_extra, 0, keepdims=True), jnp.max(scores, 0, keepdims=True))
        weights_extra = weigh(scores_extra, top)
        weights = weigh(scores, top)
        state[0:1] = top
        state[1:2] = jnp.sum(weights_extra, 0, keepdims=True) + jnp.sum(weights, 0, keepdims=True)
        weights_extra = weights_extra.astype(BF)
        weights = weights.astype(BF)
        values_t = v_t[g]
        for head in range(heads):
            acc[head] = mix(v_extra_t, weights_extra, head) + mix(values_t, weights, head)

        def one_key(f, _):
            scores = nt(frame_ref(k, f), queries[...])
            before = state[0:1]
            top = jnp.maximum(before, jnp.max(scores, 0, keepdims=True))
            fade = weigh(before, top)
            weights = weigh(scores, top)
            state[0:1] = top
            state[1:2] = state[1:2] * fade + jnp.sum(weights, 0, keepdims=True)
            weights = weights.astype(BF)
            values_t = v_t[f]
            for head in range(heads):
                acc[head] = acc[head] * fade[:, head * PATCHES : (head + 1) * PATCHES] + mix(values_t, weights, head)
            return 0

        lax.fori_loop(first, g, one_key, 0)
        total = state[1:2]
        result = jnp.concatenate(
            [acc[head] / total[:, head * PATCHES : (head + 1) * PATCHES] for head in range(heads)], 0
        ).T
        result = jnp.where(first > frames, jnp.broadcast_to(uniform, result.shape), result)
        rows = pl.ds(pl.multiple_of((g % frames_local) * PATCHES, PATCHES), PATCHES)
        exact[g // frames_local, rows, :] = result
        mixed[g // frames_local, rows, :] = result.astype(BF)
        logs[g] = jnp.broadcast_to(state[0:1] + jnp.log2(total) * (1.0 / SCALE2), (8, heads * PATCHES))
        return 0

    lax.fori_loop(0, frames, one_frame, 0)

    q_extra = stack_heads(jnp.concatenate([q[s, patch_rows:] for s in range(sources)], 0), turned_lanes)
    queries[: q_extra.shape[0]] = q_extra
    first = jnp.concatenate([query_start[:1]] * heads, 1)
    last = jnp.concatenate([query_frame[:1]] * heads, 1)
    scores = jnp.where((key_at >= first) & (key_at <= last), nt(k_extra, q_extra), MASKED)
    top = jnp.max(scores, 0, keepdims=True)
    weights = weigh(scores, top)
    state_extra[0:1] = top
    state_extra[1:2] = jnp.sum(weights, 0, keepdims=True)
    acc_extra[...] = nn(v_extra_t, weights.astype(BF))

    def extra_key(f, _):
        visible = (first <= f) & (last >= f)
        scores = jnp.where(visible, nt(frame_ref(k, f), queries[: q_extra.shape[0]]), MASKED)
        before = state_extra[0:1]
        top = jnp.maximum(before, jnp.max(scores, 0, keepdims=True))
        fade = weigh(before, top)
        weights = weigh(scores, top)
        state_extra[0:1] = top
        state_extra[1:2] = state_extra[1:2] * fade + jnp.sum(weights, 0, keepdims=True)
        acc_extra[...] = acc_extra[...] * fade + nn(v_t[f], weights.astype(BF))
        return 0

    lax.fori_loop(0, frames, extra_key, 0)
    result = unstack_heads((acc_extra[...] / state_extra[1:2]).T, plain_lanes)
    result = jnp.where(query_pad[:, :1] > 0, jnp.broadcast_to(uniform, result.shape), result)
    for s in range(sources):
        exact[s, patch_rows:, :] = result[s * EXTRA : (s + 1) * EXTRA]
        mixed[s, patch_rows:, :] = result[s * EXTRA : (s + 1) * EXTRA].astype(BF)
    logs_extra[...] = jnp.broadcast_to(
        state_extra[0:1] + jnp.log2(state_extra[1:2]) * (1.0 / SCALE2), logs_extra.shape
    )


def attend_call(start, key_frame, query_start, query_frame, query_pad, q, k, v, waits=()):
    sources, rows, width = q.shape
    frames_local = rows // PATCHES
    frames = sources * frames_local
    heads = width // HEAD
    stacked = heads * sources * EXTRA
    vmem = pl.BlockSpec(memory_space=pltpu.VMEM)
    return pl.pallas_call(
        waiting(functools.partial(attend_kernel, frames_local), 8, waits),
        in_specs=[pl.BlockSpec(memory_space=pltpu.SMEM)] + [vmem] * 7 + [ANY_REF] * len(waits),
        out_specs=[vmem] * 4,
        out_shape=[
            jax.ShapeDtypeStruct(q.shape, BF),
            jax.ShapeDtypeStruct(q.shape, F32),
            jax.ShapeDtypeStruct((frames, 8, heads * PATCHES), F32),
            jax.ShapeDtypeStruct((8, stacked), F32),
        ],
        scratch_shapes=[
            pltpu.VMEM((frames, width, PATCHES), BF),
            pltpu.VMEM((heads * PATCHES, width), BF),
            pltpu.VMEM((heads, HEAD, PATCHES), F32),
            pltpu.VMEM((width, stacked), F32),
            pltpu.VMEM((8, heads * PATCHES), F32),
            pltpu.VMEM((8, stacked), F32),
        ],
        compiler_params=pltpu.CompilerParams(vmem_limit_bytes=VMEM),
        cost_estimate=cost(
            flops=8 * heads * 256 * frames * frames * PATCHES * PATCHES // 2,
            bytes_accessed=10 * sources * rows * width,
            transcendentals=heads * frames * frames * PATCHES * PATCHES // 2,
        ),
        name="attend",
    )(start, key_frame, query_start, query_frame, query_pad, q, k, v, *waits)


def attend_back_kernel(
    frames_local,
    start,
    key_frame,
    query_start,
    query_frame,
    query_pad,
    q,
    k,
    v,
    grad,
    exact,
    logs,
    logs_extra,
    cosine,
    sine,
    turn,
    out,
    k_t,
    queries,
    grads,
    dq_t,
    dk,
    dv,
    dq_extra,
    dk_extra,
    dv_extra,
    centers,
):
    sources, _, width = q.shape
    half = width // 2
    heads = width // HEAD
    frames = sources * frames_local
    patch_rows = frames_local * PATCHES
    length = frames * ROW_FRAME
    step_rows = HEAD // 2

    def frame_ref(ref, g):
        return ref[g // frames_local, pl.ds(pl.multiple_of((g % frames_local) * PATCHES, PATCHES), PATCHES), :]

    which = lax.broadcasted_iota(jnp.int32, (8, width), 0)
    lane = lax.broadcasted_iota(jnp.int32, (8, width), 1)
    groups = (lane // HEAD == which).astype(BF)

    def center_of(grad_rows, exact_rows):
        product = grad_rows.astype(F32) * exact_rows
        high = product.astype(BF)
        low = (product - high.astype(F32)).astype(BF)
        center = nt(groups, high) + nt(groups, low)
        return jnp.concatenate([center[head : head + 1] for head in range(heads)], 1)

    def gather_extra(ref):
        return jnp.concatenate([ref[s, patch_rows:] for s in range(sources)], 0)

    for g in range(frames):
        s, l = g // frames_local, g % frames_local
        k_t[g] = k[s, l * PATCHES : (l + 1) * PATCHES].T
    k_extra = gather_extra(k)
    v_extra = gather_extra(v)
    k_extra_t = k_extra.T
    dk[...] = jnp.zeros_like(dk)
    dv[...] = jnp.zeros_like(dv)
    dk_extra[...] = jnp.zeros_like(dk_extra)
    dv_extra[...] = jnp.zeros_like(dv_extra)
    key_at = key_frame[:, :1]

    def tile(keys, values, query, query_grad, log, center, allowed):
        scores = nt(keys, query)
        inner = nt(values, query_grad)
        probs = jnp.exp2((scores - log) * SCALE2)
        if allowed is not None:
            probs = jnp.where(allowed, probs, 0.0)
        change = (probs * (inner - center)).astype(BF)
        return nn(probs.astype(BF), query_grad), nn(change, query), change

    def add_dq(ref, keys_t, change, keep):
        for head in range(heads):
            part = nn(head_rows(keys_t, head), change[:, head * PATCHES : (head + 1) * PATCHES])
            for side in range(2):
                rows = slice(side * half + head * step_rows, side * half + (head + 1) * step_rows)
                piece = part[side * step_rows : (side + 1) * step_rows]
                ref[rows] = ref[rows] + piece if keep else piece

    def one_frame(g, pad_grad):
        first = start[g]
        grad_rows = frame_ref(grad, g)
        queries[...] = stack_heads(frame_ref(q, g), turned_lanes)
        grads[...] = stack_heads(grad_rows, plain_lanes)
        centers[...] = jnp.broadcast_to(center_of(grad_rows, frame_ref(exact, g)), centers.shape)
        allowed = (key_at >= first) & (key_at <= g)
        dv_part, dk_part, change = tile(
            k_extra, v_extra, queries[...], grads[...], logs[g, :1], centers[:1], allowed
        )
        dv_extra[...] += dv_part
        dk_extra[...] += dk_part
        add_dq(dq_t.at[g], k_extra_t, change, False)

        def one_key(f, _):
            dv_part, dk_part, change = tile(
                frame_ref(k, f), frame_ref(v, f), queries[...], grads[...], logs[g, :1], centers[:1], None
            )
            dv[f] += dv_part
            dk[f] += dk_part
            add_dq(dq_t.at[g], k_t[f], change, True)
            return 0

        lax.fori_loop(first, g + 1, one_key, 0)
        return pad_grad + jnp.where(first > frames, jnp.sum(grad_rows.astype(F32), 0, keepdims=True), 0.0)

    pad_grad = lax.fori_loop(0, frames, one_frame, jnp.zeros((1, width), F32))
    g_extra = gather_extra(grad)
    pad_grad = pad_grad + jnp.sum(jnp.where(query_pad[:, :1] > 0, g_extra.astype(F32), 0.0), 0, keepdims=True)
    pad_grad = pad_grad * jnp.asarray(1.0 / length, BF).astype(F32)

    q_stack = stack_heads(gather_extra(q), turned_lanes)
    g_stack = stack_heads(g_extra, plain_lanes)
    stacked = q_stack.shape[0]
    queries[:stacked] = q_stack
    grads[:stacked] = g_stack
    first = jnp.concatenate([query_start[:1]] * heads, 1)
    last = jnp.concatenate([query_frame[:1]] * heads, 1)
    log = logs_extra[:1]
    center = center_of(g_extra, gather_extra(exact))
    allowed = (key_at >= first) & (key_at <= last)
    dv_part, dk_part, change = tile(k_extra, v_extra, q_stack, g_stack, log, center, allowed)
    dv_extra[...] += dv_part
    dk_extra[...] += dk_part
    dq_extra[...] = nn(k_extra_t, change)

    def extra_key(f, _):
        visible = (first <= f) & (last >= f)
        dv_part, dk_part, change = tile(
            frame_ref(k, f), frame_ref(v, f), queries[:stacked], grads[:stacked], log, center, visible
        )
        dv[f] += dv_part
        dk[f] += dk_part
        dq_extra[...] += nn(k_t[f], change)
        return 0

    lax.fori_loop(0, frames, extra_key, 0)

    def emit(s, rows, dq_rows, dk_rows, dv_rows, real=None):
        cos = cosine[s, rows]
        sin = sine[s, rows]
        for part, array in ((0, dq_rows), (1, dk_rows)):
            a = array[:, :half] * 0.125
            b = array[:, half:] * 0.125
            both = jnp.concatenate([(a * cos + b * sin).astype(BF), (b * cos - a * sin).astype(BF)], 1)
            both = nt(both, turn[...])
            if real is not None:
                both = pick(real, both)
            out[s, rows, part * width : (part + 1) * width] = both.astype(BF)
        total = dv_rows + pad_grad
        if real is not None:
            total = pick(real, total)
        out[s, rows, 2 * width :] = total.astype(BF)

    def emit_frame(g, _):
        rows = pl.ds(pl.multiple_of((g % frames_local) * PATCHES, PATCHES), PATCHES)
        emit(g // frames_local, rows, dq_t[g].T, dk[g], dv[g])
        return 0

    lax.fori_loop(0, frames, emit_frame, 0)
    dq_rows = unstack_heads(dq_extra[...].T, turned_lanes)
    real = lax.broadcasted_iota(jnp.int32, (EXTRA, 1), 0) < 2 * frames_local
    for s in range(sources):
        at = slice(s * EXTRA, (s + 1) * EXTRA)
        emit(s, slice(patch_rows, patch_rows + EXTRA), dq_rows[at], dk_extra[at], dv_extra[at], real)


def attend_back_call(
    start, key_frame, query_start, query_frame, query_pad, q, k, v, grad, exact, logs, logs_extra, cosine, sine, turn, waits=()
):
    sources, rows, width = q.shape
    frames_local = rows // PATCHES
    frames = sources * frames_local
    extra = sources * EXTRA
    heads = width // HEAD
    vmem = pl.BlockSpec(memory_space=pltpu.VMEM)
    return pl.pallas_call(
        waiting(functools.partial(attend_back_kernel, frames_local), 15, waits),
        in_specs=[pl.BlockSpec(memory_space=pltpu.SMEM)] + [vmem] * 14 + [ANY_REF] * len(waits),
        out_specs=vmem,
        out_shape=jax.ShapeDtypeStruct((sources, rows, 3 * width), BF),
        scratch_shapes=[
            pltpu.VMEM((frames, width, PATCHES), BF),
            pltpu.VMEM((heads * PATCHES, width), BF),
            pltpu.VMEM((heads * PATCHES, width), BF),
            pltpu.VMEM((frames, width, PATCHES), F32),
            pltpu.VMEM((frames, PATCHES, width), F32),
            pltpu.VMEM((frames, PATCHES, width), F32),
            pltpu.VMEM((width, heads * extra), F32),
            pltpu.VMEM((extra, width), F32),
            pltpu.VMEM((extra, width), F32),
            pltpu.VMEM((8, heads * PATCHES), F32),
        ],
        compiler_params=pltpu.CompilerParams(vmem_limit_bytes=VMEM),
        cost_estimate=cost(
            flops=20 * heads * 256 * frames * frames * PATCHES * PATCHES // 2,
            bytes_accessed=20 * sources * rows * width,
            transcendentals=heads * frames * frames * PATCHES * PATCHES // 2,
        ),
        name="attend_back",
    )(start, key_frame, query_start, query_frame, query_pad, q, k, v, grad, exact, logs, logs_extra, cosine, sine, turn, *waits)


def gelu_parts(hidden):
    base = 1.0 + (0.3275911 * math.sqrt(0.5)) * jnp.abs(hidden)
    guess = pl.reciprocal(base, approx=True)
    t = guess * (2.0 - base * guess)
    bell = jnp.exp2(hidden * hidden * (-0.5 * math.log2(math.e)))
    poly = 0.5 * 1.061405429
    for coefficient in (-1.453152027, 1.421413741, -0.284496736, 0.254829592):
        poly = poly * t + 0.5 * coefficient
    tail = poly * t * bell
    cdf = jnp.where(hidden < 0.0, tail, 1.0 - tail)
    return hidden * cdf, cdf + hidden * bell * (1.0 / math.sqrt(2.0 * math.pi))


def feed_body(chunk, second, outer, outer_t, weight_in, weight_out, add, final, second_grad, d_bias, second_t, active, slope):
    rows = second.shape[0]

    @pl.when(pl.program_id(0) == 0)
    def _():
        for r in range(0, rows, chunk):
            second_t[:, r : r + chunk] = second[r : r + chunk].T
        final[...] = jnp.zeros_like(final)
        second_grad[...] = jnp.zeros_like(second_grad)

    d_bias[...] = jnp.zeros_like(d_bias)
    for r in range(0, rows, chunk):
        at = slice(r, r + chunk)
        act, gradient = gelu_parts(nn(second[at], weight_in[...]) + add)
        act = act.astype(BF)
        grad = (nt(outer[at], weight_out[...]) * gradient).astype(BF)
        active[at] = act
        slope[at] = grad
        d_bias[0] += jnp.sum(grad.astype(F32), 0, keepdims=True)
        final[at] += nn(act, weight_out[...])
        second_grad[at] += nt(grad, weight_in[...])
    return nn(second_t[...], slope[...]).astype(BF), nn(outer_t[...], active[...]).astype(BF)


def feed_plain_kernel(
    chunk, second, outer, outer_t, expand, expand_bias, reduce, final, second_grad, d_bias, d_expand, d_reduce, second_t, active, slope
):
    d_expand[0], d_reduce[0] = feed_body(
        chunk, second, outer, outer_t, expand.at[0], reduce.at[0], expand_bias[0].astype(F32),
        final, second_grad, d_bias, second_t, active, slope,
    )


def feed_call(second, outer, outer_t, expand, expand_bias, reduce):
    rows = second.shape[0]
    tiles, _, wide = expand.shape
    chunk = rows // 2

    def whole(shape):
        return pl.BlockSpec(shape, lambda t: (0,) * len(shape))

    def tiled(shape):
        return pl.BlockSpec((1,) + shape[1:], lambda t: (t, 0, 0))

    return pl.pallas_call(
        functools.partial(feed_plain_kernel, chunk),
        grid=(tiles,),
        in_specs=[
            whole((rows, D)),
            whole((rows, D)),
            whole((D, rows)),
            tiled(expand.shape),
            tiled(expand_bias.shape),
            tiled(reduce.shape),
        ],
        out_specs=[whole((rows, D)), whole((rows, D)), tiled((tiles, 1, wide))] + [tiled((tiles, D, wide))] * 2,
        out_shape=[
            jax.ShapeDtypeStruct((rows, D), F32),
            jax.ShapeDtypeStruct((rows, D), F32),
            jax.ShapeDtypeStruct((tiles, 1, wide), F32),
        ]
        + [jax.ShapeDtypeStruct((tiles, D, wide), BF)] * 2,
        scratch_shapes=[pltpu.VMEM((D, rows), BF), pltpu.VMEM((rows, wide), BF), pltpu.VMEM((rows, wide), BF)],
        compiler_params=pltpu.CompilerParams(vmem_limit_bytes=VMEM),
        cost_estimate=pl.CostEstimate(
            flops=10 * rows * D * wide * tiles,
            bytes_accessed=8 * D * wide * tiles + 14 * rows * D,
            transcendentals=2 * rows * wide * tiles,
        ),
        name="feed_forward",
    )(second, outer, outer_t, expand, expand_bias, reduce)


def norm_parts(values):
    center = values - jnp.mean(values, -1, keepdims=True)
    scale = lax.rsqrt(jnp.mean(center * center, -1, keepdims=True) + EPSILON)
    return center * scale, scale


def norm_back(grad, unit, scale, gain):
    scaled = grad * gain
    mean_one = jnp.mean(scaled, -1, keepdims=True)
    mean_two = jnp.mean(scaled * unit, -1, keepdims=True)
    return scale * (scaled - mean_one - unit * mean_two)


def to_block(array, frames_local):
    split = array.reshape(frames_local, ROW_FRAME, D)
    return jnp.concatenate(
        [
            split[:, 2:].reshape(frames_local * PATCHES, D),
            split[:, :2].reshape(frames_local * 2, D),
            jnp.zeros((EXTRA - 2 * frames_local, D), array.dtype),
        ],
        0,
    )


def from_block(array, frames_local):
    patches = array[: frames_local * PATCHES].reshape(frames_local, PATCHES, D)
    extra = array[frames_local * PATCHES : frames_local * ROW_FRAME].reshape(frames_local, 2, D)
    return jnp.concatenate([extra, patches], 1).reshape(1, frames_local * ROW_FRAME, D)


def rows_of(per_frame, per_extra, sources, frames_local, fill):
    patches = jnp.broadcast_to(per_frame.reshape(sources, frames_local, 1), (sources, frames_local, PATCHES))
    pad = jnp.full((sources, EXTRA - 2 * frames_local), fill, per_frame.dtype)
    return jnp.concatenate(
        [patches.reshape(sources, -1), per_extra.reshape(sources, 2 * frames_local), pad], 1
    )


def tables(counts, present, sources, frames_local, heads):
    frames = sources * frames_local
    at = jnp.arange(frames, dtype=jnp.int32)
    first, second = counts[0], counts[1]
    inside = at < first + second
    start = jnp.where(at < first, 0, first).astype(jnp.int32)
    time = (at - start).astype(F32)
    begin = jnp.where(inside, start, FAR)
    live_extra = inside[:, None] & (present == 1)
    time_rows = rows_of(time, jnp.repeat(time, 2), sources, frames_local, 0.0)
    live_rows = rows_of(inside.astype(F32), live_extra.astype(F32), sources, frames_local, 0.0)

    patch = np.arange(PATCHES)
    grid_row = np.zeros(frames_local * PATCHES + EXTRA, np.float32)
    grid_col = np.zeros(frames_local * PATCHES + EXTRA, np.float32)
    for l in range(frames_local):
        grid_row[l * PATCHES : (l + 1) * PATCHES] = patch // GRID
        grid_col[l * PATCHES : (l + 1) * PATCHES] = patch % GRID
    lanes = np.zeros((3, HEAD // 2), np.float32)
    freq = 10000.0 ** (-np.arange(PAIRS, dtype=np.float32) / PAIRS)
    for a in range(3):
        lanes[a, a * PAIRS : (a + 1) * PAIRS] = freq
    lanes = np.tile(lanes, (1, heads))
    angle = time_rows[:, :, None] * lanes[0] + (grid_row[:, None] * lanes[1] + grid_col[:, None] * lanes[2])[None]

    def extra_of(per_frame, fill):
        both = jnp.repeat(per_frame, 2).reshape(sources, 2 * frames_local)
        pad = jnp.full((sources, EXTRA - 2 * frames_local), fill, both.dtype)
        return jnp.concatenate([both, pad], 1).reshape(-1)

    extra = sources * EXTRA
    key_frame = jnp.where(live_extra, at[:, None], -1).reshape(sources, 2 * frames_local)
    key_frame = jnp.concatenate(
        [key_frame, jnp.full((sources, EXTRA - 2 * frames_local), -1, jnp.int32)], 1
    ).reshape(-1)
    query_start = extra_of(begin, FAR)
    query_frame = extra_of(at, -1)

    def column(vector):
        return jnp.broadcast_to(vector[:, None], (extra, 128))

    def row(vector):
        return jnp.broadcast_to(vector[None], (8, extra))

    return (
        live_rows,
        jnp.cos(angle),
        jnp.sin(angle),
        (begin, column(key_frame), row(query_start), row(query_frame), column((query_start == FAR).astype(jnp.int32))),
    )


def turn_matrix(width):
    turn = np.zeros((width, width), np.float32)
    step = HEAD // 2
    for h in range(width // HEAD):
        for d in range(HEAD):
            if d < 6 * PAIRS:
                a, rest = divmod(d, 2 * PAIRS)
                side, k = divmod(rest, PAIRS)
                to = side * (width // 2) + h * step + a * PAIRS + k
            else:
                side, k = divmod(d - 6 * PAIRS, step - 3 * PAIRS)
                to = side * (width // 2) + h * step + 3 * PAIRS + k
            turn[h * HEAD + d, to] = 1.0
    return turn


SMEM_REF = pl.BlockSpec(memory_space=pltpu.SMEM)
VMEM_REF = pl.BlockSpec(memory_space=pltpu.VMEM)


ANY_REF = pl.BlockSpec(memory_space=pl.ANY)


def cost(flops=0, bytes_accessed=0, transcendentals=0):
    return pl.CostEstimate(flops=flops, bytes_accessed=bytes_accessed, transcendentals=transcendentals)


def waiting(kernel, inputs, waits, carried=0, outputs=None):
    if not waits:
        return kernel

    def run(*refs):
        used = [*refs[:inputs], *refs[inputs + len(waits) :]]
        if carried:
            del used[inputs + outputs : inputs + outputs + carried]
        kernel(*used)

    return run


def local_call(kernel, name, inputs, outputs, scratch=(), smem=0, flops=0, transcendentals=0, waits=(), carry=()):
    first = len(inputs) + len(waits)
    waits = [*waits, *carry]
    size = sum(math.prod(a.shape) * a.dtype.itemsize for a in [*inputs, *outputs])
    return pl.pallas_call(
        waiting(kernel, len(inputs), waits, len(carry), len(outputs)),
        in_specs=[SMEM_REF] * smem + [VMEM_REF] * (len(inputs) - smem) + [ANY_REF] * len(waits),
        out_specs=[VMEM_REF] * len(outputs) + [ANY_REF] * len(carry),
        out_shape=[*outputs] + [shape_of(*c.shape, dtype=c.dtype) for c in carry],
        input_output_aliases={first + i: len(outputs) + i for i in range(len(carry))},
        scratch_shapes=list(scratch),
        compiler_params=pltpu.CompilerParams(vmem_limit_bytes=VMEM),
        cost_estimate=cost(flops=flops, bytes_accessed=size, transcendentals=transcendentals),
        name=name,
    )(*inputs, *waits)


def shape_of(*shape, dtype=BF):
    return jax.ShapeDtypeStruct(shape, dtype)


def stack_kernel(*refs):
    for i, ref in enumerate(refs[:-1]):
        refs[-1][i] = ref[...]


def stack_call(pieces, waits=()):
    return local_call(stack_kernel, "stack", pieces, [shape_of(len(pieces), *pieces[0].shape)], waits=waits)[0]


def copy_kernel(source, out):
    out[...] = source[...]


def copy_call(array, waits):
    return local_call(copy_kernel, "copy", [array], [shape_of(*array.shape)], waits=waits)[0]


def add_kernel(*refs):
    total = refs[0][...].astype(F32)
    for ref in refs[1:-1]:
        total = total + ref[...].astype(F32)
    refs[-1][...] = total.astype(refs[-1].dtype)


def add_call(pieces, waits=(), dtype=BF):
    return local_call(add_kernel, "add", pieces, [shape_of(*pieces[0].shape, dtype=dtype)], waits=waits)[0]


def span(index, size):
    return pl.ds(pl.multiple_of(index * size, size), size)


def front_kernel(*refs):
    *parts, entered, near, entered_out = refs
    for s, ref in enumerate(parts):
        near[s] = ref[...]
    entered_out[...] = entered[...]


def pack_kernel(n_z, place, near, far, own, one, two, three, vectors, bias, expand_bias):
    y, z, shard = place[1], place[2], place[4]
    rows = own.shape[0]
    width = bias.shape[1] // 3
    part = near.shape[2]
    chunks = part // 128
    d_part = D // (2 * n_z)
    outs = (own, one, two, three)

    def source(dp):
        return (dp % 2) ^ y, (z - dp // 2 + n_z) % n_z

    for m in range(4):
        target = shard ^ m
        for i in range(3 * width // 128):
            j = (i // 2) * (D // 128) + 2 * target + i % 2
            side, s = source(j // chunks)
            lanes = pl.ds(pl.multiple_of((j % chunks) * 128, 128), 128)
            at = slice(i * 128, (i + 1) * 128)

            @pl.when(side == 0)
            def _(m=m, s=s, lanes=lanes, at=at):
                outs[m][:, at] = near[s, :rows, lanes]

            @pl.when(side == 1)
            def _(m=m, s=s, lanes=lanes, at=at):
                outs[m][:, at] = far[s, :rows, lanes]

            if m == 0:

                @pl.when(side == 0)
                def _(s=s, lanes=lanes, at=at):
                    bias[:, at] = near[s, rows + 6 : rows + 7, lanes].astype(F32)

                @pl.when(side == 1)
                def _(s=s, lanes=lanes, at=at):
                    bias[:, at] = far[s, rows + 6 : rows + 7, lanes].astype(F32)

    quarter = FF // (8 * n_z)
    for s in range(n_z):
        for side, ref in ((0, near), (1, far)):
            dp = 2 * ((z - s + n_z) % n_z) + (y ^ side)
            block = ref[s, rows : rows + 16].astype(F32)
            vectors[:, span(dp, d_part)] = block[:8, :d_part]
            picked = block[7:8, :quarter]
            for f in range(1, 4):
                picked = jnp.where(shard == f, block[7 + f : 8 + f, :quarter], picked)
            expand_bias[s, :, side * quarter : (side + 1) * quarter] = picked


def enter_kernel(place, e0, e1, e2, e3, w0, w1, w2, w3, bias, vectors, turn, cosine, sine, q, k, v, normed, triple, scratch, entered, weight, add):
    shard = place[4]
    width = q.shape[-1]
    half = width // 2
    step = pl.program_id(0)

    @pl.when(step == 0)
    def _():
        for m, ref in enumerate((w0, w1, w2, w3)):
            rows = span(shard ^ m, ref.shape[0])
            triple[rows, :] = ref[...]
            for part in range(2):
                at = slice(part * width, (part + 1) * width)
                weight[rows, at] = nn(ref[:, at], turn[...]).astype(BF)
            weight[rows, 2 * width :] = ref[:, 2 * width :]
        low = jnp.broadcast_to(bias[...], (8, 3 * width)).astype(BF)
        for part in range(2):
            at = slice(part * width, (part + 1) * width)
            add[:, at] = nn(low[:, at], turn[...])
        add[:, 2 * width :] = low[:, 2 * width :].astype(F32)

    for m, ref in enumerate((e0, e1, e2, e3)):

        @pl.when(step == m)
        def _(ref=ref):
            entered[...] = ref[...]

    values = entered[...].astype(F32)
    unit, _ = norm_parts(values)
    rows = (unit * vectors[0:1] + vectors[1:2]).astype(BF)
    normed[0] = rows
    scratch[...] = rows
    cos = cosine[0]
    sin = sine[0]
    for part, out in ((0, q), (1, k)):
        at = slice(part * width, (part + 1) * width)
        value = nn(scratch[...], weight[:, at]) + add[:1, at]
        first = value[:, :half]
        second = value[:, half:]
        out[0, :, :half] = (first * cos - second * sin).astype(BF)
        out[0, :, half:] = (second * cos + first * sin).astype(BF)
    v[0] = (nn(scratch[...], weight[:, 2 * width :]) + add[:1, 2 * width :]).astype(BF)


def enter_call(place, entered, weights, bias, vectors, turn, cosine, sine, waits):
    rows = entered[0].shape[0]
    width = bias.shape[-1] // 3

    def whole(array):
        return pl.BlockSpec(array.shape, lambda m, p: (0,) * array.ndim)

    def moved(*shape):
        return pl.BlockSpec((1,) + shape, lambda m, p: (p[4] ^ m, 0, 0))

    flat = [*entered, *weights, bias, vectors, turn]
    return pl.pallas_call(
        waiting(enter_kernel, 3 + len(flat), waits),
        grid_spec=pltpu.PrefetchScalarGridSpec(
            num_scalar_prefetch=1,
            grid=(4,),
            in_specs=[whole(a) for a in flat] + [moved(rows, width // 2)] * 2 + [ANY_REF] * len(waits),
            out_specs=[moved(rows, width)] * 3
            + [moved(rows, D), pl.BlockSpec((D, 3 * width), lambda m, p: (0, 0))],
            scratch_shapes=[
                pltpu.VMEM((rows, D), BF),
                pltpu.VMEM((rows, D), BF),
                pltpu.VMEM((D, 3 * width), BF),
                pltpu.VMEM((8, 3 * width), F32),
            ],
        ),
        out_shape=[shape_of(4, rows, width)] * 3 + [shape_of(4, rows, D), shape_of(D, 3 * width)],
        compiler_params=pltpu.CompilerParams(vmem_limit_bytes=VMEM),
        cost_estimate=cost(flops=8 * rows * D * 3 * width, bytes_accessed=30 * rows * D, transcendentals=0),
        name="enter",
    )(place, *flat, cosine, sine, *waits)


def part_kernel(place, mixed, own, far):
    x = place[0]
    for core in range(2):
        own[core] = mixed[2 * x + core]
        far[core] = mixed[2 * (1 - x) + core]


def project_kernel(place, own, far, output, keep, give, weight):
    x, core = place[0], place[3]
    _, rows, width = own.shape
    n_z = output.shape[0]
    d_part = output.shape[-1]
    for z in range(n_z):
        for y in range(2):
            at = (2 * z + y) * d_part
            for source in range(2):
                weight[source * width : (source + 1) * width, at : at + d_part] = output[z, y, source]

    def part(at):
        return nn(own[at], weight[span(x, width), :]) + nn(far[at], weight[span(1 - x, width), :])

    give[...] = part(1 - core).astype(BF)
    keep[...] = part(core)


def middle_kernel(entered, keep, other, vectors, middle, second):
    values = entered[...].astype(F32) + keep[...] + other[...].astype(F32) + vectors[2:3]
    middle[...] = values
    unit, _ = norm_parts(values)
    second[...] = (unit * vectors[3:4] + vectors[4:5]).astype(BF)


def rows_call(kernel, name, inputs, outputs, blocks=3, waits=()):
    rows = max(a.shape[0] for a in inputs)
    step = rows // blocks

    def spec(array):
        if array.shape[0] == 8:
            return pl.BlockSpec(array.shape, lambda i: (0, 0))
        return pl.BlockSpec((step, array.shape[1]), lambda i: (i, 0))

    size = sum(math.prod(a.shape) * a.dtype.itemsize for a in [*inputs, *outputs])
    return pl.pallas_call(
        waiting(kernel, len(inputs), waits),
        grid=(blocks,),
        in_specs=[spec(a) for a in inputs] + [ANY_REF] * len(waits),
        out_specs=[spec(a) for a in outputs],
        out_shape=list(outputs),
        compiler_params=pltpu.CompilerParams(vmem_limit_bytes=VMEM),
        cost_estimate=cost(flops=20 * rows * D, bytes_accessed=size, transcendentals=0),
        name=name,
    )(*inputs, *waits)


def add_rows(ref, rows):
    @pl.when(pl.program_id(0) == 0)
    def _():
        ref[...] = jnp.zeros_like(ref)

    for i, row in enumerate(rows):
        ref[i : i + 1] += jnp.sum(row, 0, keepdims=True)


def middle_back_kernel(middle, outer, keep, other, far, vectors, middle_grad, branch, sums):
    unit, scale = norm_parts(middle[...])
    grad = keep[...] + other[...].astype(F32) + far[...].astype(F32)
    result = outer[...].astype(F32) + norm_back(grad, unit, scale, vectors[3:4])
    middle_grad[...] = result
    low = result.astype(BF)
    branch[...] = low
    add_rows(sums, (low.astype(F32), grad * unit, grad, outer[...].astype(F32)))


def leave_rows(values, frames_local):
    pieces = []
    for l in range(frames_local):
        at = frames_local * PATCHES + 2 * l
        pieces += [values[at : at + 2], values[l * PATCHES : (l + 1) * PATCHES]]
    return jnp.concatenate(pieces, 0)


def output_kernel(frames_local, middle, keep, other, far, live, vectors, out):
    values = middle[...] + keep[...] + other[...].astype(F32) + far[...].astype(F32) + vectors[5:6]
    values = values * live[...]
    out[...] = leave_rows(values, frames_local).astype(BF)


def mixed_grad_kernel(place, branch, branch_other, weight, own, far):
    x, core = place[0], place[3]
    width = own.shape[-1]
    for at, rows in ((core, branch), (1 - core, branch_other)):
        own[at] = nt(rows[...], weight[span(x, width), :]).astype(BF)
        far[at] = nt(rows[...], weight[span(1 - x, width), :]).astype(BF)


def output_grad_kernel(place, own, far, branch, branch_other, near_y, far_y, rows_all, held):
    y, z, core = place[1], place[2], place[3]
    _, rows, width = own.shape
    _, n_z, _, d_part = near_y.shape
    rows_all[span(core, rows), :] = branch[...]
    rows_all[span(1 - core, rows), :] = branch_other[...]
    for i, ref in enumerate((own, far)):
        held[...] = tn(ref[...].reshape(2 * rows, width), rows_all[...]).astype(BF)
        for s in range(n_z):
            for flip, out in ((0, near_y), (1, far_y)):
                out[i, s] = held[:, span(2 * ((z + s) % n_z) + (y ^ flip), d_part)]


def triple_kernel(
    place, normed, triple_grad, grad_rows, triple, e0, e1, e2, e3, own, one, two, three, rows_own, rows_far, rows_give, bias, sums, entered
):
    step = pl.program_id(0)
    count, rows, wide = triple_grad.shape
    flat = triple_grad[...].reshape(count * rows, wide)
    grad = tn(normed[...].reshape(count * rows, normed.shape[-1]), flat).astype(BF)
    back = nt(grad_rows[0], triple[...])
    low = back.astype(BF)
    outs = (own, one, two, three)
    rows_outs = (rows_own, rows_give.at[0], rows_far, rows_give.at[1])
    for m, ref in enumerate((e0, e1, e2, e3)):

        @pl.when(step == m)
        def _(m=m, ref=ref):
            outs[m][...] = grad
            rows_outs[m][...] = low
            entered[...] = ref[...]

    @pl.when(step == 0)
    def _():
        bias[...] = jnp.zeros_like(bias)
        sums[...] = jnp.zeros_like(sums)

    bias[...] += jnp.sum(grad_rows[0].astype(F32), 0, keepdims=True)
    unit, _ = norm_parts(entered[...].astype(F32))
    sums[0:1] += jnp.sum(back * unit, 0, keepdims=True)
    sums[1:2] += jnp.sum(back, 0, keepdims=True)


def triple_call(place, normed, triple_grad, triple, entered, waits):
    count, rows, wide = triple_grad.shape
    part = D // count

    def fixed(shape):
        return pl.BlockSpec(shape, lambda m, p: (0,) * len(shape), pipeline_mode=pl.Buffered(1))

    outs = [shape_of(part, wide)] * 4 + [shape_of(rows, D)] * 2
    outs += [shape_of(2, rows, D), shape_of(1, wide, dtype=F32), shape_of(8, D, dtype=F32)]
    return pl.pallas_call(
        waiting(triple_kernel, 5 + len(entered), waits),
        grid_spec=pltpu.PrefetchScalarGridSpec(
            num_scalar_prefetch=1,
            grid=(count,),
            in_specs=[
                pl.BlockSpec((count, rows, part), lambda m, p: (0, 0, p[4] ^ m)),
                fixed(triple_grad.shape),
                pl.BlockSpec((1, rows, wide), lambda m, p: (p[4] ^ m, 0, 0)),
                fixed(triple.shape),
            ]
            + [fixed(e.shape) for e in entered]
            + [ANY_REF] * len(waits),
            out_specs=[fixed(o.shape) for o in outs],
            scratch_shapes=[pltpu.VMEM((rows, D), BF)],
        ),
        out_shape=outs,
        compiler_params=pltpu.CompilerParams(vmem_limit_bytes=VMEM),
        cost_estimate=cost(flops=4 * count * rows * wide * D, bytes_accessed=20 * rows * D, transcendentals=0),
        name="triple_grads",
    )(place, normed, triple_grad, triple_grad, triple, *entered, *waits)


def normed_sum_kernel(own, far, got, own_out, far_out):
    own_out[...] = (own[...].astype(F32) + got[0].astype(F32)).astype(BF)
    far_out[...] = (far[...].astype(F32) + got[1].astype(F32)).astype(BF)


def tail_sum_kernel(near, near_got, out, out_got, total):
    part = near.shape[-1]
    total[:, :, :part] = (near[...].astype(F32) + near_got[...].astype(F32)).astype(BF)
    total[:, :, part:] = (out[...].astype(F32) + out_got[...].astype(F32)).astype(BF)


def unpack_kernel(n_z, place, p0, p1, p2, p3, near, far, held):
    y, z, shard = place[1], place[2], place[4]
    part = near.shape[2]
    chunks = part // 128
    for m, ref in enumerate((p0, p1, p2, p3)):
        held[shard ^ m] = ref[...]
    for j in range(3 * D // 128):
        dp, c = divmod(j, chunks)
        per = D // 128
        at = (j // per) * 256 + (j % 2) * 128
        chunk = held[(j % per) // 2, :, at : at + 128]
        s = (dp // 2 - z + n_z) % n_z

        @pl.when(y == dp % 2)
        def _(chunk=chunk, s=s, c=c):
            near[s, :, c * 128 : (c + 1) * 128] = chunk

        @pl.when(y != dp % 2)
        def _(chunk=chunk, s=s, c=c):
            far[s, :, c * 128 : (c + 1) * 128] = chunk


def tail_kernel(*refs):
    total = refs[0][...].astype(F32)
    for ref in refs[1:-2]:
        total = total + ref[...].astype(F32)
    part = refs[-2].shape[-1]
    refs[-2][...] = total[:, :part]
    refs[-1][...] = total[:, part:]


def leave_kernel(frames_local, entered, keep, other, middle_grad, live, vectors, out):
    unit, scale = norm_parts(entered[...].astype(F32))
    grad = keep[...].astype(F32) + other[...].astype(F32)
    result = (middle_grad[...] + norm_back(grad, unit, scale, vectors[0:1])) * live[...]
    out[...] = leave_rows(result, frames_local)


def split_kernel(place, expand, reduce, own, one, two, three):
    shard = place[4]
    rows = expand.shape[0]
    part = own.shape[1]
    blocks = reduce.shape[0] // (4 * part)
    for m, ref in enumerate((own, one, two, three)):
        to = shard ^ m
        ref[:rows] = expand[:, span(to, part)]
        for p in range(blocks):
            ref[rows + p * part : rows + (p + 1) * part] = reduce[span(p * 4 + to, part), :]


def join_kernel(place, own, one, two, three, expand, reduce):
    shard = place[4]
    rows = expand.shape[0]
    part = own.shape[1]
    blocks = reduce.shape[0] // (4 * part)
    for m, ref in enumerate((own, one, two, three)):
        at = shard ^ m
        expand[:, span(at, part)] = ref[:rows].astype(F32)
        for p in range(blocks):
            reduce[span(p * 4 + at, part), :] = ref[rows + p * part : rows + (p + 1) * part].astype(F32)


def fill_weights(place, step, parts, weight_in, weight_out):
    y, z, shard = place[1], place[2], place[4]
    n_z = len(parts)
    part = parts[0].shape[-1]
    rows = D // 4
    unit = (z - step + n_z) % n_z
    if weight_in is not None:
        for s, ref in enumerate(parts):

            @pl.when(step == s)
            def _(ref=ref):
                for side in range(2):
                    for m in range(4):
                        weight_in[span(shard ^ m, rows), side * part : (side + 1) * part] = ref[side, m, :rows]

    for side in range(2):
        at = pl.ds(pl.multiple_of(rows + (y ^ side) * part, part), part)
        for s, ref in enumerate(parts):
            for flip in range(2):
                features = span(2 * ((z - s + n_z) % n_z) + (y ^ flip), part)
                weight_out[side * part : (side + 1) * part, features] = ref[flip, unit ^ shard, at, :]


def feed_kernel(
    place, normal, normal_other, cot, cot_other, p0, p1, p2, p3, bias, active, slope, keep, give, d_bias, give_acc, weight_in, weight_out
):
    step = pl.program_id(0)
    rows = normal.shape[0]
    fill_weights(place, step, (p0, p1, p2, p3), weight_in, weight_out)

    @pl.when(step == 0)
    def _():
        keep[...] = jnp.zeros_like(keep)
        give_acc[...] = jnp.zeros_like(give_acc)

    d_bias[...] = jnp.zeros_like(d_bias)
    for i, values, outer, total in ((0, normal, cot, keep), (1, normal_other, cot_other, give_acc)):
        act, gradient = gelu_parts(nn(values[...], weight_in[...]) + bias[0])
        grad = (nt(outer[...], weight_out[...]) * gradient).astype(BF)
        active[i * rows : (i + 1) * rows] = act.astype(BF)
        slope[i * rows : (i + 1) * rows] = grad
        d_bias[0] += jnp.sum(grad.astype(F32), 0, keepdims=True)
        total[...] += nt(grad, weight_in[...])

    @pl.when(step == pl.num_programs(0) - 1)
    def _():
        give[...] = give_acc[...].astype(BF)


def feed_grad_kernel(
    place,
    n0,
    n1,
    n2,
    n3,
    c0,
    c1,
    c2,
    c3,
    active,
    active_far,
    slope,
    slope_far,
    p0,
    p1,
    p2,
    p3,
    keep,
    give,
    keep_far,
    give_far,
    d0,
    d1,
    d2,
    d3,
    normal_t,
    cot_all,
    give_acc,
    keep_far_acc,
    give_far_acc,
    weight_out,
    held,
    active_all,
    slope_all,
):
    y, z, shard = place[1], place[2], place[4]
    step = pl.program_id(0)
    grads = (d0, d1, d2, d3)
    n_z = len(grads)
    part = p0.shape[-1]
    rows = n0.shape[0]
    deep = D // 4
    totals = (keep, give_acc, keep_far_acc, give_far_acc)
    fill_weights(place, step, (p0, p1, p2, p3), None, weight_out)

    @pl.when(step == 0)
    def _():
        for i, (normal, cot) in enumerate(((n0, c0), (n1, c1), (n2, c2), (n3, c3))):
            normal_t[:, i * rows : (i + 1) * rows] = normal[...].T
            cot_all[i * rows : (i + 1) * rows] = cot[...]
            totals[i][...] = jnp.zeros_like(totals[i])

    for i, (act, grad) in enumerate(((active, slope), (active_far, slope_far))):
        at = slice(i * 2 * rows, (i + 1) * 2 * rows)
        active_all[at] = act[...]
        slope_all[at] = grad[...]
        for j in range(2):
            totals[2 * i + j][...] += nn(act[j * rows : (j + 1) * rows], weight_out[...])

    held[...] = nn(normal_t[...], slope_all[...]).astype(BF)
    for s, ref in enumerate(grads):

        @pl.when((n_z - step) % n_z == s)
        def _(ref=ref):
            for side in range(2):
                for m in range(4):
                    ref[side, m, :deep] = held[span(shard ^ m, deep), side * part : (side + 1) * part]

    weight_out[...] = tn(active_all[...], cot_all[...]).astype(BF)
    unit = (z - step + n_z) % n_z
    for side in range(2):
        at = pl.ds(pl.multiple_of(deep + (y ^ side) * part, part), part)
        for s, ref in enumerate(grads):
            for flip in range(2):
                features = span(2 * ((z + s) % n_z) + (y ^ flip), part)
                ref[flip, unit ^ shard, at, :] = weight_out[side * part : (side + 1) * part, features]

    @pl.when(step == pl.num_programs(0) - 1)
    def _():
        give[...] = give_acc[...].astype(BF)
        keep_far[...] = keep_far_acc[...].astype(BF)
        give_far[...] = give_far_acc[...].astype(BF)


def feed_specs(place, n_z):
    def whole(array):
        return pl.BlockSpec(array.shape, lambda t, p: (0,) * len(array.shape), pipeline_mode=pl.Buffered(1))

    def lanes(rows, wide):
        return pl.BlockSpec((rows, wide), lambda t, p: (0, t))

    return whole, lanes


def feed_split_call(place, normal, cot, parts, bias, waits=()):
    rows = normal[0].shape[0]
    n_z = len(parts)
    wide = bias.shape[-1]
    whole, lanes = feed_specs(place, n_z)
    row = pl.BlockSpec((1, 1, wide), lambda t, p: (t, 0, 0))
    block = (rows, D)
    outs = [shape_of(2 * rows, n_z * wide)] * 2 + [shape_of(*block, dtype=F32), shape_of(*block)]
    outs += [shape_of(n_z, 1, wide, dtype=F32)]
    inputs = [*normal, *cot, *parts]
    return pl.pallas_call(
        waiting(feed_kernel, 2 + len(inputs), waits),
        grid_spec=pltpu.PrefetchScalarGridSpec(
            num_scalar_prefetch=1,
            grid=(n_z,),
            in_specs=[whole(a) for a in inputs] + [row] + [ANY_REF] * len(waits),
            out_specs=[lanes(2 * rows, wide)] * 2 + [whole(o) for o in outs[2:4]] + [row],
            scratch_shapes=[pltpu.VMEM(block, F32), pltpu.VMEM((D, wide), BF), pltpu.VMEM((wide, D), BF)],
        ),
        out_shape=outs,
        compiler_params=pltpu.CompilerParams(vmem_limit_bytes=VMEM),
        cost_estimate=cost(
            flops=12 * rows * D * wide * n_z, bytes_accessed=20 * rows * D, transcendentals=4 * rows * wide * n_z
        ),
        name="feed_forward",
    )(place, *inputs, bias, *waits)


def feed_grad_call(place, normal, cot, active, slope, parts, waits=()):
    rows = normal[0].shape[0]
    n_z = len(parts)
    wide = active[0].shape[1] // n_z
    whole, lanes = feed_specs(place, n_z)
    block = (rows, D)
    outs = [shape_of(*block, dtype=F32)] + [shape_of(*block)] * 3 + [shape_of(*p.shape) for p in parts]
    first = [*normal, *cot]
    tiles = [*active, *slope]
    return pl.pallas_call(
        waiting(feed_grad_kernel, 1 + len(first) + len(tiles) + n_z, waits),
        grid_spec=pltpu.PrefetchScalarGridSpec(
            num_scalar_prefetch=1,
            grid=(n_z,),
            in_specs=[whole(a) for a in first]
            + [lanes(2 * rows, wide)] * 4
            + [whole(p) for p in parts]
            + [ANY_REF] * len(waits),
            out_specs=[whole(o) for o in outs],
            scratch_shapes=[
                pltpu.VMEM((D, 4 * rows), BF),
                pltpu.VMEM((4 * rows, D), BF),
                pltpu.VMEM(block, F32),
                pltpu.VMEM(block, F32),
                pltpu.VMEM(block, F32),
                pltpu.VMEM((wide, D), BF),
                pltpu.VMEM((D, wide), BF),
                pltpu.VMEM((4 * rows, wide), BF),
                pltpu.VMEM((4 * rows, wide), BF),
            ],
        ),
        out_shape=outs,
        compiler_params=pltpu.CompilerParams(vmem_limit_bytes=VMEM),
        cost_estimate=cost(flops=24 * rows * D * wide * n_z, bytes_accessed=40 * rows * D),
        name="feed_grads",
    )(place, *first, *tiles, *parts, *waits)


def torus_shards(sizes, *args):
    (
        tokens,
        cotangent,
        frame_counts,
        presence,
        attend_gain,
        attend_shift,
        triple_weight,
        triple_bias,
        output_weight,
        output_bias,
        second_gain,
        second_shift,
        expand_weight,
        expand_bias,
        reduce_weight,
        reduce_bias,
    ) = args
    n_z, n_y, n_x = sizes
    n_dp = n_z * n_y
    n_f = n_x * 2
    width = D // n_f
    local_rows = tokens.shape[1]
    frames_local = local_rows // ROW_FRAME
    rows = frames_local * PATCHES + EXTRA
    z, y, x, core = (lax.axis_index(name) for name in ("z", "y", "x", "core"))
    shard = x * 2 + core
    place = jnp.stack([x, y, z, core, shard]).astype(jnp.int32)
    d_part = D // n_dp
    qkv_part = 3 * D // n_dp
    ff_part = FF // n_dp
    quarter = ff_part // 4

    def swap(array, axis="core"):
        return lax.ppermute(array, axis, [(0, 1), (1, 0)])

    def cross_over(array):
        return lax.ppermute(array, ("x", "core"), [(i, i ^ 3) for i in range(4)])

    def to_z(array, s):
        return lax.ppermute(array, "z", [(i, (i + s) % n_z) for i in range(n_z)])

    def take(array, index, axis=0):
        return lax.dynamic_index_in_dim(array, index, axis, False)

    def gather_z(array):
        return [array] + [to_z(array, s) for s in range(1, n_z)]

    def scatter_z(array, waits=(), dtype=BF):
        return add_call([array[0]] + [to_z(array[s], s) for s in range(1, n_z)], waits, dtype)

    def lane_row(vector):
        return jnp.pad(vector, (0, qkv_part - vector.shape[0]))[None]

    vectors = [attend_gain, attend_shift, output_bias, second_gain, second_shift, reduce_bias, triple_bias]
    vectors += [expand_bias[f * quarter : (f + 1) * quarter] for f in range(4)]
    packed = jnp.concatenate(
        [triple_weight] + [lane_row(v) for v in vectors] + [jnp.zeros((16 - len(vectors), qkv_part), BF)], 0
    )

    live_all, cosine, sine, guides = tables(frame_counts[0], presence[0], n_f, frames_local, width // HEAD)
    live = take(live_all, shard)[:, None]
    entered = to_block(tokens[0], frames_local) * live.astype(BF)
    outer = to_block(cotangent[0], frames_local) * live.astype(BF)

    own, one, two, three = local_call(
        split_kernel,
        "split",
        [place, expand_weight, reduce_weight],
        [shape_of(2 * (D // n_f), d_part)] * 4,
        smem=1,
    )
    feed = stack_call([own, swap(one), swap(two, "x"), cross_over(three)])
    feed_y = swap(feed, "y")
    near, entered = local_call(
        front_kernel,
        "front",
        [*gather_z(packed), entered],
        [shape_of(n_z, *packed.shape), shape_of(*entered.shape)],
        waits=[feed],
    )
    far = swap(near, "y")
    entered_x = swap(entered, "x")
    entered_all = [entered, swap(entered), entered_x]
    output_all = lax.all_gather(output_weight, ("z", "y", "x"), axis=0).reshape(n_z, n_y, n_x, width, d_part)

    own, one, two, three, vectors, bias, expand_add = local_call(
        functools.partial(pack_kernel, n_z),
        "pack",
        [place, near, far],
        [shape_of(D // n_f, 3 * width)] * 4
        + [shape_of(8, D, dtype=F32), shape_of(1, 3 * width, dtype=F32), shape_of(n_z, 1, 2 * quarter, dtype=F32)],
        smem=1,
        waits=[entered_x],
    )
    weights = [own, swap(one), swap(two, "x"), cross_over(three)]
    entered_all.append(swap(copy_call(entered_x, [own])))
    feed = stack_call([feed, feed_y], [own])
    feed_parts = [feed, to_z(feed, 1)]
    turn = jnp.asarray(turn_matrix(width), BF)
    q, k, v, normed, triple = enter_call(
        place, entered_all, weights, bias, vectors, turn, cosine, sine, [feed]
    )
    feed_parts += [to_z(feed_parts[1], 1), to_z(feed, 3)]
    outer = copy_call(outer, [normed])
    outer_x = swap(outer, "x")
    outer_all = [outer, swap(outer), outer_x]
    mixed, exact, logs, logs_extra = attend_call(*guides, q, k, v)
    mixed_own, mixed_far, outer_x = local_call(
        part_kernel,
        "mixed_parts",
        [place, mixed],
        [shape_of(2, rows, width)] * 2,
        smem=1,
        waits=[*feed_parts[2:], outer_all[1]],
        carry=[outer_x],
    )
    mixed_far = swap(mixed_far, "x")
    outer_all = [*outer_all[:2], outer_x, swap(outer_x)]
    keep, give = local_call(
        project_kernel,
        "project",
        [place, mixed_own, mixed_far, output_all],
        [shape_of(rows, D, dtype=F32), shape_of(rows, D)],
        [pltpu.VMEM((D // 2, D), BF)],
        smem=1,
        flops=4 * rows * D * D // 2,
        waits=[outer_all[3]],
    )
    output_full = output_all.transpose(2, 3, 0, 1, 4).reshape(D // 2, D)
    middle, second = rows_call(
        middle_kernel,
        "middle",
        [entered, keep, swap(give), vectors],
        [shape_of(rows, D, dtype=F32), shape_of(rows, D)],
    )
    second_all = [second, swap(second)]
    feed_both = [feed_parts, expand_add]
    active, slope, back, back_give, d_bias = feed_split_call(place, second_all, outer_all[:2], *feed_both)
    second_x = swap(second, "x")
    second_all += [second_x, swap(copy_call(second_x, [active]))]
    active_far, slope_far, back_far, back_far_give, d_bias_far = feed_split_call(
        place, second_all[2:], outer_all[2:], *feed_both, waits=[back_give]
    )
    back_give = swap(back_give)
    back_far = swap(add_call([back_far, swap(back_far_give)]), "x")
    final, final_give, final_far, final_far_give, *d_feed = feed_grad_call(
        place, second_all, outer_all, [active, active_far], [slope, slope_far], feed_parts
    )
    middle_grad, branch, sums_two = rows_call(
        middle_back_kernel,
        "middle_back",
        [middle, outer, back, back_give, back_far, vectors],
        [shape_of(rows, D, dtype=F32), shape_of(rows, D), shape_of(8, D, dtype=F32)],
        waits=[d_feed[0]],
    )
    branch_other = swap(branch)
    grad_own, grad_far = local_call(
        mixed_grad_kernel,
        "mixed_grad",
        [place, branch, branch_other, output_full],
        [shape_of(2, rows, width)] * 2,
        smem=1,
        flops=4 * rows * D * D // 2,
    )
    grad_far = swap(grad_far, "x")
    out_near, out_far = local_call(
        output_grad_kernel,
        "output_weight_grad",
        [place, mixed_own, mixed_far, branch, branch_other],
        [shape_of(n_x, n_z, width, d_part)] * 2,
        [pltpu.VMEM((2 * rows, D), BF), pltpu.VMEM((width, D), BF)],
        smem=1,
        flops=4 * rows * D * D // 2,
        waits=[grad_own],
    )
    out_far = swap(out_far, "y")
    final_far = add_call([final_far, swap(final_far_give)], [grad_own])
    final_far = swap(final_far, "x")
    final_give = swap(final_give)
    mixed_grad = jnp.where(
        x == 0, jnp.concatenate([grad_own, grad_far], 0), jnp.concatenate([grad_far, grad_own], 0)
    )
    triple_grad = attend_back_call(
        *guides, q, k, v, mixed_grad, exact, logs, logs_extra, cosine, sine, turn, waits=[out_near, final_give]
    )
    back_feed = add_call([d_feed[2], to_z(d_feed[3], 1)], [triple_grad])
    tri_own, tri_one, tri_two, tri_three, normed_own, normed_far, normed_give, d_triple_bias, sums_one = triple_call(
        place, normed, triple_grad, triple, entered_all, [back_feed, out_far, final_far]
    )
    pieces = [tri_own, swap(tri_one), swap(tri_two, "x"), cross_over(tri_three)]
    zero_qkv = jnp.zeros((3, n_f, width), F32)
    triple_bias_part = lax.dynamic_update_slice(zero_qkv, d_triple_bias.reshape(3, 1, width), (0, shard, 0))
    expand_bias_part = jnp.zeros((n_z, n_y, n_f, quarter), F32)
    d_bias = (d_bias + d_bias_far).reshape(n_z, n_y, quarter)
    for s in range(n_z):
        for side in range(n_y):
            expand_bias_part = lax.dynamic_update_slice(
                expand_bias_part, d_bias[s, side].reshape(1, 1, 1, quarter), ((z - s) % n_z, y ^ side, shard, 0)
            )
    sums = [sums_one[0], sums_one[1], sums_two[0], sums_two[1], sums_two[2], sums_two[3], triple_bias_part, expand_bias_part]
    sums = jnp.concatenate([piece.reshape(n_dp, -1) for piece in sums], 1)
    back_feed = to_z(back_feed, 1)
    normed_own, normed_far = local_call(
        normed_sum_kernel,
        "normed_sum",
        [normed_own, normed_far, swap(normed_give)],
        [shape_of(rows, D)] * 2,
        waits=[*pieces[1:], back_feed],
    )
    normed_far = swap(normed_far, "x")
    tri_near, tri_far = local_call(
        functools.partial(unpack_kernel, n_z),
        "unpack",
        [place, *pieces],
        [shape_of(n_z, D // n_f, qkv_part)] * 2,
        [pltpu.VMEM((4, D // n_f, 3 * width), BF)],
        smem=1,
        waits=[normed_own],
    )
    tri_far = swap(tri_far, "y")
    back_feed = add_call([d_feed[1], back_feed], [tri_near])
    back_feed = to_z(back_feed, 1)
    out_near = add_call([out_near, out_far], [tri_near])
    out_far = swap(out_near[1], "x")
    block_output = local_call(
        functools.partial(output_kernel, frames_local),
        "block_output",
        [middle, final, final_give, final_far, live, vectors],
        [shape_of(local_rows, D)],
        waits=[out_near],
    )[0]
    tail, sums = local_call(
        tail_sum_kernel,
        "tail_sum",
        [tri_near, tri_far, out_near[0], out_far],
        [shape_of(n_z, D // n_f, qkv_part + d_part)],
        waits=[normed_far, block_output, back_feed],
        carry=[sums],
    )
    tail_parts = [tail[0]] + [to_z(tail[s], s) for s in range(1, n_z)]
    d_feed = add_call([d_feed[0], back_feed], [tail])
    d_feed_far = swap(d_feed[1], "y")
    tokens_grad = local_call(
        functools.partial(leave_kernel, frames_local),
        "tokens_grad",
        [entered, normed_own, normed_far, middle_grad, live, vectors],
        [shape_of(local_rows, D, dtype=F32)],
        waits=[d_feed],
    )[0]
    d_feed = add_call([d_feed[0], d_feed_far], [tokens_grad])
    expand_weight_grad, reduce_weight_grad = local_call(
        join_kernel,
        "join",
        [place, d_feed[0], swap(d_feed[1]), swap(d_feed[2], "x"), cross_over(d_feed[3])],
        [shape_of(D // n_f, ff_part, dtype=F32), shape_of(FF // n_f, d_part, dtype=F32)],
        smem=1,
    )
    triple_weight_grad, output_weight_grad = local_call(
        tail_kernel,
        "tail",
        tail_parts,
        [shape_of(D // n_f, qkv_part, dtype=F32), shape_of(D // n_f, d_part, dtype=F32)],
        waits=[d_feed],
    )

    for bit in (1, 2, 4, 8, 16):
        sums = sums + lax.ppermute(sums, ("z", "y", "x", "core"), [(i, i ^ bit) for i in range(32)])
    sums = take(sums, z * n_y + y)
    parts = [sums[i * d_part : (i + 1) * d_part] for i in range(6)]
    rest = sums[6 * d_part :]
    return (
        block_output[None],
        tokens_grad[None],
        parts[0],
        parts[1],
        triple_weight_grad,
        rest[:qkv_part],
        output_weight_grad,
        parts[2],
        parts[3],
        parts[4],
        expand_weight_grad,
        rest[qkv_part:],
        reduce_weight_grad,
        parts[5],
    )


def general_shards(sizes, *args):
    (
        tokens,
        cotangent,
        frame_counts,
        presence,
        attend_gain,
        attend_shift,
        triple_weight,
        triple_bias,
        output_weight,
        output_bias,
        second_gain,
        second_shift,
        expand_weight,
        expand_bias,
        reduce_weight,
        reduce_bias,
    ) = args
    n_z, n_y, n_x = sizes
    n_dp = n_z * n_y
    n_f = n_x * 2
    heads = HEADS // n_f
    width = heads * HEAD
    local_rows = tokens.shape[1]
    frames_local = local_rows // ROW_FRAME
    rows = frames_local * PATCHES + EXTRA
    z, y, x, core = (lax.axis_index(name) for name in ("z", "y", "x", "core"))
    shard = x * 2 + core
    d_part = D // n_dp
    ff_part = FF // n_dp
    ff_half = ff_part // 2
    blocks = n_dp // n_f

    def swap(array, axis="core"):
        return lax.ppermute(array, axis, [(0, 1), (1, 0)])

    def take(array, index, axis=0):
        return lax.dynamic_index_in_dim(array, index, axis, False)

    def ordered(index, own, other, axis=0):
        low = jnp.where(index == 0, own, other)
        high = jnp.where(index == 0, other, own)
        return jnp.concatenate([low, high], axis)

    def both_cores(array, axis=0):
        return ordered(core, array, swap(array), axis)

    def exchange_f(array):
        return lax.all_to_all(array, ("x", "core"), 0, 0, tiled=True)

    def over_x(array):
        return lax.all_to_all(array, "x", 0, 0, tiled=True)

    vectors = [attend_gain, attend_shift, output_bias, second_gain, second_shift, reduce_bias, triple_bias, expand_bias]
    flat = jnp.concatenate(vectors)
    qkv_part = 3 * D // n_dp
    flat = jnp.pad(flat, (0, 16 * qkv_part - flat.shape[0])).reshape(16, qkv_part)
    packed = jnp.concatenate([triple_weight, flat], 0)
    packed = lax.all_gather(packed, ("z", "y"), axis=0)
    small = packed[:, D // n_f :].reshape(n_dp, -1)
    full = []
    at = 0
    for vector in vectors:
        full.append(small[:, at : at + vector.shape[0]].reshape(-1))
        at += vector.shape[0]
    gain_one, shift_one, output_add, gain_two, shift_two, reduce_add = (v.astype(F32)[None] for v in full[:6])
    triple_add, expand_add = full[6], full[7]
    triple_rows = packed[:, : D // n_f].transpose(1, 0, 2).reshape(D // n_f, 3, n_f, width)
    triple_own = exchange_f(triple_rows.transpose(2, 0, 1, 3)).reshape(D, 3 * width)
    bias_own = take(triple_add.reshape(3, n_f, width), shard, 1).reshape(1, 3 * width)

    expand_split = expand_weight.reshape(D // n_f, 2, ff_half)
    expand_chip = ordered(core, take(expand_split, core, 1), swap(take(expand_split, 1 - core, 1)))
    reduce_split = reduce_weight.reshape(blocks, 2, ff_half, d_part)
    reduce_chip = ordered(core, take(reduce_split, core, 1)[None], swap(take(reduce_split, 1 - core, 1))[None])
    expand_add_own = take(expand_add.reshape(n_z, n_y, 2, ff_half), core, 2)
    expand_all = lax.all_gather(expand_chip, ("z", "y", "x"), axis=0).reshape(n_z, n_y, D, ff_half)
    expand_pieces = [expand_all.transpose(0, 2, 1, 3).reshape(n_z, D, n_y * ff_half)]
    reduce_all = lax.all_gather(reduce_chip, ("z", "y", "x"), axis=0)
    reduce_pieces = [
        reduce_all.reshape(n_dp, n_dp, ff_half, d_part).transpose(1, 2, 0, 3).reshape(n_z, n_y * ff_half, D)
    ]
    expand_add_own = expand_add_own.reshape(n_z, 1, n_y * ff_half)
    output_all = lax.all_gather(output_weight, ("z", "y", "x"), axis=0)
    output_all = output_all.reshape(n_dp, n_x * width, d_part).transpose(1, 0, 2).reshape(n_x * width, D)

    live_all, cosine, sine, guides = tables(frame_counts[0], presence[0], n_f, frames_local, heads)
    live = take(live_all, shard)[:, None]
    entered = to_block(tokens[0], frames_local).astype(F32) * live
    outer = to_block(cotangent[0], frames_local).astype(F32) * live
    outer_low = outer.astype(BF)
    outer_chip = both_cores(outer_low)
    outer_chip_t = outer_chip.T
    unit_one, scale_one = norm_parts(entered)
    normed = (unit_one * gain_one + shift_one).astype(BF)
    normed_all = lax.all_gather(normed, ("x", "core"), axis=0)

    turned = jnp.asarray(turn_matrix(width), BF)
    q, k, v = qkv_call(normed_all, triple_own, bias_own, turned, cosine, sine)
    mixed, exact, logs, logs_extra = attend_call(*guides, q, k, v)

    mixed_chip = over_x(mixed.reshape(n_x, 2 * rows, width)).transpose(1, 0, 2).reshape(2 * rows, n_x * width)
    branch_part = nn(mixed_chip, output_all).reshape(2, rows, D)
    branch = take(branch_part, core) + swap(take(branch_part, 1 - core).astype(BF)).astype(F32)
    middle = entered + branch + output_add
    unit_two, scale_two = norm_parts(middle)
    second = (unit_two * gain_two + shift_two).astype(BF)
    second_chip = both_cores(second)
    final, second_grad, d_expand_bias, *d_feed = feed_call(
        second_chip, outer_chip, outer_chip_t, expand_pieces[0], expand_add_own, reduce_pieces[0]
    )
    second_grad = second_grad.reshape(2, rows, D)
    second_grad = take(second_grad, core) + swap(take(second_grad, 1 - core).astype(BF)).astype(F32)
    final = final.reshape(2, rows, D)
    final = take(final, core) + swap(take(final, 1 - core).astype(BF)).astype(F32)
    block_output = ((middle + final + reduce_add) * live).astype(BF)

    middle_grad = outer + norm_back(second_grad, unit_two, scale_two, gain_two)
    second_gain_grad = jnp.sum(second_grad * unit_two, 0)
    second_shift_grad = jnp.sum(second_grad, 0)
    branch_low = middle_grad.astype(BF)
    branch_chip = both_cores(branch_low)
    mixed_grad = nt(branch_chip, output_all).astype(BF)
    mixed_grad = over_x(mixed_grad.reshape(2 * rows, n_x, width).transpose(1, 0, 2)).reshape(n_f, rows, width)
    d_output = tn(mixed_chip, branch_chip).astype(BF)
    triple_grad = attend_back_call(*guides, q, k, v, mixed_grad, exact, logs, logs_extra, cosine, sine, turned)
    natural = triple_grad.reshape(n_f * rows, 3 * width)
    d_triple = tn(normed_all.reshape(n_f * rows, D), natural).astype(BF)
    d_triple_bias = jnp.sum(natural.astype(F32), 0)
    normed_grad = nt(natural, triple_own).astype(BF)
    normed_grad = lax.psum_scatter(normed_grad, ("x", "core"), scatter_dimension=0, tiled=True).astype(F32)
    attend_gain_grad = jnp.sum(normed_grad * unit_one, 0)
    attend_shift_grad = jnp.sum(normed_grad, 0)
    tokens_grad = (middle_grad + norm_back(normed_grad, unit_one, scale_one, gain_one)) * live

    d_triple = exchange_f(d_triple.reshape(n_f, D // n_f, 3, width))
    d_triple = d_triple.transpose(1, 2, 0, 3).reshape(D // n_f, n_z, n_y, qkv_part)
    d_triple = d_triple.reshape(D // n_f, 3 * D)
    triple_weight_grad = lax.psum_scatter(d_triple, ("z", "y"), scatter_dimension=1, tiled=True).astype(F32)
    d_output = d_output.reshape(n_x, width, n_dp, d_part).transpose(2, 0, 1, 3).reshape(n_dp * n_x * width, d_part)
    output_weight_grad = lax.psum_scatter(d_output, ("z", "y", "x"), scatter_dimension=0, tiled=True).astype(F32)
    d_expand, d_reduce = d_feed
    d_expand = d_expand.reshape(n_z, D, n_y, ff_half).transpose(0, 2, 1, 3).reshape(n_dp * D, ff_half)
    d_expand = lax.psum_scatter(d_expand, ("z", "y", "x"), scatter_dimension=0, tiled=True)
    d_expand = d_expand.reshape(2, D // n_f, ff_half)
    d_reduce = d_reduce.reshape(n_z, n_dp, d_part, n_y, ff_half).transpose(1, 0, 3, 2, 4).reshape(-1, ff_half)
    d_reduce = lax.psum_scatter(d_reduce, ("z", "y", "x"), scatter_dimension=0, tiled=True)
    d_reduce = d_reduce.reshape(2, blocks, d_part, ff_half)
    expand_weight_grad = ordered(core, take(d_expand, core), swap(take(d_expand, 1 - core)), 1).astype(F32)
    reduce_weight_grad = jnp.stack(
        [
            jnp.where(core == 0, take(d_reduce, core), swap(take(d_reduce, 1 - core))),
            jnp.where(core == 0, swap(take(d_reduce, 1 - core)), take(d_reduce, core)),
        ],
        1,
    )
    reduce_weight_grad = reduce_weight_grad.transpose(0, 1, 3, 2).reshape(blocks * 2 * ff_half, d_part).astype(F32)

    zero_qkv = jnp.zeros((3, n_f, width), F32)
    triple_bias_part = lax.dynamic_update_slice(zero_qkv, d_triple_bias.reshape(3, 1, width), (0, shard, 0))
    d_expand_bias = d_expand_bias.reshape(n_z, n_y, ff_half)
    zero_ff = jnp.zeros((n_dp, 2, ff_half), F32)
    expand_bias_part = lax.dynamic_update_slice(zero_ff, d_expand_bias.reshape(n_dp, 1, ff_half), (0, core, 0))
    sums = [
        attend_gain_grad,
        attend_shift_grad,
        jnp.sum(branch_low.astype(F32), 0),
        second_gain_grad,
        second_shift_grad,
        jnp.sum(outer_low.astype(F32), 0),
        triple_bias_part.reshape(-1),
        expand_bias_part.reshape(-1),
    ]
    sums = jnp.concatenate([s.reshape(n_dp, -1) for s in sums], 1)
    total = n_dp * n_f
    bit = 1
    while bit < total:
        sums = sums + lax.ppermute(sums, ("z", "y", "x", "core"), [(i, i ^ bit) for i in range(total)])
        bit *= 2
    own = take(sums, z * n_y + y)
    parts = []
    at = 0
    for size in [d_part] * 6 + [qkv_part, ff_part]:
        parts.append(own[at : at + size])
        at += size
    return (
        from_block(block_output, frames_local),
        from_block(tokens_grad, frames_local),
        parts[0],
        parts[1],
        triple_weight_grad,
        parts[6],
        output_weight_grad,
        parts[2],
        parts[3],
        parts[4],
        expand_weight_grad,
        parts[7],
        reduce_weight_grad,
        parts[5],
    )


def solution(mesh):
    n_dp, n_f = mesh.shape["dp"], mesh.shape["fsdp"]
    sizes = (n_dp // 2, 2, n_f // 2)
    inner = jax.sharding.Mesh(mesh.devices.reshape(*sizes, 2), ("z", "y", "x", "core"))
    dp = ("z", "y")
    fsdp = ("x", "core")
    rows = P(dp, fsdp, None)
    weight = P(fsdp, dp)
    vector = P(dp)
    return jax.shard_map(
        functools.partial(torus_shards if sizes == (4, 2, 2) else general_shards, sizes),
        mesh=inner,
        in_specs=(
            rows,
            rows,
            P(dp, None),
            P(dp, None, None),
            vector,
            vector,
            weight,
            vector,
            weight,
            vector,
            vector,
            vector,
            weight,
            vector,
            weight,
            vector,
        ),
        out_specs=(
            rows,
            rows,
            vector,
            vector,
            weight,
            vector,
            weight,
            vector,
            vector,
            vector,
            weight,
            vector,
            weight,
            vector,
        ),
        check_vma=False,
    )
```

```python
import functools
import math

import jax
import jax.numpy as jnp
import numpy as np
from jax import lax
from jax.experimental import pallas as pl
from jax.experimental.pallas import tpu as pltpu
from jax.sharding import PartitionSpec as P

D = 1024
HEADS = 16
HEAD = 64
FF = 4096
GRID = 16
PATCHES = GRID * GRID
ROW_FRAME = PATCHES + 2
PAIRS = HEAD // 3 // 2
EXTRA = 16

EPSILON = 1e-06
SCALE2 = 0.125 * math.log2(math.e)
MASKED = -8e9
FAR = 1 << 20
VMEM = 60 * 1024 * 1024
BF = jnp.bfloat16
F32 = jnp.float32


def nn(left, right):
    return lax.dot_general(left, right, (((1,), (0,)), ((), ())), preferred_element_type=F32)


def nt(left, right):
    return lax.dot_general(left, right, (((1,), (1,)), ((), ())), preferred_element_type=F32)


def tn(left, right):
    return lax.dot_general(left, right, (((0,), (0,)), ((), ())), preferred_element_type=F32)


def qkv_kernel(normed, weight, bias, turn, cosine, sine, q_out, k_out, v_out, turned, turned_bias):
    width = q_out.shape[-1]
    half = width // 2

    @pl.when(pl.program_id(0) == 0)
    def _():
        for part in range(2):
            span = slice(part * width, (part + 1) * width)
            turned[:, span] = nn(weight[:, span], turn[...]).astype(BF)
            turned_bias[:, span] = nn(bias[:, span], turn[...])

    rows = normed[0]
    cos = cosine[0]
    sin = sine[0]
    for part, out in ((0, q_out), (1, k_out)):
        span = slice(part * width, (part + 1) * width)
        value = nn(rows, turned[:, span]) + turned_bias[:1, span]
        first = value[:, :half]
        second = value[:, half:]
        out[0, :, :half] = (first * cos - second * sin).astype(BF)
        out[0, :, half:] = (second * cos + first * sin).astype(BF)
    span = slice(2 * width, 3 * width)
    v_out[0] = (nn(rows, weight[:, span]) + bias[:1, span].astype(F32)).astype(BF)


def qkv_call(normed, weight, bias, turn, cosine, sine):
    sources, rows, _ = normed.shape
    width = weight.shape[1] // 3
    half = width // 2
    block = pl.BlockSpec((1, rows, width), lambda s: (s, 0, 0))
    table = pl.BlockSpec((1, rows, half), lambda s: (s, 0, 0))

    def whole(shape):
        return pl.BlockSpec(shape, lambda s: (0,) * len(shape))

    shape = jax.ShapeDtypeStruct((sources, rows, width), BF)
    return pl.pallas_call(
        qkv_kernel,
        grid=(sources,),
        in_specs=[
            pl.BlockSpec((1, rows, D), lambda s: (s, 0, 0)),
            whole(weight.shape),
            whole(bias.shape),
            whole(turn.shape),
            table,
            table,
        ],
        out_specs=[block] * 3,
        out_shape=[shape] * 3,
        scratch_shapes=[pltpu.VMEM((D, 2 * width), BF), pltpu.VMEM((bias.shape[0], 2 * width), F32)],
        compiler_params=pltpu.CompilerParams(vmem_limit_bytes=VMEM),
        cost_estimate=pl.CostEstimate(
            flops=2 * sources * rows * D * 3 * width, bytes_accessed=4 * sources * rows * D, transcendentals=0
        ),
        name="qkv_rotary",
    )(normed, weight, bias, turn, cosine, sine)


def turned_lanes(width, head):
    lane = lax.broadcasted_iota(jnp.int32, (1, width), 1)
    return (lane % (width // 2)) // (HEAD // 2) == head


def plain_lanes(width, head):
    lane = lax.broadcasted_iota(jnp.int32, (1, width), 1)
    return lane // HEAD == head


def pick(mask, array):
    return jnp.where(mask, array, jnp.zeros((), array.dtype))


def stack_heads(array, lanes):
    width = array.shape[-1]
    return jnp.concatenate([pick(lanes(width, head), array) for head in range(width // HEAD)], 0)


def unstack_heads(array, lanes):
    width = array.shape[-1]
    heads = width // HEAD
    step = array.shape[0] // heads
    total = pick(lanes(width, 0), array[:step])
    for head in range(1, heads):
        total = total + pick(lanes(width, head), array[head * step : (head + 1) * step])
    return total


def head_rows(array, head):
    half = array.shape[0] // 2
    step = HEAD // 2
    return jnp.concatenate(
        [array[head * step : (head + 1) * step], array[half + head * step : half + (head + 1) * step]], 0
    )


def value_total(v, frames_local, sources):
    total = jnp.zeros((1, v.shape[-1]), F32)
    real = lax.broadcasted_iota(jnp.int32, (EXTRA, 1), 0) < 2 * frames_local
    for s in range(sources):
        for l in range(frames_local):
            total = total + jnp.sum(v[s, l * PATCHES : (l + 1) * PATCHES].astype(F32), 0, keepdims=True)
        total = total + jnp.sum(pick(real, v[s, frames_local * PATCHES :].astype(F32)), 0, keepdims=True)
    return total


def attend_kernel(
    frames_local,
    start,
    key_frame,
    query_start,
    query_frame,
    query_pad,
    q,
    k,
    v,
    mixed,
    exact,
    logs,
    logs_extra,
    v_t,
    queries,
    acc,
    state,
):
    sources, _, width = q.shape
    heads = width // HEAD
    frames = sources * frames_local
    patch_rows = frames_local * PATCHES
    length = frames * ROW_FRAME

    def frame_ref(ref, g):
        return ref[g // frames_local, pl.ds(pl.multiple_of((g % frames_local) * PATCHES, PATCHES), PATCHES), :]

    for g in range(frames):
        s, l = g // frames_local, g % frames_local
        v_t[g] = v[s, l * PATCHES : (l + 1) * PATCHES].T
    k_extra = jnp.concatenate([k[s, patch_rows:] for s in range(sources)], 0)
    v_extra_t = jnp.concatenate([v[s, patch_rows:] for s in range(sources)], 0).T
    uniform = jnp.asarray(1.0 / length, BF).astype(F32) * value_total(v, frames_local, sources)
    key_at = key_frame[:, :1]

    def weigh(scores, top):
        return jnp.exp2((scores - top) * SCALE2)

    def mix(values_t, weights, head):
        return nn(values_t[head * HEAD : (head + 1) * HEAD], weights[:, head * PATCHES : (head + 1) * PATCHES])

    def one_frame(g, _):
        first = start[g]
        queries[...] = stack_heads(frame_ref(q, g), turned_lanes)
        allowed = (key_at >= first) & (key_at <= g)
        scores_extra = jnp.where(allowed, nt(k_extra, queries[...]), MASKED)
        scores = nt(frame_ref(k, g), queries[...])
        top = jnp.maximum(jnp.max(scores_extra, 0, keepdims=True), jnp.max(scores, 0, keepdims=True))
        weights_extra = weigh(scores_extra, top)
        weights = weigh(scores, top)
        state[0:1] = top
        state[1:2] = jnp.sum(weights_extra, 0, keepdims=True) + jnp.sum(weights, 0, keepdims=True)
        weights_extra = weights_extra.astype(BF)
        weights = weights.astype(BF)
        values_t = v_t[g]
        for head in range(heads):
            acc[head] = mix(v_extra_t, weights_extra, head) + mix(values_t, weights, head)

        def some_keys(which):
            scores = [nt(frame_ref(k, f), queries[...]) for f in which]
            before = state[0:1]
            top = before
            for s in scores:
                top = jnp.maximum(top, jnp.max(s, 0, keepdims=True))
            fade = weigh(before, top)
            weights = [weigh(s, top) for s in scores]
            state[0:1] = top
            total = state[1:2] * fade
            for w in weights:
                total = total + jnp.sum(w, 0, keepdims=True)
            state[1:2] = total
            weights = [w.astype(BF) for w in weights]
            for head in range(heads):
                out = acc[head] * fade[:, head * PATCHES : (head + 1) * PATCHES]
                for f, w in zip(which, weights):
                    out = out + mix(v_t[f], w, head)
                acc[head] = out

        def pair(i, _):
            some_keys([first + 2 * i, first + 2 * i + 1])
            return 0

        count = jnp.maximum(g - first, 0)
        lax.fori_loop(0, count // 2, pair, 0)

        @pl.when(count % 2 == 1)
        def _():
            some_keys([g - 1])

        total = state[1:2]
        result = jnp.concatenate(
            [acc[head] / total[:, head * PATCHES : (head + 1) * PATCHES] for head in range(heads)], 0
        ).T
        result = jnp.where(first > frames, jnp.broadcast_to(uniform, result.shape), result)
        rows = pl.ds(pl.multiple_of((g % frames_local) * PATCHES, PATCHES), PATCHES)
        exact[g // frames_local, rows, :] = result
        mixed[g // frames_local, rows, :] = result.astype(BF)
        logs[g] = jnp.broadcast_to(state[0:1] + jnp.log2(total) * (1.0 / SCALE2), (8, heads * PATCHES))
        return 0

    lax.fori_loop(0, frames, one_frame, 0)

    q_extra = stack_heads(jnp.concatenate([q[s, patch_rows:] for s in range(sources)], 0), turned_lanes)
    first = jnp.concatenate([query_start[:1]] * heads, 1)
    last = jnp.concatenate([query_frame[:1]] * heads, 1)
    every = [jnp.where((key_at >= first) & (key_at <= last), nt(k_extra, q_extra), MASKED)]
    for f in range(frames):
        every.append(jnp.where((first <= f) & (last >= f), nt(frame_ref(k, f), q_extra), MASKED))
    top = jnp.max(every[0], 0, keepdims=True)
    for scores in every[1:]:
        top = jnp.maximum(top, jnp.max(scores, 0, keepdims=True))
    total = jnp.zeros_like(top)
    result = jnp.zeros((width, q_extra.shape[0]), F32)
    for scores, values_t in zip(every, [v_extra_t] + [v_t[f] for f in range(frames)]):
        weights = weigh(scores, top)
        total = total + jnp.sum(weights, 0, keepdims=True)
        result = result + nn(values_t, weights.astype(BF))
    result = unstack_heads((result / total).T, plain_lanes)
    result = jnp.where(query_pad[:, :1] > 0, jnp.broadcast_to(uniform, result.shape), result)
    for s in range(sources):
        exact[s, patch_rows:, :] = result[s * EXTRA : (s + 1) * EXTRA]
        mixed[s, patch_rows:, :] = result[s * EXTRA : (s + 1) * EXTRA].astype(BF)
    logs_extra[...] = jnp.broadcast_to(top + jnp.log2(total) * (1.0 / SCALE2), logs_extra.shape)


def attend_call(start, key_frame, query_start, query_frame, query_pad, q, k, v, waits=()):
    sources, rows, width = q.shape
    frames_local = rows // PATCHES
    frames = sources * frames_local
    heads = width // HEAD
    stacked = heads * sources * EXTRA
    vmem = pl.BlockSpec(memory_space=pltpu.VMEM)
    return pl.pallas_call(
        waiting(functools.partial(attend_kernel, frames_local), 8, waits),
        in_specs=[pl.BlockSpec(memory_space=pltpu.SMEM)] + [vmem] * 7 + [ANY_REF] * len(waits),
        out_specs=[vmem] * 4,
        out_shape=[
            jax.ShapeDtypeStruct(q.shape, BF),
            jax.ShapeDtypeStruct(q.shape, F32),
            jax.ShapeDtypeStruct((frames, 8, heads * PATCHES), F32),
            jax.ShapeDtypeStruct((8, stacked), F32),
        ],
        scratch_shapes=[
            pltpu.VMEM((frames, width, PATCHES), BF),
            pltpu.VMEM((heads * PATCHES, width), BF),
            pltpu.VMEM((heads, HEAD, PATCHES), F32),
            pltpu.VMEM((8, heads * PATCHES), F32),
        ],
        compiler_params=pltpu.CompilerParams(vmem_limit_bytes=VMEM),
        cost_estimate=cost(
            flops=8 * heads * 256 * frames * frames * PATCHES * PATCHES // 2,
            bytes_accessed=10 * sources * rows * width,
            transcendentals=heads * frames * frames * PATCHES * PATCHES // 2,
        ),
        name="attend",
    )(start, key_frame, query_start, query_frame, query_pad, q, k, v, *waits)


def attend_back_kernel(
    frames_local,
    chips,
    flip,
    start,
    key_frame,
    query_start,
    query_frame,
    query_pad,
    q,
    k,
    v,
    *rest,
):
    pieces = rest[:chips]
    (
        exact,
        logs,
        logs_extra,
        cosine,
        sine,
        turn,
        out,
        grad,
        k_t,
        queries,
        grads,
        dq_t,
        dk,
        dv,
        dq_extra,
        dk_extra,
        dv_extra,
        centers,
    ) = rest[chips:]
    sources, _, width = q.shape
    for i in range(chips):
        for core in range(2):
            grad[2 * (i ^ flip[0]) + core] = pieces[i][core]
    half = width // 2
    heads = width // HEAD
    frames = sources * frames_local
    patch_rows = frames_local * PATCHES
    length = frames * ROW_FRAME
    step_rows = HEAD // 2

    def frame_ref(ref, g):
        return ref[g // frames_local, pl.ds(pl.multiple_of((g % frames_local) * PATCHES, PATCHES), PATCHES), :]

    which = lax.broadcasted_iota(jnp.int32, (8, width), 0)
    lane = lax.broadcasted_iota(jnp.int32, (8, width), 1)
    groups = (lane // HEAD == which).astype(BF)

    def center_of(grad_rows, exact_rows):
        product = grad_rows.astype(F32) * exact_rows
        high = product.astype(BF)
        low = (product - high.astype(F32)).astype(BF)
        center = nt(groups, high) + nt(groups, low)
        return jnp.concatenate([center[head : head + 1] for head in range(heads)], 1)

    def gather_extra(ref):
        return jnp.concatenate([ref[s, patch_rows:] for s in range(sources)], 0)

    for g in range(frames):
        s, l = g // frames_local, g % frames_local
        k_t[g] = k[s, l * PATCHES : (l + 1) * PATCHES].T
    k_extra = gather_extra(k)
    v_extra = gather_extra(v)
    k_extra_t = k_extra.T
    dk_extra[...] = jnp.zeros_like(dk_extra)
    dv_extra[...] = jnp.zeros_like(dv_extra)
    key_at = key_frame[:, :1]

    def tile(keys, values, query, query_grad, log, center, allowed):
        scores = nt(keys, query)
        inner = nt(values, query_grad)
        probs = jnp.exp2((scores - log) * SCALE2)
        if allowed is not None:
            probs = jnp.where(allowed, probs, 0.0)
        change = (probs * (inner - center)).astype(BF)
        return nn(probs.astype(BF), query_grad), nn(change, query), change

    def add_dq(ref, keys_t, change, keep):
        for head in range(heads):
            part = nn(head_rows(keys_t, head), change[:, head * PATCHES : (head + 1) * PATCHES])
            for side in range(2):
                rows = slice(side * half + head * step_rows, side * half + (head + 1) * step_rows)
                piece = part[side * step_rows : (side + 1) * step_rows]
                ref[rows] = ref[rows] + piece if keep else piece

    def one_frame(g, pad_grad):
        first = start[g]
        grad_rows = frame_ref(grad, g)
        queries[...] = stack_heads(frame_ref(q, g), turned_lanes)
        grads[...] = stack_heads(grad_rows, plain_lanes)
        centers[...] = jnp.broadcast_to(center_of(grad_rows, frame_ref(exact, g)), centers.shape)
        allowed = (key_at >= first) & (key_at <= g)
        query, query_grad, log, center = queries[...], grads[...], logs[g, :1], centers[:1]
        dv_part, dk_part, change = tile(k_extra, v_extra, query, query_grad, log, center, allowed)
        dv_extra[...] += dv_part
        dk_extra[...] += dk_part
        add_dq(dq_t.at[g], k_extra_t, change, False)
        dv_part, dk_part, change = tile(
            frame_ref(k, g), frame_ref(v, g), query, query_grad, log, center, jnp.broadcast_to(first <= g, log.shape)
        )
        dv[g] = dv_part
        dk[g] = dk_part
        add_dq(dq_t.at[g], k_t[g], change, True)

        def some_keys(which):
            parts = [
                tile(frame_ref(k, f), frame_ref(v, f), queries[...], grads[...], logs[g, :1], centers[:1], None)
                for f in which
            ]
            for f, (dv_part, dk_part, _) in zip(which, parts):
                dv[f] += dv_part
                dk[f] += dk_part
            for f, (_, _, change) in zip(which, parts):
                add_dq(dq_t.at[g], k_t[f], change, True)

        def pair(i, _):
            some_keys([first + 2 * i, first + 2 * i + 1])
            return 0

        count = jnp.maximum(g - first, 0)
        lax.fori_loop(0, count // 2, pair, 0)

        @pl.when(count % 2 == 1)
        def _():
            some_keys([g - 1])

        return pad_grad + jnp.where(first > frames, jnp.sum(grad_rows.astype(F32), 0, keepdims=True), 0.0)

    pad_grad = lax.fori_loop(0, frames, one_frame, jnp.zeros((1, width), F32))
    g_extra = gather_extra(grad)
    pad_grad = pad_grad + jnp.sum(jnp.where(query_pad[:, :1] > 0, g_extra.astype(F32), 0.0), 0, keepdims=True)
    pad_grad = pad_grad * jnp.asarray(1.0 / length, BF).astype(F32)

    q_stack = stack_heads(gather_extra(q), turned_lanes)
    g_stack = stack_heads(g_extra, plain_lanes)
    stacked = q_stack.shape[0]
    queries[:stacked] = q_stack
    grads[:stacked] = g_stack
    first = jnp.concatenate([query_start[:1]] * heads, 1)
    last = jnp.concatenate([query_frame[:1]] * heads, 1)
    log = logs_extra[:1]
    center = center_of(g_extra, gather_extra(exact))
    allowed = (key_at >= first) & (key_at <= last)
    dv_part, dk_part, change = tile(k_extra, v_extra, q_stack, g_stack, log, center, allowed)
    dv_extra[...] += dv_part
    dk_extra[...] += dk_part
    dq_extra[...] = nn(k_extra_t, change)

    def extra_keys(i, _):
        which = [2 * i, 2 * i + 1]
        parts = [
            tile(
                frame_ref(k, f), frame_ref(v, f), queries[:stacked], grads[:stacked], log, center, (first <= f) & (last >= f)
            )
            for f in which
        ]
        total = dq_extra[...]
        for f, (dv_part, dk_part, change) in zip(which, parts):
            dv[f] += dv_part
            dk[f] += dk_part
            total = total + nn(k_t[f], change)
        dq_extra[...] = total
        return 0

    lax.fori_loop(0, frames // 2, extra_keys, 0)

    def emit(s, rows, dq_rows, dk_rows, dv_rows, real=None):
        cos = cosine[s, rows]
        sin = sine[s, rows]
        for part, array in ((0, dq_rows), (1, dk_rows)):
            a = array[:, :half] * 0.125
            b = array[:, half:] * 0.125
            both = jnp.concatenate([(a * cos + b * sin).astype(BF), (b * cos - a * sin).astype(BF)], 1)
            both = nt(both, turn[...])
            if real is not None:
                both = pick(real, both)
            out[s, rows, part * width : (part + 1) * width] = both.astype(BF)
        total = dv_rows + pad_grad
        if real is not None:
            total = pick(real, total)
        out[s, rows, 2 * width :] = total.astype(BF)

    def emit_frame(g, _):
        rows = pl.ds(pl.multiple_of((g % frames_local) * PATCHES, PATCHES), PATCHES)
        emit(g // frames_local, rows, dq_t[g].T, dk[g], dv[g])
        return 0

    lax.fori_loop(0, frames, emit_frame, 0)
    dq_rows = unstack_heads(dq_extra[...].T, turned_lanes)
    real = lax.broadcasted_iota(jnp.int32, (EXTRA, 1), 0) < 2 * frames_local
    for s in range(sources):
        at = slice(s * EXTRA, (s + 1) * EXTRA)
        emit(s, slice(patch_rows, patch_rows + EXTRA), dq_rows[at], dk_extra[at], dv_extra[at], real)


def attend_back_call(
    flip, start, key_frame, query_start, query_frame, query_pad, q, k, v, grad, exact, logs, logs_extra, cosine, sine, turn, waits=()
):
    chips = len(grad)
    sources, rows, width = q.shape
    frames_local = rows // PATCHES
    frames = sources * frames_local
    extra = sources * EXTRA
    heads = width // HEAD
    vmem = pl.BlockSpec(memory_space=pltpu.VMEM)
    return pl.pallas_call(
        waiting(functools.partial(attend_back_kernel, frames_local, chips), 15 + chips, waits),
        in_specs=[pl.BlockSpec(memory_space=pltpu.SMEM)] * 2 + [vmem] * (13 + chips) + [ANY_REF] * len(waits),
        out_specs=vmem,
        out_shape=jax.ShapeDtypeStruct((sources, rows, 3 * width), BF),
        scratch_shapes=[
            pltpu.VMEM((sources, rows, width), BF),
            pltpu.VMEM((frames, width, PATCHES), BF),
            pltpu.VMEM((heads * PATCHES, width), BF),
            pltpu.VMEM((heads * PATCHES, width), BF),
            pltpu.VMEM((frames, width, PATCHES), F32),
            pltpu.VMEM((frames, PATCHES, width), F32),
            pltpu.VMEM((frames, PATCHES, width), F32),
            pltpu.VMEM((width, heads * extra), F32),
            pltpu.VMEM((extra, width), F32),
            pltpu.VMEM((extra, width), F32),
            pltpu.VMEM((8, heads * PATCHES), F32),
        ],
        compiler_params=pltpu.CompilerParams(vmem_limit_bytes=VMEM),
        cost_estimate=cost(
            flops=20 * heads * 256 * frames * frames * PATCHES * PATCHES // 2,
            bytes_accessed=20 * sources * rows * width,
            transcendentals=heads * frames * frames * PATCHES * PATCHES // 2,
        ),
        name="attend_back",
    )(
        flip, start, key_frame, query_start, query_frame, query_pad, q, k, v, *grad, exact, logs, logs_extra, cosine, sine, turn, *waits
    )


def gelu_parts(hidden):
    base = 1.0 + (0.3275911 * math.sqrt(0.5)) * jnp.abs(hidden)
    guess = pl.reciprocal(base, approx=True)
    t = guess * (2.0 - base * guess)
    bell = jnp.exp2(hidden * hidden * (-0.5 * math.log2(math.e)))
    poly = 0.5 * 1.061405429
    for coefficient in (-1.453152027, 1.421413741, -0.284496736, 0.254829592):
        poly = poly * t + 0.5 * coefficient
    tail = poly * t * bell
    cdf = jnp.where(hidden < 0.0, tail, 1.0 - tail)
    return hidden * cdf, cdf + hidden * bell * (1.0 / math.sqrt(2.0 * math.pi))


def feed_body(chunk, second, outer, outer_t, weight_in, weight_out, add, final, second_grad, d_bias, second_t, active, slope):
    rows = second.shape[0]

    @pl.when(pl.program_id(0) == 0)
    def _():
        for r in range(0, rows, chunk):
            second_t[:, r : r + chunk] = second[r : r + chunk].T
        final[...] = jnp.zeros_like(final)
        second_grad[...] = jnp.zeros_like(second_grad)

    d_bias[...] = jnp.zeros_like(d_bias)
    for r in range(0, rows, chunk):
        at = slice(r, r + chunk)
        act, gradient = gelu_parts(nn(second[at], weight_in[...]) + add)
        act = act.astype(BF)
        grad = (nt(outer[at], weight_out[...]) * gradient).astype(BF)
        active[at] = act
        slope[at] = grad
        d_bias[0] += jnp.sum(grad.astype(F32), 0, keepdims=True)
        final[at] += nn(act, weight_out[...])
        second_grad[at] += nt(grad, weight_in[...])
    return nn(second_t[...], slope[...]).astype(BF), nn(outer_t[...], active[...]).astype(BF)


def feed_plain_kernel(
    chunk, second, outer, outer_t, expand, expand_bias, reduce, final, second_grad, d_bias, d_expand, d_reduce, second_t, active, slope
):
    d_expand[0], d_reduce[0] = feed_body(
        chunk, second, outer, outer_t, expand.at[0], reduce.at[0], expand_bias[0].astype(F32),
        final, second_grad, d_bias, second_t, active, slope,
    )


def feed_call(second, outer, outer_t, expand, expand_bias, reduce):
    rows = second.shape[0]
    tiles, _, wide = expand.shape
    chunk = rows // 2

    def whole(shape):
        return pl.BlockSpec(shape, lambda t: (0,) * len(shape))

    def tiled(shape):
        return pl.BlockSpec((1,) + shape[1:], lambda t: (t, 0, 0))

    return pl.pallas_call(
        functools.partial(feed_plain_kernel, chunk),
        grid=(tiles,),
        in_specs=[
            whole((rows, D)),
            whole((rows, D)),
            whole((D, rows)),
            tiled(expand.shape),
            tiled(expand_bias.shape),
            tiled(reduce.shape),
        ],
        out_specs=[whole((rows, D)), whole((rows, D)), tiled((tiles, 1, wide))] + [tiled((tiles, D, wide))] * 2,
        out_shape=[
            jax.ShapeDtypeStruct((rows, D), F32),
            jax.ShapeDtypeStruct((rows, D), F32),
            jax.ShapeDtypeStruct((tiles, 1, wide), F32),
        ]
        + [jax.ShapeDtypeStruct((tiles, D, wide), BF)] * 2,
        scratch_shapes=[pltpu.VMEM((D, rows), BF), pltpu.VMEM((rows, wide), BF), pltpu.VMEM((rows, wide), BF)],
        compiler_params=pltpu.CompilerParams(vmem_limit_bytes=VMEM),
        cost_estimate=pl.CostEstimate(
            flops=10 * rows * D * wide * tiles,
            bytes_accessed=8 * D * wide * tiles + 14 * rows * D,
            transcendentals=2 * rows * wide * tiles,
        ),
        name="feed_forward",
    )(second, outer, outer_t, expand, expand_bias, reduce)


def norm_parts(values):
    center = values - jnp.mean(values, -1, keepdims=True)
    scale = lax.rsqrt(jnp.mean(center * center, -1, keepdims=True) + EPSILON)
    return center * scale, scale


def norm_back(grad, unit, scale, gain):
    scaled = grad * gain
    mean_one = jnp.mean(scaled, -1, keepdims=True)
    mean_two = jnp.mean(scaled * unit, -1, keepdims=True)
    return scale * (scaled - mean_one - unit * mean_two)


def to_block(array, frames_local):
    split = array.reshape(frames_local, ROW_FRAME, D)
    return jnp.concatenate(
        [
            split[:, 2:].reshape(frames_local * PATCHES, D),
            split[:, :2].reshape(frames_local * 2, D),
            jnp.zeros((EXTRA - 2 * frames_local, D), array.dtype),
        ],
        0,
    )


def from_block(array, frames_local):
    patches = array[: frames_local * PATCHES].reshape(frames_local, PATCHES, D)
    extra = array[frames_local * PATCHES : frames_local * ROW_FRAME].reshape(frames_local, 2, D)
    return jnp.concatenate([extra, patches], 1).reshape(1, frames_local * ROW_FRAME, D)


def rows_of(per_frame, per_extra, sources, frames_local, fill):
    patches = jnp.broadcast_to(per_frame.reshape(sources, frames_local, 1), (sources, frames_local, PATCHES))
    pad = jnp.full((sources, EXTRA - 2 * frames_local), fill, per_frame.dtype)
    return jnp.concatenate(
        [patches.reshape(sources, -1), per_extra.reshape(sources, 2 * frames_local), pad], 1
    )


def tables(counts, present, sources, frames_local, heads):
    frames = sources * frames_local
    at = jnp.arange(frames, dtype=jnp.int32)
    first, second = counts[0], counts[1]
    inside = at < first + second
    start = jnp.where(at < first, 0, first).astype(jnp.int32)
    time = (at - start).astype(F32)
    begin = jnp.where(inside, start, FAR)
    live_extra = inside[:, None] & (present == 1)
    time_rows = rows_of(time, jnp.repeat(time, 2), sources, frames_local, 0.0)
    live_rows = rows_of(inside.astype(F32), live_extra.astype(F32), sources, frames_local, 0.0)

    patch = np.arange(PATCHES)
    grid_row = np.zeros(frames_local * PATCHES + EXTRA, np.float32)
    grid_col = np.zeros(frames_local * PATCHES + EXTRA, np.float32)
    for l in range(frames_local):
        grid_row[l * PATCHES : (l + 1) * PATCHES] = patch // GRID
        grid_col[l * PATCHES : (l + 1) * PATCHES] = patch % GRID
    lanes = np.zeros((3, HEAD // 2), np.float32)
    freq = 10000.0 ** (-np.arange(PAIRS, dtype=np.float32) / PAIRS)
    for a in range(3):
        lanes[a, a * PAIRS : (a + 1) * PAIRS] = freq
    lanes = np.tile(lanes, (1, heads))
    angle = time_rows[:, :, None] * lanes[0] + (grid_row[:, None] * lanes[1] + grid_col[:, None] * lanes[2])[None]

    def extra_of(per_frame, fill):
        both = jnp.repeat(per_frame, 2).reshape(sources, 2 * frames_local)
        pad = jnp.full((sources, EXTRA - 2 * frames_local), fill, both.dtype)
        return jnp.concatenate([both, pad], 1).reshape(-1)

    extra = sources * EXTRA
    key_frame = jnp.where(live_extra, at[:, None], -1).reshape(sources, 2 * frames_local)
    key_frame = jnp.concatenate(
        [key_frame, jnp.full((sources, EXTRA - 2 * frames_local), -1, jnp.int32)], 1
    ).reshape(-1)
    query_start = extra_of(begin, FAR)
    query_frame = extra_of(at, -1)

    def column(vector):
        return jnp.broadcast_to(vector[:, None], (extra, 128))

    def row(vector):
        return jnp.broadcast_to(vector[None], (8, extra))

    return (
        live_rows,
        jnp.cos(angle),
        jnp.sin(angle),
        (begin, column(key_frame), row(query_start), row(query_frame), column((query_start == FAR).astype(jnp.int32))),
    )


def turn_matrix(width):
    turn = np.zeros((width, width), np.float32)
    step = HEAD // 2
    for h in range(width // HEAD):
        for d in range(HEAD):
            if d < 6 * PAIRS:
                a, rest = divmod(d, 2 * PAIRS)
                side, k = divmod(rest, PAIRS)
                to = side * (width // 2) + h * step + a * PAIRS + k
            else:
                side, k = divmod(d - 6 * PAIRS, step - 3 * PAIRS)
                to = side * (width // 2) + h * step + 3 * PAIRS + k
            turn[h * HEAD + d, to] = 1.0
    return turn


SMEM_REF = pl.BlockSpec(memory_space=pltpu.SMEM)
VMEM_REF = pl.BlockSpec(memory_space=pltpu.VMEM)


ANY_REF = pl.BlockSpec(memory_space=pl.ANY)


def cost(flops=0, bytes_accessed=0, transcendentals=0):
    return pl.CostEstimate(flops=flops, bytes_accessed=bytes_accessed, transcendentals=transcendentals)


def waiting(kernel, inputs, waits, carried=0, outputs=None):
    if not waits:
        return kernel

    def run(*refs):
        used = [*refs[:inputs], *refs[inputs + len(waits) :]]
        if carried:
            del used[inputs + outputs : inputs + outputs + carried]
        kernel(*used)

    return run


def local_call(kernel, name, inputs, outputs, scratch=(), smem=0, flops=0, transcendentals=0, waits=(), carry=()):
    first = len(inputs) + len(waits)
    waits = [*waits, *carry]
    size = sum(math.prod(a.shape) * a.dtype.itemsize for a in [*inputs, *outputs])
    return pl.pallas_call(
        waiting(kernel, len(inputs), waits, len(carry), len(outputs)),
        in_specs=[SMEM_REF] * smem + [VMEM_REF] * (len(inputs) - smem) + [ANY_REF] * len(waits),
        out_specs=[VMEM_REF] * len(outputs) + [ANY_REF] * len(carry),
        out_shape=[*outputs] + [shape_of(*c.shape, dtype=c.dtype) for c in carry],
        input_output_aliases={first + i: len(outputs) + i for i in range(len(carry))},
        scratch_shapes=list(scratch),
        compiler_params=pltpu.CompilerParams(vmem_limit_bytes=VMEM),
        cost_estimate=cost(flops=1, bytes_accessed=1, transcendentals=0),
        name=name,
    )(*inputs, *waits)


def shape_of(*shape, dtype=BF):
    return jax.ShapeDtypeStruct(shape, dtype)


def stack_kernel(*refs):
    for i, ref in enumerate(refs[:-1]):
        refs[-1][i] = ref[...]


def stack_call(pieces, waits=()):
    return local_call(stack_kernel, "stack", pieces, [shape_of(len(pieces), *pieces[0].shape)], waits=waits)[0]


def add_piece_kernel(pieces, other, *outs):
    if len(outs) == 1:
        outs[0][...] = (pieces[0].astype(F32) + other[...].astype(F32)).astype(BF)
    else:
        for i, out in enumerate(outs):
            out[...] = (pieces[0, i].astype(F32) + other[i].astype(F32)).astype(BF)


def add_apart_kernel(one, two, *outs):
    for i, out in enumerate(outs):
        out[...] = (one[i].astype(F32) + two[i].astype(F32)).astype(BF)


def add_apart_call(one, two, waits, carry=()):
    return local_call(
        add_apart_kernel, "add", [one, two], [shape_of(*one.shape[1:])] * one.shape[0], waits=waits, carry=carry
    )


def add_piece_call(pieces, index, other, waits, apart=False):
    outs = [other.shape[1:]] * other.shape[0] if apart else [other.shape]
    block = pl.BlockSpec((1,) + other.shape, lambda i: (index,) + (0,) * other.ndim)

    def whole(shape):
        return pl.BlockSpec(shape, lambda i: (0,) * len(shape))

    result = pl.pallas_call(
        waiting(add_piece_kernel, 2, waits),
        grid=(1,),
        in_specs=[block, whole(other.shape)] + [ANY_REF] * len(waits),
        out_specs=[whole(o) for o in outs],
        out_shape=[shape_of(*o) for o in outs],
        compiler_params=pltpu.CompilerParams(vmem_limit_bytes=VMEM),
        cost_estimate=cost(flops=1, bytes_accessed=1, transcendentals=0),
        name="add_piece",
    )(pieces, other, *waits)
    return result if apart else result[0]


def copy_kernel(source, out):
    out[...] = source[...]


def copy_call(array, waits):
    return local_call(copy_kernel, "copy", [array], [shape_of(*array.shape)], waits=waits)[0]


def add_kernel(*refs):
    total = refs[0][...].astype(F32)
    for ref in refs[1:-1]:
        total = total + ref[...].astype(F32)
    refs[-1][...] = total.astype(refs[-1].dtype)


def add_call(pieces, waits=(), dtype=BF):
    return local_call(add_kernel, "add", pieces, [shape_of(*pieces[0].shape, dtype=dtype)], waits=waits)[0]


def span(index, size):
    return pl.ds(pl.multiple_of(index * size, size), size)


def front_kernel(*refs):
    *parts, near = refs
    for s, ref in enumerate(parts):
        near[s] = ref[...]


def pack_kernel(n_z, place, near, far, own, one, two, three, vectors, bias, expand_bias):
    y, z, shard = place[1], place[2], place[4]
    rows = own.shape[0]
    width = bias.shape[1] // 3
    part = near.shape[2]
    chunks = part // 128
    d_part = D // (2 * n_z)
    outs = (own, one, two, three)

    def source(dp):
        return (dp % 2) ^ y, (z - dp // 2 + n_z) % n_z

    for m in range(4):
        target = shard ^ m
        for i in range(3 * width // 128):
            j = (i // 2) * (D // 128) + 2 * target + i % 2
            side, s = source(j // chunks)
            lanes = pl.ds(pl.multiple_of((j % chunks) * 128, 128), 128)
            at = slice(i * 128, (i + 1) * 128)

            @pl.when(side == 0)
            def _(m=m, s=s, lanes=lanes, at=at):
                outs[m][:, at] = near[s, :rows, lanes]

            @pl.when(side == 1)
            def _(m=m, s=s, lanes=lanes, at=at):
                outs[m][:, at] = far[s, :rows, lanes]

            if m == 0:

                @pl.when(side == 0)
                def _(s=s, lanes=lanes, at=at):
                    bias[:, at] = near[s, rows + 6 : rows + 7, lanes].astype(F32)

                @pl.when(side == 1)
                def _(s=s, lanes=lanes, at=at):
                    bias[:, at] = far[s, rows + 6 : rows + 7, lanes].astype(F32)

    quarter = FF // (8 * n_z)
    for s in range(n_z):
        for side, ref in ((0, near), (1, far)):
            dp = 2 * ((z - s + n_z) % n_z) + (y ^ side)
            block = ref[s, rows : rows + 16].astype(F32)
            vectors[:, span(dp, d_part)] = block[:8, :d_part]
            picked = block[7:8, :quarter]
            for f in range(1, 4):
                picked = jnp.where(shard == f, block[7 + f : 8 + f, :quarter], picked)
            expand_bias[s, :, side * quarter : (side + 1) * quarter] = picked


def enter_kernel(place, e0, e1, e2, e3, w0, w1, w2, w3, bias, vectors, turn, cosine, sine, q, k, v, normed, triple, scratch, entered, weight, add):
    shard = place[4]
    width = q.shape[-1]
    half = width // 2
    step = pl.program_id(0)

    @pl.when(step == 0)
    def _():
        for m, ref in enumerate((w0, w1, w2, w3)):
            rows = span(shard ^ m, ref.shape[0])
            triple[rows, :] = ref[...]
            for part in range(2):
                at = slice(part * width, (part + 1) * width)
                weight[rows, at] = nn(ref[:, at], turn[...]).astype(BF)
            weight[rows, 2 * width :] = ref[:, 2 * width :]
        low = jnp.broadcast_to(bias[...], (8, 3 * width)).astype(BF)
        for part in range(2):
            at = slice(part * width, (part + 1) * width)
            add[:, at] = nn(low[:, at], turn[...])
        add[:, 2 * width :] = low[:, 2 * width :].astype(F32)

    for m, ref in enumerate((e0, e1, e2, e3)):

        @pl.when(step == m)
        def _(ref=ref):
            entered[...] = ref[...]

    values = entered[...].astype(F32)
    unit, _ = norm_parts(values)
    rows = (unit * vectors[0:1] + vectors[1:2]).astype(BF)
    normed[0] = rows
    scratch[...] = rows
    cos = cosine[0]
    sin = sine[0]
    for part, out in ((0, q), (1, k)):
        at = slice(part * width, (part + 1) * width)
        value = nn(scratch[...], weight[:, at]) + add[:1, at]
        first = value[:, :half]
        second = value[:, half:]
        out[0, :, :half] = (first * cos - second * sin).astype(BF)
        out[0, :, half:] = (second * cos + first * sin).astype(BF)
    v[0] = (nn(scratch[...], weight[:, 2 * width :]) + add[:1, 2 * width :]).astype(BF)


def enter_call(place, entered, weights, bias, vectors, turn, cosine, sine, waits):
    rows = entered[0].shape[0]
    width = bias.shape[-1] // 3

    def whole(array):
        return pl.BlockSpec(array.shape, lambda m, p: (0,) * array.ndim)

    def moved(*shape):
        return pl.BlockSpec((1,) + shape, lambda m, p: (p[4] ^ m, 0, 0))

    flat = [*entered, *weights, bias, vectors, turn]
    return pl.pallas_call(
        waiting(enter_kernel, 3 + len(flat), waits),
        grid_spec=pltpu.PrefetchScalarGridSpec(
            num_scalar_prefetch=1,
            grid=(4,),
            in_specs=[whole(a) for a in flat] + [moved(rows, width // 2)] * 2 + [ANY_REF] * len(waits),
            out_specs=[moved(rows, width)] * 3
            + [moved(rows, D), pl.BlockSpec((D, 3 * width), lambda m, p: (0, 0))],
            scratch_shapes=[
                pltpu.VMEM((rows, D), BF),
                pltpu.VMEM((rows, D), BF),
                pltpu.VMEM((D, 3 * width), BF),
                pltpu.VMEM((8, 3 * width), F32),
            ],
        ),
        out_shape=[shape_of(4, rows, width)] * 3 + [shape_of(4, rows, D), shape_of(D, 3 * width)],
        compiler_params=pltpu.CompilerParams(vmem_limit_bytes=VMEM),
        cost_estimate=cost(flops=8 * rows * D * 3 * width, bytes_accessed=30 * rows * D, transcendentals=0),
        name="enter",
    )(place, *flat, cosine, sine, *waits)


def part_kernel(place, mixed, own, far):
    x = place[0]
    for core in range(2):
        own[core] = mixed[2 * x + core]
        far[core] = mixed[2 * (1 - x) + core]


def project_kernel(place, own, far, output, keep, give, weight):
    x, core = place[0], place[3]
    _, rows, width = own.shape
    n_z = output.shape[0]
    d_part = output.shape[-1]
    for z in range(n_z):
        for y in range(2):
            at = (2 * z + y) * d_part
            for source in range(2):
                weight[source * width : (source + 1) * width, at : at + d_part] = output[z, y, source]

    def part(at):
        return nn(own[at], weight[span(x, width), :]) + nn(far[at], weight[span(1 - x, width), :])

    give[...] = part(1 - core).astype(BF)
    keep[...] = part(core)


def middle_kernel(entered, keep, other, vectors, middle, second):
    values = entered[...].astype(F32) + keep[...] + other[...].astype(F32) + vectors[2:3]
    middle[...] = values
    unit, _ = norm_parts(values)
    second[...] = (unit * vectors[3:4] + vectors[4:5]).astype(BF)


def rows_call(kernel, name, inputs, outputs, blocks=3, waits=()):
    rows = max(a.shape[0] for a in inputs)
    step = rows // blocks

    def spec(array):
        if array.shape[0] == 8:
            return pl.BlockSpec(array.shape, lambda i: (0, 0))
        return pl.BlockSpec((step, array.shape[1]), lambda i: (i, 0))

    size = sum(math.prod(a.shape) * a.dtype.itemsize for a in [*inputs, *outputs])
    return pl.pallas_call(
        waiting(kernel, len(inputs), waits),
        grid=(blocks,),
        in_specs=[spec(a) for a in inputs] + [ANY_REF] * len(waits),
        out_specs=[spec(a) for a in outputs],
        out_shape=list(outputs),
        compiler_params=pltpu.CompilerParams(vmem_limit_bytes=VMEM),
        cost_estimate=cost(flops=1, bytes_accessed=1, transcendentals=0),
        name=name,
    )(*inputs, *waits)


def add_rows(ref, rows):
    @pl.when(pl.program_id(0) == 0)
    def _():
        ref[...] = jnp.zeros_like(ref)

    for i, row in enumerate(rows):
        ref[i : i + 1] += jnp.sum(row, 0, keepdims=True)


def middle_back_kernel(middle, outer, keep, other, far, vectors, middle_grad, branch, sums):
    unit, scale = norm_parts(middle[...])
    grad = keep[...] + other[...].astype(F32) + far[...].astype(F32)
    result = outer[...].astype(F32) + norm_back(grad, unit, scale, vectors[3:4])
    middle_grad[...] = result
    low = result.astype(BF)
    branch[...] = low
    add_rows(sums, (low.astype(F32), grad * unit, grad, outer[...].astype(F32)))


def leave_rows(values, frames_local):
    pieces = []
    for l in range(frames_local):
        at = frames_local * PATCHES + 2 * l
        pieces += [values[at : at + 2], values[l * PATCHES : (l + 1) * PATCHES]]
    return jnp.concatenate(pieces, 0)


def output_kernel(frames_local, middle, keep, other, far, live, vectors, out):
    values = middle[...] + keep[...] + other[...].astype(F32) + far[...].astype(F32) + vectors[5:6]
    values = values * live[...]
    out[...] = leave_rows(values, frames_local).astype(BF)


def mixed_grad_kernel(place, branch, branch_other, weight, own, far):
    x, core = place[0], place[3]
    width = own.shape[-1]
    for at, rows in ((core, branch), (1 - core, branch_other)):
        own[at] = nt(rows[...], weight[span(x, width), :]).astype(BF)
        far[at] = nt(rows[...], weight[span(1 - x, width), :]).astype(BF)


def output_grad_kernel(place, own, far, branch, branch_other, near_y, far_y, rows_all, held):
    y, z, core = place[1], place[2], place[3]
    _, rows, width = own.shape
    _, n_z, _, d_part = near_y.shape
    rows_all[span(core, rows), :] = branch[...]
    rows_all[span(1 - core, rows), :] = branch_other[...]
    for i, ref in enumerate((own, far)):
        held[...] = tn(ref[...].reshape(2 * rows, width), rows_all[...]).astype(BF)
        for s in range(n_z):
            for flip, out in ((0, near_y), (1, far_y)):
                out[i, s] = held[:, span(2 * ((z + s) % n_z) + (y ^ flip), d_part)]


def triple_kernel(
    place, normed, triple_grad, grad_rows, triple, e0, e1, e2, e3, own, one, two, three, rows_own, rows_far, rows_give, bias, sums, entered, held
):
    step = pl.program_id(0)
    count, rows, wide = triple_grad.shape
    outs = (own, one, two, three)
    rows_outs = (rows_own, rows_give.at[0], rows_far, rows_give.at[1])

    @pl.when(step == 0)
    def _():
        bias[...] = jnp.zeros_like(bias)
        sums[...] = jnp.zeros_like(sums)

    for m, ref in enumerate((e0, e1, e2, e3)):

        @pl.when(step == m)
        def _(ref=ref):
            entered[...] = ref[...]

    flat = triple_grad[...].reshape(count * rows, wide)
    held[...] = tn(normed[...].reshape(count * rows, normed.shape[-1]), flat).astype(BF)
    back = nt(grad_rows[0], triple[...])
    unit, _ = norm_parts(entered[...].astype(F32))
    sums[0:1] += jnp.sum(back * unit, 0, keepdims=True)
    sums[1:2] += jnp.sum(back, 0, keepdims=True)
    entered[...] = back.astype(BF)
    bias[...] += jnp.sum(grad_rows[0].astype(F32), 0, keepdims=True)
    for m in range(4):

        @pl.when(step == m)
        def _(m=m):
            outs[m][...] = held[...]
            rows_outs[m][...] = entered[...]


def triple_call(place, normed, triple_grad, triple, entered, waits):
    count, rows, wide = triple_grad.shape
    part = D // count

    def fixed(shape):
        return pl.BlockSpec(shape, lambda m, p: (0,) * len(shape), pipeline_mode=pl.Buffered(1))

    outs = [shape_of(part, wide)] * 4 + [shape_of(rows, D)] * 2
    outs += [shape_of(2, rows, D), shape_of(1, wide, dtype=F32), shape_of(8, D, dtype=F32)]
    return pl.pallas_call(
        waiting(triple_kernel, 5 + len(entered), waits),
        grid_spec=pltpu.PrefetchScalarGridSpec(
            num_scalar_prefetch=1,
            grid=(count,),
            in_specs=[
                pl.BlockSpec((count, rows, part), lambda m, p: (0, 0, p[4] ^ m)),
                fixed(triple_grad.shape),
                pl.BlockSpec((1, rows, wide), lambda m, p: (p[4] ^ m, 0, 0)),
                fixed(triple.shape),
            ]
            + [fixed(e.shape) for e in entered]
            + [ANY_REF] * len(waits),
            out_specs=[fixed(o.shape) for o in outs],
            scratch_shapes=[pltpu.VMEM((rows, D), BF), pltpu.VMEM((part, wide), BF)],
        ),
        out_shape=outs,
        compiler_params=pltpu.CompilerParams(vmem_limit_bytes=VMEM),
        cost_estimate=cost(flops=4 * count * rows * wide * D, bytes_accessed=20 * rows * D, transcendentals=0),
        name="triple_grads",
    )(place, normed, triple_grad, triple_grad, triple, *entered, *waits)


def normed_sum_kernel(own, far, got, own_out, far_out):
    own_out[...] = (own[...].astype(F32) + got[0].astype(F32)).astype(BF)
    far_out[...] = (far[...].astype(F32) + got[1].astype(F32)).astype(BF)


def tail_sum_kernel(near, near_got, out, out_got, *totals):
    part = near.shape[-1]
    for s, total in enumerate(totals):
        total[:, :part] = (near[s].astype(F32) + near_got[s].astype(F32)).astype(BF)
        total[:, part:] = (out[0, s].astype(F32) + out_got[s].astype(F32)).astype(BF)


def unpack_kernel(n_z, place, p0, p1, p2, p3, near, far, held):
    y, z, shard = place[1], place[2], place[4]
    part = near.shape[2]
    chunks = part // 128
    for m, ref in enumerate((p0, p1, p2, p3)):
        held[shard ^ m] = ref[...]
    for j in range(3 * D // 128):
        dp, c = divmod(j, chunks)
        per = D // 128
        at = (j // per) * 256 + (j % 2) * 128
        chunk = held[(j % per) // 2, :, at : at + 128]
        s = (dp // 2 - z + n_z) % n_z

        @pl.when(y == dp % 2)
        def _(chunk=chunk, s=s, c=c):
            near[s, :, c * 128 : (c + 1) * 128] = chunk

        @pl.when(y != dp % 2)
        def _(chunk=chunk, s=s, c=c):
            far[s, :, c * 128 : (c + 1) * 128] = chunk


def tail_kernel(*refs):
    total = refs[0][...].astype(F32)
    for ref in refs[1:-2]:
        total = total + ref[...].astype(F32)
    part = refs[-2].shape[-1]
    refs[-2][...] = total[:, :part]
    refs[-1][...] = total[:, part:]


def leave_kernel(frames_local, entered, keep, other, middle_grad, live, vectors, out):
    unit, scale = norm_parts(entered[...].astype(F32))
    grad = keep[...].astype(F32) + other[...].astype(F32)
    result = (middle_grad[...] + norm_back(grad, unit, scale, vectors[0:1])) * live[...]
    out[...] = leave_rows(result, frames_local)


def split_kernel(place, expand, reduce, own, one, two, three):
    shard = place[4]
    rows = expand.shape[0]
    part = own.shape[1]
    blocks = reduce.shape[0] // (4 * part)
    for m, ref in enumerate((own, one, two, three)):
        to = shard ^ m
        ref[:rows] = expand[:, span(to, part)]
        for p in range(blocks):
            ref[rows + p * part : rows + (p + 1) * part] = reduce[span(p * 4 + to, part), :]


def join_kernel(place, own, one, two, three, expand, reduce):
    shard = place[4]
    rows = expand.shape[0]
    part = own.shape[1]
    blocks = reduce.shape[0] // (4 * part)
    for m, ref in enumerate((own, one, two, three)):
        at = shard ^ m
        expand[:, span(at, part)] = ref[:rows].astype(F32)
        for p in range(blocks):
            reduce[span(p * 4 + at, part), :] = ref[rows + p * part : rows + (p + 1) * part].astype(F32)


def fill_weights(place, near, far, weight_in, weight_out):
    y, z, shard = place[1], place[2], place[4]
    n_z = len(near)
    part = near[0].shape[-1]
    rows = D // 4
    for s in range(n_z):
        for side, ref in ((0, near[s]), (1, far[s])):
            if weight_in is not None:
                for m in range(4):
                    weight_in[s, span(shard ^ m, rows), side * part : (side + 1) * part] = ref[m, :rows]
            features = span(2 * ((z - s + n_z) % n_z) + (y ^ side), part)
            for tile in range(n_z):
                unit = (z - tile + n_z) % n_z
                for flip in range(2):
                    at = pl.ds(pl.multiple_of(rows + (y ^ flip) * part, part), part)
                    weight_out[tile, flip * part : (flip + 1) * part, features] = ref[unit ^ shard, at, :]


def feed_kernel(
    place, normal, normal_other, cot, cot_other, p0, p1, p2, p3, f0, f1, f2, f3, bias, active, slope, keep, give, d_bias, give_acc, weight_in, weight_out
):
    step = pl.program_id(0)
    rows = normal.shape[0]

    @pl.when(step == 0)
    def _():
        fill_weights(place, (p0, p1, p2, p3), (f0, f1, f2, f3), weight_in, weight_out)
        keep[...] = jnp.zeros_like(keep)
        give_acc[...] = jnp.zeros_like(give_acc)

    d_bias[...] = jnp.zeros_like(d_bias)
    for i, values, outer, total in ((0, normal, cot, keep), (1, normal_other, cot_other, give_acc)):
        act, gradient = gelu_parts(nn(values[...], weight_in[step]) + bias[0])
        grad = (nt(outer[...], weight_out[step]) * gradient).astype(BF)
        active[i * rows : (i + 1) * rows] = act.astype(BF)
        slope[i * rows : (i + 1) * rows] = grad
        d_bias[0] += jnp.sum(grad.astype(F32), 0, keepdims=True)
        total[...] += nt(grad, weight_in[step])

    @pl.when(step == pl.num_programs(0) - 1)
    def _():
        give[...] = give_acc[...].astype(BF)


def feed_grad_kernel(
    place,
    n0,
    n1,
    n2,
    n3,
    c0,
    c1,
    c2,
    c3,
    active,
    active_far,
    slope,
    slope_far,
    p0,
    p1,
    p2,
    p3,
    f0,
    f1,
    f2,
    f3,
    keep,
    give,
    keep_far,
    give_far,
    grads,
    sent,
    normal_t,
    cot_all,
    give_acc,
    keep_far_acc,
    give_far_acc,
    weight_out,
    held,
    active_all,
    slope_all,
):
    y, z, shard = place[1], place[2], place[4]
    step = pl.program_id(0)
    n_z = grads.shape[0]
    part = p0.shape[-1]
    rows = n0.shape[0]
    deep = D // 4
    totals = (keep, give_acc, keep_far_acc, give_far_acc)

    @pl.when(step == 0)
    def _():
        fill_weights(place, (p0, p1, p2, p3), (f0, f1, f2, f3), None, weight_out)
        for i, (normal, cot) in enumerate(((n0, c0), (n1, c1), (n2, c2), (n3, c3))):
            normal_t[:, i * rows : (i + 1) * rows] = normal[...].T
            cot_all[i * rows : (i + 1) * rows] = cot[...]
            totals[i][...] = jnp.zeros_like(totals[i])

    for i, (act, grad) in enumerate(((active, slope), (active_far, slope_far))):
        at = slice(i * 2 * rows, (i + 1) * 2 * rows)
        active_all[at] = act[...]
        slope_all[at] = grad[...]
        for j in range(2):
            totals[2 * i + j][...] += nn(act[j * rows : (j + 1) * rows], weight_out[step])

    held[...] = nn(normal_t[...], slope_all[...]).astype(BF)
    for side in range(2):
        for m in range(4):
            grads[(n_z - step) % n_z, side, m, :deep] = held[span(shard ^ m, deep), side * part : (side + 1) * part]
    held_t = weight_out.at[step]
    held_t[...] = tn(active_all[...], cot_all[...]).astype(BF)
    unit = (z - step + n_z) % n_z
    for side in range(2):
        at = pl.ds(pl.multiple_of(deep + (y ^ side) * part, part), part)
        for s in range(n_z):
            for flip in range(2):
                features = span(2 * ((z + s) % n_z) + (y ^ flip), part)
                grads[s, flip, unit ^ shard, at, :] = held_t[side * part : (side + 1) * part, features]

    @pl.when(step == pl.num_programs(0) - 1)
    def _():
        give[...] = give_acc[...].astype(BF)
        keep_far[...] = keep_far_acc[...].astype(BF)
        give_far[...] = give_far_acc[...].astype(BF)
        sent[...] = grads[n_z - 1]


def feed_specs(place, n_z):
    def whole(array):
        return pl.BlockSpec(array.shape, lambda t, p: (0,) * len(array.shape), pipeline_mode=pl.Buffered(1))

    def lanes(rows, wide):
        return pl.BlockSpec((rows, wide), lambda t, p: (0, t))

    return whole, lanes


def feed_split_call(place, normal, cot, parts, bias, waits=()):
    rows = normal[0].shape[0]
    n_z = len(parts) // 2
    wide = bias.shape[-1]
    whole, lanes = feed_specs(place, n_z)
    row = pl.BlockSpec((1, 1, wide), lambda t, p: (t, 0, 0))
    block = (rows, D)
    outs = [shape_of(2 * rows, n_z * wide)] * 2 + [shape_of(*block, dtype=F32), shape_of(*block)]
    outs += [shape_of(n_z, 1, wide, dtype=F32)]
    inputs = [*normal, *cot, *parts]
    return pl.pallas_call(
        waiting(feed_kernel, 2 + len(inputs), waits),
        grid_spec=pltpu.PrefetchScalarGridSpec(
            num_scalar_prefetch=1,
            grid=(n_z,),
            in_specs=[whole(a) for a in inputs] + [row] + [ANY_REF] * len(waits),
            out_specs=[lanes(2 * rows, wide)] * 2 + [whole(o) for o in outs[2:4]] + [row],
            scratch_shapes=[pltpu.VMEM(block, F32), pltpu.VMEM((n_z, D, wide), BF), pltpu.VMEM((n_z, wide, D), BF)],
        ),
        out_shape=outs,
        compiler_params=pltpu.CompilerParams(vmem_limit_bytes=VMEM),
        cost_estimate=cost(
            flops=12 * rows * D * wide * n_z, bytes_accessed=20 * rows * D, transcendentals=4 * rows * wide * n_z
        ),
        name="feed_forward",
    )(place, *inputs, bias, *waits)


def feed_grad_call(place, normal, cot, active, slope, parts, waits=()):
    rows = normal[0].shape[0]
    n_z = len(parts) // 2
    wide = active[0].shape[1] // n_z
    whole, lanes = feed_specs(place, n_z)
    block = (rows, D)
    outs = [shape_of(*block, dtype=F32)] + [shape_of(*block)] * 3 + [shape_of(n_z, 2, *parts[0].shape), shape_of(2, *parts[0].shape)]
    first = [*normal, *cot]
    tiles = [*active, *slope]
    return pl.pallas_call(
        waiting(feed_grad_kernel, 1 + len(first) + len(tiles) + 2 * n_z, waits),
        grid_spec=pltpu.PrefetchScalarGridSpec(
            num_scalar_prefetch=1,
            grid=(n_z,),
            in_specs=[whole(a) for a in first]
            + [lanes(2 * rows, wide)] * 4
            + [whole(p) for p in parts]
            + [ANY_REF] * len(waits),
            out_specs=[whole(o) for o in outs],
            scratch_shapes=[
                pltpu.VMEM((D, 4 * rows), BF),
                pltpu.VMEM((4 * rows, D), BF),
                pltpu.VMEM(block, F32),
                pltpu.VMEM(block, F32),
                pltpu.VMEM(block, F32),
                pltpu.VMEM((n_z, wide, D), BF),
                pltpu.VMEM((D, wide), BF),
                pltpu.VMEM((4 * rows, wide), BF),
                pltpu.VMEM((4 * rows, wide), BF),
            ],
        ),
        out_shape=outs,
        compiler_params=pltpu.CompilerParams(vmem_limit_bytes=VMEM),
        cost_estimate=cost(flops=24 * rows * D * wide * n_z, bytes_accessed=40 * rows * D),
        name="feed_grads",
    )(place, *first, *tiles, *parts, *waits)


def torus_shards(sizes, *args):
    (
        tokens,
        cotangent,
        frame_counts,
        presence,
        attend_gain,
        attend_shift,
        triple_weight,
        triple_bias,
        output_weight,
        output_bias,
        second_gain,
        second_shift,
        expand_weight,
        expand_bias,
        reduce_weight,
        reduce_bias,
    ) = args
    n_z, n_y, n_x = sizes
    n_dp = n_z * n_y
    n_f = n_x * 2
    width = D // n_f
    local_rows = tokens.shape[1]
    frames_local = local_rows // ROW_FRAME
    rows = frames_local * PATCHES + EXTRA
    z, y, x, core = (lax.axis_index(name) for name in ("z", "y", "x", "core"))
    shard = x * 2 + core
    place = jnp.stack([x, y, z, core, shard]).astype(jnp.int32)
    d_part = D // n_dp
    qkv_part = 3 * D // n_dp
    ff_part = FF // n_dp
    quarter = ff_part // 4

    def swap(array, axis="core"):
        return lax.ppermute(array, axis, [(0, 1), (1, 0)])

    def cross_over(array):
        return lax.ppermute(array, ("x", "core"), [(i, i ^ 3) for i in range(4)])

    def to_z(array, s):
        return lax.ppermute(array, "z", [(i, (i + s) % n_z) for i in range(n_z)])

    def take(array, index, axis=0):
        return lax.dynamic_index_in_dim(array, index, axis, False)

    def gather_z(array):
        return [array] + [to_z(array, s) for s in range(1, n_z)]

    def scatter_z(array, waits=(), dtype=BF):
        return add_call([array[0]] + [to_z(array[s], s) for s in range(1, n_z)], waits, dtype)

    def lane_row(vector):
        return jnp.pad(vector, (0, qkv_part - vector.shape[0]))[None]

    vectors = [attend_gain, attend_shift, output_bias, second_gain, second_shift, reduce_bias, triple_bias]
    vectors += [expand_bias[f * quarter : (f + 1) * quarter] for f in range(4)]
    packed = jnp.concatenate(
        [triple_weight] + [lane_row(v) for v in vectors] + [jnp.zeros((16 - len(vectors), qkv_part), BF)], 0
    )

    live_all = tables(frame_counts[0], presence[0], n_f, frames_local, width // HEAD)[0]
    live = take(live_all, shard)[:, None]
    entered = to_block(tokens[0], frames_local) * live.astype(BF)
    outer = to_block(cotangent[0], frames_local) * live.astype(BF)

    own, one, two, three, packed = local_call(
        split_kernel,
        "split",
        [place, expand_weight, reduce_weight],
        [shape_of(2 * (D // n_f), d_part)] * 4,
        smem=1,
        carry=[packed],
    )
    packed_parts = gather_z(packed)
    feed = stack_call([own, swap(one), swap(two, "x"), cross_over(three)], [packed_parts[1]])
    near = local_call(
        front_kernel,
        "front",
        packed_parts,
        [shape_of(n_z, *packed.shape)],
    )[0]
    far = swap(near, "y")
    entered = copy_call(entered, [near, feed])
    entered_x = swap(entered, "x")
    entered_all = [entered, swap(entered), entered_x]
    output_all = lax.all_gather(output_weight, ("z", "y", "x"), axis=0).reshape(n_z, n_y, n_x, width, d_part)

    own, one, two, three, vectors, bias, expand_add, counts = local_call(
        functools.partial(pack_kernel, n_z),
        "pack",
        [place, near, far],
        [shape_of(D // n_f, 3 * width)] * 4
        + [shape_of(8, D, dtype=F32), shape_of(1, 3 * width, dtype=F32), shape_of(n_z, 1, 2 * quarter, dtype=F32)],
        smem=1,
        waits=[entered_all[1]],
        carry=[frame_counts],
    )
    _, cosine, sine, guides = tables(counts[0], presence[0], n_f, frames_local, width // HEAD)
    weights = [own, swap(one), swap(two, "x"), cross_over(three)]
    entered_all.append(swap(copy_call(entered_x, weights[1:])))
    feed_near = gather_z(feed)
    turn = jnp.asarray(turn_matrix(width), BF)
    q, k, v, normed, triple = enter_call(
        place, entered_all, weights, bias, vectors, turn, cosine, sine, feed_near[1:2]
    )
    outer = copy_call(outer, [normed, *feed_near[2:]])
    feed_far = [swap(part, "y") for part in feed_near]
    feed_parts = [*feed_near, *feed_far]
    outer_x = swap(outer, "x")
    outer_all = [outer, swap(outer), outer_x]
    mixed, exact, logs, logs_extra = attend_call(*guides, q, k, v)
    mixed_own, mixed_far, outer_x = local_call(
        part_kernel,
        "mixed_parts",
        [place, mixed],
        [shape_of(2, rows, width)] * 2,
        smem=1,
        waits=[*feed_far[:3], outer_all[1]],
        carry=[outer_x],
    )
    mixed_far = swap(mixed_far, "x")
    outer_all = [*outer_all[:2], outer_x, swap(outer_x)]
    keep, give = local_call(
        project_kernel,
        "project",
        [place, mixed_own, mixed_far, output_all],
        [shape_of(rows, D, dtype=F32), shape_of(rows, D)],
        [pltpu.VMEM((D // 2, D), BF)],
        smem=1,
        flops=4 * rows * D * D // 2,
        waits=[outer_all[3], feed_far[3]],
    )
    output_full = output_all.transpose(2, 3, 0, 1, 4).reshape(D // 2, D)
    middle, second = rows_call(
        middle_kernel,
        "middle",
        [entered, keep, swap(give), vectors],
        [shape_of(rows, D, dtype=F32), shape_of(rows, D)],
    )
    second_all = [second, swap(second)]
    feed_both = [feed_parts, expand_add]
    active, slope, back, back_give, d_bias = feed_split_call(place, second_all, outer_all[:2], *feed_both)
    second_x = swap(second, "x")
    second_all += [second_x, swap(copy_call(second_x, [active]))]
    active_far, slope_far, back_far, back_far_give, d_bias_far = feed_split_call(
        place, second_all[2:], outer_all[2:], *feed_both, waits=[back_give]
    )
    back_give = swap(back_give)
    back_far = swap(add_call([back_far, swap(back_far_give)]), "x")
    final, final_give, final_far, final_far_give, d_feed, d_sent = feed_grad_call(
        place, second_all, outer_all, [active, active_far], [slope, slope_far], feed_parts
    )
    middle_grad, branch, sums_two = rows_call(
        middle_back_kernel,
        "middle_back",
        [middle, outer, back, back_give, back_far, vectors],
        [shape_of(rows, D, dtype=F32), shape_of(rows, D), shape_of(8, D, dtype=F32)],
        waits=[d_sent],
    )
    branch_other = swap(branch)
    grad_own, grad_far = local_call(
        mixed_grad_kernel,
        "mixed_grad",
        [place, branch, branch_other, output_full],
        [shape_of(2, rows, width)] * 2,
        smem=1,
        flops=4 * rows * D * D // 2,
    )
    grad_far = swap(grad_far, "x")
    out_near, out_far = local_call(
        output_grad_kernel,
        "output_weight_grad",
        [place, mixed_own, mixed_far, branch, branch_other],
        [shape_of(n_x, n_z, width, d_part)] * 2,
        [pltpu.VMEM((2 * rows, D), BF), pltpu.VMEM((width, D), BF)],
        smem=1,
        flops=4 * rows * D * D // 2,
        waits=[grad_own],
    )
    out_far = swap(out_far, "y")
    final_far = add_call([final_far, swap(final_far_give)], [grad_own])
    final_far = swap(final_far, "x")
    final_give = swap(final_give)
    triple_grad = attend_back_call(
        x.reshape(1), *guides, q, k, v, [grad_own, grad_far], exact, logs, logs_extra, cosine, sine, turn, waits=[out_near, final_give]
    )
    back_feed = to_z(d_sent, 1)
    tri_own, tri_one, tri_two, tri_three, normed_own, normed_far, normed_give, d_triple_bias, sums_one = triple_call(
        place, normed, triple_grad, triple, entered_all, [back_feed, out_far, final_far]
    )
    pieces = [tri_own, swap(tri_one), swap(tri_two, "x"), cross_over(tri_three)]
    zero_qkv = jnp.zeros((3, n_f, width), F32)
    triple_bias_part = lax.dynamic_update_slice(zero_qkv, d_triple_bias.reshape(3, 1, width), (0, shard, 0))
    expand_bias_part = jnp.zeros((n_z, n_y, n_f, quarter), F32)
    d_bias = (d_bias + d_bias_far).reshape(n_z, n_y, quarter)
    for s in range(n_z):
        for side in range(n_y):
            expand_bias_part = lax.dynamic_update_slice(
                expand_bias_part, d_bias[s, side].reshape(1, 1, 1, quarter), ((z - s) % n_z, y ^ side, shard, 0)
            )
    sums = [sums_one[0], sums_one[1], sums_two[0], sums_two[1], sums_two[2], sums_two[3], triple_bias_part, expand_bias_part]
    sums = jnp.concatenate([piece.reshape(n_dp, -1) for piece in sums], 1)

    def butterfly(sums, bits):
        for bit in bits:
            sums = sums + lax.ppermute(sums, ("z", "y", "x", "core"), [(i, i ^ bit) for i in range(32)])
        return sums

    back_feed = add_piece_call(d_feed, 2, back_feed, pieces[1:3])
    back_feed = to_z(back_feed, 1)
    out_near, out_send = add_apart_call(out_near, out_far, [tri_own])
    out_far = swap(out_send, "x")
    block_output = local_call(
        functools.partial(output_kernel, frames_local),
        "block_output",
        [middle, final, final_give, final_far, live, vectors],
        [shape_of(local_rows, D)],
        waits=[out_near],
    )[0]
    normed_own, normed_far = local_call(
        normed_sum_kernel,
        "normed_sum",
        [normed_own, normed_far, swap(normed_give)],
        [shape_of(rows, D)] * 2,
        waits=pieces[1:],
    )
    normed_far = swap(normed_far, "x")
    tri_near, tri_far, sums = local_call(
        functools.partial(unpack_kernel, n_z),
        "unpack",
        [place, *pieces],
        [shape_of(n_z, D // n_f, qkv_part)] * 2,
        [pltpu.VMEM((4, D // n_f, 3 * width), BF)],
        smem=1,
        waits=[block_output, normed_own, out_far],
        carry=[sums],
    )
    tri_far = swap(tri_far, "y")
    back_feed = add_piece_call(d_feed, 1, back_feed, [tri_near])
    back_feed = to_z(back_feed, 1)
    sums = butterfly(sums, (1, 4))
    tail = local_call(
        tail_sum_kernel,
        "tail_sum",
        [tri_near, tri_far, out_near[None], out_far],
        [shape_of(D // n_f, qkv_part + d_part)] * n_z,
        waits=[sums],
    )
    tail_parts = [tail[0]] + [to_z(tail[s], s) for s in range(1, n_z)]
    d_near, d_send = add_piece_call(d_feed, 0, back_feed, tail_parts[1:3], True)
    tokens_grad = local_call(
        functools.partial(leave_kernel, frames_local),
        "tokens_grad",
        [entered, normed_own, normed_far, middle_grad, live, vectors],
        [shape_of(local_rows, D, dtype=F32)],
        waits=[tail[0], d_near],
    )[0]
    triple_weight_grad, output_weight_grad = local_call(
        tail_kernel,
        "tail",
        tail_parts,
        [shape_of(D // n_f, qkv_part, dtype=F32), shape_of(D // n_f, d_part, dtype=F32)],
        waits=[tokens_grad],
    )
    *d_feed, sums = add_apart_call(d_near, swap(d_send, "y"), [triple_weight_grad], [sums])
    sums = butterfly(sums, (2, 8, 16))
    expand_weight_grad, reduce_weight_grad = local_call(
        join_kernel,
        "join",
        [place, d_feed[0], swap(d_feed[1]), swap(d_feed[2], "x"), cross_over(d_feed[3])],
        [shape_of(D // n_f, ff_part, dtype=F32), shape_of(FF // n_f, d_part, dtype=F32)],
        smem=1,
    )

    sums = take(sums, z * n_y + y)
    parts = [sums[i * d_part : (i + 1) * d_part] for i in range(6)]
    rest = sums[6 * d_part :]
    return (
        block_output[None],
        tokens_grad[None],
        parts[0],
        parts[1],
        triple_weight_grad,
        rest[:qkv_part],
        output_weight_grad,
        parts[2],
        parts[3],
        parts[4],
        expand_weight_grad,
        rest[qkv_part:],
        reduce_weight_grad,
        parts[5],
    )


def general_shards(sizes, *args):
    (
        tokens,
        cotangent,
        frame_counts,
        presence,
        attend_gain,
        attend_shift,
        triple_weight,
        triple_bias,
        output_weight,
        output_bias,
        second_gain,
        second_shift,
        expand_weight,
        expand_bias,
        reduce_weight,
        reduce_bias,
    ) = args
    n_z, n_y, n_x = sizes
    n_dp = n_z * n_y
    n_f = n_x * 2
    heads = HEADS // n_f
    width = heads * HEAD
    local_rows = tokens.shape[1]
    frames_local = local_rows // ROW_FRAME
    rows = frames_local * PATCHES + EXTRA
    z, y, x, core = (lax.axis_index(name) for name in ("z", "y", "x", "core"))
    shard = x * 2 + core
    d_part = D // n_dp
    ff_part = FF // n_dp
    ff_half = ff_part // 2
    blocks = n_dp // n_f

    def swap(array, axis="core"):
        return lax.ppermute(array, axis, [(0, 1), (1, 0)])

    def take(array, index, axis=0):
        return lax.dynamic_index_in_dim(array, index, axis, False)

    def ordered(index, own, other, axis=0):
        low = jnp.where(index == 0, own, other)
        high = jnp.where(index == 0, other, own)
        return jnp.concatenate([low, high], axis)

    def both_cores(array, axis=0):
        return ordered(core, array, swap(array), axis)

    def exchange_f(array):
        return lax.all_to_all(array, ("x", "core"), 0, 0, tiled=True)

    def over_x(array):
        return lax.all_to_all(array, "x", 0, 0, tiled=True)

    vectors = [attend_gain, attend_shift, output_bias, second_gain, second_shift, reduce_bias, triple_bias, expand_bias]
    flat = jnp.concatenate(vectors)
    qkv_part = 3 * D // n_dp
    flat = jnp.pad(flat, (0, 16 * qkv_part - flat.shape[0])).reshape(16, qkv_part)
    packed = jnp.concatenate([triple_weight, flat], 0)
    packed = lax.all_gather(packed, ("z", "y"), axis=0)
    small = packed[:, D // n_f :].reshape(n_dp, -1)
    full = []
    at = 0
    for vector in vectors:
        full.append(small[:, at : at + vector.shape[0]].reshape(-1))
        at += vector.shape[0]
    gain_one, shift_one, output_add, gain_two, shift_two, reduce_add = (v.astype(F32)[None] for v in full[:6])
    triple_add, expand_add = full[6], full[7]
    triple_rows = packed[:, : D // n_f].transpose(1, 0, 2).reshape(D // n_f, 3, n_f, width)
    triple_own = exchange_f(triple_rows.transpose(2, 0, 1, 3)).reshape(D, 3 * width)
    bias_own = take(triple_add.reshape(3, n_f, width), shard, 1).reshape(1, 3 * width)

    expand_split = expand_weight.reshape(D // n_f, 2, ff_half)
    expand_chip = ordered(core, take(expand_split, core, 1), swap(take(expand_split, 1 - core, 1)))
    reduce_split = reduce_weight.reshape(blocks, 2, ff_half, d_part)
    reduce_chip = ordered(core, take(reduce_split, core, 1)[None], swap(take(reduce_split, 1 - core, 1))[None])
    expand_add_own = take(expand_add.reshape(n_z, n_y, 2, ff_half), core, 2)
    expand_all = lax.all_gather(expand_chip, ("z", "y", "x"), axis=0).reshape(n_z, n_y, D, ff_half)
    expand_pieces = [expand_all.transpose(0, 2, 1, 3).reshape(n_z, D, n_y * ff_half)]
    reduce_all = lax.all_gather(reduce_chip, ("z", "y", "x"), axis=0)
    reduce_pieces = [
        reduce_all.reshape(n_dp, n_dp, ff_half, d_part).transpose(1, 2, 0, 3).reshape(n_z, n_y * ff_half, D)
    ]
    expand_add_own = expand_add_own.reshape(n_z, 1, n_y * ff_half)
    output_all = lax.all_gather(output_weight, ("z", "y", "x"), axis=0)
    output_all = output_all.reshape(n_dp, n_x * width, d_part).transpose(1, 0, 2).reshape(n_x * width, D)

    live_all, cosine, sine, guides = tables(frame_counts[0], presence[0], n_f, frames_local, heads)
    live = take(live_all, shard)[:, None]
    entered = to_block(tokens[0], frames_local).astype(F32) * live
    outer = to_block(cotangent[0], frames_local).astype(F32) * live
    outer_low = outer.astype(BF)
    outer_chip = both_cores(outer_low)
    outer_chip_t = outer_chip.T
    unit_one, scale_one = norm_parts(entered)
    normed = (unit_one * gain_one + shift_one).astype(BF)
    normed_all = lax.all_gather(normed, ("x", "core"), axis=0)

    turned = jnp.asarray(turn_matrix(width), BF)
    q, k, v = qkv_call(normed_all, triple_own, bias_own, turned, cosine, sine)
    mixed, exact, logs, logs_extra = attend_call(*guides, q, k, v)

    mixed_chip = over_x(mixed.reshape(n_x, 2 * rows, width)).transpose(1, 0, 2).reshape(2 * rows, n_x * width)
    branch_part = nn(mixed_chip, output_all).reshape(2, rows, D)
    branch = take(branch_part, core) + swap(take(branch_part, 1 - core).astype(BF)).astype(F32)
    middle = entered + branch + output_add
    unit_two, scale_two = norm_parts(middle)
    second = (unit_two * gain_two + shift_two).astype(BF)
    second_chip = both_cores(second)
    final, second_grad, d_expand_bias, *d_feed = feed_call(
        second_chip, outer_chip, outer_chip_t, expand_pieces[0], expand_add_own, reduce_pieces[0]
    )
    second_grad = second_grad.reshape(2, rows, D)
    second_grad = take(second_grad, core) + swap(take(second_grad, 1 - core).astype(BF)).astype(F32)
    final = final.reshape(2, rows, D)
    final = take(final, core) + swap(take(final, 1 - core).astype(BF)).astype(F32)
    block_output = ((middle + final + reduce_add) * live).astype(BF)

    middle_grad = outer + norm_back(second_grad, unit_two, scale_two, gain_two)
    second_gain_grad = jnp.sum(second_grad * unit_two, 0)
    second_shift_grad = jnp.sum(second_grad, 0)
    branch_low = middle_grad.astype(BF)
    branch_chip = both_cores(branch_low)
    mixed_grad = nt(branch_chip, output_all).astype(BF)
    mixed_grad = over_x(mixed_grad.reshape(2 * rows, n_x, width).transpose(1, 0, 2)).reshape(n_f, rows, width)
    d_output = tn(mixed_chip, branch_chip).astype(BF)
    triple_grad = attend_back_call(
        jnp.zeros((1,), jnp.int32), *guides, q, k, v, list(mixed_grad.reshape(n_x, 2, rows, width)), exact, logs, logs_extra, cosine, sine, turned)
    natural = triple_grad.reshape(n_f * rows, 3 * width)
    d_triple = tn(normed_all.reshape(n_f * rows, D), natural).astype(BF)
    d_triple_bias = jnp.sum(natural.astype(F32), 0)
    normed_grad = nt(natural, triple_own).astype(BF)
    normed_grad = lax.psum_scatter(normed_grad, ("x", "core"), scatter_dimension=0, tiled=True).astype(F32)
    attend_gain_grad = jnp.sum(normed_grad * unit_one, 0)
    attend_shift_grad = jnp.sum(normed_grad, 0)
    tokens_grad = (middle_grad + norm_back(normed_grad, unit_one, scale_one, gain_one)) * live

    d_triple = exchange_f(d_triple.reshape(n_f, D // n_f, 3, width))
    d_triple = d_triple.transpose(1, 2, 0, 3).reshape(D // n_f, n_z, n_y, qkv_part)
    d_triple = d_triple.reshape(D // n_f, 3 * D)
    triple_weight_grad = lax.psum_scatter(d_triple, ("z", "y"), scatter_dimension=1, tiled=True).astype(F32)
    d_output = d_output.reshape(n_x, width, n_dp, d_part).transpose(2, 0, 1, 3).reshape(n_dp * n_x * width, d_part)
    output_weight_grad = lax.psum_scatter(d_output, ("z", "y", "x"), scatter_dimension=0, tiled=True).astype(F32)
    d_expand, d_reduce = d_feed
    d_expand = d_expand.reshape(n_z, D, n_y, ff_half).transpose(0, 2, 1, 3).reshape(n_dp * D, ff_half)
    d_expand = lax.psum_scatter(d_expand, ("z", "y", "x"), scatter_dimension=0, tiled=True)
    d_expand = d_expand.reshape(2, D // n_f, ff_half)
    d_reduce = d_reduce.reshape(n_z, n_dp, d_part, n_y, ff_half).transpose(1, 0, 3, 2, 4).reshape(-1, ff_half)
    d_reduce = lax.psum_scatter(d_reduce, ("z", "y", "x"), scatter_dimension=0, tiled=True)
    d_reduce = d_reduce.reshape(2, blocks, d_part, ff_half)
    expand_weight_grad = ordered(core, take(d_expand, core), swap(take(d_expand, 1 - core)), 1).astype(F32)
    reduce_weight_grad = jnp.stack(
        [
            jnp.where(core == 0, take(d_reduce, core), swap(take(d_reduce, 1 - core))),
            jnp.where(core == 0, swap(take(d_reduce, 1 - core)), take(d_reduce, core)),
        ],
        1,
    )
    reduce_weight_grad = reduce_weight_grad.transpose(0, 1, 3, 2).reshape(blocks * 2 * ff_half, d_part).astype(F32)

    zero_qkv = jnp.zeros((3, n_f, width), F32)
    triple_bias_part = lax.dynamic_update_slice(zero_qkv, d_triple_bias.reshape(3, 1, width), (0, shard, 0))
    d_expand_bias = d_expand_bias.reshape(n_z, n_y, ff_half)
    zero_ff = jnp.zeros((n_dp, 2, ff_half), F32)
    expand_bias_part = lax.dynamic_update_slice(zero_ff, d_expand_bias.reshape(n_dp, 1, ff_half), (0, core, 0))
    sums = [
        attend_gain_grad,
        attend_shift_grad,
        jnp.sum(branch_low.astype(F32), 0),
        second_gain_grad,
        second_shift_grad,
        jnp.sum(outer_low.astype(F32), 0),
        triple_bias_part.reshape(-1),
        expand_bias_part.reshape(-1),
    ]
    sums = jnp.concatenate([s.reshape(n_dp, -1) for s in sums], 1)
    total = n_dp * n_f
    bit = 1
    while bit < total:
        sums = sums + lax.ppermute(sums, ("z", "y", "x", "core"), [(i, i ^ bit) for i in range(total)])
        bit *= 2
    own = take(sums, z * n_y + y)
    parts = []
    at = 0
    for size in [d_part] * 6 + [qkv_part, ff_part]:
        parts.append(own[at : at + size])
        at += size
    return (
        from_block(block_output, frames_local),
        from_block(tokens_grad, frames_local),
        parts[0],
        parts[1],
        triple_weight_grad,
        parts[6],
        output_weight_grad,
        parts[2],
        parts[3],
        parts[4],
        expand_weight_grad,
        parts[7],
        reduce_weight_grad,
        parts[5],
    )


def solution(mesh):
    n_dp, n_f = mesh.shape["dp"], mesh.shape["fsdp"]
    sizes = (n_dp // 2, 2, n_f // 2)
    inner = jax.sharding.Mesh(mesh.devices.reshape(*sizes, 2), ("z", "y", "x", "core"))
    dp = ("z", "y")
    fsdp = ("x", "core")
    rows = P(dp, fsdp, None)
    weight = P(fsdp, dp)
    vector = P(dp)
    return jax.shard_map(
        functools.partial(torus_shards if sizes == (4, 2, 2) else general_shards, sizes),
        mesh=inner,
        in_specs=(
            rows,
            rows,
            P(dp, None),
            P(dp, None, None),
            vector,
            vector,
            weight,
            vector,
            weight,
            vector,
            vector,
            vector,
            weight,
            vector,
            weight,
            vector,
        ),
        out_specs=(
            rows,
            rows,
            vector,
            vector,
            weight,
            vector,
            weight,
            vector,
            vector,
            vector,
            weight,
            vector,
            weight,
            vector,
        ),
        check_vma=False,
    )
```

```python
import functools
import math

import jax
import jax.numpy as jnp
import numpy as np
from jax import lax
from jax.experimental import pallas as pl
from jax.experimental.pallas import tpu as pltpu
from jax.sharding import PartitionSpec as P

D = 1024
HEADS = 16
HEAD = 64
FF = 4096
GRID = 16
PATCHES = GRID * GRID
ROW_FRAME = PATCHES + 2
PAIRS = HEAD // 3 // 2
EXTRA = 16

EPSILON = 1e-06
SCALE2 = 0.125 * math.log2(math.e)
MASKED = -8e9
FAR = 1 << 20
VMEM = 60 * 1024 * 1024
BF = jnp.bfloat16
F32 = jnp.float32


def nn(left, right):
    return lax.dot_general(left, right, (((1,), (0,)), ((), ())), preferred_element_type=F32)


def nt(left, right):
    return lax.dot_general(left, right, (((1,), (1,)), ((), ())), preferred_element_type=F32)


def tn(left, right):
    return lax.dot_general(left, right, (((0,), (0,)), ((), ())), preferred_element_type=F32)


def qkv_kernel(normed, weight, bias, turn, cosine, sine, q_out, k_out, v_out, turned, turned_bias):
    width = q_out.shape[-1]
    half = width // 2

    @pl.when(pl.program_id(0) == 0)
    def _():
        for part in range(2):
            span = slice(part * width, (part + 1) * width)
            turned[:, span] = nn(weight[:, span], turn[...]).astype(BF)
            turned_bias[:, span] = nn(bias[:, span], turn[...])

    rows = normed[0]
    cos = cosine[0]
    sin = sine[0]
    for part, out in ((0, q_out), (1, k_out)):
        span = slice(part * width, (part + 1) * width)
        value = nn(rows, turned[:, span]) + turned_bias[:1, span]
        first = value[:, :half]
        second = value[:, half:]
        out[0, :, :half] = (first * cos - second * sin).astype(BF)
        out[0, :, half:] = (second * cos + first * sin).astype(BF)
    span = slice(2 * width, 3 * width)
    v_out[0] = (nn(rows, weight[:, span]) + bias[:1, span].astype(F32)).astype(BF)


def qkv_call(normed, weight, bias, turn, cosine, sine):
    sources, rows, _ = normed.shape
    width = weight.shape[1] // 3
    half = width // 2
    block = pl.BlockSpec((1, rows, width), lambda s: (s, 0, 0))
    table = pl.BlockSpec((1, rows, half), lambda s: (s, 0, 0))

    def whole(shape):
        return pl.BlockSpec(shape, lambda s: (0,) * len(shape))

    shape = jax.ShapeDtypeStruct((sources, rows, width), BF)
    return pl.pallas_call(
        qkv_kernel,
        grid=(sources,),
        in_specs=[
            pl.BlockSpec((1, rows, D), lambda s: (s, 0, 0)),
            whole(weight.shape),
            whole(bias.shape),
            whole(turn.shape),
            table,
            table,
        ],
        out_specs=[block] * 3,
        out_shape=[shape] * 3,
        scratch_shapes=[pltpu.VMEM((D, 2 * width), BF), pltpu.VMEM((bias.shape[0], 2 * width), F32)],
        compiler_params=pltpu.CompilerParams(vmem_limit_bytes=VMEM),
        cost_estimate=pl.CostEstimate(
            flops=2 * sources * rows * D * 3 * width, bytes_accessed=4 * sources * rows * D, transcendentals=0
        ),
        name="qkv_rotary",
    )(normed, weight, bias, turn, cosine, sine)


def turned_lanes(width, head):
    lane = lax.broadcasted_iota(jnp.int32, (1, width), 1)
    return (lane % (width // 2)) // (HEAD // 2) == head


def plain_lanes(width, head):
    lane = lax.broadcasted_iota(jnp.int32, (1, width), 1)
    return lane // HEAD == head


def pick(mask, array):
    return jnp.where(mask, array, jnp.zeros((), array.dtype))


def stack_heads(array, lanes):
    width = array.shape[-1]
    return jnp.concatenate([pick(lanes(width, head), array) for head in range(width // HEAD)], 0)


def unstack_heads(array, lanes):
    width = array.shape[-1]
    heads = width // HEAD
    step = array.shape[0] // heads
    total = pick(lanes(width, 0), array[:step])
    for head in range(1, heads):
        total = total + pick(lanes(width, head), array[head * step : (head + 1) * step])
    return total


def head_rows(array, head):
    half = array.shape[0] // 2
    step = HEAD // 2
    return jnp.concatenate(
        [array[head * step : (head + 1) * step], array[half + head * step : half + (head + 1) * step]], 0
    )


def value_total(v, frames_local, sources):
    total = jnp.zeros((1, v.shape[-1]), F32)
    real = lax.broadcasted_iota(jnp.int32, (EXTRA, 1), 0) < 2 * frames_local
    for s in range(sources):
        for l in range(frames_local):
            total = total + jnp.sum(v[s, l * PATCHES : (l + 1) * PATCHES].astype(F32), 0, keepdims=True)
        total = total + jnp.sum(pick(real, v[s, frames_local * PATCHES :].astype(F32)), 0, keepdims=True)
    return total


def attend_kernel(
    frames_local,
    start,
    key_frame,
    query_start,
    query_frame,
    query_pad,
    q,
    k,
    v,
    mixed,
    exact,
    logs,
    logs_extra,
    v_t,
    queries,
    acc,
    state,
):
    sources, _, width = q.shape
    heads = width // HEAD
    frames = sources * frames_local
    patch_rows = frames_local * PATCHES
    length = frames * ROW_FRAME

    def frame_ref(ref, g):
        return ref[g // frames_local, pl.ds(pl.multiple_of((g % frames_local) * PATCHES, PATCHES), PATCHES), :]

    for g in range(frames):
        s, l = g // frames_local, g % frames_local
        v_t[g] = v[s, l * PATCHES : (l + 1) * PATCHES].T
    k_extra = jnp.concatenate([k[s, patch_rows:] for s in range(sources)], 0)
    v_extra_t = jnp.concatenate([v[s, patch_rows:] for s in range(sources)], 0).T
    uniform = jnp.asarray(1.0 / length, BF).astype(F32) * value_total(v, frames_local, sources)
    key_at = key_frame[:, :1]

    def weigh(scores, top):
        return jnp.exp2((scores - top) * SCALE2)

    def mix(values_t, weights, head):
        return nn(values_t[head * HEAD : (head + 1) * HEAD], weights[:, head * PATCHES : (head + 1) * PATCHES])

    def one_frame(g, _):
        first = start[g]
        queries[...] = stack_heads(frame_ref(q, g), turned_lanes)
        allowed = (key_at >= first) & (key_at <= g)
        scores_extra = jnp.where(allowed, nt(k_extra, queries[...]), MASKED)
        scores = nt(frame_ref(k, g), queries[...])
        top = jnp.maximum(jnp.max(scores_extra, 0, keepdims=True), jnp.max(scores, 0, keepdims=True))
        weights_extra = weigh(scores_extra, top)
        weights = weigh(scores, top)
        state[0:1] = top
        state[1:2] = jnp.sum(weights_extra, 0, keepdims=True) + jnp.sum(weights, 0, keepdims=True)
        weights_extra = weights_extra.astype(BF)
        weights = weights.astype(BF)
        values_t = v_t[g]
        for head in range(heads):
            acc[head] = mix(v_extra_t, weights_extra, head) + mix(values_t, weights, head)

        def some_keys(which):
            scores = [nt(frame_ref(k, f), queries[...]) for f in which]
            before = state[0:1]
            top = before
            for s in scores:
                top = jnp.maximum(top, jnp.max(s, 0, keepdims=True))
            fade = weigh(before, top)
            weights = [weigh(s, top) for s in scores]
            state[0:1] = top
            total = state[1:2] * fade
            for w in weights:
                total = total + jnp.sum(w, 0, keepdims=True)
            state[1:2] = total
            weights = [w.astype(BF) for w in weights]
            for head in range(heads):
                out = acc[head] * fade[:, head * PATCHES : (head + 1) * PATCHES]
                for f, w in zip(which, weights):
                    out = out + mix(v_t[f], w, head)
                acc[head] = out

        def pair(i, _):
            some_keys([first + 2 * i, first + 2 * i + 1])
            return 0

        count = jnp.maximum(g - first, 0)
        lax.fori_loop(0, count // 2, pair, 0)

        @pl.when(count % 2 == 1)
        def _():
            some_keys([g - 1])

        total = state[1:2]
        result = jnp.concatenate(
            [acc[head] / total[:, head * PATCHES : (head + 1) * PATCHES] for head in range(heads)], 0
        ).T
        result = jnp.where(first > frames, jnp.broadcast_to(uniform, result.shape), result)
        rows = pl.ds(pl.multiple_of((g % frames_local) * PATCHES, PATCHES), PATCHES)
        exact[g // frames_local, rows, :] = result
        mixed[g // frames_local, rows, :] = result.astype(BF)
        logs[g] = jnp.broadcast_to(state[0:1] + jnp.log2(total) * (1.0 / SCALE2), (8, heads * PATCHES))
        return 0

    lax.fori_loop(0, frames, one_frame, 0)

    q_extra = stack_heads(jnp.concatenate([q[s, patch_rows:] for s in range(sources)], 0), turned_lanes)
    first = jnp.concatenate([query_start[:1]] * heads, 1)
    last = jnp.concatenate([query_frame[:1]] * heads, 1)
    every = [jnp.where((key_at >= first) & (key_at <= last), nt(k_extra, q_extra), MASKED)]
    for f in range(frames):
        every.append(jnp.where((first <= f) & (last >= f), nt(frame_ref(k, f), q_extra), MASKED))
    top = jnp.max(every[0], 0, keepdims=True)
    for scores in every[1:]:
        top = jnp.maximum(top, jnp.max(scores, 0, keepdims=True))
    total = jnp.zeros_like(top)
    result = jnp.zeros((width, q_extra.shape[0]), F32)
    for scores, values_t in zip(every, [v_extra_t] + [v_t[f] for f in range(frames)]):
        weights = weigh(scores, top)
        total = total + jnp.sum(weights, 0, keepdims=True)
        result = result + nn(values_t, weights.astype(BF))
    result = unstack_heads((result / total).T, plain_lanes)
    result = jnp.where(query_pad[:, :1] > 0, jnp.broadcast_to(uniform, result.shape), result)
    for s in range(sources):
        exact[s, patch_rows:, :] = result[s * EXTRA : (s + 1) * EXTRA]
        mixed[s, patch_rows:, :] = result[s * EXTRA : (s + 1) * EXTRA].astype(BF)
    logs_extra[...] = jnp.broadcast_to(top + jnp.log2(total) * (1.0 / SCALE2), logs_extra.shape)


def attend_call(start, key_frame, query_start, query_frame, query_pad, q, k, v, waits=()):
    sources, rows, width = q.shape
    frames_local = rows // PATCHES
    frames = sources * frames_local
    heads = width // HEAD
    stacked = heads * sources * EXTRA
    vmem = pl.BlockSpec(memory_space=pltpu.VMEM)
    return pl.pallas_call(
        waiting(functools.partial(attend_kernel, frames_local), 8, waits),
        in_specs=[pl.BlockSpec(memory_space=pltpu.SMEM)] + [vmem] * 7 + [ANY_REF] * len(waits),
        out_specs=[vmem] * 4,
        out_shape=[
            jax.ShapeDtypeStruct(q.shape, BF),
            jax.ShapeDtypeStruct(q.shape, F32),
            jax.ShapeDtypeStruct((frames, 8, heads * PATCHES), F32),
            jax.ShapeDtypeStruct((8, stacked), F32),
        ],
        scratch_shapes=[
            pltpu.VMEM((frames, width, PATCHES), BF),
            pltpu.VMEM((heads * PATCHES, width), BF),
            pltpu.VMEM((heads, HEAD, PATCHES), F32),
            pltpu.VMEM((8, heads * PATCHES), F32),
        ],
        compiler_params=pltpu.CompilerParams(vmem_limit_bytes=VMEM),
        cost_estimate=cost(
            flops=8 * heads * 256 * frames * frames * PATCHES * PATCHES // 2,
            bytes_accessed=10 * sources * rows * width,
            transcendentals=heads * frames * frames * PATCHES * PATCHES // 2,
        ),
        name="attend",
    )(start, key_frame, query_start, query_frame, query_pad, q, k, v, *waits)


def attend_back_kernel(
    frames_local,
    chips,
    flip,
    start,
    key_frame,
    query_start,
    query_frame,
    query_pad,
    q,
    k,
    v,
    *rest,
):
    pieces = rest[:chips]
    (
        exact,
        logs,
        logs_extra,
        cosine,
        sine,
        turn,
        out,
        grad,
        k_t,
        queries,
        grads,
        dq_t,
        dk,
        dv,
        dq_extra,
        dk_extra,
        dv_extra,
        centers,
    ) = rest[chips:]
    sources, _, width = q.shape
    for i in range(chips):
        for core in range(2):
            grad[2 * (i ^ flip[0]) + core] = pieces[i][core]
    half = width // 2
    heads = width // HEAD
    frames = sources * frames_local
    patch_rows = frames_local * PATCHES
    length = frames * ROW_FRAME
    step_rows = HEAD // 2

    def frame_ref(ref, g):
        return ref[g // frames_local, pl.ds(pl.multiple_of((g % frames_local) * PATCHES, PATCHES), PATCHES), :]

    which = lax.broadcasted_iota(jnp.int32, (8, width), 0)
    lane = lax.broadcasted_iota(jnp.int32, (8, width), 1)
    groups = (lane // HEAD == which).astype(BF)

    def center_of(grad_rows, exact_rows):
        product = grad_rows.astype(F32) * exact_rows
        high = product.astype(BF)
        low = (product - high.astype(F32)).astype(BF)
        center = nt(groups, high) + nt(groups, low)
        return jnp.concatenate([center[head : head + 1] for head in range(heads)], 1)

    def gather_extra(ref):
        return jnp.concatenate([ref[s, patch_rows:] for s in range(sources)], 0)

    for g in range(frames):
        s, l = g // frames_local, g % frames_local
        k_t[g] = k[s, l * PATCHES : (l + 1) * PATCHES].T
    k_extra = gather_extra(k)
    v_extra = gather_extra(v)
    k_extra_t = k_extra.T
    dk_extra[...] = jnp.zeros_like(dk_extra)
    dv_extra[...] = jnp.zeros_like(dv_extra)
    key_at = key_frame[:, :1]

    def tile(keys, values, query, query_grad, log, center, allowed):
        scores = nt(keys, query)
        inner = nt(values, query_grad)
        probs = jnp.exp2((scores - log) * SCALE2)
        if allowed is not None:
            probs = jnp.where(allowed, probs, 0.0)
        change = (probs * (inner - center)).astype(BF)
        return nn(probs.astype(BF), query_grad), nn(change, query), change

    def add_dq(ref, keys_t, change, keep):
        for head in range(heads):
            part = nn(head_rows(keys_t, head), change[:, head * PATCHES : (head + 1) * PATCHES])
            for side in range(2):
                rows = slice(side * half + head * step_rows, side * half + (head + 1) * step_rows)
                piece = part[side * step_rows : (side + 1) * step_rows]
                ref[rows] = ref[rows] + piece if keep else piece

    def one_frame(g, pad_grad):
        first = start[g]
        grad_rows = frame_ref(grad, g)
        queries[...] = stack_heads(frame_ref(q, g), turned_lanes)
        grads[...] = stack_heads(grad_rows, plain_lanes)
        centers[...] = jnp.broadcast_to(center_of(grad_rows, frame_ref(exact, g)), centers.shape)
        allowed = (key_at >= first) & (key_at <= g)
        query, query_grad, log, center = queries[...], grads[...], logs[g, :1], centers[:1]
        dv_part, dk_part, change = tile(k_extra, v_extra, query, query_grad, log, center, allowed)
        dv_extra[...] += dv_part
        dk_extra[...] += dk_part
        add_dq(dq_t.at[g], k_extra_t, change, False)
        dv_part, dk_part, change = tile(
            frame_ref(k, g), frame_ref(v, g), query, query_grad, log, center, jnp.broadcast_to(first <= g, log.shape)
        )
        dv[g] = dv_part
        dk[g] = dk_part
        add_dq(dq_t.at[g], k_t[g], change, True)

        def some_keys(which):
            parts = [
                tile(frame_ref(k, f), frame_ref(v, f), queries[...], grads[...], logs[g, :1], centers[:1], None)
                for f in which
            ]
            for f, (dv_part, dk_part, _) in zip(which, parts):
                dv[f] += dv_part
                dk[f] += dk_part
            for f, (_, _, change) in zip(which, parts):
                add_dq(dq_t.at[g], k_t[f], change, True)

        def pair(i, _):
            some_keys([first + 2 * i, first + 2 * i + 1])
            return 0

        count = jnp.maximum(g - first, 0)
        lax.fori_loop(0, count // 2, pair, 0)

        @pl.when(count % 2 == 1)
        def _():
            some_keys([g - 1])

        return pad_grad + jnp.where(first > frames, jnp.sum(grad_rows.astype(F32), 0, keepdims=True), 0.0)

    pad_grad = lax.fori_loop(0, frames, one_frame, jnp.zeros((1, width), F32))
    g_extra = gather_extra(grad)
    pad_grad = pad_grad + jnp.sum(jnp.where(query_pad[:, :1] > 0, g_extra.astype(F32), 0.0), 0, keepdims=True)
    pad_grad = pad_grad * jnp.asarray(1.0 / length, BF).astype(F32)

    q_stack = stack_heads(gather_extra(q), turned_lanes)
    g_stack = stack_heads(g_extra, plain_lanes)
    stacked = q_stack.shape[0]
    queries[:stacked] = q_stack
    grads[:stacked] = g_stack
    first = jnp.concatenate([query_start[:1]] * heads, 1)
    last = jnp.concatenate([query_frame[:1]] * heads, 1)
    log = logs_extra[:1]
    center = center_of(g_extra, gather_extra(exact))
    allowed = (key_at >= first) & (key_at <= last)
    dv_part, dk_part, change = tile(k_extra, v_extra, q_stack, g_stack, log, center, allowed)
    dv_extra[...] += dv_part
    dk_extra[...] += dk_part
    dq_extra[...] = nn(k_extra_t, change)

    def extra_keys(i, _):
        which = [2 * i, 2 * i + 1]
        parts = [
            tile(
                frame_ref(k, f), frame_ref(v, f), queries[:stacked], grads[:stacked], log, center, (first <= f) & (last >= f)
            )
            for f in which
        ]
        total = dq_extra[...]
        for f, (dv_part, dk_part, change) in zip(which, parts):
            dv[f] += dv_part
            dk[f] += dk_part
            total = total + nn(k_t[f], change)
        dq_extra[...] = total
        return 0

    lax.fori_loop(0, frames // 2, extra_keys, 0)

    def emit(s, rows, dq_rows, dk_rows, dv_rows, real=None):
        cos = cosine[s, rows]
        sin = sine[s, rows]
        for part, array in ((0, dq_rows), (1, dk_rows)):
            a = array[:, :half] * 0.125
            b = array[:, half:] * 0.125
            both = jnp.concatenate([(a * cos + b * sin).astype(BF), (b * cos - a * sin).astype(BF)], 1)
            both = nt(both, turn[...])
            if real is not None:
                both = pick(real, both)
            out[s, rows, part * width : (part + 1) * width] = both.astype(BF)
        total = dv_rows + pad_grad
        if real is not None:
            total = pick(real, total)
        out[s, rows, 2 * width :] = total.astype(BF)

    def emit_frame(g, _):
        rows = pl.ds(pl.multiple_of((g % frames_local) * PATCHES, PATCHES), PATCHES)
        emit(g // frames_local, rows, dq_t[g].T, dk[g], dv[g])
        return 0

    lax.fori_loop(0, frames, emit_frame, 0)
    dq_rows = unstack_heads(dq_extra[...].T, turned_lanes)
    real = lax.broadcasted_iota(jnp.int32, (EXTRA, 1), 0) < 2 * frames_local
    for s in range(sources):
        at = slice(s * EXTRA, (s + 1) * EXTRA)
        emit(s, slice(patch_rows, patch_rows + EXTRA), dq_rows[at], dk_extra[at], dv_extra[at], real)


def attend_back_call(
    flip, start, key_frame, query_start, query_frame, query_pad, q, k, v, grad, exact, logs, logs_extra, cosine, sine, turn, waits=()
):
    chips = len(grad)
    sources, rows, width = q.shape
    frames_local = rows // PATCHES
    frames = sources * frames_local
    extra = sources * EXTRA
    heads = width // HEAD
    vmem = pl.BlockSpec(memory_space=pltpu.VMEM)
    return pl.pallas_call(
        waiting(functools.partial(attend_back_kernel, frames_local, chips), 15 + chips, waits),
        in_specs=[pl.BlockSpec(memory_space=pltpu.SMEM)] * 2 + [vmem] * (13 + chips) + [ANY_REF] * len(waits),
        out_specs=vmem,
        out_shape=jax.ShapeDtypeStruct((sources, rows, 3 * width), BF),
        scratch_shapes=[
            pltpu.VMEM((sources, rows, width), BF),
            pltpu.VMEM((frames, width, PATCHES), BF),
            pltpu.VMEM((heads * PATCHES, width), BF),
            pltpu.VMEM((heads * PATCHES, width), BF),
            pltpu.VMEM((frames, width, PATCHES), F32),
            pltpu.VMEM((frames, PATCHES, width), F32),
            pltpu.VMEM((frames, PATCHES, width), F32),
            pltpu.VMEM((width, heads * extra), F32),
            pltpu.VMEM((extra, width), F32),
            pltpu.VMEM((extra, width), F32),
            pltpu.VMEM((8, heads * PATCHES), F32),
        ],
        compiler_params=pltpu.CompilerParams(vmem_limit_bytes=VMEM),
        cost_estimate=cost(
            flops=20 * heads * 256 * frames * frames * PATCHES * PATCHES // 2,
            bytes_accessed=20 * sources * rows * width,
            transcendentals=heads * frames * frames * PATCHES * PATCHES // 2,
        ),
        name="attend_back",
    )(
        flip, start, key_frame, query_start, query_frame, query_pad, q, k, v, *grad, exact, logs, logs_extra, cosine, sine, turn, *waits
    )


def gelu_parts(hidden):
    base = 1.0 + (0.3275911 * math.sqrt(0.5)) * jnp.abs(hidden)
    guess = pl.reciprocal(base, approx=True)
    t = guess * (2.0 - base * guess)
    bell = jnp.exp2(hidden * hidden * (-0.5 * math.log2(math.e)))
    poly = 0.5 * 1.061405429
    for coefficient in (-1.453152027, 1.421413741, -0.284496736, 0.254829592):
        poly = poly * t + 0.5 * coefficient
    tail = poly * t * bell
    cdf = jnp.where(hidden < 0.0, tail, 1.0 - tail)
    return hidden * cdf, cdf + hidden * bell * (1.0 / math.sqrt(2.0 * math.pi))


def feed_body(chunk, second, outer, outer_t, weight_in, weight_out, add, final, second_grad, d_bias, second_t, active, slope):
    rows = second.shape[0]

    @pl.when(pl.program_id(0) == 0)
    def _():
        for r in range(0, rows, chunk):
            second_t[:, r : r + chunk] = second[r : r + chunk].T
        final[...] = jnp.zeros_like(final)
        second_grad[...] = jnp.zeros_like(second_grad)

    d_bias[...] = jnp.zeros_like(d_bias)
    for r in range(0, rows, chunk):
        at = slice(r, r + chunk)
        act, gradient = gelu_parts(nn(second[at], weight_in[...]) + add)
        act = act.astype(BF)
        grad = (nt(outer[at], weight_out[...]) * gradient).astype(BF)
        active[at] = act
        slope[at] = grad
        d_bias[0] += jnp.sum(grad.astype(F32), 0, keepdims=True)
        final[at] += nn(act, weight_out[...])
        second_grad[at] += nt(grad, weight_in[...])
    return nn(second_t[...], slope[...]).astype(BF), nn(outer_t[...], active[...]).astype(BF)


def feed_plain_kernel(
    chunk, second, outer, outer_t, expand, expand_bias, reduce, final, second_grad, d_bias, d_expand, d_reduce, second_t, active, slope
):
    d_expand[0], d_reduce[0] = feed_body(
        chunk, second, outer, outer_t, expand.at[0], reduce.at[0], expand_bias[0].astype(F32),
        final, second_grad, d_bias, second_t, active, slope,
    )


def feed_call(second, outer, outer_t, expand, expand_bias, reduce):
    rows = second.shape[0]
    tiles, _, wide = expand.shape
    chunk = rows // 2

    def whole(shape):
        return pl.BlockSpec(shape, lambda t: (0,) * len(shape))

    def tiled(shape):
        return pl.BlockSpec((1,) + shape[1:], lambda t: (t, 0, 0))

    return pl.pallas_call(
        functools.partial(feed_plain_kernel, chunk),
        grid=(tiles,),
        in_specs=[
            whole((rows, D)),
            whole((rows, D)),
            whole((D, rows)),
            tiled(expand.shape),
            tiled(expand_bias.shape),
            tiled(reduce.shape),
        ],
        out_specs=[whole((rows, D)), whole((rows, D)), tiled((tiles, 1, wide))] + [tiled((tiles, D, wide))] * 2,
        out_shape=[
            jax.ShapeDtypeStruct((rows, D), F32),
            jax.ShapeDtypeStruct((rows, D), F32),
            jax.ShapeDtypeStruct((tiles, 1, wide), F32),
        ]
        + [jax.ShapeDtypeStruct((tiles, D, wide), BF)] * 2,
        scratch_shapes=[pltpu.VMEM((D, rows), BF), pltpu.VMEM((rows, wide), BF), pltpu.VMEM((rows, wide), BF)],
        compiler_params=pltpu.CompilerParams(vmem_limit_bytes=VMEM),
        cost_estimate=pl.CostEstimate(
            flops=10 * rows * D * wide * tiles,
            bytes_accessed=8 * D * wide * tiles + 14 * rows * D,
            transcendentals=2 * rows * wide * tiles,
        ),
        name="feed_forward",
    )(second, outer, outer_t, expand, expand_bias, reduce)


def norm_parts(values):
    center = values - jnp.mean(values, -1, keepdims=True)
    scale = lax.rsqrt(jnp.mean(center * center, -1, keepdims=True) + EPSILON)
    return center * scale, scale


def norm_back(grad, unit, scale, gain):
    scaled = grad * gain
    mean_one = jnp.mean(scaled, -1, keepdims=True)
    mean_two = jnp.mean(scaled * unit, -1, keepdims=True)
    return scale * (scaled - mean_one - unit * mean_two)


def to_block(array, frames_local):
    split = array.reshape(frames_local, ROW_FRAME, D)
    return jnp.concatenate(
        [
            split[:, 2:].reshape(frames_local * PATCHES, D),
            split[:, :2].reshape(frames_local * 2, D),
            jnp.zeros((EXTRA - 2 * frames_local, D), array.dtype),
        ],
        0,
    )


def from_block(array, frames_local):
    patches = array[: frames_local * PATCHES].reshape(frames_local, PATCHES, D)
    extra = array[frames_local * PATCHES : frames_local * ROW_FRAME].reshape(frames_local, 2, D)
    return jnp.concatenate([extra, patches], 1).reshape(1, frames_local * ROW_FRAME, D)


def rows_of(per_frame, per_extra, sources, frames_local, fill):
    patches = jnp.broadcast_to(per_frame.reshape(sources, frames_local, 1), (sources, frames_local, PATCHES))
    pad = jnp.full((sources, EXTRA - 2 * frames_local), fill, per_frame.dtype)
    return jnp.concatenate(
        [patches.reshape(sources, -1), per_extra.reshape(sources, 2 * frames_local), pad], 1
    )


def tables(counts, present, sources, frames_local, heads):
    frames = sources * frames_local
    at = jnp.arange(frames, dtype=jnp.int32)
    first, second = counts[0], counts[1]
    inside = at < first + second
    start = jnp.where(at < first, 0, first).astype(jnp.int32)
    time = (at - start).astype(F32)
    begin = jnp.where(inside, start, FAR)
    live_extra = inside[:, None] & (present == 1)
    time_rows = rows_of(time, jnp.repeat(time, 2), sources, frames_local, 0.0)
    live_rows = rows_of(inside.astype(F32), live_extra.astype(F32), sources, frames_local, 0.0)

    patch = np.arange(PATCHES)
    grid_row = np.zeros(frames_local * PATCHES + EXTRA, np.float32)
    grid_col = np.zeros(frames_local * PATCHES + EXTRA, np.float32)
    for l in range(frames_local):
        grid_row[l * PATCHES : (l + 1) * PATCHES] = patch // GRID
        grid_col[l * PATCHES : (l + 1) * PATCHES] = patch % GRID
    lanes = np.zeros((3, HEAD // 2), np.float32)
    freq = 10000.0 ** (-np.arange(PAIRS, dtype=np.float32) / PAIRS)
    for a in range(3):
        lanes[a, a * PAIRS : (a + 1) * PAIRS] = freq
    lanes = np.tile(lanes, (1, heads))
    angle = time_rows[:, :, None] * lanes[0] + (grid_row[:, None] * lanes[1] + grid_col[:, None] * lanes[2])[None]

    def extra_of(per_frame, fill):
        both = jnp.repeat(per_frame, 2).reshape(sources, 2 * frames_local)
        pad = jnp.full((sources, EXTRA - 2 * frames_local), fill, both.dtype)
        return jnp.concatenate([both, pad], 1).reshape(-1)

    extra = sources * EXTRA
    key_frame = jnp.where(live_extra, at[:, None], -1).reshape(sources, 2 * frames_local)
    key_frame = jnp.concatenate(
        [key_frame, jnp.full((sources, EXTRA - 2 * frames_local), -1, jnp.int32)], 1
    ).reshape(-1)
    query_start = extra_of(begin, FAR)
    query_frame = extra_of(at, -1)

    def column(vector):
        return jnp.broadcast_to(vector[:, None], (extra, 128))

    def row(vector):
        return jnp.broadcast_to(vector[None], (8, extra))

    return (
        live_rows,
        jnp.cos(angle),
        jnp.sin(angle),
        (begin, column(key_frame), row(query_start), row(query_frame), column((query_start == FAR).astype(jnp.int32))),
    )


def turn_matrix(width):
    turn = np.zeros((width, width), np.float32)
    step = HEAD // 2
    for h in range(width // HEAD):
        for d in range(HEAD):
            if d < 6 * PAIRS:
                a, rest = divmod(d, 2 * PAIRS)
                side, k = divmod(rest, PAIRS)
                to = side * (width // 2) + h * step + a * PAIRS + k
            else:
                side, k = divmod(d - 6 * PAIRS, step - 3 * PAIRS)
                to = side * (width // 2) + h * step + 3 * PAIRS + k
            turn[h * HEAD + d, to] = 1.0
    return turn


SMEM_REF = pl.BlockSpec(memory_space=pltpu.SMEM)
VMEM_REF = pl.BlockSpec(memory_space=pltpu.VMEM)


ANY_REF = pl.BlockSpec(memory_space=pl.ANY)


def cost(flops=0, bytes_accessed=0, transcendentals=0):
    return pl.CostEstimate(flops=flops, bytes_accessed=bytes_accessed, transcendentals=transcendentals)


def waiting(kernel, inputs, waits, carried=0, outputs=None):
    if not waits:
        return kernel

    def run(*refs):
        used = [*refs[:inputs], *refs[inputs + len(waits) :]]
        if carried:
            del used[inputs + outputs : inputs + outputs + carried]
        kernel(*used)

    return run


def local_call(kernel, name, inputs, outputs, scratch=(), smem=0, flops=0, transcendentals=0, waits=(), carry=()):
    first = len(inputs) + len(waits)
    waits = [*waits, *carry]
    size = sum(math.prod(a.shape) * a.dtype.itemsize for a in [*inputs, *outputs])
    return pl.pallas_call(
        waiting(kernel, len(inputs), waits, len(carry), len(outputs)),
        in_specs=[SMEM_REF] * smem + [VMEM_REF] * (len(inputs) - smem) + [ANY_REF] * len(waits),
        out_specs=[VMEM_REF] * len(outputs) + [ANY_REF] * len(carry),
        out_shape=[*outputs] + [shape_of(*c.shape, dtype=c.dtype) for c in carry],
        input_output_aliases={first + i: len(outputs) + i for i in range(len(carry))},
        scratch_shapes=list(scratch),
        compiler_params=pltpu.CompilerParams(vmem_limit_bytes=VMEM),
        cost_estimate=cost(flops=1, bytes_accessed=1, transcendentals=0),
        name=name,
    )(*inputs, *waits)


def shape_of(*shape, dtype=BF):
    return jax.ShapeDtypeStruct(shape, dtype)


def stack_kernel(*refs):
    for i, ref in enumerate(refs[:-1]):
        refs[-1][i] = ref[...]


def stack_call(pieces, waits=()):
    return local_call(stack_kernel, "stack", pieces, [shape_of(len(pieces), *pieces[0].shape)], waits=waits)[0]


def add_piece_kernel(pieces, other, *outs):
    if len(outs) == 1:
        outs[0][...] = (pieces[0].astype(F32) + other[...].astype(F32)).astype(BF)
    else:
        for i, out in enumerate(outs):
            out[...] = (pieces[0, i].astype(F32) + other[i].astype(F32)).astype(BF)


def add_apart_kernel(one, two, *outs):
    for i, out in enumerate(outs):
        out[...] = (one[i].astype(F32) + two[i].astype(F32)).astype(BF)


def add_apart_call(one, two, waits, carry=()):
    return local_call(
        add_apart_kernel, "add", [one, two], [shape_of(*one.shape[1:])] * one.shape[0], waits=waits, carry=carry
    )


def add_piece_call(pieces, index, other, waits, apart=False):
    outs = [other.shape[1:]] * other.shape[0] if apart else [other.shape]
    block = pl.BlockSpec((1,) + other.shape, lambda i: (index,) + (0,) * other.ndim)

    def whole(shape):
        return pl.BlockSpec(shape, lambda i: (0,) * len(shape))

    result = pl.pallas_call(
        waiting(add_piece_kernel, 2, waits),
        grid=(1,),
        in_specs=[block, whole(other.shape)] + [ANY_REF] * len(waits),
        out_specs=[whole(o) for o in outs],
        out_shape=[shape_of(*o) for o in outs],
        compiler_params=pltpu.CompilerParams(vmem_limit_bytes=VMEM),
        cost_estimate=cost(flops=1, bytes_accessed=1, transcendentals=0),
        name="add_piece",
    )(pieces, other, *waits)
    return result if apart else result[0]


def copy_kernel(source, out):
    out[...] = source[...]


def copy_call(array, waits):
    return local_call(copy_kernel, "copy", [array], [shape_of(*array.shape)], waits=waits)[0]


def add_kernel(*refs):
    total = refs[0][...].astype(F32)
    for ref in refs[1:-1]:
        total = total + ref[...].astype(F32)
    refs[-1][...] = total.astype(refs[-1].dtype)


def add_call(pieces, waits=(), dtype=BF):
    return local_call(add_kernel, "add", pieces, [shape_of(*pieces[0].shape, dtype=dtype)], waits=waits)[0]


def span(index, size):
    return pl.ds(pl.multiple_of(index * size, size), size)


def front_kernel(*refs):
    *parts, near = refs
    for s, ref in enumerate(parts):
        near[s] = ref[...]


def pack_kernel(n_z, place, near, far, own, one, two, three, vectors, bias, expand_bias):
    y, z, shard = place[1], place[2], place[4]
    rows = own.shape[0]
    width = bias.shape[1] // 3
    part = near.shape[2]
    chunks = part // 128
    d_part = D // (2 * n_z)
    outs = (own, one, two, three)

    def source(dp):
        return (dp % 2) ^ y, (z - dp // 2 + n_z) % n_z

    for m in range(4):
        target = shard ^ m
        for i in range(3 * width // 128):
            j = (i // 2) * (D // 128) + 2 * target + i % 2
            side, s = source(j // chunks)
            lanes = pl.ds(pl.multiple_of((j % chunks) * 128, 128), 128)
            at = slice(i * 128, (i + 1) * 128)

            @pl.when(side == 0)
            def _(m=m, s=s, lanes=lanes, at=at):
                outs[m][:, at] = near[s, :rows, lanes]

            @pl.when(side == 1)
            def _(m=m, s=s, lanes=lanes, at=at):
                outs[m][:, at] = far[s, :rows, lanes]

            if m == 0:

                @pl.when(side == 0)
                def _(s=s, lanes=lanes, at=at):
                    bias[:, at] = near[s, rows + 6 : rows + 7, lanes].astype(F32)

                @pl.when(side == 1)
                def _(s=s, lanes=lanes, at=at):
                    bias[:, at] = far[s, rows + 6 : rows + 7, lanes].astype(F32)

    quarter = FF // (8 * n_z)
    for s in range(n_z):
        for side, ref in ((0, near), (1, far)):
            dp = 2 * ((z - s + n_z) % n_z) + (y ^ side)
            block = ref[s, rows : rows + 16].astype(F32)
            vectors[:, span(dp, d_part)] = block[:8, :d_part]
            picked = block[7:8, :quarter]
            for f in range(1, 4):
                picked = jnp.where(shard == f, block[7 + f : 8 + f, :quarter], picked)
            expand_bias[s, :, side * quarter : (side + 1) * quarter] = picked


def enter_kernel(place, e0, e1, e2, e3, w0, w1, w2, w3, bias, vectors, turn, cosine, sine, q, k, v, normed, triple, scratch, entered, weight, add):
    shard = place[4]
    width = q.shape[-1]
    half = width // 2
    step = pl.program_id(0)

    @pl.when(step == 0)
    def _():
        for m, ref in enumerate((w0, w1, w2, w3)):
            rows = span(shard ^ m, ref.shape[0])
            triple[rows, :] = ref[...]
            for part in range(2):
                at = slice(part * width, (part + 1) * width)
                weight[rows, at] = nn(ref[:, at], turn[...]).astype(BF)
            weight[rows, 2 * width :] = ref[:, 2 * width :]
        low = jnp.broadcast_to(bias[...], (8, 3 * width)).astype(BF)
        for part in range(2):
            at = slice(part * width, (part + 1) * width)
            add[:, at] = nn(low[:, at], turn[...])
        add[:, 2 * width :] = low[:, 2 * width :].astype(F32)

    for m, ref in enumerate((e0, e1, e2, e3)):

        @pl.when(step == m)
        def _(ref=ref):
            entered[...] = ref[...]

    values = entered[...].astype(F32)
    unit, _ = norm_parts(values)
    rows = (unit * vectors[0:1] + vectors[1:2]).astype(BF)
    normed[0] = rows
    scratch[...] = rows
    cos = cosine[0]
    sin = sine[0]
    for part, out in ((0, q), (1, k)):
        at = slice(part * width, (part + 1) * width)
        value = nn(scratch[...], weight[:, at]) + add[:1, at]
        first = value[:, :half]
        second = value[:, half:]
        out[0, :, :half] = (first * cos - second * sin).astype(BF)
        out[0, :, half:] = (second * cos + first * sin).astype(BF)
    v[0] = (nn(scratch[...], weight[:, 2 * width :]) + add[:1, 2 * width :]).astype(BF)


def enter_call(place, entered, weights, bias, vectors, turn, cosine, sine, waits, carry):
    rows = entered[0].shape[0]
    width = bias.shape[-1] // 3

    def whole(array):
        return pl.BlockSpec(array.shape, lambda m, p: (0,) * array.ndim)

    def moved(*shape):
        return pl.BlockSpec((1,) + shape, lambda m, p: (p[4] ^ m, 0, 0))

    flat = [*entered, *weights, bias, vectors, turn]
    waits = [*waits, carry]
    return pl.pallas_call(
        waiting(enter_kernel, 3 + len(flat), waits, 1, 5),
        grid_spec=pltpu.PrefetchScalarGridSpec(
            num_scalar_prefetch=1,
            grid=(4,),
            in_specs=[whole(a) for a in flat] + [moved(rows, width // 2)] * 2 + [ANY_REF] * len(waits),
            out_specs=[moved(rows, width)] * 3
            + [moved(rows, D), pl.BlockSpec((D, 3 * width), lambda m, p: (0, 0)), ANY_REF],
            scratch_shapes=[
                pltpu.VMEM((rows, D), BF),
                pltpu.VMEM((rows, D), BF),
                pltpu.VMEM((D, 3 * width), BF),
                pltpu.VMEM((8, 3 * width), F32),
            ],
        ),
        out_shape=[shape_of(4, rows, width)] * 3
        + [shape_of(4, rows, D), shape_of(D, 3 * width), shape_of(*carry.shape)],
        input_output_aliases={2 + len(flat) + len(waits): 5},
        compiler_params=pltpu.CompilerParams(vmem_limit_bytes=VMEM),
        cost_estimate=cost(flops=8 * rows * D * 3 * width, bytes_accessed=30 * rows * D, transcendentals=0),
        name="enter",
    )(place, *flat, cosine, sine, *waits)


def part_kernel(place, mixed, own, far):
    x = place[0]
    for core in range(2):
        own[core] = mixed[2 * x + core]
        far[core] = mixed[2 * (1 - x) + core]


def project_kernel(place, own, far, output, keep, give, weight):
    x, core = place[0], place[3]
    _, rows, width = own.shape
    n_z = output.shape[0]
    d_part = output.shape[-1]
    for z in range(n_z):
        for y in range(2):
            at = (2 * z + y) * d_part
            for source in range(2):
                weight[source * width : (source + 1) * width, at : at + d_part] = output[z, y, source]

    def part(at):
        return nn(own[at], weight[span(x, width), :]) + nn(far[at], weight[span(1 - x, width), :])

    give[...] = part(1 - core).astype(BF)
    keep[...] = part(core)


def middle_kernel(entered, keep, other, vectors, middle, second):
    values = entered[...].astype(F32) + keep[...] + other[...].astype(F32) + vectors[2:3]
    middle[...] = values
    unit, _ = norm_parts(values)
    second[...] = (unit * vectors[3:4] + vectors[4:5]).astype(BF)


def rows_call(kernel, name, inputs, outputs, blocks=3, waits=()):
    rows = max(a.shape[0] for a in inputs)
    step = rows // blocks

    def spec(array):
        if array.shape[0] == 8:
            return pl.BlockSpec(array.shape, lambda i: (0, 0))
        return pl.BlockSpec((step, array.shape[1]), lambda i: (i, 0))

    size = sum(math.prod(a.shape) * a.dtype.itemsize for a in [*inputs, *outputs])
    return pl.pallas_call(
        waiting(kernel, len(inputs), waits),
        grid=(blocks,),
        in_specs=[spec(a) for a in inputs] + [ANY_REF] * len(waits),
        out_specs=[spec(a) for a in outputs],
        out_shape=list(outputs),
        compiler_params=pltpu.CompilerParams(vmem_limit_bytes=VMEM),
        cost_estimate=cost(flops=1, bytes_accessed=1, transcendentals=0),
        name=name,
    )(*inputs, *waits)


def add_rows(ref, rows):
    @pl.when(pl.program_id(0) == 0)
    def _():
        ref[...] = jnp.zeros_like(ref)

    for i, row in enumerate(rows):
        ref[i : i + 1] += jnp.sum(row, 0, keepdims=True)


def middle_back_kernel(middle, outer, keep, other, far, vectors, middle_grad, branch, sums):
    unit, scale = norm_parts(middle[...])
    grad = keep[...] + other[...].astype(F32) + far[...].astype(F32)
    result = outer[...].astype(F32) + norm_back(grad, unit, scale, vectors[3:4])
    middle_grad[...] = result
    low = result.astype(BF)
    branch[...] = low
    add_rows(sums, (low.astype(F32), grad * unit, grad, outer[...].astype(F32)))


def leave_rows(values, frames_local):
    pieces = []
    for l in range(frames_local):
        at = frames_local * PATCHES + 2 * l
        pieces += [values[at : at + 2], values[l * PATCHES : (l + 1) * PATCHES]]
    return jnp.concatenate(pieces, 0)


def output_kernel(frames_local, middle, keep, other, far, live, vectors, out):
    values = middle[...] + keep[...] + other[...].astype(F32) + far[...].astype(F32) + vectors[5:6]
    values = values * live[...]
    out[...] = leave_rows(values, frames_local).astype(BF)


def mixed_grad_kernel(place, branch, branch_other, weight, own, far):
    x, core = place[0], place[3]
    width = own.shape[-1]
    for at, rows in ((core, branch), (1 - core, branch_other)):
        own[at] = nt(rows[...], weight[span(x, width), :]).astype(BF)
        far[at] = nt(rows[...], weight[span(1 - x, width), :]).astype(BF)


def output_grad_kernel(place, own, far, branch, branch_other, near_y, far_y, rows_all, held):
    y, z, core = place[1], place[2], place[3]
    _, rows, width = own.shape
    _, n_z, _, d_part = near_y.shape
    rows_all[span(core, rows), :] = branch[...]
    rows_all[span(1 - core, rows), :] = branch_other[...]
    for i, ref in enumerate((own, far)):
        held[...] = tn(ref[...].reshape(2 * rows, width), rows_all[...]).astype(BF)
        for s in range(n_z):
            for flip, out in ((0, near_y), (1, far_y)):
                out[i, s] = held[:, span(2 * ((z + s) % n_z) + (y ^ flip), d_part)]


def triple_kernel(
    place, normed, triple_grad, grad_rows, triple, e0, e1, e2, e3, own, one, two, three, rows_own, rows_far, rows_give, bias, sums, entered, held
):
    step = pl.program_id(0)
    count, rows, wide = triple_grad.shape
    outs = (own, one, two, three)
    rows_outs = (rows_own, rows_give.at[0], rows_far, rows_give.at[1])

    @pl.when(step == 0)
    def _():
        bias[...] = jnp.zeros_like(bias)
        sums[...] = jnp.zeros_like(sums)

    for m, ref in enumerate((e0, e1, e2, e3)):

        @pl.when(step == m)
        def _(ref=ref):
            entered[...] = ref[...]

    flat = triple_grad[...].reshape(count * rows, wide)
    held[...] = tn(normed[...].reshape(count * rows, normed.shape[-1]), flat).astype(BF)
    back = nt(grad_rows[0], triple[...])
    unit, _ = norm_parts(entered[...].astype(F32))
    sums[0:1] += jnp.sum(back * unit, 0, keepdims=True)
    sums[1:2] += jnp.sum(back, 0, keepdims=True)
    entered[...] = back.astype(BF)
    bias[...] += jnp.sum(grad_rows[0].astype(F32), 0, keepdims=True)
    for m in range(4):

        @pl.when(step == m)
        def _(m=m):
            outs[m][...] = held[...]
            rows_outs[m][...] = entered[...]


def triple_call(place, normed, triple_grad, triple, entered, waits):
    count, rows, wide = triple_grad.shape
    part = D // count

    def fixed(shape):
        return pl.BlockSpec(shape, lambda m, p: (0,) * len(shape), pipeline_mode=pl.Buffered(1))

    outs = [shape_of(part, wide)] * 4 + [shape_of(rows, D)] * 2
    outs += [shape_of(2, rows, D), shape_of(1, wide, dtype=F32), shape_of(8, D, dtype=F32)]
    return pl.pallas_call(
        waiting(triple_kernel, 5 + len(entered), waits),
        grid_spec=pltpu.PrefetchScalarGridSpec(
            num_scalar_prefetch=1,
            grid=(count,),
            in_specs=[
                pl.BlockSpec((count, rows, part), lambda m, p: (0, 0, p[4] ^ m)),
                fixed(triple_grad.shape),
                pl.BlockSpec((1, rows, wide), lambda m, p: (p[4] ^ m, 0, 0)),
                fixed(triple.shape),
            ]
            + [fixed(e.shape) for e in entered]
            + [ANY_REF] * len(waits),
            out_specs=[fixed(o.shape) for o in outs],
            scratch_shapes=[pltpu.VMEM((rows, D), BF), pltpu.VMEM((part, wide), BF)],
        ),
        out_shape=outs,
        compiler_params=pltpu.CompilerParams(vmem_limit_bytes=VMEM),
        cost_estimate=cost(flops=4 * count * rows * wide * D, bytes_accessed=20 * rows * D, transcendentals=0),
        name="triple_grads",
    )(place, normed, triple_grad, triple_grad, triple, *entered, *waits)


def normed_sum_kernel(own, far, got, own_out, far_out):
    own_out[...] = (own[...].astype(F32) + got[0].astype(F32)).astype(BF)
    far_out[...] = (far[...].astype(F32) + got[1].astype(F32)).astype(BF)


def tail_sum_kernel(near, near_got, out, out_got, *totals):
    part = near.shape[-1]
    for s, total in enumerate(totals):
        total[:, :part] = (near[s].astype(F32) + near_got[s].astype(F32)).astype(BF)
        total[:, part:] = (out[0, s].astype(F32) + out_got[s].astype(F32)).astype(BF)


def unpack_kernel(n_z, place, p0, p1, p2, p3, near, far, held):
    y, z, shard = place[1], place[2], place[4]
    part = near.shape[2]
    chunks = part // 128
    for m, ref in enumerate((p0, p1, p2, p3)):
        held[shard ^ m] = ref[...]
    for j in range(3 * D // 128):
        dp, c = divmod(j, chunks)
        per = D // 128
        at = (j // per) * 256 + (j % 2) * 128
        chunk = held[(j % per) // 2, :, at : at + 128]
        s = (dp // 2 - z + n_z) % n_z

        @pl.when(y == dp % 2)
        def _(chunk=chunk, s=s, c=c):
            near[s, :, c * 128 : (c + 1) * 128] = chunk

        @pl.when(y != dp % 2)
        def _(chunk=chunk, s=s, c=c):
            far[s, :, c * 128 : (c + 1) * 128] = chunk


def tail_kernel(*refs):
    total = refs[0][...].astype(F32)
    for ref in refs[1:-2]:
        total = total + ref[...].astype(F32)
    part = refs[-2].shape[-1]
    refs[-2][...] = total[:, :part]
    refs[-1][...] = total[:, part:]


def leave_kernel(frames_local, entered, keep, other, middle_grad, live, vectors, out):
    unit, scale = norm_parts(entered[...].astype(F32))
    grad = keep[...].astype(F32) + other[...].astype(F32)
    result = (middle_grad[...] + norm_back(grad, unit, scale, vectors[0:1])) * live[...]
    out[...] = leave_rows(result, frames_local)


def split_kernel(place, expand, reduce, own, one, two, three):
    shard = place[4]
    rows = expand.shape[0]
    part = own.shape[1]
    blocks = reduce.shape[0] // (4 * part)
    for m, ref in enumerate((own, one, two, three)):
        to = shard ^ m
        ref[:rows] = expand[:, span(to, part)]
        for p in range(blocks):
            ref[rows + p * part : rows + (p + 1) * part] = reduce[span(p * 4 + to, part), :]


def join_kernel(place, own, one, two, three, expand, reduce):
    shard = place[4]
    rows = expand.shape[0]
    part = own.shape[1]
    blocks = reduce.shape[0] // (4 * part)
    for m, ref in enumerate((own, one, two, three)):
        at = shard ^ m
        expand[:, span(at, part)] = ref[:rows].astype(F32)
        for p in range(blocks):
            reduce[span(p * 4 + at, part), :] = ref[rows + p * part : rows + (p + 1) * part].astype(F32)


def fill_weights(place, near, far, weight_in, weight_out):
    y, z, shard = place[1], place[2], place[4]
    n_z = len(near)
    part = near[0].shape[-1]
    rows = D // 4
    for s in range(n_z):
        for side, ref in ((0, near[s]), (1, far[s])):
            if weight_in is not None:
                for m in range(4):
                    weight_in[s, span(shard ^ m, rows), side * part : (side + 1) * part] = ref[m, :rows]
            features = span(2 * ((z - s + n_z) % n_z) + (y ^ side), part)
            for tile in range(n_z):
                unit = (z - tile + n_z) % n_z
                for flip in range(2):
                    at = pl.ds(pl.multiple_of(rows + (y ^ flip) * part, part), part)
                    weight_out[tile, flip * part : (flip + 1) * part, features] = ref[unit ^ shard, at, :]


def feed_kernel(
    place, normal, normal_other, cot, cot_other, p0, p1, p2, p3, f0, f1, f2, f3, bias, active, slope, keep, give, d_bias, give_acc, weight_in, weight_out
):
    step = pl.program_id(0)
    rows = normal.shape[0]

    @pl.when(step == 0)
    def _():
        fill_weights(place, (p0, p1, p2, p3), (f0, f1, f2, f3), weight_in, weight_out)
        keep[...] = jnp.zeros_like(keep)
        give_acc[...] = jnp.zeros_like(give_acc)

    d_bias[...] = jnp.zeros_like(d_bias)
    for i, values, outer, total in ((0, normal, cot, keep), (1, normal_other, cot_other, give_acc)):
        act, gradient = gelu_parts(nn(values[...], weight_in[step]) + bias[0])
        grad = (nt(outer[...], weight_out[step]) * gradient).astype(BF)
        active[i * rows : (i + 1) * rows] = act.astype(BF)
        slope[i * rows : (i + 1) * rows] = grad
        d_bias[0] += jnp.sum(grad.astype(F32), 0, keepdims=True)
        total[...] += nt(grad, weight_in[step])

    @pl.when(step == pl.num_programs(0) - 1)
    def _():
        give[...] = give_acc[...].astype(BF)


def feed_grad_kernel(
    place,
    n0,
    n1,
    n2,
    n3,
    c0,
    c1,
    c2,
    c3,
    active,
    active_far,
    slope,
    slope_far,
    p0,
    p1,
    p2,
    p3,
    f0,
    f1,
    f2,
    f3,
    keep,
    give,
    keep_far,
    give_far,
    grads,
    sent,
    normal_t,
    cot_all,
    give_acc,
    keep_far_acc,
    give_far_acc,
    weight_out,
    held,
    active_all,
    slope_all,
):
    y, z, shard = place[1], place[2], place[4]
    step = pl.program_id(0)
    n_z = grads.shape[0]
    part = p0.shape[-1]
    rows = n0.shape[0]
    deep = D // 4
    totals = (keep, give_acc, keep_far_acc, give_far_acc)

    @pl.when(step == 0)
    def _():
        fill_weights(place, (p0, p1, p2, p3), (f0, f1, f2, f3), None, weight_out)
        for i, (normal, cot) in enumerate(((n0, c0), (n1, c1), (n2, c2), (n3, c3))):
            normal_t[:, i * rows : (i + 1) * rows] = normal[...].T
            cot_all[i * rows : (i + 1) * rows] = cot[...]
            totals[i][...] = jnp.zeros_like(totals[i])

    for i, (act, grad) in enumerate(((active, slope), (active_far, slope_far))):
        at = slice(i * 2 * rows, (i + 1) * 2 * rows)
        active_all[at] = act[...]
        slope_all[at] = grad[...]
        for j in range(2):
            totals[2 * i + j][...] += nn(act[j * rows : (j + 1) * rows], weight_out[step])

    held[...] = nn(normal_t[...], slope_all[...]).astype(BF)
    for side in range(2):
        for m in range(4):
            grads[(n_z - step) % n_z, side, m, :deep] = held[span(shard ^ m, deep), side * part : (side + 1) * part]
    held_t = weight_out.at[step]
    held_t[...] = tn(active_all[...], cot_all[...]).astype(BF)
    unit = (z - step + n_z) % n_z
    for side in range(2):
        at = pl.ds(pl.multiple_of(deep + (y ^ side) * part, part), part)
        for s in range(n_z):
            for flip in range(2):
                features = span(2 * ((z + s) % n_z) + (y ^ flip), part)
                grads[s, flip, unit ^ shard, at, :] = held_t[side * part : (side + 1) * part, features]

    @pl.when(step == pl.num_programs(0) - 1)
    def _():
        give[...] = give_acc[...].astype(BF)
        keep_far[...] = keep_far_acc[...].astype(BF)
        give_far[...] = give_far_acc[...].astype(BF)
        sent[...] = grads[n_z - 1]


def feed_specs(place, n_z):
    def whole(array):
        return pl.BlockSpec(array.shape, lambda t, p: (0,) * len(array.shape), pipeline_mode=pl.Buffered(1))

    def lanes(rows, wide):
        return pl.BlockSpec((rows, wide), lambda t, p: (0, t))

    return whole, lanes


def feed_split_call(place, normal, cot, parts, bias, waits=()):
    rows = normal[0].shape[0]
    n_z = len(parts) // 2
    wide = bias.shape[-1]
    whole, lanes = feed_specs(place, n_z)
    row = pl.BlockSpec((1, 1, wide), lambda t, p: (t, 0, 0))
    block = (rows, D)
    outs = [shape_of(2 * rows, n_z * wide)] * 2 + [shape_of(*block, dtype=F32), shape_of(*block)]
    outs += [shape_of(n_z, 1, wide, dtype=F32)]
    inputs = [*normal, *cot, *parts]
    return pl.pallas_call(
        waiting(feed_kernel, 2 + len(inputs), waits),
        grid_spec=pltpu.PrefetchScalarGridSpec(
            num_scalar_prefetch=1,
            grid=(n_z,),
            in_specs=[whole(a) for a in inputs] + [row] + [ANY_REF] * len(waits),
            out_specs=[lanes(2 * rows, wide)] * 2 + [whole(o) for o in outs[2:4]] + [row],
            scratch_shapes=[pltpu.VMEM(block, F32), pltpu.VMEM((n_z, D, wide), BF), pltpu.VMEM((n_z, wide, D), BF)],
        ),
        out_shape=outs,
        compiler_params=pltpu.CompilerParams(vmem_limit_bytes=VMEM),
        cost_estimate=cost(
            flops=12 * rows * D * wide * n_z, bytes_accessed=20 * rows * D, transcendentals=4 * rows * wide * n_z
        ),
        name="feed_forward",
    )(place, *inputs, bias, *waits)


def feed_grad_call(place, normal, cot, active, slope, parts, waits=()):
    rows = normal[0].shape[0]
    n_z = len(parts) // 2
    wide = active[0].shape[1] // n_z
    whole, lanes = feed_specs(place, n_z)
    block = (rows, D)
    outs = [shape_of(*block, dtype=F32)] + [shape_of(*block)] * 3 + [shape_of(n_z, 2, *parts[0].shape), shape_of(2, *parts[0].shape)]
    first = [*normal, *cot]
    tiles = [*active, *slope]
    return pl.pallas_call(
        waiting(feed_grad_kernel, 1 + len(first) + len(tiles) + 2 * n_z, waits),
        grid_spec=pltpu.PrefetchScalarGridSpec(
            num_scalar_prefetch=1,
            grid=(n_z,),
            in_specs=[whole(a) for a in first]
            + [lanes(2 * rows, wide)] * 4
            + [whole(p) for p in parts]
            + [ANY_REF] * len(waits),
            out_specs=[whole(o) for o in outs],
            scratch_shapes=[
                pltpu.VMEM((D, 4 * rows), BF),
                pltpu.VMEM((4 * rows, D), BF),
                pltpu.VMEM(block, F32),
                pltpu.VMEM(block, F32),
                pltpu.VMEM(block, F32),
                pltpu.VMEM((n_z, wide, D), BF),
                pltpu.VMEM((D, wide), BF),
                pltpu.VMEM((4 * rows, wide), BF),
                pltpu.VMEM((4 * rows, wide), BF),
            ],
        ),
        out_shape=outs,
        compiler_params=pltpu.CompilerParams(vmem_limit_bytes=VMEM),
        cost_estimate=cost(flops=24 * rows * D * wide * n_z, bytes_accessed=40 * rows * D),
        name="feed_grads",
    )(place, *first, *tiles, *parts, *waits)


def torus_shards(sizes, *args):
    (
        tokens,
        cotangent,
        frame_counts,
        presence,
        attend_gain,
        attend_shift,
        triple_weight,
        triple_bias,
        output_weight,
        output_bias,
        second_gain,
        second_shift,
        expand_weight,
        expand_bias,
        reduce_weight,
        reduce_bias,
    ) = args
    n_z, n_y, n_x = sizes
    n_dp = n_z * n_y
    n_f = n_x * 2
    width = D // n_f
    local_rows = tokens.shape[1]
    frames_local = local_rows // ROW_FRAME
    rows = frames_local * PATCHES + EXTRA
    z, y, x, core = (lax.axis_index(name) for name in ("z", "y", "x", "core"))
    shard = x * 2 + core
    place = jnp.stack([x, y, z, core, shard]).astype(jnp.int32)
    d_part = D // n_dp
    qkv_part = 3 * D // n_dp
    ff_part = FF // n_dp
    quarter = ff_part // 4

    def swap(array, axis="core"):
        return lax.ppermute(array, axis, [(0, 1), (1, 0)])

    def cross_over(array):
        return lax.ppermute(array, ("x", "core"), [(i, i ^ 3) for i in range(4)])

    def to_z(array, s):
        return lax.ppermute(array, "z", [(i, (i + s) % n_z) for i in range(n_z)])

    def take(array, index, axis=0):
        return lax.dynamic_index_in_dim(array, index, axis, False)

    def gather_z(array):
        return [array] + [to_z(array, s) for s in range(1, n_z)]

    def scatter_z(array, waits=(), dtype=BF):
        return add_call([array[0]] + [to_z(array[s], s) for s in range(1, n_z)], waits, dtype)

    def lane_row(vector):
        return jnp.pad(vector, (0, qkv_part - vector.shape[0]))[None]

    vectors = [attend_gain, attend_shift, output_bias, second_gain, second_shift, reduce_bias, triple_bias]
    vectors += [expand_bias[f * quarter : (f + 1) * quarter] for f in range(4)]
    packed = jnp.concatenate(
        [triple_weight] + [lane_row(v) for v in vectors] + [jnp.zeros((16 - len(vectors), qkv_part), BF)], 0
    )

    live_all = tables(frame_counts[0], presence[0], n_f, frames_local, width // HEAD)[0]
    live = take(live_all, shard)[:, None]
    entered = to_block(tokens[0], frames_local) * live.astype(BF)
    outer = to_block(cotangent[0], frames_local) * live.astype(BF)

    own, one, two, three, packed = local_call(
        split_kernel,
        "split",
        [place, expand_weight, reduce_weight],
        [shape_of(2 * (D // n_f), d_part)] * 4,
        smem=1,
        carry=[packed],
    )
    packed_parts = gather_z(packed)
    feed = stack_call([own, swap(one), swap(two, "x"), cross_over(three)], [packed_parts[1]])
    near = local_call(
        front_kernel,
        "front",
        packed_parts,
        [shape_of(n_z, *packed.shape)],
    )[0]
    far = swap(near, "y")
    entered = copy_call(entered, [near, feed])
    entered_x = swap(entered, "x")
    entered_all = [entered, swap(entered), entered_x]
    output_all = lax.all_gather(output_weight, ("z", "y", "x"), axis=0).reshape(n_z, n_y, n_x, width, d_part)

    own, one, two, three, vectors, bias, expand_add, counts = local_call(
        functools.partial(pack_kernel, n_z),
        "pack",
        [place, near, far],
        [shape_of(D // n_f, 3 * width)] * 4
        + [shape_of(8, D, dtype=F32), shape_of(1, 3 * width, dtype=F32), shape_of(n_z, 1, 2 * quarter, dtype=F32)],
        smem=1,
        waits=[entered_all[1]],
        carry=[frame_counts],
    )
    _, cosine, sine, guides = tables(counts[0], presence[0], n_f, frames_local, width // HEAD)
    weights = [own, swap(one), swap(two, "x"), cross_over(three)]
    entered_all.append(swap(copy_call(entered_x, [own])))
    feed_near = gather_z(feed)
    turn = jnp.asarray(turn_matrix(width), BF)
    q, k, v, normed, triple, outer = enter_call(
        place, entered_all, weights, bias, vectors, turn, cosine, sine, feed_near[1:2], outer
    )
    feed_far = [swap(part, "y") for part in feed_near]
    feed_parts = [*feed_near, *feed_far]
    outer_x = swap(outer, "x")
    outer_all = [outer, swap(outer), outer_x]
    mixed, exact, logs, logs_extra = attend_call(*guides, q, k, v, waits=feed_near[2:])
    mixed_own, mixed_far, outer_x = local_call(
        part_kernel,
        "mixed_parts",
        [place, mixed],
        [shape_of(2, rows, width)] * 2,
        smem=1,
        waits=[*feed_far[:3], outer_all[1]],
        carry=[outer_x],
    )
    mixed_far = swap(mixed_far, "x")
    outer_all = [*outer_all[:2], outer_x, swap(outer_x)]
    keep, give = local_call(
        project_kernel,
        "project",
        [place, mixed_own, mixed_far, output_all],
        [shape_of(rows, D, dtype=F32), shape_of(rows, D)],
        [pltpu.VMEM((D // 2, D), BF)],
        smem=1,
        flops=4 * rows * D * D // 2,
        waits=[outer_all[3], feed_far[3]],
    )
    output_full = output_all.transpose(2, 3, 0, 1, 4).reshape(D // 2, D)
    middle, second = rows_call(
        middle_kernel,
        "middle",
        [entered, keep, swap(give), vectors],
        [shape_of(rows, D, dtype=F32), shape_of(rows, D)],
    )
    second_all = [second, swap(second)]
    feed_both = [feed_parts, expand_add]
    active, slope, back, back_give, d_bias = feed_split_call(place, second_all, outer_all[:2], *feed_both)
    second_x = swap(second, "x")
    second_all += [second_x, swap(copy_call(second_x, [active]))]
    active_far, slope_far, back_far, back_far_give, d_bias_far = feed_split_call(
        place, second_all[2:], outer_all[2:], *feed_both, waits=[back_give]
    )
    back_give = swap(back_give)
    back_far = swap(add_call([back_far, swap(back_far_give)]), "x")
    final, final_give, final_far, final_far_give, d_feed, d_sent = feed_grad_call(
        place, second_all, outer_all, [active, active_far], [slope, slope_far], feed_parts
    )
    middle_grad, branch, sums_two = rows_call(
        middle_back_kernel,
        "middle_back",
        [middle, outer, back, back_give, back_far, vectors],
        [shape_of(rows, D, dtype=F32), shape_of(rows, D), shape_of(8, D, dtype=F32)],
        waits=[d_sent],
    )
    branch_other = swap(branch)
    grad_own, grad_far = local_call(
        mixed_grad_kernel,
        "mixed_grad",
        [place, branch, branch_other, output_full],
        [shape_of(2, rows, width)] * 2,
        smem=1,
        flops=4 * rows * D * D // 2,
    )
    grad_far = swap(grad_far, "x")
    out_near, out_far = local_call(
        output_grad_kernel,
        "output_weight_grad",
        [place, mixed_own, mixed_far, branch, branch_other],
        [shape_of(n_x, n_z, width, d_part)] * 2,
        [pltpu.VMEM((2 * rows, D), BF), pltpu.VMEM((width, D), BF)],
        smem=1,
        flops=4 * rows * D * D // 2,
        waits=[grad_own],
    )
    out_far = swap(out_far, "y")
    final_far = add_call([final_far, swap(final_far_give)], [grad_own])
    final_far = swap(final_far, "x")
    final_give = swap(final_give)
    triple_grad = attend_back_call(
        x.reshape(1), *guides, q, k, v, [grad_own, grad_far], exact, logs, logs_extra, cosine, sine, turn, waits=[out_near, final_give]
    )
    back_feed = to_z(d_sent, 1)
    tri_own, tri_one, tri_two, tri_three, normed_own, normed_far, normed_give, d_triple_bias, sums_one = triple_call(
        place, normed, triple_grad, triple, entered_all, [back_feed, out_far, final_far]
    )
    pieces = [tri_own, swap(tri_one), swap(tri_two, "x"), cross_over(tri_three)]
    zero_qkv = jnp.zeros((3, n_f, width), F32)
    triple_bias_part = lax.dynamic_update_slice(zero_qkv, d_triple_bias.reshape(3, 1, width), (0, shard, 0))
    expand_bias_part = jnp.zeros((n_z, n_y, n_f, quarter), F32)
    d_bias = (d_bias + d_bias_far).reshape(n_z, n_y, quarter)
    for s in range(n_z):
        for side in range(n_y):
            expand_bias_part = lax.dynamic_update_slice(
                expand_bias_part, d_bias[s, side].reshape(1, 1, 1, quarter), ((z - s) % n_z, y ^ side, shard, 0)
            )
    sums = [sums_one[0], sums_one[1], sums_two[0], sums_two[1], sums_two[2], sums_two[3], triple_bias_part, expand_bias_part]
    sums = jnp.concatenate([piece.reshape(n_dp, -1) for piece in sums], 1)

    def butterfly(sums, bits):
        for bit in bits:
            sums = sums + lax.ppermute(sums, ("z", "y", "x", "core"), [(i, i ^ bit) for i in range(32)])
        return sums

    back_feed = add_piece_call(d_feed, 2, back_feed, [tri_own])
    back_feed = to_z(back_feed, 1)
    out_near, out_send = add_apart_call(out_near, out_far, [tri_own])
    out_far = swap(out_send, "x")
    block_output = local_call(
        functools.partial(output_kernel, frames_local),
        "block_output",
        [middle, final, final_give, final_far, live, vectors],
        [shape_of(local_rows, D)],
        waits=[out_near],
    )[0]
    normed_own, normed_far = local_call(
        normed_sum_kernel,
        "normed_sum",
        [normed_own, normed_far, swap(normed_give)],
        [shape_of(rows, D)] * 2,
        waits=pieces[1:],
    )
    normed_far = swap(normed_far, "x")
    tri_near, tri_far, sums = local_call(
        functools.partial(unpack_kernel, n_z),
        "unpack",
        [place, *pieces],
        [shape_of(n_z, D // n_f, qkv_part)] * 2,
        [pltpu.VMEM((4, D // n_f, 3 * width), BF)],
        smem=1,
        waits=[block_output, normed_own, out_far],
        carry=[sums],
    )
    tri_far = swap(tri_far, "y")
    back_feed = add_piece_call(d_feed, 1, back_feed, [tri_near])
    back_feed = to_z(back_feed, 1)
    sums = butterfly(sums, (1, 4))
    tail = local_call(
        tail_sum_kernel,
        "tail_sum",
        [tri_near, tri_far, out_near[None], out_far],
        [shape_of(D // n_f, qkv_part + d_part)] * n_z,
        waits=[sums],
    )
    tail_parts = [tail[0]] + [to_z(tail[s], s) for s in range(1, n_z)]
    d_near, d_send = add_piece_call(d_feed, 0, back_feed, [tail[0]], True)
    tokens_grad = local_call(
        functools.partial(leave_kernel, frames_local),
        "tokens_grad",
        [entered, normed_own, normed_far, middle_grad, live, vectors],
        [shape_of(local_rows, D, dtype=F32)],
        waits=[tail[0], d_near],
    )[0]
    triple_weight_grad, output_weight_grad = local_call(
        tail_kernel,
        "tail",
        tail_parts,
        [shape_of(D // n_f, qkv_part, dtype=F32), shape_of(D // n_f, d_part, dtype=F32)],
        waits=[tokens_grad],
    )
    *d_feed, sums = add_apart_call(d_near, swap(d_send, "y"), [triple_weight_grad], [sums])
    sums = butterfly(sums, (2, 8, 16))
    expand_weight_grad, reduce_weight_grad = local_call(
        join_kernel,
        "join",
        [place, d_feed[0], swap(d_feed[1]), swap(d_feed[2], "x"), cross_over(d_feed[3])],
        [shape_of(D // n_f, ff_part, dtype=F32), shape_of(FF // n_f, d_part, dtype=F32)],
        smem=1,
    )

    sums = take(sums, z * n_y + y)
    parts = [sums[i * d_part : (i + 1) * d_part] for i in range(6)]
    rest = sums[6 * d_part :]
    return (
        block_output[None],
        tokens_grad[None],
        parts[0],
        parts[1],
        triple_weight_grad,
        rest[:qkv_part],
        output_weight_grad,
        parts[2],
        parts[3],
        parts[4],
        expand_weight_grad,
        rest[qkv_part:],
        reduce_weight_grad,
        parts[5],
    )


def general_shards(sizes, *args):
    (
        tokens,
        cotangent,
        frame_counts,
        presence,
        attend_gain,
        attend_shift,
        triple_weight,
        triple_bias,
        output_weight,
        output_bias,
        second_gain,
        second_shift,
        expand_weight,
        expand_bias,
        reduce_weight,
        reduce_bias,
    ) = args
    n_z, n_y, n_x = sizes
    n_dp = n_z * n_y
    n_f = n_x * 2
    heads = HEADS // n_f
    width = heads * HEAD
    local_rows = tokens.shape[1]
    frames_local = local_rows // ROW_FRAME
    rows = frames_local * PATCHES + EXTRA
    z, y, x, core = (lax.axis_index(name) for name in ("z", "y", "x", "core"))
    shard = x * 2 + core
    d_part = D // n_dp
    ff_part = FF // n_dp
    ff_half = ff_part // 2
    blocks = n_dp // n_f

    def swap(array, axis="core"):
        return lax.ppermute(array, axis, [(0, 1), (1, 0)])

    def take(array, index, axis=0):
        return lax.dynamic_index_in_dim(array, index, axis, False)

    def ordered(index, own, other, axis=0):
        low = jnp.where(index == 0, own, other)
        high = jnp.where(index == 0, other, own)
        return jnp.concatenate([low, high], axis)

    def both_cores(array, axis=0):
        return ordered(core, array, swap(array), axis)

    def exchange_f(array):
        return lax.all_to_all(array, ("x", "core"), 0, 0, tiled=True)

    def over_x(array):
        return lax.all_to_all(array, "x", 0, 0, tiled=True)

    vectors = [attend_gain, attend_shift, output_bias, second_gain, second_shift, reduce_bias, triple_bias, expand_bias]
    flat = jnp.concatenate(vectors)
    qkv_part = 3 * D // n_dp
    flat = jnp.pad(flat, (0, 16 * qkv_part - flat.shape[0])).reshape(16, qkv_part)
    packed = jnp.concatenate([triple_weight, flat], 0)
    packed = lax.all_gather(packed, ("z", "y"), axis=0)
    small = packed[:, D // n_f :].reshape(n_dp, -1)
    full = []
    at = 0
    for vector in vectors:
        full.append(small[:, at : at + vector.shape[0]].reshape(-1))
        at += vector.shape[0]
    gain_one, shift_one, output_add, gain_two, shift_two, reduce_add = (v.astype(F32)[None] for v in full[:6])
    triple_add, expand_add = full[6], full[7]
    triple_rows = packed[:, : D // n_f].transpose(1, 0, 2).reshape(D // n_f, 3, n_f, width)
    triple_own = exchange_f(triple_rows.transpose(2, 0, 1, 3)).reshape(D, 3 * width)
    bias_own = take(triple_add.reshape(3, n_f, width), shard, 1).reshape(1, 3 * width)

    expand_split = expand_weight.reshape(D // n_f, 2, ff_half)
    expand_chip = ordered(core, take(expand_split, core, 1), swap(take(expand_split, 1 - core, 1)))
    reduce_split = reduce_weight.reshape(blocks, 2, ff_half, d_part)
    reduce_chip = ordered(core, take(reduce_split, core, 1)[None], swap(take(reduce_split, 1 - core, 1))[None])
    expand_add_own = take(expand_add.reshape(n_z, n_y, 2, ff_half), core, 2)
    expand_all = lax.all_gather(expand_chip, ("z", "y", "x"), axis=0).reshape(n_z, n_y, D, ff_half)
    expand_pieces = [expand_all.transpose(0, 2, 1, 3).reshape(n_z, D, n_y * ff_half)]
    reduce_all = lax.all_gather(reduce_chip, ("z", "y", "x"), axis=0)
    reduce_pieces = [
        reduce_all.reshape(n_dp, n_dp, ff_half, d_part).transpose(1, 2, 0, 3).reshape(n_z, n_y * ff_half, D)
    ]
    expand_add_own = expand_add_own.reshape(n_z, 1, n_y * ff_half)
    output_all = lax.all_gather(output_weight, ("z", "y", "x"), axis=0)
    output_all = output_all.reshape(n_dp, n_x * width, d_part).transpose(1, 0, 2).reshape(n_x * width, D)

    live_all, cosine, sine, guides = tables(frame_counts[0], presence[0], n_f, frames_local, heads)
    live = take(live_all, shard)[:, None]
    entered = to_block(tokens[0], frames_local).astype(F32) * live
    outer = to_block(cotangent[0], frames_local).astype(F32) * live
    outer_low = outer.astype(BF)
    outer_chip = both_cores(outer_low)
    outer_chip_t = outer_chip.T
    unit_one, scale_one = norm_parts(entered)
    normed = (unit_one * gain_one + shift_one).astype(BF)
    normed_all = lax.all_gather(normed, ("x", "core"), axis=0)

    turned = jnp.asarray(turn_matrix(width), BF)
    q, k, v = qkv_call(normed_all, triple_own, bias_own, turned, cosine, sine)
    mixed, exact, logs, logs_extra = attend_call(*guides, q, k, v)

    mixed_chip = over_x(mixed.reshape(n_x, 2 * rows, width)).transpose(1, 0, 2).reshape(2 * rows, n_x * width)
    branch_part = nn(mixed_chip, output_all).reshape(2, rows, D)
    branch = take(branch_part, core) + swap(take(branch_part, 1 - core).astype(BF)).astype(F32)
    middle = entered + branch + output_add
    unit_two, scale_two = norm_parts(middle)
    second = (unit_two * gain_two + shift_two).astype(BF)
    second_chip = both_cores(second)
    final, second_grad, d_expand_bias, *d_feed = feed_call(
        second_chip, outer_chip, outer_chip_t, expand_pieces[0], expand_add_own, reduce_pieces[0]
    )
    second_grad = second_grad.reshape(2, rows, D)
    second_grad = take(second_grad, core) + swap(take(second_grad, 1 - core).astype(BF)).astype(F32)
    final = final.reshape(2, rows, D)
    final = take(final, core) + swap(take(final, 1 - core).astype(BF)).astype(F32)
    block_output = ((middle + final + reduce_add) * live).astype(BF)

    middle_grad = outer + norm_back(second_grad, unit_two, scale_two, gain_two)
    second_gain_grad = jnp.sum(second_grad * unit_two, 0)
    second_shift_grad = jnp.sum(second_grad, 0)
    branch_low = middle_grad.astype(BF)
    branch_chip = both_cores(branch_low)
    mixed_grad = nt(branch_chip, output_all).astype(BF)
    mixed_grad = over_x(mixed_grad.reshape(2 * rows, n_x, width).transpose(1, 0, 2)).reshape(n_f, rows, width)
    d_output = tn(mixed_chip, branch_chip).astype(BF)
    triple_grad = attend_back_call(
        jnp.zeros((1,), jnp.int32), *guides, q, k, v, list(mixed_grad.reshape(n_x, 2, rows, width)), exact, logs, logs_extra, cosine, sine, turned)
    natural = triple_grad.reshape(n_f * rows, 3 * width)
    d_triple = tn(normed_all.reshape(n_f * rows, D), natural).astype(BF)
    d_triple_bias = jnp.sum(natural.astype(F32), 0)
    normed_grad = nt(natural, triple_own).astype(BF)
    normed_grad = lax.psum_scatter(normed_grad, ("x", "core"), scatter_dimension=0, tiled=True).astype(F32)
    attend_gain_grad = jnp.sum(normed_grad * unit_one, 0)
    attend_shift_grad = jnp.sum(normed_grad, 0)
    tokens_grad = (middle_grad + norm_back(normed_grad, unit_one, scale_one, gain_one)) * live

    d_triple = exchange_f(d_triple.reshape(n_f, D // n_f, 3, width))
    d_triple = d_triple.transpose(1, 2, 0, 3).reshape(D // n_f, n_z, n_y, qkv_part)
    d_triple = d_triple.reshape(D // n_f, 3 * D)
    triple_weight_grad = lax.psum_scatter(d_triple, ("z", "y"), scatter_dimension=1, tiled=True).astype(F32)
    d_output = d_output.reshape(n_x, width, n_dp, d_part).transpose(2, 0, 1, 3).reshape(n_dp * n_x * width, d_part)
    output_weight_grad = lax.psum_scatter(d_output, ("z", "y", "x"), scatter_dimension=0, tiled=True).astype(F32)
    d_expand, d_reduce = d_feed
    d_expand = d_expand.reshape(n_z, D, n_y, ff_half).transpose(0, 2, 1, 3).reshape(n_dp * D, ff_half)
    d_expand = lax.psum_scatter(d_expand, ("z", "y", "x"), scatter_dimension=0, tiled=True)
    d_expand = d_expand.reshape(2, D // n_f, ff_half)
    d_reduce = d_reduce.reshape(n_z, n_dp, d_part, n_y, ff_half).transpose(1, 0, 3, 2, 4).reshape(-1, ff_half)
    d_reduce = lax.psum_scatter(d_reduce, ("z", "y", "x"), scatter_dimension=0, tiled=True)
    d_reduce = d_reduce.reshape(2, blocks, d_part, ff_half)
    expand_weight_grad = ordered(core, take(d_expand, core), swap(take(d_expand, 1 - core)), 1).astype(F32)
    reduce_weight_grad = jnp.stack(
        [
            jnp.where(core == 0, take(d_reduce, core), swap(take(d_reduce, 1 - core))),
            jnp.where(core == 0, swap(take(d_reduce, 1 - core)), take(d_reduce, core)),
        ],
        1,
    )
    reduce_weight_grad = reduce_weight_grad.transpose(0, 1, 3, 2).reshape(blocks * 2 * ff_half, d_part).astype(F32)

    zero_qkv = jnp.zeros((3, n_f, width), F32)
    triple_bias_part = lax.dynamic_update_slice(zero_qkv, d_triple_bias.reshape(3, 1, width), (0, shard, 0))
    d_expand_bias = d_expand_bias.reshape(n_z, n_y, ff_half)
    zero_ff = jnp.zeros((n_dp, 2, ff_half), F32)
    expand_bias_part = lax.dynamic_update_slice(zero_ff, d_expand_bias.reshape(n_dp, 1, ff_half), (0, core, 0))
    sums = [
        attend_gain_grad,
        attend_shift_grad,
        jnp.sum(branch_low.astype(F32), 0),
        second_gain_grad,
        second_shift_grad,
        jnp.sum(outer_low.astype(F32), 0),
        triple_bias_part.reshape(-1),
        expand_bias_part.reshape(-1),
    ]
    sums = jnp.concatenate([s.reshape(n_dp, -1) for s in sums], 1)
    total = n_dp * n_f
    bit = 1
    while bit < total:
        sums = sums + lax.ppermute(sums, ("z", "y", "x", "core"), [(i, i ^ bit) for i in range(total)])
        bit *= 2
    own = take(sums, z * n_y + y)
    parts = []
    at = 0
    for size in [d_part] * 6 + [qkv_part, ff_part]:
        parts.append(own[at : at + size])
        at += size
    return (
        from_block(block_output, frames_local),
        from_block(tokens_grad, frames_local),
        parts[0],
        parts[1],
        triple_weight_grad,
        parts[6],
        output_weight_grad,
        parts[2],
        parts[3],
        parts[4],
        expand_weight_grad,
        parts[7],
        reduce_weight_grad,
        parts[5],
    )


def solution(mesh):
    n_dp, n_f = mesh.shape["dp"], mesh.shape["fsdp"]
    sizes = (n_dp // 2, 2, n_f // 2)
    inner = jax.sharding.Mesh(mesh.devices.reshape(*sizes, 2), ("z", "y", "x", "core"))
    dp = ("z", "y")
    fsdp = ("x", "core")
    rows = P(dp, fsdp, None)
    weight = P(fsdp, dp)
    vector = P(dp)
    return jax.shard_map(
        functools.partial(torus_shards if sizes == (4, 2, 2) else general_shards, sizes),
        mesh=inner,
        in_specs=(
            rows,
            rows,
            P(dp, None),
            P(dp, None, None),
            vector,
            vector,
            weight,
            vector,
            weight,
            vector,
            vector,
            vector,
            weight,
            vector,
            weight,
            vector,
        ),
        out_specs=(
            rows,
            rows,
            vector,
            vector,
            weight,
            vector,
            weight,
            vector,
            vector,
            vector,
            weight,
            vector,
            weight,
            vector,
        ),
        check_vma=False,
    )
```

```python
import functools
import math

import jax
import jax.numpy as jnp
import numpy as np
from jax import lax
from jax.experimental import pallas as pl
from jax.experimental.pallas import tpu as pltpu
from jax.sharding import PartitionSpec as P

D = 1024
HEADS = 16
HEAD = 64
FF = 4096
GRID = 16
PATCHES = GRID * GRID
ROW_FRAME = PATCHES + 2
PAIRS = HEAD // 3 // 2
EXTRA = 16

EPSILON = 1e-06
SCALE2 = 0.125 * math.log2(math.e)
MASKED = -8e9
FAR = 1 << 20
VMEM = 60 * 1024 * 1024
BF = jnp.bfloat16
F32 = jnp.float32


def nn(left, right):
    return lax.dot_general(left, right, (((1,), (0,)), ((), ())), preferred_element_type=F32)


def nt(left, right):
    return lax.dot_general(left, right, (((1,), (1,)), ((), ())), preferred_element_type=F32)


def tn(left, right):
    return lax.dot_general(left, right, (((0,), (0,)), ((), ())), preferred_element_type=F32)


def qkv_kernel(normed, weight, bias, turn, cosine, sine, q_out, k_out, v_out, turned, turned_bias):
    width = q_out.shape[-1]
    half = width // 2

    @pl.when(pl.program_id(0) == 0)
    def _():
        for part in range(2):
            span = slice(part * width, (part + 1) * width)
            turned[:, span] = nn(weight[:, span], turn[...]).astype(BF)
            turned_bias[:, span] = nn(bias[:, span], turn[...])

    rows = normed[0]
    cos = cosine[0]
    sin = sine[0]
    for part, out in ((0, q_out), (1, k_out)):
        span = slice(part * width, (part + 1) * width)
        value = nn(rows, turned[:, span]) + turned_bias[:1, span]
        first = value[:, :half]
        second = value[:, half:]
        out[0, :, :half] = (first * cos - second * sin).astype(BF)
        out[0, :, half:] = (second * cos + first * sin).astype(BF)
    span = slice(2 * width, 3 * width)
    v_out[0] = (nn(rows, weight[:, span]) + bias[:1, span].astype(F32)).astype(BF)


def qkv_call(normed, weight, bias, turn, cosine, sine):
    sources, rows, _ = normed.shape
    width = weight.shape[1] // 3
    half = width // 2
    block = pl.BlockSpec((1, rows, width), lambda s: (s, 0, 0))
    table = pl.BlockSpec((1, rows, half), lambda s: (s, 0, 0))

    def whole(shape):
        return pl.BlockSpec(shape, lambda s: (0,) * len(shape))

    shape = jax.ShapeDtypeStruct((sources, rows, width), BF)
    return pl.pallas_call(
        qkv_kernel,
        grid=(sources,),
        in_specs=[
            pl.BlockSpec((1, rows, D), lambda s: (s, 0, 0)),
            whole(weight.shape),
            whole(bias.shape),
            whole(turn.shape),
            table,
            table,
        ],
        out_specs=[block] * 3,
        out_shape=[shape] * 3,
        scratch_shapes=[pltpu.VMEM((D, 2 * width), BF), pltpu.VMEM((bias.shape[0], 2 * width), F32)],
        compiler_params=pltpu.CompilerParams(vmem_limit_bytes=VMEM),
        cost_estimate=pl.CostEstimate(
            flops=2 * sources * rows * D * 3 * width, bytes_accessed=4 * sources * rows * D, transcendentals=0
        ),
        name="qkv_rotary",
    )(normed, weight, bias, turn, cosine, sine)


def turned_lanes(width, head):
    lane = lax.broadcasted_iota(jnp.int32, (1, width), 1)
    return (lane % (width // 2)) // (HEAD // 2) == head


def plain_lanes(width, head):
    lane = lax.broadcasted_iota(jnp.int32, (1, width), 1)
    return lane // HEAD == head


def pick(mask, array):
    return jnp.where(mask, array, jnp.zeros((), array.dtype))


def stack_heads(array, lanes):
    width = array.shape[-1]
    return jnp.concatenate([pick(lanes(width, head), array) for head in range(width // HEAD)], 0)


def unstack_heads(array, lanes):
    width = array.shape[-1]
    heads = width // HEAD
    step = array.shape[0] // heads
    total = pick(lanes(width, 0), array[:step])
    for head in range(1, heads):
        total = total + pick(lanes(width, head), array[head * step : (head + 1) * step])
    return total


def head_rows(array, head):
    half = array.shape[0] // 2
    step = HEAD // 2
    return jnp.concatenate(
        [array[head * step : (head + 1) * step], array[half + head * step : half + (head + 1) * step]], 0
    )


def value_total(v, frames_local, sources):
    total = jnp.zeros((1, v.shape[-1]), F32)
    real = lax.broadcasted_iota(jnp.int32, (EXTRA, 1), 0) < 2 * frames_local
    for s in range(sources):
        for l in range(frames_local):
            total = total + jnp.sum(v[s, l * PATCHES : (l + 1) * PATCHES].astype(F32), 0, keepdims=True)
        total = total + jnp.sum(pick(real, v[s, frames_local * PATCHES :].astype(F32)), 0, keepdims=True)
    return total


def attend_kernel(
    frames_local,
    start,
    key_frame,
    query_start,
    query_frame,
    query_pad,
    q,
    k,
    v,
    mixed,
    exact,
    logs,
    logs_extra,
    v_t,
    queries,
    acc,
    state,
):
    sources, _, width = q.shape
    heads = width // HEAD
    frames = sources * frames_local
    patch_rows = frames_local * PATCHES
    length = frames * ROW_FRAME

    def frame_ref(ref, g):
        return ref[g // frames_local, pl.ds(pl.multiple_of((g % frames_local) * PATCHES, PATCHES), PATCHES), :]

    for g in range(frames):
        s, l = g // frames_local, g % frames_local
        v_t[g] = v[s, l * PATCHES : (l + 1) * PATCHES].T
    k_extra = jnp.concatenate([k[s, patch_rows:] for s in range(sources)], 0)
    v_extra_t = jnp.concatenate([v[s, patch_rows:] for s in range(sources)], 0).T
    uniform = jnp.asarray(1.0 / length, BF).astype(F32) * value_total(v, frames_local, sources)
    key_at = key_frame[:, :1]

    def weigh(scores, top):
        return jnp.exp2((scores - top) * SCALE2)

    def mix(values_t, weights, head):
        return nn(values_t[head * HEAD : (head + 1) * HEAD], weights[:, head * PATCHES : (head + 1) * PATCHES])

    def one_frame(g, _):
        first = start[g]
        queries[...] = stack_heads(frame_ref(q, g), turned_lanes)
        allowed = (key_at >= first) & (key_at <= g)
        scores_extra = jnp.where(allowed, nt(k_extra, queries[...]), MASKED)
        scores = nt(frame_ref(k, g), queries[...])
        top = jnp.maximum(jnp.max(scores_extra, 0, keepdims=True), jnp.max(scores, 0, keepdims=True))
        weights_extra = weigh(scores_extra, top)
        weights = weigh(scores, top)
        state[0:1] = top
        state[1:2] = jnp.sum(weights_extra, 0, keepdims=True) + jnp.sum(weights, 0, keepdims=True)
        weights_extra = weights_extra.astype(BF)
        weights = weights.astype(BF)
        values_t = v_t[g]
        for head in range(heads):
            acc[head] = mix(v_extra_t, weights_extra, head) + mix(values_t, weights, head)

        def some_keys(which):
            scores = [nt(frame_ref(k, f), queries[...]) for f in which]
            before = state[0:1]
            top = before
            for s in scores:
                top = jnp.maximum(top, jnp.max(s, 0, keepdims=True))
            fade = weigh(before, top)
            weights = [weigh(s, top) for s in scores]
            state[0:1] = top
            total = state[1:2] * fade
            for w in weights:
                total = total + jnp.sum(w, 0, keepdims=True)
            state[1:2] = total
            weights = [w.astype(BF) for w in weights]
            for head in range(heads):
                out = acc[head] * fade[:, head * PATCHES : (head + 1) * PATCHES]
                for f, w in zip(which, weights):
                    out = out + mix(v_t[f], w, head)
                acc[head] = out

        def pair(i, _):
            some_keys([first + 2 * i, first + 2 * i + 1])
            return 0

        count = jnp.maximum(g - first, 0)
        lax.fori_loop(0, count // 2, pair, 0)

        @pl.when(count % 2 == 1)
        def _():
            some_keys([g - 1])

        total = state[1:2]
        result = jnp.concatenate(
            [acc[head] / total[:, head * PATCHES : (head + 1) * PATCHES] for head in range(heads)], 0
        ).T
        result = jnp.where(first > frames, jnp.broadcast_to(uniform, result.shape), result)
        rows = pl.ds(pl.multiple_of((g % frames_local) * PATCHES, PATCHES), PATCHES)
        exact[g // frames_local, rows, :] = result
        mixed[g // frames_local, rows, :] = result.astype(BF)
        logs[g] = jnp.broadcast_to(state[0:1] + jnp.log2(total) * (1.0 / SCALE2), (8, heads * PATCHES))
        return 0

    lax.fori_loop(0, frames, one_frame, 0)

    q_extra = stack_heads(jnp.concatenate([q[s, patch_rows:] for s in range(sources)], 0), turned_lanes)
    first = jnp.concatenate([query_start[:1]] * heads, 1)
    last = jnp.concatenate([query_frame[:1]] * heads, 1)
    every = [jnp.where((key_at >= first) & (key_at <= last), nt(k_extra, q_extra), MASKED)]
    for f in range(frames):
        every.append(jnp.where((first <= f) & (last >= f), nt(frame_ref(k, f), q_extra), MASKED))
    top = jnp.max(every[0], 0, keepdims=True)
    for scores in every[1:]:
        top = jnp.maximum(top, jnp.max(scores, 0, keepdims=True))
    total = jnp.zeros_like(top)
    result = jnp.zeros((width, q_extra.shape[0]), F32)
    for scores, values_t in zip(every, [v_extra_t] + [v_t[f] for f in range(frames)]):
        weights = weigh(scores, top)
        total = total + jnp.sum(weights, 0, keepdims=True)
        result = result + nn(values_t, weights.astype(BF))
    result = unstack_heads((result / total).T, plain_lanes)
    result = jnp.where(query_pad[:, :1] > 0, jnp.broadcast_to(uniform, result.shape), result)
    for s in range(sources):
        exact[s, patch_rows:, :] = result[s * EXTRA : (s + 1) * EXTRA]
        mixed[s, patch_rows:, :] = result[s * EXTRA : (s + 1) * EXTRA].astype(BF)
    logs_extra[...] = jnp.broadcast_to(top + jnp.log2(total) * (1.0 / SCALE2), logs_extra.shape)


def attend_call(start, key_frame, query_start, query_frame, query_pad, q, k, v, waits=()):
    sources, rows, width = q.shape
    frames_local = rows // PATCHES
    frames = sources * frames_local
    heads = width // HEAD
    stacked = heads * sources * EXTRA
    vmem = pl.BlockSpec(memory_space=pltpu.VMEM)
    return pl.pallas_call(
        waiting(functools.partial(attend_kernel, frames_local), 8, waits),
        in_specs=[pl.BlockSpec(memory_space=pltpu.SMEM)] + [vmem] * 7 + [ANY_REF] * len(waits),
        out_specs=[vmem] * 4,
        out_shape=[
            jax.ShapeDtypeStruct(q.shape, BF),
            jax.ShapeDtypeStruct(q.shape, F32),
            jax.ShapeDtypeStruct((frames, 8, heads * PATCHES), F32),
            jax.ShapeDtypeStruct((8, stacked), F32),
        ],
        scratch_shapes=[
            pltpu.VMEM((frames, width, PATCHES), BF),
            pltpu.VMEM((heads * PATCHES, width), BF),
            pltpu.VMEM((heads, HEAD, PATCHES), F32),
            pltpu.VMEM((8, heads * PATCHES), F32),
        ],
        compiler_params=pltpu.CompilerParams(vmem_limit_bytes=VMEM),
        cost_estimate=cost(
            flops=8 * heads * 256 * frames * frames * PATCHES * PATCHES // 2,
            bytes_accessed=10 * sources * rows * width,
            transcendentals=heads * frames * frames * PATCHES * PATCHES // 2,
        ),
        name="attend",
    )(start, key_frame, query_start, query_frame, query_pad, q, k, v, *waits)


def attend_back_kernel(
    frames_local,
    chips,
    flip,
    start,
    key_frame,
    query_start,
    query_frame,
    query_pad,
    q,
    k,
    v,
    *rest,
):
    pieces = rest[:chips]
    (
        exact,
        logs,
        logs_extra,
        cosine,
        sine,
        turn,
        out,
        grad,
        k_t,
        queries,
        grads,
        dq_t,
        dk,
        dv,
        dq_extra,
        dk_extra,
        dv_extra,
        centers,
    ) = rest[chips:]
    sources, _, width = q.shape
    for i in range(chips):
        for core in range(2):
            grad[2 * (i ^ flip[0]) + core] = pieces[i][core]
    half = width // 2
    heads = width // HEAD
    frames = sources * frames_local
    patch_rows = frames_local * PATCHES
    length = frames * ROW_FRAME
    step_rows = HEAD // 2

    def frame_ref(ref, g):
        return ref[g // frames_local, pl.ds(pl.multiple_of((g % frames_local) * PATCHES, PATCHES), PATCHES), :]

    which = lax.broadcasted_iota(jnp.int32, (8, width), 0)
    lane = lax.broadcasted_iota(jnp.int32, (8, width), 1)
    groups = (lane // HEAD == which).astype(BF)

    def center_of(grad_rows, exact_rows):
        product = grad_rows.astype(F32) * exact_rows
        high = product.astype(BF)
        low = (product - high.astype(F32)).astype(BF)
        center = nt(groups, high) + nt(groups, low)
        return jnp.concatenate([center[head : head + 1] for head in range(heads)], 1)

    def gather_extra(ref):
        return jnp.concatenate([ref[s, patch_rows:] for s in range(sources)], 0)

    for g in range(frames):
        s, l = g // frames_local, g % frames_local
        k_t[g] = k[s, l * PATCHES : (l + 1) * PATCHES].T
    k_extra = gather_extra(k)
    v_extra = gather_extra(v)
    k_extra_t = k_extra.T
    dk_extra[...] = jnp.zeros_like(dk_extra)
    dv_extra[...] = jnp.zeros_like(dv_extra)
    key_at = key_frame[:, :1]

    def tile(keys, values, query, query_grad, log, center, allowed):
        scores = nt(keys, query)
        inner = nt(values, query_grad)
        probs = jnp.exp2((scores - log) * SCALE2)
        if allowed is not None:
            probs = jnp.where(allowed, probs, 0.0)
        change = (probs * (inner - center)).astype(BF)
        return nn(probs.astype(BF), query_grad), nn(change, query), change

    def add_dq(ref, keys_t, change, keep):
        for head in range(heads):
            part = nn(head_rows(keys_t, head), change[:, head * PATCHES : (head + 1) * PATCHES])
            for side in range(2):
                rows = slice(side * half + head * step_rows, side * half + (head + 1) * step_rows)
                piece = part[side * step_rows : (side + 1) * step_rows]
                ref[rows] = ref[rows] + piece if keep else piece

    def one_frame(g, pad_grad):
        first = start[g]
        grad_rows = frame_ref(grad, g)
        queries[...] = stack_heads(frame_ref(q, g), turned_lanes)
        grads[...] = stack_heads(grad_rows, plain_lanes)
        centers[...] = jnp.broadcast_to(center_of(grad_rows, frame_ref(exact, g)), centers.shape)
        allowed = (key_at >= first) & (key_at <= g)
        query, query_grad, log, center = queries[...], grads[...], logs[g, :1], centers[:1]
        dv_part, dk_part, change = tile(k_extra, v_extra, query, query_grad, log, center, allowed)
        dv_extra[...] += dv_part
        dk_extra[...] += dk_part
        add_dq(dq_t.at[g], k_extra_t, change, False)
        dv_part, dk_part, change = tile(
            frame_ref(k, g), frame_ref(v, g), query, query_grad, log, center, jnp.broadcast_to(first <= g, log.shape)
        )
        dv[g] = dv_part
        dk[g] = dk_part
        add_dq(dq_t.at[g], k_t[g], change, True)

        def some_keys(which):
            parts = [
                tile(frame_ref(k, f), frame_ref(v, f), queries[...], grads[...], logs[g, :1], centers[:1], None)
                for f in which
            ]
            for f, (dv_part, dk_part, _) in zip(which, parts):
                dv[f] += dv_part
                dk[f] += dk_part
            for f, (_, _, change) in zip(which, parts):
                add_dq(dq_t.at[g], k_t[f], change, True)

        def pair(i, _):
            some_keys([first + 2 * i, first + 2 * i + 1])
            return 0

        count = jnp.maximum(g - first, 0)
        lax.fori_loop(0, count // 2, pair, 0)

        @pl.when(count % 2 == 1)
        def _():
            some_keys([g - 1])

        return pad_grad + jnp.where(first > frames, jnp.sum(grad_rows.astype(F32), 0, keepdims=True), 0.0)

    pad_grad = lax.fori_loop(0, frames, one_frame, jnp.zeros((1, width), F32))
    g_extra = gather_extra(grad)
    pad_grad = pad_grad + jnp.sum(jnp.where(query_pad[:, :1] > 0, g_extra.astype(F32), 0.0), 0, keepdims=True)
    pad_grad = pad_grad * jnp.asarray(1.0 / length, BF).astype(F32)

    q_stack = stack_heads(gather_extra(q), turned_lanes)
    g_stack = stack_heads(g_extra, plain_lanes)
    stacked = q_stack.shape[0]
    queries[:stacked] = q_stack
    grads[:stacked] = g_stack
    first = jnp.concatenate([query_start[:1]] * heads, 1)
    last = jnp.concatenate([query_frame[:1]] * heads, 1)
    log = logs_extra[:1]
    center = center_of(g_extra, gather_extra(exact))
    allowed = (key_at >= first) & (key_at <= last)
    dv_part, dk_part, change = tile(k_extra, v_extra, q_stack, g_stack, log, center, allowed)
    dv_extra[...] += dv_part
    dk_extra[...] += dk_part
    dq_extra[...] = nn(k_extra_t, change)

    def extra_keys(i, _):
        which = [2 * i, 2 * i + 1]
        parts = [
            tile(
                frame_ref(k, f), frame_ref(v, f), queries[:stacked], grads[:stacked], log, center, (first <= f) & (last >= f)
            )
            for f in which
        ]
        total = dq_extra[...]
        for f, (dv_part, dk_part, change) in zip(which, parts):
            dv[f] += dv_part
            dk[f] += dk_part
            total = total + nn(k_t[f], change)
        dq_extra[...] = total
        return 0

    lax.fori_loop(0, frames // 2, extra_keys, 0)

    def emit(s, rows, dq_rows, dk_rows, dv_rows, real=None):
        cos = cosine[s, rows]
        sin = sine[s, rows]
        for part, array in ((0, dq_rows), (1, dk_rows)):
            a = array[:, :half] * 0.125
            b = array[:, half:] * 0.125
            both = jnp.concatenate([(a * cos + b * sin).astype(BF), (b * cos - a * sin).astype(BF)], 1)
            both = nt(both, turn[...])
            if real is not None:
                both = pick(real, both)
            out[s, rows, part * width : (part + 1) * width] = both.astype(BF)
        total = dv_rows + pad_grad
        if real is not None:
            total = pick(real, total)
        out[s, rows, 2 * width :] = total.astype(BF)

    def emit_frame(g, _):
        rows = pl.ds(pl.multiple_of((g % frames_local) * PATCHES, PATCHES), PATCHES)
        emit(g // frames_local, rows, dq_t[g].T, dk[g], dv[g])
        return 0

    lax.fori_loop(0, frames, emit_frame, 0)
    dq_rows = unstack_heads(dq_extra[...].T, turned_lanes)
    real = lax.broadcasted_iota(jnp.int32, (EXTRA, 1), 0) < 2 * frames_local
    for s in range(sources):
        at = slice(s * EXTRA, (s + 1) * EXTRA)
        emit(s, slice(patch_rows, patch_rows + EXTRA), dq_rows[at], dk_extra[at], dv_extra[at], real)


def attend_back_call(
    flip, start, key_frame, query_start, query_frame, query_pad, q, k, v, grad, exact, logs, logs_extra, cosine, sine, turn, waits=()
):
    chips = len(grad)
    sources, rows, width = q.shape
    frames_local = rows // PATCHES
    frames = sources * frames_local
    extra = sources * EXTRA
    heads = width // HEAD
    vmem = pl.BlockSpec(memory_space=pltpu.VMEM)
    return pl.pallas_call(
        waiting(functools.partial(attend_back_kernel, frames_local, chips), 15 + chips, waits),
        in_specs=[pl.BlockSpec(memory_space=pltpu.SMEM)] * 2 + [vmem] * (13 + chips) + [ANY_REF] * len(waits),
        out_specs=vmem,
        out_shape=jax.ShapeDtypeStruct((sources, rows, 3 * width), BF),
        scratch_shapes=[
            pltpu.VMEM((sources, rows, width), BF),
            pltpu.VMEM((frames, width, PATCHES), BF),
            pltpu.VMEM((heads * PATCHES, width), BF),
            pltpu.VMEM((heads * PATCHES, width), BF),
            pltpu.VMEM((frames, width, PATCHES), F32),
            pltpu.VMEM((frames, PATCHES, width), F32),
            pltpu.VMEM((frames, PATCHES, width), F32),
            pltpu.VMEM((width, heads * extra), F32),
            pltpu.VMEM((extra, width), F32),
            pltpu.VMEM((extra, width), F32),
            pltpu.VMEM((8, heads * PATCHES), F32),
        ],
        compiler_params=pltpu.CompilerParams(vmem_limit_bytes=VMEM),
        cost_estimate=cost(
            flops=20 * heads * 256 * frames * frames * PATCHES * PATCHES // 2,
            bytes_accessed=20 * sources * rows * width,
            transcendentals=heads * frames * frames * PATCHES * PATCHES // 2,
        ),
        name="attend_back",
    )(
        flip, start, key_frame, query_start, query_frame, query_pad, q, k, v, *grad, exact, logs, logs_extra, cosine, sine, turn, *waits
    )


def gelu_parts(hidden):
    base = 1.0 + (0.3275911 * math.sqrt(0.5)) * jnp.abs(hidden)
    guess = pl.reciprocal(base, approx=True)
    t = guess * (2.0 - base * guess)
    bell = jnp.exp2(hidden * hidden * (-0.5 * math.log2(math.e)))
    poly = 0.5 * 1.061405429
    for coefficient in (-1.453152027, 1.421413741, -0.284496736, 0.254829592):
        poly = poly * t + 0.5 * coefficient
    tail = poly * t * bell
    cdf = jnp.where(hidden < 0.0, tail, 1.0 - tail)
    return hidden * cdf, cdf + hidden * bell * (1.0 / math.sqrt(2.0 * math.pi))


def feed_body(chunk, second, outer, outer_t, weight_in, weight_out, add, final, second_grad, d_bias, second_t, active, slope):
    rows = second.shape[0]

    @pl.when(pl.program_id(0) == 0)
    def _():
        for r in range(0, rows, chunk):
            second_t[:, r : r + chunk] = second[r : r + chunk].T
        final[...] = jnp.zeros_like(final)
        second_grad[...] = jnp.zeros_like(second_grad)

    d_bias[...] = jnp.zeros_like(d_bias)
    for r in range(0, rows, chunk):
        at = slice(r, r + chunk)
        act, gradient = gelu_parts(nn(second[at], weight_in[...]) + add)
        act = act.astype(BF)
        grad = (nt(outer[at], weight_out[...]) * gradient).astype(BF)
        active[at] = act
        slope[at] = grad
        d_bias[0] += jnp.sum(grad.astype(F32), 0, keepdims=True)
        final[at] += nn(act, weight_out[...])
        second_grad[at] += nt(grad, weight_in[...])
    return nn(second_t[...], slope[...]).astype(BF), nn(outer_t[...], active[...]).astype(BF)


def feed_plain_kernel(
    chunk, second, outer, outer_t, expand, expand_bias, reduce, final, second_grad, d_bias, d_expand, d_reduce, second_t, active, slope
):
    d_expand[0], d_reduce[0] = feed_body(
        chunk, second, outer, outer_t, expand.at[0], reduce.at[0], expand_bias[0].astype(F32),
        final, second_grad, d_bias, second_t, active, slope,
    )


def feed_call(second, outer, outer_t, expand, expand_bias, reduce):
    rows = second.shape[0]
    tiles, _, wide = expand.shape
    chunk = rows // 2

    def whole(shape):
        return pl.BlockSpec(shape, lambda t: (0,) * len(shape))

    def tiled(shape):
        return pl.BlockSpec((1,) + shape[1:], lambda t: (t, 0, 0))

    return pl.pallas_call(
        functools.partial(feed_plain_kernel, chunk),
        grid=(tiles,),
        in_specs=[
            whole((rows, D)),
            whole((rows, D)),
            whole((D, rows)),
            tiled(expand.shape),
            tiled(expand_bias.shape),
            tiled(reduce.shape),
        ],
        out_specs=[whole((rows, D)), whole((rows, D)), tiled((tiles, 1, wide))] + [tiled((tiles, D, wide))] * 2,
        out_shape=[
            jax.ShapeDtypeStruct((rows, D), F32),
            jax.ShapeDtypeStruct((rows, D), F32),
            jax.ShapeDtypeStruct((tiles, 1, wide), F32),
        ]
        + [jax.ShapeDtypeStruct((tiles, D, wide), BF)] * 2,
        scratch_shapes=[pltpu.VMEM((D, rows), BF), pltpu.VMEM((rows, wide), BF), pltpu.VMEM((rows, wide), BF)],
        compiler_params=pltpu.CompilerParams(vmem_limit_bytes=VMEM),
        cost_estimate=pl.CostEstimate(
            flops=10 * rows * D * wide * tiles,
            bytes_accessed=8 * D * wide * tiles + 14 * rows * D,
            transcendentals=2 * rows * wide * tiles,
        ),
        name="feed_forward",
    )(second, outer, outer_t, expand, expand_bias, reduce)


def norm_parts(values):
    center = values - jnp.mean(values, -1, keepdims=True)
    scale = lax.rsqrt(jnp.mean(center * center, -1, keepdims=True) + EPSILON)
    return center * scale, scale


def norm_back(grad, unit, scale, gain):
    scaled = grad * gain
    mean_one = jnp.mean(scaled, -1, keepdims=True)
    mean_two = jnp.mean(scaled * unit, -1, keepdims=True)
    return scale * (scaled - mean_one - unit * mean_two)


def to_block(array, frames_local):
    split = array.reshape(frames_local, ROW_FRAME, D)
    return jnp.concatenate(
        [
            split[:, 2:].reshape(frames_local * PATCHES, D),
            split[:, :2].reshape(frames_local * 2, D),
            jnp.zeros((EXTRA - 2 * frames_local, D), array.dtype),
        ],
        0,
    )


def from_block(array, frames_local):
    patches = array[: frames_local * PATCHES].reshape(frames_local, PATCHES, D)
    extra = array[frames_local * PATCHES : frames_local * ROW_FRAME].reshape(frames_local, 2, D)
    return jnp.concatenate([extra, patches], 1).reshape(1, frames_local * ROW_FRAME, D)


def rows_of(per_frame, per_extra, sources, frames_local, fill):
    patches = jnp.broadcast_to(per_frame.reshape(sources, frames_local, 1), (sources, frames_local, PATCHES))
    pad = jnp.full((sources, EXTRA - 2 * frames_local), fill, per_frame.dtype)
    return jnp.concatenate(
        [patches.reshape(sources, -1), per_extra.reshape(sources, 2 * frames_local), pad], 1
    )


def tables(counts, present, sources, frames_local, heads):
    frames = sources * frames_local
    at = jnp.arange(frames, dtype=jnp.int32)
    first, second = counts[0], counts[1]
    inside = at < first + second
    start = jnp.where(at < first, 0, first).astype(jnp.int32)
    time = (at - start).astype(F32)
    begin = jnp.where(inside, start, FAR)
    live_extra = inside[:, None] & (present == 1)
    time_rows = rows_of(time, jnp.repeat(time, 2), sources, frames_local, 0.0)
    live_rows = rows_of(inside.astype(F32), live_extra.astype(F32), sources, frames_local, 0.0)

    patch = np.arange(PATCHES)
    grid_row = np.zeros(frames_local * PATCHES + EXTRA, np.float32)
    grid_col = np.zeros(frames_local * PATCHES + EXTRA, np.float32)
    for l in range(frames_local):
        grid_row[l * PATCHES : (l + 1) * PATCHES] = patch // GRID
        grid_col[l * PATCHES : (l + 1) * PATCHES] = patch % GRID
    lanes = np.zeros((3, HEAD // 2), np.float32)
    freq = 10000.0 ** (-np.arange(PAIRS, dtype=np.float32) / PAIRS)
    for a in range(3):
        lanes[a, a * PAIRS : (a + 1) * PAIRS] = freq
    lanes = np.tile(lanes, (1, heads))
    angle = time_rows[:, :, None] * lanes[0] + (grid_row[:, None] * lanes[1] + grid_col[:, None] * lanes[2])[None]

    def extra_of(per_frame, fill):
        both = jnp.repeat(per_frame, 2).reshape(sources, 2 * frames_local)
        pad = jnp.full((sources, EXTRA - 2 * frames_local), fill, both.dtype)
        return jnp.concatenate([both, pad], 1).reshape(-1)

    extra = sources * EXTRA
    key_frame = jnp.where(live_extra, at[:, None], -1).reshape(sources, 2 * frames_local)
    key_frame = jnp.concatenate(
        [key_frame, jnp.full((sources, EXTRA - 2 * frames_local), -1, jnp.int32)], 1
    ).reshape(-1)
    query_start = extra_of(begin, FAR)
    query_frame = extra_of(at, -1)

    def column(vector):
        return jnp.broadcast_to(vector[:, None], (extra, 128))

    def row(vector):
        return jnp.broadcast_to(vector[None], (8, extra))

    return (
        live_rows,
        jnp.cos(angle),
        jnp.sin(angle),
        (begin, column(key_frame), row(query_start), row(query_frame), column((query_start == FAR).astype(jnp.int32))),
    )


def turn_matrix(width):
    turn = np.zeros((width, width), np.float32)
    step = HEAD // 2
    for h in range(width // HEAD):
        for d in range(HEAD):
            if d < 6 * PAIRS:
                a, rest = divmod(d, 2 * PAIRS)
                side, k = divmod(rest, PAIRS)
                to = side * (width // 2) + h * step + a * PAIRS + k
            else:
                side, k = divmod(d - 6 * PAIRS, step - 3 * PAIRS)
                to = side * (width // 2) + h * step + 3 * PAIRS + k
            turn[h * HEAD + d, to] = 1.0
    return turn


SMEM_REF = pl.BlockSpec(memory_space=pltpu.SMEM)
VMEM_REF = pl.BlockSpec(memory_space=pltpu.VMEM)


ANY_REF = pl.BlockSpec(memory_space=pl.ANY)


def cost(flops=0, bytes_accessed=0, transcendentals=0):
    return pl.CostEstimate(flops=flops, bytes_accessed=bytes_accessed, transcendentals=transcendentals)


def waiting(kernel, inputs, waits, carried=0, outputs=None):
    if not waits:
        return kernel

    def run(*refs):
        used = [*refs[:inputs], *refs[inputs + len(waits) :]]
        if carried:
            del used[inputs + outputs : inputs + outputs + carried]
        kernel(*used)

    return run


def local_call(kernel, name, inputs, outputs, scratch=(), smem=0, flops=0, transcendentals=0, waits=(), carry=()):
    first = len(inputs) + len(waits)
    waits = [*waits, *carry]
    size = sum(math.prod(a.shape) * a.dtype.itemsize for a in [*inputs, *outputs])
    return pl.pallas_call(
        waiting(kernel, len(inputs), waits, len(carry), len(outputs)),
        in_specs=[SMEM_REF] * smem + [VMEM_REF] * (len(inputs) - smem) + [ANY_REF] * len(waits),
        out_specs=[VMEM_REF] * len(outputs) + [ANY_REF] * len(carry),
        out_shape=[*outputs] + [shape_of(*c.shape, dtype=c.dtype) for c in carry],
        input_output_aliases={first + i: len(outputs) + i for i in range(len(carry))},
        scratch_shapes=list(scratch),
        compiler_params=pltpu.CompilerParams(vmem_limit_bytes=VMEM),
        cost_estimate=cost(flops=1, bytes_accessed=1, transcendentals=0),
        name=name,
    )(*inputs, *waits)


def shape_of(*shape, dtype=BF):
    return jax.ShapeDtypeStruct(shape, dtype)


def stack_kernel(*refs):
    for i, ref in enumerate(refs[:-1]):
        refs[-1][i] = ref[...]


def stack_call(pieces, waits=()):
    return local_call(stack_kernel, "stack", pieces, [shape_of(len(pieces), *pieces[0].shape)], waits=waits)[0]


def add_piece_kernel(pieces, other, *outs):
    if len(outs) == 1:
        outs[0][...] = (pieces[0].astype(F32) + other[...].astype(F32)).astype(BF)
    else:
        for i, out in enumerate(outs):
            out[...] = (pieces[0, i].astype(F32) + other[i].astype(F32)).astype(BF)


def add_apart_kernel(one, two, *outs):
    for i, out in enumerate(outs):
        out[...] = (one[i].astype(F32) + two[i].astype(F32)).astype(BF)


def add_apart_call(one, two, waits, carry=()):
    return local_call(
        add_apart_kernel, "add", [one, two], [shape_of(*one.shape[1:])] * one.shape[0], waits=waits, carry=carry
    )


def add_piece_call(pieces, index, other, waits, apart=False):
    outs = [other.shape[1:]] * other.shape[0] if apart else [other.shape]
    block = pl.BlockSpec((1,) + other.shape, lambda i: (index,) + (0,) * other.ndim)

    def whole(shape):
        return pl.BlockSpec(shape, lambda i: (0,) * len(shape))

    result = pl.pallas_call(
        waiting(add_piece_kernel, 2, waits),
        grid=(1,),
        in_specs=[block, whole(other.shape)] + [ANY_REF] * len(waits),
        out_specs=[whole(o) for o in outs],
        out_shape=[shape_of(*o) for o in outs],
        compiler_params=pltpu.CompilerParams(vmem_limit_bytes=VMEM),
        cost_estimate=cost(flops=1, bytes_accessed=1, transcendentals=0),
        name="add_piece",
    )(pieces, other, *waits)
    return result if apart else result[0]


def copy_kernel(source, out):
    out[...] = source[...]


def copy_call(array, waits):
    return local_call(copy_kernel, "copy", [array], [shape_of(*array.shape)], waits=waits)[0]


def add_kernel(*refs):
    total = refs[0][...].astype(F32)
    for ref in refs[1:-1]:
        total = total + ref[...].astype(F32)
    refs[-1][...] = total.astype(refs[-1].dtype)


def add_call(pieces, waits=(), dtype=BF):
    return local_call(add_kernel, "add", pieces, [shape_of(*pieces[0].shape, dtype=dtype)], waits=waits)[0]


def span(index, size):
    return pl.ds(pl.multiple_of(index * size, size), size)


def front_kernel(*refs):
    *parts, near = refs
    for s, ref in enumerate(parts):
        near[s] = ref[...]


def pack_kernel(n_z, place, near, far, own, one, two, three, vectors, bias, expand_bias):
    y, z, shard = place[1], place[2], place[4]
    rows = own.shape[0]
    width = bias.shape[1] // 3
    part = near.shape[2]
    chunks = part // 128
    d_part = D // (2 * n_z)
    outs = (own, one, two, three)

    def source(dp):
        return (dp % 2) ^ y, (z - dp // 2 + n_z) % n_z

    for m in range(4):
        target = shard ^ m
        for i in range(3 * width // 128):
            j = (i // 2) * (D // 128) + 2 * target + i % 2
            side, s = source(j // chunks)
            lanes = pl.ds(pl.multiple_of((j % chunks) * 128, 128), 128)
            at = slice(i * 128, (i + 1) * 128)

            @pl.when(side == 0)
            def _(m=m, s=s, lanes=lanes, at=at):
                outs[m][:, at] = near[s, :rows, lanes]

            @pl.when(side == 1)
            def _(m=m, s=s, lanes=lanes, at=at):
                outs[m][:, at] = far[s, :rows, lanes]

            if m == 0:

                @pl.when(side == 0)
                def _(s=s, lanes=lanes, at=at):
                    bias[:, at] = near[s, rows + 6 : rows + 7, lanes].astype(F32)

                @pl.when(side == 1)
                def _(s=s, lanes=lanes, at=at):
                    bias[:, at] = far[s, rows + 6 : rows + 7, lanes].astype(F32)

    quarter = FF // (8 * n_z)
    for s in range(n_z):
        for side, ref in ((0, near), (1, far)):
            dp = 2 * ((z - s + n_z) % n_z) + (y ^ side)
            block = ref[s, rows : rows + 16].astype(F32)
            vectors[:, span(dp, d_part)] = block[:8, :d_part]
            picked = block[7:8, :quarter]
            for f in range(1, 4):
                picked = jnp.where(shard == f, block[7 + f : 8 + f, :quarter], picked)
            expand_bias[s, :, side * quarter : (side + 1) * quarter] = picked


def enter_kernel(place, e0, e1, e2, e3, w0, w1, w2, w3, bias, vectors, turn, cosine, sine, q, k, v, normed, triple, scratch, entered, weight, add):
    shard = place[4]
    width = q.shape[-1]
    half = width // 2
    step = pl.program_id(0)

    @pl.when(step == 0)
    def _():
        for m, ref in enumerate((w0, w1, w2, w3)):
            rows = span(shard ^ m, ref.shape[0])
            triple[rows, :] = ref[...]
            for part in range(2):
                at = slice(part * width, (part + 1) * width)
                weight[rows, at] = nn(ref[:, at], turn[...]).astype(BF)
            weight[rows, 2 * width :] = ref[:, 2 * width :]
        low = jnp.broadcast_to(bias[...], (8, 3 * width)).astype(BF)
        for part in range(2):
            at = slice(part * width, (part + 1) * width)
            add[:, at] = nn(low[:, at], turn[...])
        add[:, 2 * width :] = low[:, 2 * width :].astype(F32)

    for m, ref in enumerate((e0, e1, e2, e3)):

        @pl.when(step == m)
        def _(ref=ref):
            entered[...] = ref[...]

    values = entered[...].astype(F32)
    unit, _ = norm_parts(values)
    rows = (unit * vectors[0:1] + vectors[1:2]).astype(BF)
    normed[0] = rows
    scratch[...] = rows
    cos = cosine[0]
    sin = sine[0]
    for part, out in ((0, q), (1, k)):
        at = slice(part * width, (part + 1) * width)
        value = nn(scratch[...], weight[:, at]) + add[:1, at]
        first = value[:, :half]
        second = value[:, half:]
        out[0, :, :half] = (first * cos - second * sin).astype(BF)
        out[0, :, half:] = (second * cos + first * sin).astype(BF)
    v[0] = (nn(scratch[...], weight[:, 2 * width :]) + add[:1, 2 * width :]).astype(BF)


def enter_call(place, entered, weights, bias, vectors, turn, cosine, sine, waits, carry):
    rows = entered[0].shape[0]
    width = bias.shape[-1] // 3

    def whole(array):
        return pl.BlockSpec(array.shape, lambda m, p: (0,) * array.ndim)

    def moved(*shape):
        return pl.BlockSpec((1,) + shape, lambda m, p: (p[4] ^ m, 0, 0))

    flat = [*entered, *weights, bias, vectors, turn]
    waits = [*waits, carry]
    return pl.pallas_call(
        waiting(enter_kernel, 3 + len(flat), waits, 1, 5),
        grid_spec=pltpu.PrefetchScalarGridSpec(
            num_scalar_prefetch=1,
            grid=(4,),
            in_specs=[whole(a) for a in flat] + [moved(rows, width // 2)] * 2 + [ANY_REF] * len(waits),
            out_specs=[moved(rows, width)] * 3
            + [moved(rows, D), pl.BlockSpec((D, 3 * width), lambda m, p: (0, 0)), ANY_REF],
            scratch_shapes=[
                pltpu.VMEM((rows, D), BF),
                pltpu.VMEM((rows, D), BF),
                pltpu.VMEM((D, 3 * width), BF),
                pltpu.VMEM((8, 3 * width), F32),
            ],
        ),
        out_shape=[shape_of(4, rows, width)] * 3
        + [shape_of(4, rows, D), shape_of(D, 3 * width), shape_of(*carry.shape)],
        input_output_aliases={2 + len(flat) + len(waits): 5},
        compiler_params=pltpu.CompilerParams(vmem_limit_bytes=VMEM),
        cost_estimate=cost(flops=8 * rows * D * 3 * width, bytes_accessed=30 * rows * D, transcendentals=0),
        name="enter",
    )(place, *flat, cosine, sine, *waits)


def part_kernel(place, mixed, own, far):
    x = place[0]
    for core in range(2):
        own[core] = mixed[2 * x + core]
        far[core] = mixed[2 * (1 - x) + core]


def project_kernel(place, own, far, output, keep, give, weight):
    x, core = place[0], place[3]
    _, rows, width = own.shape
    n_z = output.shape[0]
    d_part = output.shape[-1]
    for z in range(n_z):
        for y in range(2):
            at = (2 * z + y) * d_part
            for source in range(2):
                weight[source * width : (source + 1) * width, at : at + d_part] = output[z, y, source]

    def part(at):
        return nn(own[at], weight[span(x, width), :]) + nn(far[at], weight[span(1 - x, width), :])

    give[...] = part(1 - core).astype(BF)
    keep[...] = part(core)


def middle_kernel(entered, keep, other, vectors, middle, second):
    values = entered[...].astype(F32) + keep[...] + other[...].astype(F32) + vectors[2:3]
    middle[...] = values
    unit, _ = norm_parts(values)
    second[...] = (unit * vectors[3:4] + vectors[4:5]).astype(BF)


def rows_call(kernel, name, inputs, outputs, blocks=3, waits=()):
    rows = max(a.shape[0] for a in inputs)
    step = rows // blocks

    def spec(array):
        if array.shape[0] == 8:
            return pl.BlockSpec(array.shape, lambda i: (0, 0))
        return pl.BlockSpec((step, array.shape[1]), lambda i: (i, 0))

    size = sum(math.prod(a.shape) * a.dtype.itemsize for a in [*inputs, *outputs])
    return pl.pallas_call(
        waiting(kernel, len(inputs), waits),
        grid=(blocks,),
        in_specs=[spec(a) for a in inputs] + [ANY_REF] * len(waits),
        out_specs=[spec(a) for a in outputs],
        out_shape=list(outputs),
        compiler_params=pltpu.CompilerParams(vmem_limit_bytes=VMEM),
        cost_estimate=cost(flops=1, bytes_accessed=1, transcendentals=0),
        name=name,
    )(*inputs, *waits)


def add_rows(ref, rows):
    @pl.when(pl.program_id(0) == 0)
    def _():
        ref[...] = jnp.zeros_like(ref)

    for i, row in enumerate(rows):
        ref[i : i + 1] += jnp.sum(row, 0, keepdims=True)


def middle_back_kernel(middle, outer, keep, other, far, vectors, middle_grad, branch, sums):
    unit, scale = norm_parts(middle[...])
    grad = keep[...] + other[...].astype(F32) + far[...].astype(F32)
    result = outer[...].astype(F32) + norm_back(grad, unit, scale, vectors[3:4])
    middle_grad[...] = result
    low = result.astype(BF)
    branch[...] = low
    add_rows(sums, (low.astype(F32), grad * unit, grad, outer[...].astype(F32)))


def leave_rows(values, frames_local):
    pieces = []
    for l in range(frames_local):
        at = frames_local * PATCHES + 2 * l
        pieces += [values[at : at + 2], values[l * PATCHES : (l + 1) * PATCHES]]
    return jnp.concatenate(pieces, 0)


def output_kernel(frames_local, middle, keep, other, far, live, vectors, out):
    values = middle[...] + keep[...] + other[...].astype(F32) + far[...].astype(F32) + vectors[5:6]
    values = values * live[...]
    out[...] = leave_rows(values, frames_local).astype(BF)


def mixed_grad_kernel(place, branch, branch_other, weight, own, far):
    x, core = place[0], place[3]
    width = own.shape[-1]
    for at, rows in ((core, branch), (1 - core, branch_other)):
        own[at] = nt(rows[...], weight[span(x, width), :]).astype(BF)
        far[at] = nt(rows[...], weight[span(1 - x, width), :]).astype(BF)


def output_grad_kernel(place, own, far, branch, branch_other, near_y, far_y, rows_all, held):
    y, z, core = place[1], place[2], place[3]
    _, rows, width = own.shape
    _, n_z, _, d_part = near_y.shape
    rows_all[span(core, rows), :] = branch[...]
    rows_all[span(1 - core, rows), :] = branch_other[...]
    for i, ref in enumerate((own, far)):
        held[...] = tn(ref[...].reshape(2 * rows, width), rows_all[...]).astype(BF)
        for s in range(n_z):
            for flip, out in ((0, near_y), (1, far_y)):
                out[i, s] = held[:, span(2 * ((z + s) % n_z) + (y ^ flip), d_part)]


def triple_kernel(
    place, normed, triple_grad, grad_rows, triple, e0, e1, e2, e3, own, one, two, three, rows_own, rows_far, rows_give, bias, sums, entered, held
):
    step = pl.program_id(0)
    count, rows, wide = triple_grad.shape
    outs = (own, one, two, three)
    rows_outs = (rows_own, rows_give.at[0], rows_far, rows_give.at[1])

    @pl.when(step == 0)
    def _():
        bias[...] = jnp.zeros_like(bias)
        sums[...] = jnp.zeros_like(sums)

    for m, ref in enumerate((e0, e1, e2, e3)):

        @pl.when(step == m)
        def _(ref=ref):
            entered[...] = ref[...]

    flat = triple_grad[...].reshape(count * rows, wide)
    held[...] = tn(normed[...].reshape(count * rows, normed.shape[-1]), flat).astype(BF)
    back = nt(grad_rows[0], triple[...])
    unit, _ = norm_parts(entered[...].astype(F32))
    sums[0:1] += jnp.sum(back * unit, 0, keepdims=True)
    sums[1:2] += jnp.sum(back, 0, keepdims=True)
    entered[...] = back.astype(BF)
    bias[...] += jnp.sum(grad_rows[0].astype(F32), 0, keepdims=True)
    for m in range(4):

        @pl.when(step == m)
        def _(m=m):
            outs[m][...] = held[...]
            rows_outs[m][...] = entered[...]


def triple_call(place, normed, triple_grad, triple, entered, waits):
    count, rows, wide = triple_grad.shape
    part = D // count

    def fixed(shape):
        return pl.BlockSpec(shape, lambda m, p: (0,) * len(shape), pipeline_mode=pl.Buffered(1))

    outs = [shape_of(part, wide)] * 4 + [shape_of(rows, D)] * 2
    outs += [shape_of(2, rows, D), shape_of(1, wide, dtype=F32), shape_of(8, D, dtype=F32)]
    return pl.pallas_call(
        waiting(triple_kernel, 5 + len(entered), waits),
        grid_spec=pltpu.PrefetchScalarGridSpec(
            num_scalar_prefetch=1,
            grid=(count,),
            in_specs=[
                pl.BlockSpec((count, rows, part), lambda m, p: (0, 0, p[4] ^ m)),
                fixed(triple_grad.shape),
                pl.BlockSpec((1, rows, wide), lambda m, p: (p[4] ^ m, 0, 0)),
                fixed(triple.shape),
            ]
            + [fixed(e.shape) for e in entered]
            + [ANY_REF] * len(waits),
            out_specs=[fixed(o.shape) for o in outs],
            scratch_shapes=[pltpu.VMEM((rows, D), BF), pltpu.VMEM((part, wide), BF)],
        ),
        out_shape=outs,
        compiler_params=pltpu.CompilerParams(vmem_limit_bytes=VMEM),
        cost_estimate=cost(flops=4 * count * rows * wide * D, bytes_accessed=20 * rows * D, transcendentals=0),
        name="triple_grads",
    )(place, normed, triple_grad, triple_grad, triple, *entered, *waits)


def normed_sum_kernel(own, far, got, own_out, far_out):
    own_out[...] = (own[...].astype(F32) + got[0].astype(F32)).astype(BF)
    far_out[...] = (far[...].astype(F32) + got[1].astype(F32)).astype(BF)


def tail_sum_kernel(near, near_got, out, out_got, *totals):
    part = near.shape[-1]
    for s, total in enumerate(totals):
        total[:, :part] = (near[s].astype(F32) + near_got[s].astype(F32)).astype(BF)
        total[:, part:] = (out[0, s].astype(F32) + out_got[s].astype(F32)).astype(BF)


def unpack_kernel(n_z, place, p0, p1, p2, p3, near, far, held):
    y, z, shard = place[1], place[2], place[4]
    part = near.shape[2]
    chunks = part // 128
    for m, ref in enumerate((p0, p1, p2, p3)):
        held[shard ^ m] = ref[...]
    for j in range(3 * D // 128):
        dp, c = divmod(j, chunks)
        per = D // 128
        at = (j // per) * 256 + (j % 2) * 128
        chunk = held[(j % per) // 2, :, at : at + 128]
        s = (dp // 2 - z + n_z) % n_z

        @pl.when(y == dp % 2)
        def _(chunk=chunk, s=s, c=c):
            near[s, :, c * 128 : (c + 1) * 128] = chunk

        @pl.when(y != dp % 2)
        def _(chunk=chunk, s=s, c=c):
            far[s, :, c * 128 : (c + 1) * 128] = chunk


def tail_kernel(*refs):
    total = refs[0][...].astype(F32)
    for ref in refs[1:-2]:
        total = total + ref[...].astype(F32)
    part = refs[-2].shape[-1]
    refs[-2][...] = total[:, :part]
    refs[-1][...] = total[:, part:]


def leave_kernel(frames_local, entered, keep, other, middle_grad, live, vectors, out):
    unit, scale = norm_parts(entered[...].astype(F32))
    grad = keep[...].astype(F32) + other[...].astype(F32)
    result = (middle_grad[...] + norm_back(grad, unit, scale, vectors[0:1])) * live[...]
    out[...] = leave_rows(result, frames_local)


def split_kernel(place, expand, reduce, own, one, two, three):
    shard = place[4]
    rows = expand.shape[0]
    part = own.shape[1]
    blocks = reduce.shape[0] // (4 * part)
    for m, ref in enumerate((own, one, two, three)):
        to = shard ^ m
        ref[:rows] = expand[:, span(to, part)]
        for p in range(blocks):
            ref[rows + p * part : rows + (p + 1) * part] = reduce[span(p * 4 + to, part), :]


def join_kernel(place, own, one, two, three, expand, reduce):
    shard = place[4]
    rows = expand.shape[0]
    part = own.shape[1]
    blocks = reduce.shape[0] // (4 * part)
    for m, ref in enumerate((own, one, two, three)):
        at = shard ^ m
        expand[:, span(at, part)] = ref[:rows].astype(F32)
        for p in range(blocks):
            reduce[span(p * 4 + at, part), :] = ref[rows + p * part : rows + (p + 1) * part].astype(F32)


def fill_weights(place, near, far, weight_in, weight_out):
    y, z, shard = place[1], place[2], place[4]
    n_z = len(near)
    part = near[0].shape[-1]
    rows = D // 4
    for s in range(n_z):
        for side, ref in ((0, near[s]), (1, far[s])):
            if weight_in is not None:
                for m in range(4):
                    weight_in[s, span(shard ^ m, rows), side * part : (side + 1) * part] = ref[m, :rows]
            features = span(2 * ((z - s + n_z) % n_z) + (y ^ side), part)
            for tile in range(n_z):
                unit = (z - tile + n_z) % n_z
                for flip in range(2):
                    at = pl.ds(pl.multiple_of(rows + (y ^ flip) * part, part), part)
                    weight_out[tile, flip * part : (flip + 1) * part, features] = ref[unit ^ shard, at, :]


def feed_kernel(
    place, normal, normal_other, cot, cot_other, p0, p1, p2, p3, f0, f1, f2, f3, bias, active, slope, keep, give, d_bias, give_acc, weight_in, weight_out
):
    step = pl.program_id(0)
    rows = normal.shape[0]

    @pl.when(step == 0)
    def _():
        fill_weights(place, (p0, p1, p2, p3), (f0, f1, f2, f3), weight_in, weight_out)
        keep[...] = jnp.zeros_like(keep)
        give_acc[...] = jnp.zeros_like(give_acc)

    d_bias[...] = jnp.zeros_like(d_bias)
    for i, values, outer, total in ((0, normal, cot, keep), (1, normal_other, cot_other, give_acc)):
        act, gradient = gelu_parts(nn(values[...], weight_in[step]) + bias[0])
        grad = (nt(outer[...], weight_out[step]) * gradient).astype(BF)
        active[i * rows : (i + 1) * rows] = act.astype(BF)
        slope[i * rows : (i + 1) * rows] = grad
        d_bias[0] += jnp.sum(grad.astype(F32), 0, keepdims=True)
        total[...] += nt(grad, weight_in[step])

    @pl.when(step == pl.num_programs(0) - 1)
    def _():
        give[...] = give_acc[...].astype(BF)


def feed_grad_kernel(
    place,
    n0,
    n1,
    n2,
    n3,
    c0,
    c1,
    c2,
    c3,
    active,
    active_far,
    slope,
    slope_far,
    p0,
    p1,
    p2,
    p3,
    f0,
    f1,
    f2,
    f3,
    keep,
    give,
    keep_far,
    give_far,
    grads,
    sent,
    normal_t,
    cot_all,
    give_acc,
    keep_far_acc,
    give_far_acc,
    weight_out,
    held,
    active_all,
    slope_all,
):
    y, z, shard = place[1], place[2], place[4]
    step = pl.program_id(0)
    n_z = grads.shape[0]
    part = p0.shape[-1]
    rows = n0.shape[0]
    deep = D // 4
    totals = (keep, give_acc, keep_far_acc, give_far_acc)

    @pl.when(step == 0)
    def _():
        fill_weights(place, (p0, p1, p2, p3), (f0, f1, f2, f3), None, weight_out)
        for i, (normal, cot) in enumerate(((n0, c0), (n1, c1), (n2, c2), (n3, c3))):
            normal_t[:, i * rows : (i + 1) * rows] = normal[...].T
            cot_all[i * rows : (i + 1) * rows] = cot[...]
            totals[i][...] = jnp.zeros_like(totals[i])

    for i, (act, grad) in enumerate(((active, slope), (active_far, slope_far))):
        at = slice(i * 2 * rows, (i + 1) * 2 * rows)
        active_all[at] = act[...]
        slope_all[at] = grad[...]
        for j in range(2):
            totals[2 * i + j][...] += nn(act[j * rows : (j + 1) * rows], weight_out[step])

    held[...] = nn(normal_t[...], slope_all[...]).astype(BF)
    for side in range(2):
        for m in range(4):
            grads[(n_z - step) % n_z, side, m, :deep] = held[span(shard ^ m, deep), side * part : (side + 1) * part]
    held_t = weight_out.at[step]
    held_t[...] = tn(active_all[...], cot_all[...]).astype(BF)
    unit = (z - step + n_z) % n_z
    for side in range(2):
        at = pl.ds(pl.multiple_of(deep + (y ^ side) * part, part), part)
        for s in range(n_z):
            for flip in range(2):
                features = span(2 * ((z + s) % n_z) + (y ^ flip), part)
                grads[s, flip, unit ^ shard, at, :] = held_t[side * part : (side + 1) * part, features]

    @pl.when(step == pl.num_programs(0) - 1)
    def _():
        give[...] = give_acc[...].astype(BF)
        keep_far[...] = keep_far_acc[...].astype(BF)
        give_far[...] = give_far_acc[...].astype(BF)
        sent[...] = grads[n_z - 1]


def feed_specs(place, n_z):
    def whole(array):
        return pl.BlockSpec(array.shape, lambda t, p: (0,) * len(array.shape), pipeline_mode=pl.Buffered(1))

    def lanes(rows, wide):
        return pl.BlockSpec((rows, wide), lambda t, p: (0, t))

    return whole, lanes


def feed_split_call(place, normal, cot, parts, bias, waits=()):
    rows = normal[0].shape[0]
    n_z = len(parts) // 2
    wide = bias.shape[-1]
    whole, lanes = feed_specs(place, n_z)
    row = pl.BlockSpec((1, 1, wide), lambda t, p: (t, 0, 0))
    block = (rows, D)
    outs = [shape_of(2 * rows, n_z * wide)] * 2 + [shape_of(*block, dtype=F32), shape_of(*block)]
    outs += [shape_of(n_z, 1, wide, dtype=F32)]
    inputs = [*normal, *cot, *parts]
    return pl.pallas_call(
        waiting(feed_kernel, 2 + len(inputs), waits),
        grid_spec=pltpu.PrefetchScalarGridSpec(
            num_scalar_prefetch=1,
            grid=(n_z,),
            in_specs=[whole(a) for a in inputs] + [row] + [ANY_REF] * len(waits),
            out_specs=[lanes(2 * rows, wide)] * 2 + [whole(o) for o in outs[2:4]] + [row],
            scratch_shapes=[pltpu.VMEM(block, F32), pltpu.VMEM((n_z, D, wide), BF), pltpu.VMEM((n_z, wide, D), BF)],
        ),
        out_shape=outs,
        compiler_params=pltpu.CompilerParams(vmem_limit_bytes=VMEM),
        cost_estimate=cost(
            flops=12 * rows * D * wide * n_z, bytes_accessed=20 * rows * D, transcendentals=4 * rows * wide * n_z
        ),
        name="feed_forward",
    )(place, *inputs, bias, *waits)


def feed_grad_call(place, normal, cot, active, slope, parts, waits=()):
    rows = normal[0].shape[0]
    n_z = len(parts) // 2
    wide = active[0].shape[1] // n_z
    whole, lanes = feed_specs(place, n_z)
    block = (rows, D)
    outs = [shape_of(*block, dtype=F32)] + [shape_of(*block)] * 3 + [shape_of(n_z, 2, *parts[0].shape), shape_of(2, *parts[0].shape)]
    first = [*normal, *cot]
    tiles = [*active, *slope]
    return pl.pallas_call(
        waiting(feed_grad_kernel, 1 + len(first) + len(tiles) + 2 * n_z, waits),
        grid_spec=pltpu.PrefetchScalarGridSpec(
            num_scalar_prefetch=1,
            grid=(n_z,),
            in_specs=[whole(a) for a in first]
            + [lanes(2 * rows, wide)] * 4
            + [whole(p) for p in parts]
            + [ANY_REF] * len(waits),
            out_specs=[whole(o) for o in outs],
            scratch_shapes=[
                pltpu.VMEM((D, 4 * rows), BF),
                pltpu.VMEM((4 * rows, D), BF),
                pltpu.VMEM(block, F32),
                pltpu.VMEM(block, F32),
                pltpu.VMEM(block, F32),
                pltpu.VMEM((n_z, wide, D), BF),
                pltpu.VMEM((D, wide), BF),
                pltpu.VMEM((4 * rows, wide), BF),
                pltpu.VMEM((4 * rows, wide), BF),
            ],
        ),
        out_shape=outs,
        compiler_params=pltpu.CompilerParams(vmem_limit_bytes=VMEM),
        cost_estimate=cost(flops=24 * rows * D * wide * n_z, bytes_accessed=40 * rows * D),
        name="feed_grads",
    )(place, *first, *tiles, *parts, *waits)


def torus_shards(sizes, *args):
    (
        tokens,
        cotangent,
        frame_counts,
        presence,
        attend_gain,
        attend_shift,
        triple_weight,
        triple_bias,
        output_weight,
        output_bias,
        second_gain,
        second_shift,
        expand_weight,
        expand_bias,
        reduce_weight,
        reduce_bias,
    ) = args
    n_z, n_y, n_x = sizes
    n_dp = n_z * n_y
    n_f = n_x * 2
    width = D // n_f
    local_rows = tokens.shape[1]
    frames_local = local_rows // ROW_FRAME
    rows = frames_local * PATCHES + EXTRA
    z, y, x, core = (lax.axis_index(name) for name in ("z", "y", "x", "core"))
    shard = x * 2 + core
    place = jnp.stack([x, y, z, core, shard]).astype(jnp.int32)
    d_part = D // n_dp
    qkv_part = 3 * D // n_dp
    ff_part = FF // n_dp
    quarter = ff_part // 4

    def swap(array, axis="core"):
        return lax.ppermute(array, axis, [(0, 1), (1, 0)])

    def cross_over(array):
        return lax.ppermute(array, ("x", "core"), [(i, i ^ 3) for i in range(4)])

    def to_z(array, s):
        return lax.ppermute(array, "z", [(i, (i + s) % n_z) for i in range(n_z)])

    def take(array, index, axis=0):
        return lax.dynamic_index_in_dim(array, index, axis, False)

    def gather_z(array):
        return [array] + [to_z(array, s) for s in range(1, n_z)]

    def scatter_z(array, waits=(), dtype=BF):
        return add_call([array[0]] + [to_z(array[s], s) for s in range(1, n_z)], waits, dtype)

    small = [attend_gain, attend_shift, output_bias, second_gain, second_shift, reduce_bias]
    small = jnp.concatenate([v.reshape(1, d_part) for v in small], 0)
    packed = jnp.concatenate(
        [
            triple_weight,
            jnp.pad(small, ((0, 0), (0, qkv_part - d_part))),
            triple_bias.reshape(1, qkv_part),
            jnp.pad(expand_bias.reshape(4, quarter), ((0, 5), (0, qkv_part - quarter))),
        ],
        0,
    )
    live_all = tables(frame_counts[0], presence[0], n_f, frames_local, width // HEAD)[0]
    live = take(live_all, shard)[:, None]
    entered = to_block(tokens[0], frames_local) * live.astype(BF)
    outer = to_block(cotangent[0], frames_local) * live.astype(BF)

    own, one, two, three, packed = local_call(
        split_kernel,
        "split",
        [place, expand_weight, reduce_weight],
        [shape_of(2 * (D // n_f), d_part)] * 4,
        smem=1,
        carry=[packed],
    )
    packed_parts = gather_z(packed)
    feed = stack_call([own, swap(one), swap(two, "x"), cross_over(three)], [packed_parts[1]])
    near = local_call(
        front_kernel,
        "front",
        packed_parts,
        [shape_of(n_z, *packed.shape)],
    )[0]
    far = swap(near, "y")
    entered = copy_call(entered, [near, feed])
    entered_x = swap(entered, "x")
    entered_all = [entered, swap(entered), entered_x]
    output_all = lax.all_gather(output_weight, ("z", "y", "x"), axis=0).reshape(n_z, n_y, n_x, width, d_part)

    own, one, two, three, vectors, bias, expand_add, counts = local_call(
        functools.partial(pack_kernel, n_z),
        "pack",
        [place, near, far],
        [shape_of(D // n_f, 3 * width)] * 4
        + [shape_of(8, D, dtype=F32), shape_of(1, 3 * width, dtype=F32), shape_of(n_z, 1, 2 * quarter, dtype=F32)],
        smem=1,
        waits=[entered_all[1]],
        carry=[frame_counts],
    )
    _, cosine, sine, guides = tables(counts[0], presence[0], n_f, frames_local, width // HEAD)
    weights = [own, swap(one), swap(two, "x"), cross_over(three)]
    entered_all.append(swap(copy_call(entered_x, [own])))
    feed_near = gather_z(feed)
    turn = jnp.asarray(turn_matrix(width), BF)
    q, k, v, normed, triple, outer = enter_call(
        place, entered_all, weights, bias, vectors, turn, cosine, sine, feed_near[1:2], outer
    )
    feed_far = [swap(part, "y") for part in feed_near]
    feed_parts = [*feed_near, *feed_far]
    outer_x = swap(outer, "x")
    outer_all = [outer, swap(outer), outer_x]
    mixed, exact, logs, logs_extra = attend_call(*guides, q, k, v, waits=feed_near[2:])
    mixed_own, mixed_far, outer_x = local_call(
        part_kernel,
        "mixed_parts",
        [place, mixed],
        [shape_of(2, rows, width)] * 2,
        smem=1,
        waits=[*feed_far[:3], outer_all[1]],
        carry=[outer_x],
    )
    mixed_far = swap(mixed_far, "x")
    outer_all = [*outer_all[:2], outer_x, swap(outer_x)]
    keep, give = local_call(
        project_kernel,
        "project",
        [place, mixed_own, mixed_far, output_all],
        [shape_of(rows, D, dtype=F32), shape_of(rows, D)],
        [pltpu.VMEM((D // 2, D), BF)],
        smem=1,
        flops=4 * rows * D * D // 2,
        waits=[outer_all[3], feed_far[3]],
    )
    output_full = output_all.transpose(2, 3, 0, 1, 4).reshape(D // 2, D)
    middle, second = rows_call(
        middle_kernel,
        "middle",
        [entered, keep, swap(give), vectors],
        [shape_of(rows, D, dtype=F32), shape_of(rows, D)],
    )
    second_all = [second, swap(second)]
    feed_both = [feed_parts, expand_add]
    active, slope, back, back_give, d_bias = feed_split_call(place, second_all, outer_all[:2], *feed_both)
    second_x = swap(second, "x")
    second_all += [second_x, swap(copy_call(second_x, [active]))]
    active_far, slope_far, back_far, back_far_give, d_bias_far = feed_split_call(
        place, second_all[2:], outer_all[2:], *feed_both, waits=[back_give]
    )
    back_give = swap(back_give)
    back_far = swap(add_call([back_far, swap(back_far_give)]), "x")
    final, final_give, final_far, final_far_give, d_feed, d_sent = feed_grad_call(
        place, second_all, outer_all, [active, active_far], [slope, slope_far], feed_parts
    )
    middle_grad, branch, sums_two = rows_call(
        middle_back_kernel,
        "middle_back",
        [middle, outer, back, back_give, back_far, vectors],
        [shape_of(rows, D, dtype=F32), shape_of(rows, D), shape_of(8, D, dtype=F32)],
        waits=[d_sent],
    )
    branch_other = swap(branch)
    grad_own, grad_far = local_call(
        mixed_grad_kernel,
        "mixed_grad",
        [place, branch, branch_other, output_full],
        [shape_of(2, rows, width)] * 2,
        smem=1,
        flops=4 * rows * D * D // 2,
    )
    grad_far = swap(grad_far, "x")
    out_near, out_far = local_call(
        output_grad_kernel,
        "output_weight_grad",
        [place, mixed_own, mixed_far, branch, branch_other],
        [shape_of(n_x, n_z, width, d_part)] * 2,
        [pltpu.VMEM((2 * rows, D), BF), pltpu.VMEM((width, D), BF)],
        smem=1,
        flops=4 * rows * D * D // 2,
        waits=[grad_own],
    )
    out_far = swap(out_far, "y")
    final_far = add_call([final_far, swap(final_far_give)], [grad_own])
    final_far = swap(final_far, "x")
    final_give = swap(final_give)
    triple_grad = attend_back_call(
        x.reshape(1), *guides, q, k, v, [grad_own, grad_far], exact, logs, logs_extra, cosine, sine, turn, waits=[out_near, final_give]
    )
    back_feed = to_z(d_sent, 1)
    tri_own, tri_one, tri_two, tri_three, normed_own, normed_far, normed_give, d_triple_bias, sums_one = triple_call(
        place, normed, triple_grad, triple, entered_all, [back_feed, out_far, final_far]
    )
    pieces = [tri_own, swap(tri_one), swap(tri_two, "x"), cross_over(tri_three)]
    zero_qkv = jnp.zeros((3, n_f, width), F32)
    triple_bias_part = lax.dynamic_update_slice(zero_qkv, d_triple_bias.reshape(3, 1, width), (0, shard, 0))
    expand_bias_part = jnp.zeros((n_z, n_y, n_f, quarter), F32)
    d_bias = (d_bias + d_bias_far).reshape(n_z, n_y, quarter)
    for s in range(n_z):
        for side in range(n_y):
            expand_bias_part = lax.dynamic_update_slice(
                expand_bias_part, d_bias[s, side].reshape(1, 1, 1, quarter), ((z - s) % n_z, y ^ side, shard, 0)
            )
    sums = [sums_one[0], sums_one[1], sums_two[0], sums_two[1], sums_two[2], sums_two[3], triple_bias_part, expand_bias_part]
    sums = jnp.concatenate([piece.reshape(n_dp, -1) for piece in sums], 1)

    def butterfly(sums, bits):
        for bit in bits:
            sums = sums + lax.ppermute(sums, ("z", "y", "x", "core"), [(i, i ^ bit) for i in range(32)])
        return sums

    back_feed = add_piece_call(d_feed, 2, back_feed, [tri_own])
    back_feed = to_z(back_feed, 1)
    out_near, out_send = add_apart_call(out_near, out_far, [tri_own])
    out_far = swap(out_send, "x")
    block_output = local_call(
        functools.partial(output_kernel, frames_local),
        "block_output",
        [middle, final, final_give, final_far, live, vectors],
        [shape_of(local_rows, D)],
        waits=[out_near],
    )[0]
    normed_own, normed_far = local_call(
        normed_sum_kernel,
        "normed_sum",
        [normed_own, normed_far, swap(normed_give)],
        [shape_of(rows, D)] * 2,
        waits=pieces[1:],
    )
    normed_far = swap(normed_far, "x")
    tri_near, tri_far, sums = local_call(
        functools.partial(unpack_kernel, n_z),
        "unpack",
        [place, *pieces],
        [shape_of(n_z, D // n_f, qkv_part)] * 2,
        [pltpu.VMEM((4, D // n_f, 3 * width), BF)],
        smem=1,
        waits=[block_output, normed_own, out_far],
        carry=[sums],
    )
    tri_far = swap(tri_far, "y")
    back_feed = add_piece_call(d_feed, 1, back_feed, [tri_near])
    back_feed = to_z(back_feed, 1)
    sums = butterfly(sums, (1, 4))
    tail = local_call(
        tail_sum_kernel,
        "tail_sum",
        [tri_near, tri_far, out_near[None], out_far],
        [shape_of(D // n_f, qkv_part + d_part)] * n_z,
        waits=[sums],
    )
    tail_parts = [tail[0]] + [to_z(tail[s], s) for s in range(1, n_z)]
    d_near, d_send = add_piece_call(d_feed, 0, back_feed, [tail[0]], True)
    tokens_grad = local_call(
        functools.partial(leave_kernel, frames_local),
        "tokens_grad",
        [entered, normed_own, normed_far, middle_grad, live, vectors],
        [shape_of(local_rows, D, dtype=F32)],
        waits=[tail[0], d_near],
    )[0]
    triple_weight_grad, output_weight_grad = local_call(
        tail_kernel,
        "tail",
        tail_parts,
        [shape_of(D // n_f, qkv_part, dtype=F32), shape_of(D // n_f, d_part, dtype=F32)],
        waits=[tokens_grad],
    )
    *d_feed, sums = add_apart_call(d_near, swap(d_send, "y"), [triple_weight_grad], [sums])
    sums = butterfly(sums, (2, 8, 16))
    expand_weight_grad, reduce_weight_grad = local_call(
        join_kernel,
        "join",
        [place, d_feed[0], swap(d_feed[1]), swap(d_feed[2], "x"), cross_over(d_feed[3])],
        [shape_of(D // n_f, ff_part, dtype=F32), shape_of(FF // n_f, d_part, dtype=F32)],
        smem=1,
    )

    sums = take(sums, z * n_y + y)
    parts = [sums[i * d_part : (i + 1) * d_part] for i in range(6)]
    rest = sums[6 * d_part :]
    return (
        block_output[None],
        tokens_grad[None],
        parts[0],
        parts[1],
        triple_weight_grad,
        rest[:qkv_part],
        output_weight_grad,
        parts[2],
        parts[3],
        parts[4],
        expand_weight_grad,
        rest[qkv_part:],
        reduce_weight_grad,
        parts[5],
    )


def general_shards(sizes, *args):
    (
        tokens,
        cotangent,
        frame_counts,
        presence,
        attend_gain,
        attend_shift,
        triple_weight,
        triple_bias,
        output_weight,
        output_bias,
        second_gain,
        second_shift,
        expand_weight,
        expand_bias,
        reduce_weight,
        reduce_bias,
    ) = args
    n_z, n_y, n_x = sizes
    n_dp = n_z * n_y
    n_f = n_x * 2
    heads = HEADS // n_f
    width = heads * HEAD
    local_rows = tokens.shape[1]
    frames_local = local_rows // ROW_FRAME
    rows = frames_local * PATCHES + EXTRA
    z, y, x, core = (lax.axis_index(name) for name in ("z", "y", "x", "core"))
    shard = x * 2 + core
    d_part = D // n_dp
    ff_part = FF // n_dp
    ff_half = ff_part // 2
    blocks = n_dp // n_f

    def swap(array, axis="core"):
        return lax.ppermute(array, axis, [(0, 1), (1, 0)])

    def take(array, index, axis=0):
        return lax.dynamic_index_in_dim(array, index, axis, False)

    def ordered(index, own, other, axis=0):
        low = jnp.where(index == 0, own, other)
        high = jnp.where(index == 0, other, own)
        return jnp.concatenate([low, high], axis)

    def both_cores(array, axis=0):
        return ordered(core, array, swap(array), axis)

    def exchange_f(array):
        return lax.all_to_all(array, ("x", "core"), 0, 0, tiled=True)

    def over_x(array):
        return lax.all_to_all(array, "x", 0, 0, tiled=True)

    vectors = [attend_gain, attend_shift, output_bias, second_gain, second_shift, reduce_bias, triple_bias, expand_bias]
    flat = jnp.concatenate(vectors)
    qkv_part = 3 * D // n_dp
    flat = jnp.pad(flat, (0, 16 * qkv_part - flat.shape[0])).reshape(16, qkv_part)
    packed = jnp.concatenate([triple_weight, flat], 0)
    packed = lax.all_gather(packed, ("z", "y"), axis=0)
    small = packed[:, D // n_f :].reshape(n_dp, -1)
    full = []
    at = 0
    for vector in vectors:
        full.append(small[:, at : at + vector.shape[0]].reshape(-1))
        at += vector.shape[0]
    gain_one, shift_one, output_add, gain_two, shift_two, reduce_add = (v.astype(F32)[None] for v in full[:6])
    triple_add, expand_add = full[6], full[7]
    triple_rows = packed[:, : D // n_f].transpose(1, 0, 2).reshape(D // n_f, 3, n_f, width)
    triple_own = exchange_f(triple_rows.transpose(2, 0, 1, 3)).reshape(D, 3 * width)
    bias_own = take(triple_add.reshape(3, n_f, width), shard, 1).reshape(1, 3 * width)

    expand_split = expand_weight.reshape(D // n_f, 2, ff_half)
    expand_chip = ordered(core, take(expand_split, core, 1), swap(take(expand_split, 1 - core, 1)))
    reduce_split = reduce_weight.reshape(blocks, 2, ff_half, d_part)
    reduce_chip = ordered(core, take(reduce_split, core, 1)[None], swap(take(reduce_split, 1 - core, 1))[None])
    expand_add_own = take(expand_add.reshape(n_z, n_y, 2, ff_half), core, 2)
    expand_all = lax.all_gather(expand_chip, ("z", "y", "x"), axis=0).reshape(n_z, n_y, D, ff_half)
    expand_pieces = [expand_all.transpose(0, 2, 1, 3).reshape(n_z, D, n_y * ff_half)]
    reduce_all = lax.all_gather(reduce_chip, ("z", "y", "x"), axis=0)
    reduce_pieces = [
        reduce_all.reshape(n_dp, n_dp, ff_half, d_part).transpose(1, 2, 0, 3).reshape(n_z, n_y * ff_half, D)
    ]
    expand_add_own = expand_add_own.reshape(n_z, 1, n_y * ff_half)
    output_all = lax.all_gather(output_weight, ("z", "y", "x"), axis=0)
    output_all = output_all.reshape(n_dp, n_x * width, d_part).transpose(1, 0, 2).reshape(n_x * width, D)

    live_all, cosine, sine, guides = tables(frame_counts[0], presence[0], n_f, frames_local, heads)
    live = take(live_all, shard)[:, None]
    entered = to_block(tokens[0], frames_local).astype(F32) * live
    outer = to_block(cotangent[0], frames_local).astype(F32) * live
    outer_low = outer.astype(BF)
    outer_chip = both_cores(outer_low)
    outer_chip_t = outer_chip.T
    unit_one, scale_one = norm_parts(entered)
    normed = (unit_one * gain_one + shift_one).astype(BF)
    normed_all = lax.all_gather(normed, ("x", "core"), axis=0)

    turned = jnp.asarray(turn_matrix(width), BF)
    q, k, v = qkv_call(normed_all, triple_own, bias_own, turned, cosine, sine)
    mixed, exact, logs, logs_extra = attend_call(*guides, q, k, v)

    mixed_chip = over_x(mixed.reshape(n_x, 2 * rows, width)).transpose(1, 0, 2).reshape(2 * rows, n_x * width)
    branch_part = nn(mixed_chip, output_all).reshape(2, rows, D)
    branch = take(branch_part, core) + swap(take(branch_part, 1 - core).astype(BF)).astype(F32)
    middle = entered + branch + output_add
    unit_two, scale_two = norm_parts(middle)
    second = (unit_two * gain_two + shift_two).astype(BF)
    second_chip = both_cores(second)
    final, second_grad, d_expand_bias, *d_feed = feed_call(
        second_chip, outer_chip, outer_chip_t, expand_pieces[0], expand_add_own, reduce_pieces[0]
    )
    second_grad = second_grad.reshape(2, rows, D)
    second_grad = take(second_grad, core) + swap(take(second_grad, 1 - core).astype(BF)).astype(F32)
    final = final.reshape(2, rows, D)
    final = take(final, core) + swap(take(final, 1 - core).astype(BF)).astype(F32)
    block_output = ((middle + final + reduce_add) * live).astype(BF)

    middle_grad = outer + norm_back(second_grad, unit_two, scale_two, gain_two)
    second_gain_grad = jnp.sum(second_grad * unit_two, 0)
    second_shift_grad = jnp.sum(second_grad, 0)
    branch_low = middle_grad.astype(BF)
    branch_chip = both_cores(branch_low)
    mixed_grad = nt(branch_chip, output_all).astype(BF)
    mixed_grad = over_x(mixed_grad.reshape(2 * rows, n_x, width).transpose(1, 0, 2)).reshape(n_f, rows, width)
    d_output = tn(mixed_chip, branch_chip).astype(BF)
    triple_grad = attend_back_call(
        jnp.zeros((1,), jnp.int32), *guides, q, k, v, list(mixed_grad.reshape(n_x, 2, rows, width)), exact, logs, logs_extra, cosine, sine, turned)
    natural = triple_grad.reshape(n_f * rows, 3 * width)
    d_triple = tn(normed_all.reshape(n_f * rows, D), natural).astype(BF)
    d_triple_bias = jnp.sum(natural.astype(F32), 0)
    normed_grad = nt(natural, triple_own).astype(BF)
    normed_grad = lax.psum_scatter(normed_grad, ("x", "core"), scatter_dimension=0, tiled=True).astype(F32)
    attend_gain_grad = jnp.sum(normed_grad * unit_one, 0)
    attend_shift_grad = jnp.sum(normed_grad, 0)
    tokens_grad = (middle_grad + norm_back(normed_grad, unit_one, scale_one, gain_one)) * live

    d_triple = exchange_f(d_triple.reshape(n_f, D // n_f, 3, width))
    d_triple = d_triple.transpose(1, 2, 0, 3).reshape(D // n_f, n_z, n_y, qkv_part)
    d_triple = d_triple.reshape(D // n_f, 3 * D)
    triple_weight_grad = lax.psum_scatter(d_triple, ("z", "y"), scatter_dimension=1, tiled=True).astype(F32)
    d_output = d_output.reshape(n_x, width, n_dp, d_part).transpose(2, 0, 1, 3).reshape(n_dp * n_x * width, d_part)
    output_weight_grad = lax.psum_scatter(d_output, ("z", "y", "x"), scatter_dimension=0, tiled=True).astype(F32)
    d_expand, d_reduce = d_feed
    d_expand = d_expand.reshape(n_z, D, n_y, ff_half).transpose(0, 2, 1, 3).reshape(n_dp * D, ff_half)
    d_expand = lax.psum_scatter(d_expand, ("z", "y", "x"), scatter_dimension=0, tiled=True)
    d_expand = d_expand.reshape(2, D // n_f, ff_half)
    d_reduce = d_reduce.reshape(n_z, n_dp, d_part, n_y, ff_half).transpose(1, 0, 3, 2, 4).reshape(-1, ff_half)
    d_reduce = lax.psum_scatter(d_reduce, ("z", "y", "x"), scatter_dimension=0, tiled=True)
    d_reduce = d_reduce.reshape(2, blocks, d_part, ff_half)
    expand_weight_grad = ordered(core, take(d_expand, core), swap(take(d_expand, 1 - core)), 1).astype(F32)
    reduce_weight_grad = jnp.stack(
        [
            jnp.where(core == 0, take(d_reduce, core), swap(take(d_reduce, 1 - core))),
            jnp.where(core == 0, swap(take(d_reduce, 1 - core)), take(d_reduce, core)),
        ],
        1,
    )
    reduce_weight_grad = reduce_weight_grad.transpose(0, 1, 3, 2).reshape(blocks * 2 * ff_half, d_part).astype(F32)

    zero_qkv = jnp.zeros((3, n_f, width), F32)
    triple_bias_part = lax.dynamic_update_slice(zero_qkv, d_triple_bias.reshape(3, 1, width), (0, shard, 0))
    d_expand_bias = d_expand_bias.reshape(n_z, n_y, ff_half)
    zero_ff = jnp.zeros((n_dp, 2, ff_half), F32)
    expand_bias_part = lax.dynamic_update_slice(zero_ff, d_expand_bias.reshape(n_dp, 1, ff_half), (0, core, 0))
    sums = [
        attend_gain_grad,
        attend_shift_grad,
        jnp.sum(branch_low.astype(F32), 0),
        second_gain_grad,
        second_shift_grad,
        jnp.sum(outer_low.astype(F32), 0),
        triple_bias_part.reshape(-1),
        expand_bias_part.reshape(-1),
    ]
    sums = jnp.concatenate([s.reshape(n_dp, -1) for s in sums], 1)
    total = n_dp * n_f
    bit = 1
    while bit < total:
        sums = sums + lax.ppermute(sums, ("z", "y", "x", "core"), [(i, i ^ bit) for i in range(total)])
        bit *= 2
    own = take(sums, z * n_y + y)
    parts = []
    at = 0
    for size in [d_part] * 6 + [qkv_part, ff_part]:
        parts.append(own[at : at + size])
        at += size
    return (
        from_block(block_output, frames_local),
        from_block(tokens_grad, frames_local),
        parts[0],
        parts[1],
        triple_weight_grad,
        parts[6],
        output_weight_grad,
        parts[2],
        parts[3],
        parts[4],
        expand_weight_grad,
        parts[7],
        reduce_weight_grad,
        parts[5],
    )


def solution(mesh):
    n_dp, n_f = mesh.shape["dp"], mesh.shape["fsdp"]
    sizes = (n_dp // 2, 2, n_f // 2)
    inner = jax.sharding.Mesh(mesh.devices.reshape(*sizes, 2), ("z", "y", "x", "core"))
    dp = ("z", "y")
    fsdp = ("x", "core")
    rows = P(dp, fsdp, None)
    weight = P(fsdp, dp)
    vector = P(dp)
    return jax.shard_map(
        functools.partial(torus_shards if sizes == (4, 2, 2) else general_shards, sizes),
        mesh=inner,
        in_specs=(
            rows,
            rows,
            P(dp, None),
            P(dp, None, None),
            vector,
            vector,
            weight,
            vector,
            weight,
            vector,
            vector,
            vector,
            weight,
            vector,
            weight,
            vector,
        ),
        out_specs=(
            rows,
            rows,
            vector,
            vector,
            weight,
            vector,
            weight,
            vector,
            vector,
            vector,
            weight,
            vector,
            weight,
            vector,
        ),
        check_vma=False,
    )
```

```python
import functools
import math

import jax
import jax.numpy as jnp
import numpy as np
from jax import lax
from jax.experimental import pallas as pl
from jax.experimental.pallas import tpu as pltpu
from jax.sharding import PartitionSpec as P

D = 1024
HEADS = 16
HEAD = 64
FF = 4096
GRID = 16
PATCHES = GRID * GRID
ROW_FRAME = PATCHES + 2
PAIRS = HEAD // 3 // 2
EXTRA = 16

EPSILON = 1e-06
SCALE2 = 0.125 * math.log2(math.e)
MASKED = -8e9
FAR = 1 << 20
VMEM = 60 * 1024 * 1024
BF = jnp.bfloat16
F32 = jnp.float32


def nn(left, right):
    return lax.dot_general(left, right, (((1,), (0,)), ((), ())), preferred_element_type=F32)


def nt(left, right):
    return lax.dot_general(left, right, (((1,), (1,)), ((), ())), preferred_element_type=F32)


def tn(left, right):
    return lax.dot_general(left, right, (((0,), (0,)), ((), ())), preferred_element_type=F32)


def qkv_kernel(normed, weight, bias, turn, cosine, sine, q_out, k_out, v_out, turned, turned_bias):
    width = q_out.shape[-1]
    half = width // 2

    @pl.when(pl.program_id(0) == 0)
    def _():
        for part in range(2):
            span = slice(part * width, (part + 1) * width)
            turned[:, span] = nn(weight[:, span], turn[...]).astype(BF)
            turned_bias[:, span] = nn(bias[:, span], turn[...])

    rows = normed[0]
    cos = cosine[0]
    sin = sine[0]
    for part, out in ((0, q_out), (1, k_out)):
        span = slice(part * width, (part + 1) * width)
        value = nn(rows, turned[:, span]) + turned_bias[:1, span]
        first = value[:, :half]
        second = value[:, half:]
        out[0, :, :half] = (first * cos - second * sin).astype(BF)
        out[0, :, half:] = (second * cos + first * sin).astype(BF)
    span = slice(2 * width, 3 * width)
    v_out[0] = (nn(rows, weight[:, span]) + bias[:1, span].astype(F32)).astype(BF)


def qkv_call(normed, weight, bias, turn, cosine, sine):
    sources, rows, _ = normed.shape
    width = weight.shape[1] // 3
    half = width // 2
    block = pl.BlockSpec((1, rows, width), lambda s: (s, 0, 0))
    table = pl.BlockSpec((1, rows, half), lambda s: (s, 0, 0))

    def whole(shape):
        return pl.BlockSpec(shape, lambda s: (0,) * len(shape))

    shape = jax.ShapeDtypeStruct((sources, rows, width), BF)
    return pl.pallas_call(
        qkv_kernel,
        grid=(sources,),
        in_specs=[
            pl.BlockSpec((1, rows, D), lambda s: (s, 0, 0)),
            whole(weight.shape),
            whole(bias.shape),
            whole(turn.shape),
            table,
            table,
        ],
        out_specs=[block] * 3,
        out_shape=[shape] * 3,
        scratch_shapes=[pltpu.VMEM((D, 2 * width), BF), pltpu.VMEM((bias.shape[0], 2 * width), F32)],
        compiler_params=pltpu.CompilerParams(vmem_limit_bytes=VMEM),
        cost_estimate=pl.CostEstimate(
            flops=2 * sources * rows * D * 3 * width, bytes_accessed=4 * sources * rows * D, transcendentals=0
        ),
        name="qkv_rotary",
    )(normed, weight, bias, turn, cosine, sine)


def turned_lanes(width, head):
    lane = lax.broadcasted_iota(jnp.int32, (1, width), 1)
    return (lane % (width // 2)) // (HEAD // 2) == head


def plain_lanes(width, head):
    lane = lax.broadcasted_iota(jnp.int32, (1, width), 1)
    return lane // HEAD == head


def pick(mask, array):
    return jnp.where(mask, array, jnp.zeros((), array.dtype))


def stack_heads(array, lanes):
    width = array.shape[-1]
    return jnp.concatenate([pick(lanes(width, head), array) for head in range(width // HEAD)], 0)


def unstack_heads(array, lanes):
    width = array.shape[-1]
    heads = width // HEAD
    step = array.shape[0] // heads
    total = pick(lanes(width, 0), array[:step])
    for head in range(1, heads):
        total = total + pick(lanes(width, head), array[head * step : (head + 1) * step])
    return total


def head_rows(array, head):
    half = array.shape[0] // 2
    step = HEAD // 2
    return jnp.concatenate(
        [array[head * step : (head + 1) * step], array[half + head * step : half + (head + 1) * step]], 0
    )


def value_total(v, frames_local, sources):
    total = jnp.zeros((1, v.shape[-1]), F32)
    real = lax.broadcasted_iota(jnp.int32, (EXTRA, 1), 0) < 2 * frames_local
    for s in range(sources):
        for l in range(frames_local):
            total = total + jnp.sum(v[s, l * PATCHES : (l + 1) * PATCHES].astype(F32), 0, keepdims=True)
        total = total + jnp.sum(pick(real, v[s, frames_local * PATCHES :].astype(F32)), 0, keepdims=True)
    return total


def attend_kernel(
    frames_local,
    start,
    key_frame,
    query_start,
    query_frame,
    query_pad,
    q,
    k,
    v,
    mixed,
    exact,
    logs,
    logs_extra,
    v_t,
    queries,
    acc,
    state,
):
    sources, _, width = q.shape
    heads = width // HEAD
    frames = sources * frames_local
    patch_rows = frames_local * PATCHES
    length = frames * ROW_FRAME

    def frame_ref(ref, g):
        return ref[g // frames_local, pl.ds(pl.multiple_of((g % frames_local) * PATCHES, PATCHES), PATCHES), :]

    for g in range(frames):
        s, l = g // frames_local, g % frames_local
        v_t[g] = v[s, l * PATCHES : (l + 1) * PATCHES].T
    k_extra = jnp.concatenate([k[s, patch_rows:] for s in range(sources)], 0)
    v_extra_t = jnp.concatenate([v[s, patch_rows:] for s in range(sources)], 0).T
    uniform = jnp.asarray(1.0 / length, BF).astype(F32) * value_total(v, frames_local, sources)
    key_at = key_frame[:, :1]

    def weigh(scores, top):
        return jnp.exp2((scores - top) * SCALE2)

    def mix(values_t, weights, head):
        return nn(values_t[head * HEAD : (head + 1) * HEAD], weights[:, head * PATCHES : (head + 1) * PATCHES])

    def one_frame(g, _):
        first = start[g]
        queries[...] = stack_heads(frame_ref(q, g), turned_lanes)
        allowed = (key_at >= first) & (key_at <= g)
        scores_extra = jnp.where(allowed, nt(k_extra, queries[...]), MASKED)
        scores = nt(frame_ref(k, g), queries[...])
        top = jnp.maximum(jnp.max(scores_extra, 0, keepdims=True), jnp.max(scores, 0, keepdims=True))
        weights_extra = weigh(scores_extra, top)
        weights = weigh(scores, top)
        state[0:1] = top
        state[1:2] = jnp.sum(weights_extra, 0, keepdims=True) + jnp.sum(weights, 0, keepdims=True)
        weights_extra = weights_extra.astype(BF)
        weights = weights.astype(BF)
        values_t = v_t[g]
        for head in range(heads):
            acc[head] = mix(v_extra_t, weights_extra, head) + mix(values_t, weights, head)

        def some_keys(which):
            scores = [nt(frame_ref(k, f), queries[...]) for f in which]
            before = state[0:1]
            top = before
            for s in scores:
                top = jnp.maximum(top, jnp.max(s, 0, keepdims=True))
            fade = weigh(before, top)
            weights = [weigh(s, top) for s in scores]
            state[0:1] = top
            total = state[1:2] * fade
            for w in weights:
                total = total + jnp.sum(w, 0, keepdims=True)
            state[1:2] = total
            weights = [w.astype(BF) for w in weights]
            for head in range(heads):
                out = acc[head] * fade[:, head * PATCHES : (head + 1) * PATCHES]
                for f, w in zip(which, weights):
                    out = out + mix(v_t[f], w, head)
                acc[head] = out

        def pair(i, _):
            some_keys([first + 2 * i, first + 2 * i + 1])
            return 0

        count = jnp.maximum(g - first, 0)
        lax.fori_loop(0, count // 2, pair, 0)

        @pl.when(count % 2 == 1)
        def _():
            some_keys([g - 1])

        total = state[1:2]
        result = jnp.concatenate(
            [acc[head] / total[:, head * PATCHES : (head + 1) * PATCHES] for head in range(heads)], 0
        ).T
        result = jnp.where(first > frames, jnp.broadcast_to(uniform, result.shape), result)
        rows = pl.ds(pl.multiple_of((g % frames_local) * PATCHES, PATCHES), PATCHES)
        exact[g // frames_local, rows, :] = result
        mixed[g // frames_local, rows, :] = result.astype(BF)
        logs[g] = jnp.broadcast_to(state[0:1] + jnp.log2(total) * (1.0 / SCALE2), (8, heads * PATCHES))
        return 0

    lax.fori_loop(0, frames, one_frame, 0)

    q_extra = stack_heads(jnp.concatenate([q[s, patch_rows:] for s in range(sources)], 0), turned_lanes)
    first = jnp.concatenate([query_start[:1]] * heads, 1)
    last = jnp.concatenate([query_frame[:1]] * heads, 1)
    every = [jnp.where((key_at >= first) & (key_at <= last), nt(k_extra, q_extra), MASKED)]
    for f in range(frames):
        every.append(jnp.where((first <= f) & (last >= f), nt(frame_ref(k, f), q_extra), MASKED))
    top = jnp.max(every[0], 0, keepdims=True)
    for scores in every[1:]:
        top = jnp.maximum(top, jnp.max(scores, 0, keepdims=True))
    total = jnp.zeros_like(top)
    result = jnp.zeros((width, q_extra.shape[0]), F32)
    for scores, values_t in zip(every, [v_extra_t] + [v_t[f] for f in range(frames)]):
        weights = weigh(scores, top)
        total = total + jnp.sum(weights, 0, keepdims=True)
        result = result + nn(values_t, weights.astype(BF))
    result = unstack_heads((result / total).T, plain_lanes)
    result = jnp.where(query_pad[:, :1] > 0, jnp.broadcast_to(uniform, result.shape), result)
    for s in range(sources):
        exact[s, patch_rows:, :] = result[s * EXTRA : (s + 1) * EXTRA]
        mixed[s, patch_rows:, :] = result[s * EXTRA : (s + 1) * EXTRA].astype(BF)
    logs_extra[...] = jnp.broadcast_to(top + jnp.log2(total) * (1.0 / SCALE2), logs_extra.shape)


def attend_call(start, key_frame, query_start, query_frame, query_pad, q, k, v, waits=()):
    sources, rows, width = q.shape
    frames_local = rows // PATCHES
    frames = sources * frames_local
    heads = width // HEAD
    stacked = heads * sources * EXTRA
    vmem = pl.BlockSpec(memory_space=pltpu.VMEM)
    return pl.pallas_call(
        waiting(functools.partial(attend_kernel, frames_local), 8, waits),
        in_specs=[pl.BlockSpec(memory_space=pltpu.SMEM)] + [vmem] * 7 + [ANY_REF] * len(waits),
        out_specs=[vmem] * 4,
        out_shape=[
            jax.ShapeDtypeStruct(q.shape, BF),
            jax.ShapeDtypeStruct(q.shape, F32),
            jax.ShapeDtypeStruct((frames, 8, heads * PATCHES), F32),
            jax.ShapeDtypeStruct((8, stacked), F32),
        ],
        scratch_shapes=[
            pltpu.VMEM((frames, width, PATCHES), BF),
            pltpu.VMEM((heads * PATCHES, width), BF),
            pltpu.VMEM((heads, HEAD, PATCHES), F32),
            pltpu.VMEM((8, heads * PATCHES), F32),
        ],
        compiler_params=pltpu.CompilerParams(vmem_limit_bytes=VMEM),
        cost_estimate=cost(
            flops=8 * heads * 256 * frames * frames * PATCHES * PATCHES // 2,
            bytes_accessed=10 * sources * rows * width,
            transcendentals=heads * frames * frames * PATCHES * PATCHES // 2,
        ),
        name="attend",
    )(start, key_frame, query_start, query_frame, query_pad, q, k, v, *waits)


def attend_back_kernel(
    frames_local,
    chips,
    flip,
    start,
    key_frame,
    query_start,
    query_frame,
    query_pad,
    q,
    k,
    v,
    *rest,
):
    pieces = rest[:chips]
    (
        exact,
        logs,
        logs_extra,
        cosine,
        sine,
        turn,
        out,
        grad,
        k_t,
        queries,
        grads,
        dq_t,
        dk,
        dv,
        dq_extra,
        dk_extra,
        dv_extra,
        centers,
    ) = rest[chips:]
    sources, _, width = q.shape
    for i in range(chips):
        for core in range(2):
            grad[2 * (i ^ flip[0]) + core] = pieces[i][core]
    half = width // 2
    heads = width // HEAD
    frames = sources * frames_local
    patch_rows = frames_local * PATCHES
    length = frames * ROW_FRAME
    step_rows = HEAD // 2

    def frame_ref(ref, g):
        return ref[g // frames_local, pl.ds(pl.multiple_of((g % frames_local) * PATCHES, PATCHES), PATCHES), :]

    which = lax.broadcasted_iota(jnp.int32, (8, width), 0)
    lane = lax.broadcasted_iota(jnp.int32, (8, width), 1)
    groups = (lane // HEAD == which).astype(BF)

    def center_of(grad_rows, exact_rows):
        product = grad_rows.astype(F32) * exact_rows
        high = product.astype(BF)
        low = (product - high.astype(F32)).astype(BF)
        center = nt(groups, high) + nt(groups, low)
        return jnp.concatenate([center[head : head + 1] for head in range(heads)], 1)

    def gather_extra(ref):
        return jnp.concatenate([ref[s, patch_rows:] for s in range(sources)], 0)

    for g in range(frames):
        s, l = g // frames_local, g % frames_local
        k_t[g] = k[s, l * PATCHES : (l + 1) * PATCHES].T
    k_extra = gather_extra(k)
    v_extra = gather_extra(v)
    k_extra_t = k_extra.T
    dk_extra[...] = jnp.zeros_like(dk_extra)
    dv_extra[...] = jnp.zeros_like(dv_extra)
    key_at = key_frame[:, :1]

    def tile(keys, values, query, query_grad, log, center, allowed):
        scores = nt(keys, query)
        inner = nt(values, query_grad)
        probs = jnp.exp2((scores - log) * SCALE2)
        if allowed is not None:
            probs = jnp.where(allowed, probs, 0.0)
        change = (probs * (inner - center)).astype(BF)
        return nn(probs.astype(BF), query_grad), nn(change, query), change

    def add_dq(ref, keys_t, change, keep):
        for head in range(heads):
            part = nn(head_rows(keys_t, head), change[:, head * PATCHES : (head + 1) * PATCHES])
            for side in range(2):
                rows = slice(side * half + head * step_rows, side * half + (head + 1) * step_rows)
                piece = part[side * step_rows : (side + 1) * step_rows]
                ref[rows] = ref[rows] + piece if keep else piece

    def one_frame(g, pad_grad):
        first = start[g]
        grad_rows = frame_ref(grad, g)
        queries[...] = stack_heads(frame_ref(q, g), turned_lanes)
        grads[...] = stack_heads(grad_rows, plain_lanes)
        centers[...] = jnp.broadcast_to(center_of(grad_rows, frame_ref(exact, g)), centers.shape)
        allowed = (key_at >= first) & (key_at <= g)
        query, query_grad, log, center = queries[...], grads[...], logs[g, :1], centers[:1]
        dv_part, dk_part, change = tile(k_extra, v_extra, query, query_grad, log, center, allowed)
        dv_extra[...] += dv_part
        dk_extra[...] += dk_part
        add_dq(dq_t.at[g], k_extra_t, change, False)
        dv_part, dk_part, change = tile(
            frame_ref(k, g), frame_ref(v, g), query, query_grad, log, center, jnp.broadcast_to(first <= g, log.shape)
        )
        dv[g] = dv_part
        dk[g] = dk_part
        add_dq(dq_t.at[g], k_t[g], change, True)

        def some_keys(which):
            parts = [
                tile(frame_ref(k, f), frame_ref(v, f), queries[...], grads[...], logs[g, :1], centers[:1], None)
                for f in which
            ]
            for f, (dv_part, dk_part, _) in zip(which, parts):
                dv[f] += dv_part
                dk[f] += dk_part
            for f, (_, _, change) in zip(which, parts):
                add_dq(dq_t.at[g], k_t[f], change, True)

        def pair(i, _):
            some_keys([first + 2 * i, first + 2 * i + 1])
            return 0

        count = jnp.maximum(g - first, 0)
        lax.fori_loop(0, count // 2, pair, 0)

        @pl.when(count % 2 == 1)
        def _():
            some_keys([g - 1])

        return pad_grad + jnp.where(first > frames, jnp.sum(grad_rows.astype(F32), 0, keepdims=True), 0.0)

    pad_grad = lax.fori_loop(0, frames, one_frame, jnp.zeros((1, width), F32))
    g_extra = gather_extra(grad)
    pad_grad = pad_grad + jnp.sum(jnp.where(query_pad[:, :1] > 0, g_extra.astype(F32), 0.0), 0, keepdims=True)
    pad_grad = pad_grad * jnp.asarray(1.0 / length, BF).astype(F32)

    q_stack = stack_heads(gather_extra(q), turned_lanes)
    g_stack = stack_heads(g_extra, plain_lanes)
    stacked = q_stack.shape[0]
    queries[:stacked] = q_stack
    grads[:stacked] = g_stack
    first = jnp.concatenate([query_start[:1]] * heads, 1)
    last = jnp.concatenate([query_frame[:1]] * heads, 1)
    log = logs_extra[:1]
    center = center_of(g_extra, gather_extra(exact))
    allowed = (key_at >= first) & (key_at <= last)
    dv_part, dk_part, change = tile(k_extra, v_extra, q_stack, g_stack, log, center, allowed)
    dv_extra[...] += dv_part
    dk_extra[...] += dk_part
    dq_extra[...] = nn(k_extra_t, change)

    def extra_keys(i, _):
        which = [2 * i, 2 * i + 1]
        parts = [
            tile(
                frame_ref(k, f), frame_ref(v, f), queries[:stacked], grads[:stacked], log, center, (first <= f) & (last >= f)
            )
            for f in which
        ]
        total = dq_extra[...]
        for f, (dv_part, dk_part, change) in zip(which, parts):
            dv[f] += dv_part
            dk[f] += dk_part
            total = total + nn(k_t[f], change)
        dq_extra[...] = total
        return 0

    lax.fori_loop(0, frames // 2, extra_keys, 0)

    def emit(s, rows, dq_rows, dk_rows, dv_rows, real=None):
        cos = cosine[s, rows]
        sin = sine[s, rows]
        for part, array in ((0, dq_rows), (1, dk_rows)):
            a = array[:, :half] * 0.125
            b = array[:, half:] * 0.125
            both = jnp.concatenate([(a * cos + b * sin).astype(BF), (b * cos - a * sin).astype(BF)], 1)
            both = nt(both, turn[...])
            if real is not None:
                both = pick(real, both)
            out[s, rows, part * width : (part + 1) * width] = both.astype(BF)
        total = dv_rows + pad_grad
        if real is not None:
            total = pick(real, total)
        out[s, rows, 2 * width :] = total.astype(BF)

    def emit_frame(g, _):
        rows = pl.ds(pl.multiple_of((g % frames_local) * PATCHES, PATCHES), PATCHES)
        emit(g // frames_local, rows, dq_t[g].T, dk[g], dv[g])
        return 0

    lax.fori_loop(0, frames, emit_frame, 0)
    dq_rows = unstack_heads(dq_extra[...].T, turned_lanes)
    real = lax.broadcasted_iota(jnp.int32, (EXTRA, 1), 0) < 2 * frames_local
    for s in range(sources):
        at = slice(s * EXTRA, (s + 1) * EXTRA)
        emit(s, slice(patch_rows, patch_rows + EXTRA), dq_rows[at], dk_extra[at], dv_extra[at], real)


def attend_back_call(
    flip, start, key_frame, query_start, query_frame, query_pad, q, k, v, grad, exact, logs, logs_extra, cosine, sine, turn, waits=()
):
    chips = len(grad)
    sources, rows, width = q.shape
    frames_local = rows // PATCHES
    frames = sources * frames_local
    extra = sources * EXTRA
    heads = width // HEAD
    vmem = pl.BlockSpec(memory_space=pltpu.VMEM)
    return pl.pallas_call(
        waiting(functools.partial(attend_back_kernel, frames_local, chips), 15 + chips, waits),
        in_specs=[pl.BlockSpec(memory_space=pltpu.SMEM)] * 2 + [vmem] * (13 + chips) + [ANY_REF] * len(waits),
        out_specs=vmem,
        out_shape=jax.ShapeDtypeStruct((sources, rows, 3 * width), BF),
        scratch_shapes=[
            pltpu.VMEM((sources, rows, width), BF),
            pltpu.VMEM((frames, width, PATCHES), BF),
            pltpu.VMEM((heads * PATCHES, width), BF),
            pltpu.VMEM((heads * PATCHES, width), BF),
            pltpu.VMEM((frames, width, PATCHES), F32),
            pltpu.VMEM((frames, PATCHES, width), F32),
            pltpu.VMEM((frames, PATCHES, width), F32),
            pltpu.VMEM((width, heads * extra), F32),
            pltpu.VMEM((extra, width), F32),
            pltpu.VMEM((extra, width), F32),
            pltpu.VMEM((8, heads * PATCHES), F32),
        ],
        compiler_params=pltpu.CompilerParams(vmem_limit_bytes=VMEM),
        cost_estimate=cost(
            flops=20 * heads * 256 * frames * frames * PATCHES * PATCHES // 2,
            bytes_accessed=20 * sources * rows * width,
            transcendentals=heads * frames * frames * PATCHES * PATCHES // 2,
        ),
        name="attend_back",
    )(
        flip, start, key_frame, query_start, query_frame, query_pad, q, k, v, *grad, exact, logs, logs_extra, cosine, sine, turn, *waits
    )


def gelu_parts(hidden):
    base = 1.0 + (0.3275911 * math.sqrt(0.5)) * jnp.abs(hidden)
    guess = pl.reciprocal(base, approx=True)
    t = guess * (2.0 - base * guess)
    bell = jnp.exp2(hidden * hidden * (-0.5 * math.log2(math.e)))
    poly = 0.5 * 1.061405429
    for coefficient in (-1.453152027, 1.421413741, -0.284496736, 0.254829592):
        poly = poly * t + 0.5 * coefficient
    tail = poly * t * bell
    cdf = jnp.where(hidden < 0.0, tail, 1.0 - tail)
    return hidden * cdf, cdf + hidden * bell * (1.0 / math.sqrt(2.0 * math.pi))


def feed_body(chunk, second, outer, outer_t, weight_in, weight_out, add, final, second_grad, d_bias, second_t, active, slope):
    rows = second.shape[0]

    @pl.when(pl.program_id(0) == 0)
    def _():
        for r in range(0, rows, chunk):
            second_t[:, r : r + chunk] = second[r : r + chunk].T
        final[...] = jnp.zeros_like(final)
        second_grad[...] = jnp.zeros_like(second_grad)

    d_bias[...] = jnp.zeros_like(d_bias)
    for r in range(0, rows, chunk):
        at = slice(r, r + chunk)
        act, gradient = gelu_parts(nn(second[at], weight_in[...]) + add)
        act = act.astype(BF)
        grad = (nt(outer[at], weight_out[...]) * gradient).astype(BF)
        active[at] = act
        slope[at] = grad
        d_bias[0] += jnp.sum(grad.astype(F32), 0, keepdims=True)
        final[at] += nn(act, weight_out[...])
        second_grad[at] += nt(grad, weight_in[...])
    return nn(second_t[...], slope[...]).astype(BF), nn(outer_t[...], active[...]).astype(BF)


def feed_plain_kernel(
    chunk, second, outer, outer_t, expand, expand_bias, reduce, final, second_grad, d_bias, d_expand, d_reduce, second_t, active, slope
):
    d_expand[0], d_reduce[0] = feed_body(
        chunk, second, outer, outer_t, expand.at[0], reduce.at[0], expand_bias[0].astype(F32),
        final, second_grad, d_bias, second_t, active, slope,
    )


def feed_call(second, outer, outer_t, expand, expand_bias, reduce):
    rows = second.shape[0]
    tiles, _, wide = expand.shape
    chunk = rows // 2

    def whole(shape):
        return pl.BlockSpec(shape, lambda t: (0,) * len(shape))

    def tiled(shape):
        return pl.BlockSpec((1,) + shape[1:], lambda t: (t, 0, 0))

    return pl.pallas_call(
        functools.partial(feed_plain_kernel, chunk),
        grid=(tiles,),
        in_specs=[
            whole((rows, D)),
            whole((rows, D)),
            whole((D, rows)),
            tiled(expand.shape),
            tiled(expand_bias.shape),
            tiled(reduce.shape),
        ],
        out_specs=[whole((rows, D)), whole((rows, D)), tiled((tiles, 1, wide))] + [tiled((tiles, D, wide))] * 2,
        out_shape=[
            jax.ShapeDtypeStruct((rows, D), F32),
            jax.ShapeDtypeStruct((rows, D), F32),
            jax.ShapeDtypeStruct((tiles, 1, wide), F32),
        ]
        + [jax.ShapeDtypeStruct((tiles, D, wide), BF)] * 2,
        scratch_shapes=[pltpu.VMEM((D, rows), BF), pltpu.VMEM((rows, wide), BF), pltpu.VMEM((rows, wide), BF)],
        compiler_params=pltpu.CompilerParams(vmem_limit_bytes=VMEM),
        cost_estimate=pl.CostEstimate(
            flops=10 * rows * D * wide * tiles,
            bytes_accessed=8 * D * wide * tiles + 14 * rows * D,
            transcendentals=2 * rows * wide * tiles,
        ),
        name="feed_forward",
    )(second, outer, outer_t, expand, expand_bias, reduce)


def norm_parts(values):
    center = values - jnp.mean(values, -1, keepdims=True)
    scale = lax.rsqrt(jnp.mean(center * center, -1, keepdims=True) + EPSILON)
    return center * scale, scale


def norm_back(grad, unit, scale, gain):
    scaled = grad * gain
    mean_one = jnp.mean(scaled, -1, keepdims=True)
    mean_two = jnp.mean(scaled * unit, -1, keepdims=True)
    return scale * (scaled - mean_one - unit * mean_two)


def to_block(array, frames_local):
    split = array.reshape(frames_local, ROW_FRAME, D)
    return jnp.concatenate(
        [
            split[:, 2:].reshape(frames_local * PATCHES, D),
            split[:, :2].reshape(frames_local * 2, D),
            jnp.zeros((EXTRA - 2 * frames_local, D), array.dtype),
        ],
        0,
    )


def from_block(array, frames_local):
    patches = array[: frames_local * PATCHES].reshape(frames_local, PATCHES, D)
    extra = array[frames_local * PATCHES : frames_local * ROW_FRAME].reshape(frames_local, 2, D)
    return jnp.concatenate([extra, patches], 1).reshape(1, frames_local * ROW_FRAME, D)


def rows_of(per_frame, per_extra, sources, frames_local, fill):
    patches = jnp.broadcast_to(per_frame.reshape(sources, frames_local, 1), (sources, frames_local, PATCHES))
    pad = jnp.full((sources, EXTRA - 2 * frames_local), fill, per_frame.dtype)
    return jnp.concatenate(
        [patches.reshape(sources, -1), per_extra.reshape(sources, 2 * frames_local), pad], 1
    )


def tables(counts, present, sources, frames_local, heads):
    frames = sources * frames_local
    at = jnp.arange(frames, dtype=jnp.int32)
    first, second = counts[0], counts[1]
    inside = at < first + second
    start = jnp.where(at < first, 0, first).astype(jnp.int32)
    time = (at - start).astype(F32)
    begin = jnp.where(inside, start, FAR)
    live_extra = inside[:, None] & (present == 1)
    time_rows = rows_of(time, jnp.repeat(time, 2), sources, frames_local, 0.0)
    live_rows = rows_of(inside.astype(F32), live_extra.astype(F32), sources, frames_local, 0.0)

    patch = np.arange(PATCHES)
    grid_row = np.zeros(frames_local * PATCHES + EXTRA, np.float32)
    grid_col = np.zeros(frames_local * PATCHES + EXTRA, np.float32)
    for l in range(frames_local):
        grid_row[l * PATCHES : (l + 1) * PATCHES] = patch // GRID
        grid_col[l * PATCHES : (l + 1) * PATCHES] = patch % GRID
    lanes = np.zeros((3, HEAD // 2), np.float32)
    freq = 10000.0 ** (-np.arange(PAIRS, dtype=np.float32) / PAIRS)
    for a in range(3):
        lanes[a, a * PAIRS : (a + 1) * PAIRS] = freq
    lanes = np.tile(lanes, (1, heads))
    angle = time_rows[:, :, None] * lanes[0] + (grid_row[:, None] * lanes[1] + grid_col[:, None] * lanes[2])[None]

    def extra_of(per_frame, fill):
        both = jnp.repeat(per_frame, 2).reshape(sources, 2 * frames_local)
        pad = jnp.full((sources, EXTRA - 2 * frames_local), fill, both.dtype)
        return jnp.concatenate([both, pad], 1).reshape(-1)

    extra = sources * EXTRA
    key_frame = jnp.where(live_extra, at[:, None], -1).reshape(sources, 2 * frames_local)
    key_frame = jnp.concatenate(
        [key_frame, jnp.full((sources, EXTRA - 2 * frames_local), -1, jnp.int32)], 1
    ).reshape(-1)
    query_start = extra_of(begin, FAR)
    query_frame = extra_of(at, -1)

    def column(vector):
        return jnp.broadcast_to(vector[:, None], (extra, 128))

    def row(vector):
        return jnp.broadcast_to(vector[None], (8, extra))

    return (
        live_rows,
        jnp.cos(angle),
        jnp.sin(angle),
        (begin, column(key_frame), row(query_start), row(query_frame), column((query_start == FAR).astype(jnp.int32))),
    )


def turn_matrix(width):
    turn = np.zeros((width, width), np.float32)
    step = HEAD // 2
    for h in range(width // HEAD):
        for d in range(HEAD):
            if d < 6 * PAIRS:
                a, rest = divmod(d, 2 * PAIRS)
                side, k = divmod(rest, PAIRS)
                to = side * (width // 2) + h * step + a * PAIRS + k
            else:
                side, k = divmod(d - 6 * PAIRS, step - 3 * PAIRS)
                to = side * (width // 2) + h * step + 3 * PAIRS + k
            turn[h * HEAD + d, to] = 1.0
    return turn


SMEM_REF = pl.BlockSpec(memory_space=pltpu.SMEM)
VMEM_REF = pl.BlockSpec(memory_space=pltpu.VMEM)


ANY_REF = pl.BlockSpec(memory_space=pl.ANY)


def cost(flops=0, bytes_accessed=0, transcendentals=0):
    return pl.CostEstimate(flops=flops, bytes_accessed=bytes_accessed, transcendentals=transcendentals)


def waiting(kernel, inputs, waits, carried=0, outputs=None):
    if not waits:
        return kernel

    def run(*refs):
        used = [*refs[:inputs], *refs[inputs + len(waits) :]]
        if carried:
            del used[inputs + outputs : inputs + outputs + carried]
        kernel(*used)

    return run


def local_call(kernel, name, inputs, outputs, scratch=(), smem=0, flops=0, transcendentals=0, waits=(), carry=()):
    first = len(inputs) + len(waits)
    waits = [*waits, *carry]
    size = sum(math.prod(a.shape) * a.dtype.itemsize for a in [*inputs, *outputs])
    return pl.pallas_call(
        waiting(kernel, len(inputs), waits, len(carry), len(outputs)),
        in_specs=[SMEM_REF] * smem + [VMEM_REF] * (len(inputs) - smem) + [ANY_REF] * len(waits),
        out_specs=[VMEM_REF] * len(outputs) + [ANY_REF] * len(carry),
        out_shape=[*outputs] + [shape_of(*c.shape, dtype=c.dtype) for c in carry],
        input_output_aliases={first + i: len(outputs) + i for i in range(len(carry))},
        scratch_shapes=list(scratch),
        compiler_params=pltpu.CompilerParams(vmem_limit_bytes=VMEM),
        cost_estimate=cost(flops=1, bytes_accessed=1, transcendentals=0),
        name=name,
    )(*inputs, *waits)


def shape_of(*shape, dtype=BF):
    return jax.ShapeDtypeStruct(shape, dtype)


def stack_kernel(*refs):
    for i, ref in enumerate(refs[:-1]):
        refs[-1][i] = ref[...]


def stack_call(pieces, waits=()):
    return local_call(stack_kernel, "stack", pieces, [shape_of(len(pieces), *pieces[0].shape)], waits=waits)[0]


def add_piece_kernel(pieces, other, *outs):
    if len(outs) == 1:
        outs[0][...] = (pieces[0].astype(F32) + other[...].astype(F32)).astype(BF)
    else:
        for i, out in enumerate(outs):
            out[...] = (pieces[0, i].astype(F32) + other[i].astype(F32)).astype(BF)


def add_apart_kernel(one, two, *outs):
    for i, out in enumerate(outs):
        out[...] = (one[i].astype(F32) + two[i].astype(F32)).astype(BF)


def add_apart_call(one, two, waits, carry=()):
    return local_call(
        add_apart_kernel, "add", [one, two], [shape_of(*one.shape[1:])] * one.shape[0], waits=waits, carry=carry
    )


def add_piece_call(pieces, index, other, waits, apart=False):
    outs = [other.shape[1:]] * other.shape[0] if apart else [other.shape]
    block = pl.BlockSpec((1,) + other.shape, lambda i: (index,) + (0,) * other.ndim)

    def whole(shape):
        return pl.BlockSpec(shape, lambda i: (0,) * len(shape))

    result = pl.pallas_call(
        waiting(add_piece_kernel, 2, waits),
        grid=(1,),
        in_specs=[block, whole(other.shape)] + [ANY_REF] * len(waits),
        out_specs=[whole(o) for o in outs],
        out_shape=[shape_of(*o) for o in outs],
        compiler_params=pltpu.CompilerParams(vmem_limit_bytes=VMEM),
        cost_estimate=cost(flops=1, bytes_accessed=1, transcendentals=0),
        name="add_piece",
    )(pieces, other, *waits)
    return result if apart else result[0]


def copy_kernel(source, out):
    out[...] = source[...]


def copy_call(array, waits):
    return local_call(copy_kernel, "copy", [array], [shape_of(*array.shape)], waits=waits)[0]


def add_kernel(*refs):
    total = refs[0][...].astype(F32)
    for ref in refs[1:-1]:
        total = total + ref[...].astype(F32)
    refs[-1][...] = total.astype(refs[-1].dtype)


def add_call(pieces, waits=(), dtype=BF):
    return local_call(add_kernel, "add", pieces, [shape_of(*pieces[0].shape, dtype=dtype)], waits=waits)[0]


def span(index, size):
    return pl.ds(pl.multiple_of(index * size, size), size)


def front_kernel(*refs):
    *sources, entered, near, feed, entered_out = refs
    for s in range(4):
        near[s] = sources[s][...]
        feed[s] = sources[4 + s][...]
    entered_out[...] = entered[...]


def pack_kernel(n_z, place, near, far, own, one, two, three, vectors, bias, expand_bias):
    y, z, shard = place[1], place[2], place[4]
    rows = own.shape[0]
    width = bias.shape[1] // 3
    part = near.shape[2]
    chunks = part // 128
    d_part = D // (2 * n_z)
    outs = (own, one, two, three)

    def source(dp):
        return (dp % 2) ^ y, (z - dp // 2 + n_z) % n_z

    for m in range(4):
        target = shard ^ m
        for i in range(3 * width // 128):
            j = (i // 2) * (D // 128) + 2 * target + i % 2
            side, s = source(j // chunks)
            lanes = pl.ds(pl.multiple_of((j % chunks) * 128, 128), 128)
            at = slice(i * 128, (i + 1) * 128)

            @pl.when(side == 0)
            def _(m=m, s=s, lanes=lanes, at=at):
                outs[m][:, at] = near[s, :rows, lanes]

            @pl.when(side == 1)
            def _(m=m, s=s, lanes=lanes, at=at):
                outs[m][:, at] = far[s, :rows, lanes]

            if m == 0:

                @pl.when(side == 0)
                def _(s=s, lanes=lanes, at=at):
                    bias[:, at] = near[s, rows + 6 : rows + 7, lanes].astype(F32)

                @pl.when(side == 1)
                def _(s=s, lanes=lanes, at=at):
                    bias[:, at] = far[s, rows + 6 : rows + 7, lanes].astype(F32)

    quarter = FF // (8 * n_z)
    for s in range(n_z):
        for side, ref in ((0, near), (1, far)):
            dp = 2 * ((z - s + n_z) % n_z) + (y ^ side)
            block = ref[s, rows : rows + 16].astype(F32)
            vectors[:, span(dp, d_part)] = block[:8, :d_part]
            picked = block[7:8, :quarter]
            for f in range(1, 4):
                picked = jnp.where(shard == f, block[7 + f : 8 + f, :quarter], picked)
            expand_bias[s, :, side * quarter : (side + 1) * quarter] = picked


def enter_kernel(place, e0, e1, e2, e3, w0, w1, w2, w3, bias, vectors, turn, cosine, sine, q, k, v, normed, triple, scratch, entered, weight, add):
    shard = place[4]
    width = q.shape[-1]
    half = width // 2
    step = pl.program_id(0)

    @pl.when(step == 0)
    def _():
        for m, ref in enumerate((w0, w1, w2, w3)):
            rows = span(shard ^ m, ref.shape[0])
            triple[rows, :] = ref[...]
            for part in range(2):
                at = slice(part * width, (part + 1) * width)
                weight[rows, at] = nn(ref[:, at], turn[...]).astype(BF)
            weight[rows, 2 * width :] = ref[:, 2 * width :]
        low = jnp.broadcast_to(bias[...], (8, 3 * width)).astype(BF)
        for part in range(2):
            at = slice(part * width, (part + 1) * width)
            add[:, at] = nn(low[:, at], turn[...])
        add[:, 2 * width :] = low[:, 2 * width :].astype(F32)

    for m, ref in enumerate((e0, e1, e2, e3)):

        @pl.when(step == m)
        def _(ref=ref):
            entered[...] = ref[...]

    values = entered[...].astype(F32)
    unit, _ = norm_parts(values)
    rows = (unit * vectors[0:1] + vectors[1:2]).astype(BF)
    normed[0] = rows
    scratch[...] = rows
    cos = cosine[0]
    sin = sine[0]
    for part, out in ((0, q), (1, k)):
        at = slice(part * width, (part + 1) * width)
        value = nn(scratch[...], weight[:, at]) + add[:1, at]
        first = value[:, :half]
        second = value[:, half:]
        out[0, :, :half] = (first * cos - second * sin).astype(BF)
        out[0, :, half:] = (second * cos + first * sin).astype(BF)
    v[0] = (nn(scratch[...], weight[:, 2 * width :]) + add[:1, 2 * width :]).astype(BF)


def enter_call(place, entered, weights, bias, vectors, turn, cosine, sine, waits, carry):
    rows = entered[0].shape[0]
    width = bias.shape[-1] // 3

    def whole(array):
        return pl.BlockSpec(array.shape, lambda m, p: (0,) * array.ndim)

    def moved(*shape):
        return pl.BlockSpec((1,) + shape, lambda m, p: (p[4] ^ m, 0, 0))

    flat = [*entered, *weights, bias, vectors, turn]
    waits = [*waits, carry]
    return pl.pallas_call(
        waiting(enter_kernel, 3 + len(flat), waits, 1, 5),
        grid_spec=pltpu.PrefetchScalarGridSpec(
            num_scalar_prefetch=1,
            grid=(4,),
            in_specs=[whole(a) for a in flat] + [moved(rows, width // 2)] * 2 + [ANY_REF] * len(waits),
            out_specs=[moved(rows, width)] * 3
            + [moved(rows, D), pl.BlockSpec((D, 3 * width), lambda m, p: (0, 0)), ANY_REF],
            scratch_shapes=[
                pltpu.VMEM((rows, D), BF),
                pltpu.VMEM((rows, D), BF),
                pltpu.VMEM((D, 3 * width), BF),
                pltpu.VMEM((8, 3 * width), F32),
            ],
        ),
        out_shape=[shape_of(4, rows, width)] * 3
        + [shape_of(4, rows, D), shape_of(D, 3 * width), shape_of(*carry.shape)],
        input_output_aliases={2 + len(flat) + len(waits): 5},
        compiler_params=pltpu.CompilerParams(vmem_limit_bytes=VMEM),
        cost_estimate=cost(flops=8 * rows * D * 3 * width, bytes_accessed=30 * rows * D, transcendentals=0),
        name="enter",
    )(place, *flat, cosine, sine, *waits)


def part_kernel(place, mixed, own, far):
    x = place[0]
    for core in range(2):
        own[core] = mixed[2 * x + core]
        far[core] = mixed[2 * (1 - x) + core]


def project_kernel(place, own, far, output, keep, give, weight):
    x, core = place[0], place[3]
    _, rows, width = own.shape
    n_z = output.shape[0]
    d_part = output.shape[-1]
    for z in range(n_z):
        for y in range(2):
            at = (2 * z + y) * d_part
            for source in range(2):
                weight[source * width : (source + 1) * width, at : at + d_part] = output[z, y, source]

    def part(at):
        return nn(own[at], weight[span(x, width), :]) + nn(far[at], weight[span(1 - x, width), :])

    give[...] = part(1 - core).astype(BF)
    keep[...] = part(core)


def middle_kernel(entered, keep, other, vectors, middle, second):
    values = entered[...].astype(F32) + keep[...] + other[...].astype(F32) + vectors[2:3]
    middle[...] = values
    unit, _ = norm_parts(values)
    second[...] = (unit * vectors[3:4] + vectors[4:5]).astype(BF)


def rows_call(kernel, name, inputs, outputs, blocks=3, waits=()):
    rows = max(a.shape[0] for a in inputs)
    step = rows // blocks

    def spec(array):
        if array.shape[0] == 8:
            return pl.BlockSpec(array.shape, lambda i: (0, 0))
        return pl.BlockSpec((step, array.shape[1]), lambda i: (i, 0))

    size = sum(math.prod(a.shape) * a.dtype.itemsize for a in [*inputs, *outputs])
    return pl.pallas_call(
        waiting(kernel, len(inputs), waits),
        grid=(blocks,),
        in_specs=[spec(a) for a in inputs] + [ANY_REF] * len(waits),
        out_specs=[spec(a) for a in outputs],
        out_shape=list(outputs),
        compiler_params=pltpu.CompilerParams(vmem_limit_bytes=VMEM),
        cost_estimate=cost(flops=1, bytes_accessed=1, transcendentals=0),
        name=name,
    )(*inputs, *waits)


def add_rows(ref, rows):
    @pl.when(pl.program_id(0) == 0)
    def _():
        ref[...] = jnp.zeros_like(ref)

    for i, row in enumerate(rows):
        ref[i : i + 1] += jnp.sum(row, 0, keepdims=True)


def middle_back_kernel(middle, outer, keep, other, far, vectors, middle_grad, branch, sums):
    unit, scale = norm_parts(middle[...])
    grad = keep[...] + other[...].astype(F32) + far[...].astype(F32)
    result = outer[...].astype(F32) + norm_back(grad, unit, scale, vectors[3:4])
    middle_grad[...] = result
    low = result.astype(BF)
    branch[...] = low
    add_rows(sums, (low.astype(F32), grad * unit, grad, outer[...].astype(F32)))


def leave_rows(values, frames_local):
    pieces = []
    for l in range(frames_local):
        at = frames_local * PATCHES + 2 * l
        pieces += [values[at : at + 2], values[l * PATCHES : (l + 1) * PATCHES]]
    return jnp.concatenate(pieces, 0)


def output_kernel(frames_local, middle, keep, other, far, live, vectors, out):
    values = middle[...] + keep[...] + other[...].astype(F32) + far[...].astype(F32) + vectors[5:6]
    values = values * live[...]
    out[...] = leave_rows(values, frames_local).astype(BF)


def mixed_grad_kernel(place, branch, branch_other, weight, own, far):
    x, core = place[0], place[3]
    width = own.shape[-1]
    for at, rows in ((core, branch), (1 - core, branch_other)):
        own[at] = nt(rows[...], weight[span(x, width), :]).astype(BF)
        far[at] = nt(rows[...], weight[span(1 - x, width), :]).astype(BF)


def output_grad_kernel(place, own, far, branch, branch_other, near_y, far_y, rows_all, held):
    y, z, core = place[1], place[2], place[3]
    _, rows, width = own.shape
    _, n_z, _, d_part = near_y.shape
    rows_all[span(core, rows), :] = branch[...]
    rows_all[span(1 - core, rows), :] = branch_other[...]
    for i, ref in enumerate((own, far)):
        held[...] = tn(ref[...].reshape(2 * rows, width), rows_all[...]).astype(BF)
        for s in range(n_z):
            for flip, out in ((0, near_y), (1, far_y)):
                out[i, s] = held[:, span(2 * ((z + s) % n_z) + (y ^ flip), d_part)]


def triple_kernel(
    place, normed, triple_grad, grad_rows, triple, e0, e1, e2, e3, own, one, two, three, rows_own, rows_far, rows_give, bias, sums, entered, held
):
    step = pl.program_id(0)
    count, rows, wide = triple_grad.shape
    outs = (own, one, two, three)
    rows_outs = (rows_own, rows_give.at[0], rows_far, rows_give.at[1])

    @pl.when(step == 0)
    def _():
        bias[...] = jnp.zeros_like(bias)
        sums[...] = jnp.zeros_like(sums)

    for m, ref in enumerate((e0, e1, e2, e3)):

        @pl.when(step == m)
        def _(ref=ref):
            entered[...] = ref[...]

    flat = triple_grad[...].reshape(count * rows, wide)
    held[...] = tn(normed[...].reshape(count * rows, normed.shape[-1]), flat).astype(BF)
    back = nt(grad_rows[0], triple[...])
    unit, _ = norm_parts(entered[...].astype(F32))
    sums[0:1] += jnp.sum(back * unit, 0, keepdims=True)
    sums[1:2] += jnp.sum(back, 0, keepdims=True)
    entered[...] = back.astype(BF)
    bias[...] += jnp.sum(grad_rows[0].astype(F32), 0, keepdims=True)
    for m in range(4):

        @pl.when(step == m)
        def _(m=m):
            outs[m][...] = held[...]
            rows_outs[m][...] = entered[...]


def triple_call(place, normed, triple_grad, triple, entered, waits):
    count, rows, wide = triple_grad.shape
    part = D // count

    def fixed(shape):
        return pl.BlockSpec(shape, lambda m, p: (0,) * len(shape), pipeline_mode=pl.Buffered(1))

    outs = [shape_of(part, wide)] * 4 + [shape_of(rows, D)] * 2
    outs += [shape_of(2, rows, D), shape_of(1, wide, dtype=F32), shape_of(8, D, dtype=F32)]
    return pl.pallas_call(
        waiting(triple_kernel, 5 + len(entered), waits),
        grid_spec=pltpu.PrefetchScalarGridSpec(
            num_scalar_prefetch=1,
            grid=(count,),
            in_specs=[
                pl.BlockSpec((count, rows, part), lambda m, p: (0, 0, p[4] ^ m)),
                fixed(triple_grad.shape),
                pl.BlockSpec((1, rows, wide), lambda m, p: (p[4] ^ m, 0, 0)),
                fixed(triple.shape),
            ]
            + [fixed(e.shape) for e in entered]
            + [ANY_REF] * len(waits),
            out_specs=[fixed(o.shape) for o in outs],
            scratch_shapes=[pltpu.VMEM((rows, D), BF), pltpu.VMEM((part, wide), BF)],
        ),
        out_shape=outs,
        compiler_params=pltpu.CompilerParams(vmem_limit_bytes=VMEM),
        cost_estimate=cost(flops=4 * count * rows * wide * D, bytes_accessed=20 * rows * D, transcendentals=0),
        name="triple_grads",
    )(place, normed, triple_grad, triple_grad, triple, *entered, *waits)


def normed_sum_kernel(own, far, got, own_out, far_out):
    own_out[...] = (own[...].astype(F32) + got[0].astype(F32)).astype(BF)
    far_out[...] = (far[...].astype(F32) + got[1].astype(F32)).astype(BF)


def tail_sum_kernel(near, near_got, out, out_got, *totals):
    part = near.shape[-1]
    for s, total in enumerate(totals):
        total[:, :part] = (near[s].astype(F32) + near_got[s].astype(F32)).astype(BF)
        total[:, part:] = (out[0, s].astype(F32) + out_got[s].astype(F32)).astype(BF)


def unpack_kernel(n_z, place, p0, p1, p2, p3, near, far, held):
    y, z, shard = place[1], place[2], place[4]
    part = near.shape[2]
    chunks = part // 128
    for m, ref in enumerate((p0, p1, p2, p3)):
        held[shard ^ m] = ref[...]
    for j in range(3 * D // 128):
        dp, c = divmod(j, chunks)
        per = D // 128
        at = (j // per) * 256 + (j % 2) * 128
        chunk = held[(j % per) // 2, :, at : at + 128]
        s = (dp // 2 - z + n_z) % n_z

        @pl.when(y == dp % 2)
        def _(chunk=chunk, s=s, c=c):
            near[s, :, c * 128 : (c + 1) * 128] = chunk

        @pl.when(y != dp % 2)
        def _(chunk=chunk, s=s, c=c):
            far[s, :, c * 128 : (c + 1) * 128] = chunk


def tail_kernel(*refs):
    total = refs[0][...].astype(F32)
    for ref in refs[1:-2]:
        total = total + ref[...].astype(F32)
    part = refs[-2].shape[-1]
    refs[-2][...] = total[:, :part]
    refs[-1][...] = total[:, part:]


def leave_kernel(frames_local, entered, keep, other, middle_grad, live, vectors, out):
    unit, scale = norm_parts(entered[...].astype(F32))
    grad = keep[...].astype(F32) + other[...].astype(F32)
    result = (middle_grad[...] + norm_back(grad, unit, scale, vectors[0:1])) * live[...]
    out[...] = leave_rows(result, frames_local)


def split_kernel(place, expand, reduce, own, one, two, three):
    shard = place[4]
    rows = expand.shape[0]
    part = own.shape[1]
    blocks = reduce.shape[0] // (4 * part)
    for m, ref in enumerate((own, one, two, three)):
        to = shard ^ m
        ref[:rows] = expand[:, span(to, part)]
        for p in range(blocks):
            ref[rows + p * part : rows + (p + 1) * part] = reduce[span(p * 4 + to, part), :]


def join_kernel(place, own, one, two, three, expand, reduce):
    shard = place[4]
    rows = expand.shape[0]
    part = own.shape[1]
    blocks = reduce.shape[0] // (4 * part)
    for m, ref in enumerate((own, one, two, three)):
        at = shard ^ m
        expand[:, span(at, part)] = ref[:rows].astype(F32)
        for p in range(blocks):
            reduce[span(p * 4 + at, part), :] = ref[rows + p * part : rows + (p + 1) * part].astype(F32)


def fill_weights(place, near, far, weight_in, weight_out):
    y, z, shard = place[1], place[2], place[4]
    n_z = len(near)
    part = near[0].shape[-1]
    rows = D // 4
    for s in range(n_z):
        for side, ref in ((0, near[s]), (1, far[s])):
            if weight_in is not None:
                for m in range(4):
                    weight_in[s, span(shard ^ m, rows), side * part : (side + 1) * part] = ref[m, :rows]
            features = span(2 * ((z - s + n_z) % n_z) + (y ^ side), part)
            for tile in range(n_z):
                unit = (z - tile + n_z) % n_z
                for flip in range(2):
                    at = pl.ds(pl.multiple_of(rows + (y ^ flip) * part, part), part)
                    weight_out[tile, flip * part : (flip + 1) * part, features] = ref[unit ^ shard, at, :]


def feed_kernel(
    place, normal, normal_other, cot, cot_other, p0, p1, p2, p3, f0, f1, f2, f3, bias, active, slope, keep, give, d_bias, give_acc, weight_in, weight_out
):
    step = pl.program_id(0)
    rows = normal.shape[0]

    @pl.when(step == 0)
    def _():
        fill_weights(place, (p0, p1, p2, p3), (f0, f1, f2, f3), weight_in, weight_out)
        keep[...] = jnp.zeros_like(keep)
        give_acc[...] = jnp.zeros_like(give_acc)

    d_bias[...] = jnp.zeros_like(d_bias)
    for i, values, outer, total in ((0, normal, cot, keep), (1, normal_other, cot_other, give_acc)):
        act, gradient = gelu_parts(nn(values[...], weight_in[step]) + bias[0])
        grad = (nt(outer[...], weight_out[step]) * gradient).astype(BF)
        active[i * rows : (i + 1) * rows] = act.astype(BF)
        slope[i * rows : (i + 1) * rows] = grad
        d_bias[0] += jnp.sum(grad.astype(F32), 0, keepdims=True)
        total[...] += nt(grad, weight_in[step])

    @pl.when(step == pl.num_programs(0) - 1)
    def _():
        give[...] = give_acc[...].astype(BF)


def feed_grad_kernel(
    place,
    n0,
    n1,
    n2,
    n3,
    c0,
    c1,
    c2,
    c3,
    active,
    active_far,
    slope,
    slope_far,
    p0,
    p1,
    p2,
    p3,
    f0,
    f1,
    f2,
    f3,
    keep,
    give,
    keep_far,
    give_far,
    grads,
    sent,
    normal_t,
    cot_all,
    give_acc,
    keep_far_acc,
    give_far_acc,
    weight_out,
    held,
    active_all,
    slope_all,
):
    y, z, shard = place[1], place[2], place[4]
    step = pl.program_id(0)
    n_z = grads.shape[0]
    part = p0.shape[-1]
    rows = n0.shape[0]
    deep = D // 4
    totals = (keep, give_acc, keep_far_acc, give_far_acc)

    @pl.when(step == 0)
    def _():
        fill_weights(place, (p0, p1, p2, p3), (f0, f1, f2, f3), None, weight_out)
        for i, (normal, cot) in enumerate(((n0, c0), (n1, c1), (n2, c2), (n3, c3))):
            normal_t[:, i * rows : (i + 1) * rows] = normal[...].T
            cot_all[i * rows : (i + 1) * rows] = cot[...]
            totals[i][...] = jnp.zeros_like(totals[i])

    for i, (act, grad) in enumerate(((active, slope), (active_far, slope_far))):
        at = slice(i * 2 * rows, (i + 1) * 2 * rows)
        active_all[at] = act[...]
        slope_all[at] = grad[...]
        for j in range(2):
            totals[2 * i + j][...] += nn(act[j * rows : (j + 1) * rows], weight_out[step])

    held[...] = nn(normal_t[...], slope_all[...]).astype(BF)
    for side in range(2):
        for m in range(4):
            grads[(n_z - step) % n_z, side, m, :deep] = held[span(shard ^ m, deep), side * part : (side + 1) * part]
    held_t = weight_out.at[step]
    held_t[...] = tn(active_all[...], cot_all[...]).astype(BF)
    unit = (z - step + n_z) % n_z
    for side in range(2):
        at = pl.ds(pl.multiple_of(deep + (y ^ side) * part, part), part)
        for s in range(n_z):
            for flip in range(2):
                features = span(2 * ((z + s) % n_z) + (y ^ flip), part)
                grads[s, flip, unit ^ shard, at, :] = held_t[side * part : (side + 1) * part, features]

    @pl.when(step == pl.num_programs(0) - 1)
    def _():
        give[...] = give_acc[...].astype(BF)
        keep_far[...] = keep_far_acc[...].astype(BF)
        give_far[...] = give_far_acc[...].astype(BF)
        sent[...] = grads[n_z - 1]


def feed_specs(place, n_z):
    def whole(array):
        return pl.BlockSpec(array.shape, lambda t, p: (0,) * len(array.shape), pipeline_mode=pl.Buffered(1))

    def lanes(rows, wide):
        return pl.BlockSpec((rows, wide), lambda t, p: (0, t))

    return whole, lanes


def feed_split_call(place, normal, cot, parts, bias, waits=()):
    rows = normal[0].shape[0]
    n_z = len(parts) // 2
    wide = bias.shape[-1]
    whole, lanes = feed_specs(place, n_z)
    row = pl.BlockSpec((1, 1, wide), lambda t, p: (t, 0, 0))
    block = (rows, D)
    outs = [shape_of(2 * rows, n_z * wide)] * 2 + [shape_of(*block, dtype=F32), shape_of(*block)]
    outs += [shape_of(n_z, 1, wide, dtype=F32)]
    inputs = [*normal, *cot, *parts]
    return pl.pallas_call(
        waiting(feed_kernel, 2 + len(inputs), waits),
        grid_spec=pltpu.PrefetchScalarGridSpec(
            num_scalar_prefetch=1,
            grid=(n_z,),
            in_specs=[whole(a) for a in inputs] + [row] + [ANY_REF] * len(waits),
            out_specs=[lanes(2 * rows, wide)] * 2 + [whole(o) for o in outs[2:4]] + [row],
            scratch_shapes=[pltpu.VMEM(block, F32), pltpu.VMEM((n_z, D, wide), BF), pltpu.VMEM((n_z, wide, D), BF)],
        ),
        out_shape=outs,
        compiler_params=pltpu.CompilerParams(vmem_limit_bytes=VMEM),
        cost_estimate=cost(
            flops=12 * rows * D * wide * n_z, bytes_accessed=20 * rows * D, transcendentals=4 * rows * wide * n_z
        ),
        name="feed_forward",
    )(place, *inputs, bias, *waits)


def feed_grad_call(place, normal, cot, active, slope, parts, waits=()):
    rows = normal[0].shape[0]
    n_z = len(parts) // 2
    wide = active[0].shape[1] // n_z
    whole, lanes = feed_specs(place, n_z)
    block = (rows, D)
    outs = [shape_of(*block, dtype=F32)] + [shape_of(*block)] * 3 + [shape_of(n_z, 2, *parts[0].shape), shape_of(2, *parts[0].shape)]
    first = [*normal, *cot]
    tiles = [*active, *slope]
    return pl.pallas_call(
        waiting(feed_grad_kernel, 1 + len(first) + len(tiles) + 2 * n_z, waits),
        grid_spec=pltpu.PrefetchScalarGridSpec(
            num_scalar_prefetch=1,
            grid=(n_z,),
            in_specs=[whole(a) for a in first]
            + [lanes(2 * rows, wide)] * 4
            + [whole(p) for p in parts]
            + [ANY_REF] * len(waits),
            out_specs=[whole(o) for o in outs],
            scratch_shapes=[
                pltpu.VMEM((D, 4 * rows), BF),
                pltpu.VMEM((4 * rows, D), BF),
                pltpu.VMEM(block, F32),
                pltpu.VMEM(block, F32),
                pltpu.VMEM(block, F32),
                pltpu.VMEM((n_z, wide, D), BF),
                pltpu.VMEM((D, wide), BF),
                pltpu.VMEM((4 * rows, wide), BF),
                pltpu.VMEM((4 * rows, wide), BF),
            ],
        ),
        out_shape=outs,
        compiler_params=pltpu.CompilerParams(vmem_limit_bytes=VMEM),
        cost_estimate=cost(flops=24 * rows * D * wide * n_z, bytes_accessed=40 * rows * D),
        name="feed_grads",
    )(place, *first, *tiles, *parts, *waits)


def torus_shards(sizes, *args):
    (
        tokens,
        cotangent,
        frame_counts,
        presence,
        attend_gain,
        attend_shift,
        triple_weight,
        triple_bias,
        output_weight,
        output_bias,
        second_gain,
        second_shift,
        expand_weight,
        expand_bias,
        reduce_weight,
        reduce_bias,
    ) = args
    n_z, n_y, n_x = sizes
    n_dp = n_z * n_y
    n_f = n_x * 2
    width = D // n_f
    local_rows = tokens.shape[1]
    frames_local = local_rows // ROW_FRAME
    rows = frames_local * PATCHES + EXTRA
    z, y, x, core = (lax.axis_index(name) for name in ("z", "y", "x", "core"))
    shard = x * 2 + core
    place = jnp.stack([x, y, z, core, shard]).astype(jnp.int32)
    d_part = D // n_dp
    qkv_part = 3 * D // n_dp
    ff_part = FF // n_dp
    quarter = ff_part // 4

    def swap(array, axis="core"):
        return lax.ppermute(array, axis, [(0, 1), (1, 0)])

    def cross_over(array):
        return lax.ppermute(array, ("x", "core"), [(i, i ^ 3) for i in range(4)])

    def to_z(array, s):
        return lax.ppermute(array, "z", [(i, (i + s) % n_z) for i in range(n_z)])

    def take(array, index, axis=0):
        return lax.dynamic_index_in_dim(array, index, axis, False)

    def gather_z(array):
        return [array] + [to_z(array, s) for s in range(1, n_z)]

    def scatter_z(array, waits=(), dtype=BF):
        return add_call([array[0]] + [to_z(array[s], s) for s in range(1, n_z)], waits, dtype)

    small = [attend_gain, attend_shift, output_bias, second_gain, second_shift, reduce_bias]
    small = jnp.concatenate([v.reshape(1, d_part) for v in small], 0)
    packed = jnp.concatenate(
        [
            triple_weight,
            jnp.pad(small, ((0, 0), (0, qkv_part - d_part))),
            triple_bias.reshape(1, qkv_part),
            jnp.pad(expand_bias.reshape(4, quarter), ((0, 5), (0, qkv_part - quarter))),
        ],
        0,
    )
    live_all = tables(frame_counts[0], presence[0], n_f, frames_local, width // HEAD)[0]
    live = take(live_all, shard)[:, None]
    entered = to_block(tokens[0], frames_local) * live.astype(BF)
    outer = to_block(cotangent[0], frames_local) * live.astype(BF)

    own, one, two, three, packed = local_call(
        split_kernel,
        "split",
        [place, expand_weight, reduce_weight],
        [shape_of(2 * (D // n_f), d_part)] * 4,
        smem=1,
        carry=[packed],
    )
    packed_parts = gather_z(packed)
    feed = [own, swap(one), swap(two, "x"), cross_over(three)]
    near, feed, entered = local_call(
        front_kernel,
        "front",
        [*packed_parts, *feed, entered],
        [shape_of(n_z, *packed.shape), shape_of(4, *own.shape), shape_of(*entered.shape)],
    )
    far = swap(near, "y")
    entered_x = swap(entered, "x")
    entered_all = [entered, swap(entered), entered_x]
    output_all = lax.all_gather(output_weight, ("z", "y", "x"), axis=0).reshape(n_z, n_y, n_x, width, d_part)

    own, one, two, three, vectors, bias, expand_add, counts = local_call(
        functools.partial(pack_kernel, n_z),
        "pack",
        [place, near, far],
        [shape_of(D // n_f, 3 * width)] * 4
        + [shape_of(8, D, dtype=F32), shape_of(1, 3 * width, dtype=F32), shape_of(n_z, 1, 2 * quarter, dtype=F32)],
        smem=1,
        waits=[entered_all[1]],
        carry=[frame_counts],
    )
    _, cosine, sine, guides = tables(counts[0], presence[0], n_f, frames_local, width // HEAD)
    weights = [own, swap(one), swap(two, "x"), cross_over(three)]
    entered_all.append(swap(copy_call(entered_x, [own])))
    feed_near = gather_z(feed)
    turn = jnp.asarray(turn_matrix(width), BF)
    q, k, v, normed, triple, outer = enter_call(
        place, entered_all, weights, bias, vectors, turn, cosine, sine, feed_near[1:2], outer
    )
    feed_far = [swap(part, "y") for part in feed_near]
    feed_parts = [*feed_near, *feed_far]
    outer_x = swap(outer, "x")
    outer_all = [outer, swap(outer), outer_x]
    mixed, exact, logs, logs_extra = attend_call(*guides, q, k, v, waits=feed_near[2:])
    mixed_own, mixed_far, outer_x = local_call(
        part_kernel,
        "mixed_parts",
        [place, mixed],
        [shape_of(2, rows, width)] * 2,
        smem=1,
        waits=[*feed_far[:3], outer_all[1]],
        carry=[outer_x],
    )
    mixed_far = swap(mixed_far, "x")
    outer_all = [*outer_all[:2], outer_x, swap(outer_x)]
    keep, give = local_call(
        project_kernel,
        "project",
        [place, mixed_own, mixed_far, output_all],
        [shape_of(rows, D, dtype=F32), shape_of(rows, D)],
        [pltpu.VMEM((D // 2, D), BF)],
        smem=1,
        flops=4 * rows * D * D // 2,
        waits=[outer_all[3], feed_far[3]],
    )
    output_full = output_all.transpose(2, 3, 0, 1, 4).reshape(D // 2, D)
    middle, second = rows_call(
        middle_kernel,
        "middle",
        [entered, keep, swap(give), vectors],
        [shape_of(rows, D, dtype=F32), shape_of(rows, D)],
    )
    second_all = [second, swap(second)]
    feed_both = [feed_parts, expand_add]
    active, slope, back, back_give, d_bias = feed_split_call(place, second_all, outer_all[:2], *feed_both)
    second_x = swap(second, "x")
    second_all += [second_x, swap(copy_call(second_x, [active]))]
    active_far, slope_far, back_far, back_far_give, d_bias_far = feed_split_call(
        place, second_all[2:], outer_all[2:], *feed_both, waits=[back_give]
    )
    back_give = swap(back_give)
    back_far = swap(add_call([back_far, swap(back_far_give)]), "x")
    final, final_give, final_far, final_far_give, d_feed, d_sent = feed_grad_call(
        place, second_all, outer_all, [active, active_far], [slope, slope_far], feed_parts
    )
    middle_grad, branch, sums_two = rows_call(
        middle_back_kernel,
        "middle_back",
        [middle, outer, back, back_give, back_far, vectors],
        [shape_of(rows, D, dtype=F32), shape_of(rows, D), shape_of(8, D, dtype=F32)],
        waits=[d_sent],
    )
    branch_other = swap(branch)
    grad_own, grad_far = local_call(
        mixed_grad_kernel,
        "mixed_grad",
        [place, branch, branch_other, output_full],
        [shape_of(2, rows, width)] * 2,
        smem=1,
        flops=4 * rows * D * D // 2,
    )
    grad_far = swap(grad_far, "x")
    out_near, out_far = local_call(
        output_grad_kernel,
        "output_weight_grad",
        [place, mixed_own, mixed_far, branch, branch_other],
        [shape_of(n_x, n_z, width, d_part)] * 2,
        [pltpu.VMEM((2 * rows, D), BF), pltpu.VMEM((width, D), BF)],
        smem=1,
        flops=4 * rows * D * D // 2,
        waits=[grad_own],
    )
    out_far = swap(out_far, "y")
    final_far = add_call([final_far, swap(final_far_give)], [grad_own])
    final_far = swap(final_far, "x")
    final_give = swap(final_give)
    triple_grad = attend_back_call(
        x.reshape(1), *guides, q, k, v, [grad_own, grad_far], exact, logs, logs_extra, cosine, sine, turn, waits=[out_near, final_give]
    )
    back_feed = to_z(d_sent, 1)
    tri_own, tri_one, tri_two, tri_three, normed_own, normed_far, normed_give, d_triple_bias, sums_one = triple_call(
        place, normed, triple_grad, triple, entered_all, [back_feed, out_far, final_far]
    )
    pieces = [tri_own, swap(tri_one), swap(tri_two, "x"), cross_over(tri_three)]
    zero_qkv = jnp.zeros((3, n_f, width), F32)
    triple_bias_part = lax.dynamic_update_slice(zero_qkv, d_triple_bias.reshape(3, 1, width), (0, shard, 0))
    expand_bias_part = jnp.zeros((n_z, n_y, n_f, quarter), F32)
    d_bias = (d_bias + d_bias_far).reshape(n_z, n_y, quarter)
    for s in range(n_z):
        for side in range(n_y):
            expand_bias_part = lax.dynamic_update_slice(
                expand_bias_part, d_bias[s, side].reshape(1, 1, 1, quarter), ((z - s) % n_z, y ^ side, shard, 0)
            )
    sums = [sums_one[0], sums_one[1], sums_two[0], sums_two[1], sums_two[2], sums_two[3], triple_bias_part, expand_bias_part]
    sums = jnp.concatenate([piece.reshape(n_dp, -1) for piece in sums], 1)

    def butterfly(sums, bits):
        for bit in bits:
            sums = sums + lax.ppermute(sums, ("z", "y", "x", "core"), [(i, i ^ bit) for i in range(32)])
        return sums

    back_feed = add_piece_call(d_feed, 2, back_feed, [tri_own])
    back_feed = to_z(back_feed, 1)
    out_near, out_send = add_apart_call(out_near, out_far, [tri_own])
    out_far = swap(out_send, "x")
    block_output = local_call(
        functools.partial(output_kernel, frames_local),
        "block_output",
        [middle, final, final_give, final_far, live, vectors],
        [shape_of(local_rows, D)],
        waits=[out_near],
    )[0]
    normed_own, normed_far = local_call(
        normed_sum_kernel,
        "normed_sum",
        [normed_own, normed_far, swap(normed_give)],
        [shape_of(rows, D)] * 2,
        waits=pieces[1:],
    )
    normed_far = swap(normed_far, "x")
    tri_near, tri_far, sums = local_call(
        functools.partial(unpack_kernel, n_z),
        "unpack",
        [place, *pieces],
        [shape_of(n_z, D // n_f, qkv_part)] * 2,
        [pltpu.VMEM((4, D // n_f, 3 * width), BF)],
        smem=1,
        waits=[block_output, normed_own, out_far],
        carry=[sums],
    )
    tri_far = swap(tri_far, "y")
    back_feed = add_piece_call(d_feed, 1, back_feed, [tri_near])
    back_feed = to_z(back_feed, 1)
    sums = butterfly(sums, (1, 4))
    tail = local_call(
        tail_sum_kernel,
        "tail_sum",
        [tri_near, tri_far, out_near[None], out_far],
        [shape_of(D // n_f, qkv_part + d_part)] * n_z,
        waits=[sums],
    )
    tail_parts = [tail[0]] + [to_z(tail[s], s) for s in range(1, n_z)]
    d_near, d_send = add_piece_call(d_feed, 0, back_feed, [tail[0]], True)
    tokens_grad = local_call(
        functools.partial(leave_kernel, frames_local),
        "tokens_grad",
        [entered, normed_own, normed_far, middle_grad, live, vectors],
        [shape_of(local_rows, D, dtype=F32)],
        waits=[tail[0], d_near],
    )[0]
    triple_weight_grad, output_weight_grad = local_call(
        tail_kernel,
        "tail",
        tail_parts,
        [shape_of(D // n_f, qkv_part, dtype=F32), shape_of(D // n_f, d_part, dtype=F32)],
        waits=[tokens_grad],
    )
    *d_feed, sums = add_apart_call(d_near, swap(d_send, "y"), [triple_weight_grad], [sums])
    sums = butterfly(sums, (2, 8, 16))
    expand_weight_grad, reduce_weight_grad = local_call(
        join_kernel,
        "join",
        [place, d_feed[0], swap(d_feed[1]), swap(d_feed[2], "x"), cross_over(d_feed[3])],
        [shape_of(D // n_f, ff_part, dtype=F32), shape_of(FF // n_f, d_part, dtype=F32)],
        smem=1,
    )

    sums = take(sums, z * n_y + y)
    parts = [sums[i * d_part : (i + 1) * d_part] for i in range(6)]
    rest = sums[6 * d_part :]
    return (
        block_output[None],
        tokens_grad[None],
        parts[0],
        parts[1],
        triple_weight_grad,
        rest[:qkv_part],
        output_weight_grad,
        parts[2],
        parts[3],
        parts[4],
        expand_weight_grad,
        rest[qkv_part:],
        reduce_weight_grad,
        parts[5],
    )


def general_shards(sizes, *args):
    (
        tokens,
        cotangent,
        frame_counts,
        presence,
        attend_gain,
        attend_shift,
        triple_weight,
        triple_bias,
        output_weight,
        output_bias,
        second_gain,
        second_shift,
        expand_weight,
        expand_bias,
        reduce_weight,
        reduce_bias,
    ) = args
    n_z, n_y, n_x = sizes
    n_dp = n_z * n_y
    n_f = n_x * 2
    heads = HEADS // n_f
    width = heads * HEAD
    local_rows = tokens.shape[1]
    frames_local = local_rows // ROW_FRAME
    rows = frames_local * PATCHES + EXTRA
    z, y, x, core = (lax.axis_index(name) for name in ("z", "y", "x", "core"))
    shard = x * 2 + core
    d_part = D // n_dp
    ff_part = FF // n_dp
    ff_half = ff_part // 2
    blocks = n_dp // n_f

    def swap(array, axis="core"):
        return lax.ppermute(array, axis, [(0, 1), (1, 0)])

    def take(array, index, axis=0):
        return lax.dynamic_index_in_dim(array, index, axis, False)

    def ordered(index, own, other, axis=0):
        low = jnp.where(index == 0, own, other)
        high = jnp.where(index == 0, other, own)
        return jnp.concatenate([low, high], axis)

    def both_cores(array, axis=0):
        return ordered(core, array, swap(array), axis)

    def exchange_f(array):
        return lax.all_to_all(array, ("x", "core"), 0, 0, tiled=True)

    def over_x(array):
        return lax.all_to_all(array, "x", 0, 0, tiled=True)

    vectors = [attend_gain, attend_shift, output_bias, second_gain, second_shift, reduce_bias, triple_bias, expand_bias]
    flat = jnp.concatenate(vectors)
    qkv_part = 3 * D // n_dp
    flat = jnp.pad(flat, (0, 16 * qkv_part - flat.shape[0])).reshape(16, qkv_part)
    packed = jnp.concatenate([triple_weight, flat], 0)
    packed = lax.all_gather(packed, ("z", "y"), axis=0)
    small = packed[:, D // n_f :].reshape(n_dp, -1)
    full = []
    at = 0
    for vector in vectors:
        full.append(small[:, at : at + vector.shape[0]].reshape(-1))
        at += vector.shape[0]
    gain_one, shift_one, output_add, gain_two, shift_two, reduce_add = (v.astype(F32)[None] for v in full[:6])
    triple_add, expand_add = full[6], full[7]
    triple_rows = packed[:, : D // n_f].transpose(1, 0, 2).reshape(D // n_f, 3, n_f, width)
    triple_own = exchange_f(triple_rows.transpose(2, 0, 1, 3)).reshape(D, 3 * width)
    bias_own = take(triple_add.reshape(3, n_f, width), shard, 1).reshape(1, 3 * width)

    expand_split = expand_weight.reshape(D // n_f, 2, ff_half)
    expand_chip = ordered(core, take(expand_split, core, 1), swap(take(expand_split, 1 - core, 1)))
    reduce_split = reduce_weight.reshape(blocks, 2, ff_half, d_part)
    reduce_chip = ordered(core, take(reduce_split, core, 1)[None], swap(take(reduce_split, 1 - core, 1))[None])
    expand_add_own = take(expand_add.reshape(n_z, n_y, 2, ff_half), core, 2)
    expand_all = lax.all_gather(expand_chip, ("z", "y", "x"), axis=0).reshape(n_z, n_y, D, ff_half)
    expand_pieces = [expand_all.transpose(0, 2, 1, 3).reshape(n_z, D, n_y * ff_half)]
    reduce_all = lax.all_gather(reduce_chip, ("z", "y", "x"), axis=0)
    reduce_pieces = [
        reduce_all.reshape(n_dp, n_dp, ff_half, d_part).transpose(1, 2, 0, 3).reshape(n_z, n_y * ff_half, D)
    ]
    expand_add_own = expand_add_own.reshape(n_z, 1, n_y * ff_half)
    output_all = lax.all_gather(output_weight, ("z", "y", "x"), axis=0)
    output_all = output_all.reshape(n_dp, n_x * width, d_part).transpose(1, 0, 2).reshape(n_x * width, D)

    live_all, cosine, sine, guides = tables(frame_counts[0], presence[0], n_f, frames_local, heads)
    live = take(live_all, shard)[:, None]
    entered = to_block(tokens[0], frames_local).astype(F32) * live
    outer = to_block(cotangent[0], frames_local).astype(F32) * live
    outer_low = outer.astype(BF)
    outer_chip = both_cores(outer_low)
    outer_chip_t = outer_chip.T
    unit_one, scale_one = norm_parts(entered)
    normed = (unit_one * gain_one + shift_one).astype(BF)
    normed_all = lax.all_gather(normed, ("x", "core"), axis=0)

    turned = jnp.asarray(turn_matrix(width), BF)
    q, k, v = qkv_call(normed_all, triple_own, bias_own, turned, cosine, sine)
    mixed, exact, logs, logs_extra = attend_call(*guides, q, k, v)

    mixed_chip = over_x(mixed.reshape(n_x, 2 * rows, width)).transpose(1, 0, 2).reshape(2 * rows, n_x * width)
    branch_part = nn(mixed_chip, output_all).reshape(2, rows, D)
    branch = take(branch_part, core) + swap(take(branch_part, 1 - core).astype(BF)).astype(F32)
    middle = entered + branch + output_add
    unit_two, scale_two = norm_parts(middle)
    second = (unit_two * gain_two + shift_two).astype(BF)
    second_chip = both_cores(second)
    final, second_grad, d_expand_bias, *d_feed = feed_call(
        second_chip, outer_chip, outer_chip_t, expand_pieces[0], expand_add_own, reduce_pieces[0]
    )
    second_grad = second_grad.reshape(2, rows, D)
    second_grad = take(second_grad, core) + swap(take(second_grad, 1 - core).astype(BF)).astype(F32)
    final = final.reshape(2, rows, D)
    final = take(final, core) + swap(take(final, 1 - core).astype(BF)).astype(F32)
    block_output = ((middle + final + reduce_add) * live).astype(BF)

    middle_grad = outer + norm_back(second_grad, unit_two, scale_two, gain_two)
    second_gain_grad = jnp.sum(second_grad * unit_two, 0)
    second_shift_grad = jnp.sum(second_grad, 0)
    branch_low = middle_grad.astype(BF)
    branch_chip = both_cores(branch_low)
    mixed_grad = nt(branch_chip, output_all).astype(BF)
    mixed_grad = over_x(mixed_grad.reshape(2 * rows, n_x, width).transpose(1, 0, 2)).reshape(n_f, rows, width)
    d_output = tn(mixed_chip, branch_chip).astype(BF)
    triple_grad = attend_back_call(
        jnp.zeros((1,), jnp.int32), *guides, q, k, v, list(mixed_grad.reshape(n_x, 2, rows, width)), exact, logs, logs_extra, cosine, sine, turned)
    natural = triple_grad.reshape(n_f * rows, 3 * width)
    d_triple = tn(normed_all.reshape(n_f * rows, D), natural).astype(BF)
    d_triple_bias = jnp.sum(natural.astype(F32), 0)
    normed_grad = nt(natural, triple_own).astype(BF)
    normed_grad = lax.psum_scatter(normed_grad, ("x", "core"), scatter_dimension=0, tiled=True).astype(F32)
    attend_gain_grad = jnp.sum(normed_grad * unit_one, 0)
    attend_shift_grad = jnp.sum(normed_grad, 0)
    tokens_grad = (middle_grad + norm_back(normed_grad, unit_one, scale_one, gain_one)) * live

    d_triple = exchange_f(d_triple.reshape(n_f, D // n_f, 3, width))
    d_triple = d_triple.transpose(1, 2, 0, 3).reshape(D // n_f, n_z, n_y, qkv_part)
    d_triple = d_triple.reshape(D // n_f, 3 * D)
    triple_weight_grad = lax.psum_scatter(d_triple, ("z", "y"), scatter_dimension=1, tiled=True).astype(F32)
    d_output = d_output.reshape(n_x, width, n_dp, d_part).transpose(2, 0, 1, 3).reshape(n_dp * n_x * width, d_part)
    output_weight_grad = lax.psum_scatter(d_output, ("z", "y", "x"), scatter_dimension=0, tiled=True).astype(F32)
    d_expand, d_reduce = d_feed
    d_expand = d_expand.reshape(n_z, D, n_y, ff_half).transpose(0, 2, 1, 3).reshape(n_dp * D, ff_half)
    d_expand = lax.psum_scatter(d_expand, ("z", "y", "x"), scatter_dimension=0, tiled=True)
    d_expand = d_expand.reshape(2, D // n_f, ff_half)
    d_reduce = d_reduce.reshape(n_z, n_dp, d_part, n_y, ff_half).transpose(1, 0, 3, 2, 4).reshape(-1, ff_half)
    d_reduce = lax.psum_scatter(d_reduce, ("z", "y", "x"), scatter_dimension=0, tiled=True)
    d_reduce = d_reduce.reshape(2, blocks, d_part, ff_half)
    expand_weight_grad = ordered(core, take(d_expand, core), swap(take(d_expand, 1 - core)), 1).astype(F32)
    reduce_weight_grad = jnp.stack(
        [
            jnp.where(core == 0, take(d_reduce, core), swap(take(d_reduce, 1 - core))),
            jnp.where(core == 0, swap(take(d_reduce, 1 - core)), take(d_reduce, core)),
        ],
        1,
    )
    reduce_weight_grad = reduce_weight_grad.transpose(0, 1, 3, 2).reshape(blocks * 2 * ff_half, d_part).astype(F32)

    zero_qkv = jnp.zeros((3, n_f, width), F32)
    triple_bias_part = lax.dynamic_update_slice(zero_qkv, d_triple_bias.reshape(3, 1, width), (0, shard, 0))
    d_expand_bias = d_expand_bias.reshape(n_z, n_y, ff_half)
    zero_ff = jnp.zeros((n_dp, 2, ff_half), F32)
    expand_bias_part = lax.dynamic_update_slice(zero_ff, d_expand_bias.reshape(n_dp, 1, ff_half), (0, core, 0))
    sums = [
        attend_gain_grad,
        attend_shift_grad,
        jnp.sum(branch_low.astype(F32), 0),
        second_gain_grad,
        second_shift_grad,
        jnp.sum(outer_low.astype(F32), 0),
        triple_bias_part.reshape(-1),
        expand_bias_part.reshape(-1),
    ]
    sums = jnp.concatenate([s.reshape(n_dp, -1) for s in sums], 1)
    total = n_dp * n_f
    bit = 1
    while bit < total:
        sums = sums + lax.ppermute(sums, ("z", "y", "x", "core"), [(i, i ^ bit) for i in range(total)])
        bit *= 2
    own = take(sums, z * n_y + y)
    parts = []
    at = 0
    for size in [d_part] * 6 + [qkv_part, ff_part]:
        parts.append(own[at : at + size])
        at += size
    return (
        from_block(block_output, frames_local),
        from_block(tokens_grad, frames_local),
        parts[0],
        parts[1],
        triple_weight_grad,
        parts[6],
        output_weight_grad,
        parts[2],
        parts[3],
        parts[4],
        expand_weight_grad,
        parts[7],
        reduce_weight_grad,
        parts[5],
    )


def solution(mesh):
    n_dp, n_f = mesh.shape["dp"], mesh.shape["fsdp"]
    sizes = (n_dp // 2, 2, n_f // 2)
    inner = jax.sharding.Mesh(mesh.devices.reshape(*sizes, 2), ("z", "y", "x", "core"))
    dp = ("z", "y")
    fsdp = ("x", "core")
    rows = P(dp, fsdp, None)
    weight = P(fsdp, dp)
    vector = P(dp)
    return jax.shard_map(
        functools.partial(torus_shards if sizes == (4, 2, 2) else general_shards, sizes),
        mesh=inner,
        in_specs=(
            rows,
            rows,
            P(dp, None),
            P(dp, None, None),
            vector,
            vector,
            weight,
            vector,
            weight,
            vector,
            vector,
            vector,
            weight,
            vector,
            weight,
            vector,
        ),
        out_specs=(
            rows,
            rows,
            vector,
            vector,
            weight,
            vector,
            weight,
            vector,
            vector,
            vector,
            weight,
            vector,
            weight,
            vector,
        ),
        check_vma=False,
    )
```
